32 devices in a mesh: dp: 4 (over x, core), fsdp: 8 (over z, y).
Axes of the slice: x: 2, y: 2, z: 4, core: 2. Of those that a mesh axis runs over, the one named last changes fastest.
Arguments:
- patch_embeddings: bfloat16 [59392, 384], P(('dp', 'fsdp')), may hold values from -25 to 25, as said below
- view_side_tokens: int32 [512], P(('dp', 'fsdp')), may hold values from 6 to 14, as said below
- projection_masters: float32 [12, 384, 384], P(None, 'fsdp'), may hold values from -2 to 2, as said below
- channel_coefficients: float32 [29, 384], P(None, 'fsdp'), may hold values from -1.2 to 1.3, as said below
- head_sharpness: float32 [8], replicated, may hold values from 12 to 24
- output_adjoint: bfloat16 [59392, 384], P(('dp', 'fsdp')), may hold values from -6 to 6
- leading_covariance: float32 [16, 384, 384], P('fsdp'), as said below
- trailing_covariance: float32 [16, 384, 384], P('fsdp'), as said below
- leading_root_preconditioner: float32 [16, 384, 384], P('fsdp'), as said below
- trailing_root_preconditioner: float32 [16, 384, 384], P('fsdp'), as said below
- channel_energy_average: float32 [29, 384], P(None, 'fsdp'), as said below
- sharpness_energy_average: float32 [8], replicated, as said below
- storage_position_map: int32 [12], replicated, may hold values from 0 to 15, as said below
Outputs:
- layer_output: bfloat16 [59392, 384], P(('dp', 'fsdp'))
- incoming_tokens_grad: bfloat16 [59392, 384], P(('dp', 'fsdp'))
- projection_derivative_sum: float32 [12, 384, 384], P(None, 'fsdp')
- leading_covariance_renewed: float32 [16, 384, 384], P('fsdp')
- trailing_covariance_renewed: float32 [16, 384, 384], P('fsdp')
- projection_updated: float32 [12, 384, 384], P(None, 'fsdp')
- weight_copy: bfloat16 [12, 384, 384], P(None, 'fsdp')
- channel_params_grad: float32 [29, 384], P(None, 'fsdp')
- channel_energy_renewed: float32 [29, 384], P(None, 'fsdp')
- channel_params_updated: float32 [29, 384], P(None, 'fsdp')
- sharpness_derivative: float32 [8], replicated
- sharpness_energy_renewed: float32 [8], replicated
- sharpness_updated: float32 [8], replicated
The draws below stay inside these ranges and needn't reach their ends.
Inputs may be any that keep to these rules, and one draw needn't show every extreme that they name: `view_side_tokens`: the crops of one device fill its first rows in order, a crop of side s holding s * s rows; the rows after them are not read; on some device they fill all 1856 rows. Distinct. Block b's statistics and roots are in slot storage_position_map[b], which index storage_position_map[b] // 2 of fsdp holds; some index of fsdp holds 2 blocks; the roots of slots without a block are not read. `patch_embeddings`: Activations. `projection_masters`: blocks of weights. `channel_coefficients`: Gains, biases and taps. `leading_covariance`: Symmetric. `trailing_covariance`: Symmetric. `leading_root_preconditioner`: Symmetric. `trailing_root_preconditioner`: Symmetric. `channel_energy_average`: Positive. `sharpness_energy_average`: Positive.
All inputs are finite; a program needn't handle non-finite values.
Results may differ from the reference program's by a relative error of at most 0.007.
The reference program's roundings to bfloat16 on the way count: a program that leaves them out, or rounds other values in their place, can miss the bound.
Values may be sent and summed in bfloat16 or wider, within the bound.
A program may use at most 256 MiB of HBM per device.

```python
import math
import jax
import jax.numpy as jnp
from jax import lax

CHANNEL_DIM = 384
HEAD_NUMBER = 8
HDIM = 48
MLP = 1536
GSIDE = 14
LSIDE = 6
NV = 29
CROPS_DEV = 16
GMAX = 8
TOK_DEV = 1856
TOKENS = 59392
NBLK = 12
SLOTS = 16
N_DP = 4
N_FSDP = 8


def live_count():
    return N_DP * N_FSDP * (LSIDE * LSIDE * CROPS_DEV + (GSIDE * GSIDE - LSIDE * LSIDE) * GMAX * 0.5)


def grad_scale():
    return 0.4 * math.sqrt(live_count())


def state_scale():
    return 0.8 * math.sqrt(live_count())


def square_table(key, center, low_factor, high_factor, off_weight):
    diagonal_key, noise_key = jax.random.split(key)
    diagonal = jnp.exp(jax.random.uniform(diagonal_key, (SLOTS, CHANNEL_DIM), jnp.float32, math.log(low_factor), math.log(high_factor)))
    noise = jnp.clip(jax.random.normal(noise_key, (SLOTS, CHANNEL_DIM, CHANNEL_DIM), jnp.float32), -4.0, 4.0)
    symmetric = (noise + jnp.swapaxes(noise, 1, 2)) * (off_weight / math.sqrt(2.0 * CHANNEL_DIM))
    identity = (jnp.arange(CHANNEL_DIM)[:, None] == jnp.arange(CHANNEL_DIM)[None, :]).astype(jnp.float32)
    return center * (identity[None, :, :] * diagonal[:, None, :] + symmetric)


def draw_patch_embeddings(key, part):
    key = jax.random.fold_in(key, 11)
    normal_key, row_key, column_key = jax.random.split(key, 3)
    normal_part = jnp.clip(jax.random.normal(normal_key, (TOKENS, CHANNEL_DIM), jnp.float32), -5.0, 5.0)
    row_scale = jnp.exp(jax.random.uniform(row_key, (TOKENS, 1), jnp.float32, math.log(0.5), math.log(2.0)))
    column_scale = jnp.exp(jax.random.uniform(column_key, (1, CHANNEL_DIM), jnp.float32, math.log(0.4), math.log(2.5)))
    return (normal_part * row_scale * column_scale).astype(jnp.bfloat16)


def draw_view_side_tokens(key, part):
    key = jax.random.fold_in(key, 12)
    jitter_key, busiest_key, order_key = jax.random.split(key, 3)
    device_total = N_DP * N_FSDP
    device = jnp.arange(device_total, dtype=jnp.int32)
    outer_index = device // N_FSDP
    inner_index = device % N_FSDP
    outer_span = max(N_DP - 1, 1)
    inner_span = max(N_FSDP - 1, 1)
    rising = GMAX * (inner_index * outer_span + outer_index * inner_span) // (2 * outer_span * inner_span)
    jitter = jax.random.randint(jitter_key, (device_total,), -1, 2, dtype=jnp.int32)
    global_count = jnp.clip(rising + jitter, 0, GMAX)
    busiest = jax.random.randint(busiest_key, (), 0, device_total, dtype=jnp.int32)
    global_count = jnp.where(device == busiest, GMAX, global_count)
    order_keys = jax.random.split(order_key, device_total)
    crop_order = jax.vmap(lambda one_key: jax.random.permutation(one_key, CROPS_DEV))(order_keys)
    side_table = jnp.where(crop_order < global_count[:, None], GSIDE, LSIDE)
    return side_table.reshape(-1).astype(jnp.int32)


def draw_projection_masters(key, part):
    key = jax.random.fold_in(key, 13)
    normal_part = jnp.clip(jax.random.normal(key, (NBLK, CHANNEL_DIM, CHANNEL_DIM), jnp.float32), -4.0, 4.0)
    block_index = jnp.arange(NBLK)[:, None, None]
    block_scale = jnp.where(block_index == 3, 2.0 / math.sqrt(CHANNEL_DIM), jnp.where(block_index >= NBLK - MLP // CHANNEL_DIM, 1.0 / math.sqrt(MLP), 1.0 / math.sqrt(CHANNEL_DIM)))
    return normal_part * block_scale


def draw_channel_coefficients(key, part):
    key = jax.random.fold_in(key, 14)
    gain_key, signed_key = jax.random.split(key)
    gain_values = jax.random.uniform(gain_key, (NV, CHANNEL_DIM), jnp.float32, 0.7, 1.3)
    signed = jnp.clip(jax.random.normal(signed_key, (NV, CHANNEL_DIM), jnp.float32), -3.0, 3.0)
    row_index = jnp.arange(NV)[:, None]
    bias_rows = (row_index == 1) | (row_index == 4) | (row_index == 6) | (row_index == 9)
    return jnp.where(row_index >= 11, signed / 3.0, jnp.where(bias_rows, 0.2 * signed, gain_values))


def draw_leading_covariance(key, part):
    key = jax.random.fold_in(key, 15)
    return square_table(key, CHANNEL_DIM * state_scale() ** 2, 1.0, 4.0, 0.5)


def draw_trailing_covariance(key, part):
    key = jax.random.fold_in(key, 16)
    return square_table(key, CHANNEL_DIM * state_scale() ** 2, 1.0, 4.0, 0.5)


def draw_leading_root_preconditioner(key, part):
    key = jax.random.fold_in(key, 17)
    return square_table(key, (CHANNEL_DIM * grad_scale() ** 2) ** (-0.25), 1.0, 2.0, 0.5)


def draw_trailing_root_preconditioner(key, part):
    key = jax.random.fold_in(key, 18)
    return square_table(key, (CHANNEL_DIM * grad_scale() ** 2) ** (-0.25), 1.0, 2.0, 0.5)


def draw_channel_energy_average(key, part):
    key = jax.random.fold_in(key, 19)
    factor = jnp.exp(jax.random.uniform(key, (NV, CHANNEL_DIM), jnp.float32, 0.0, math.log(4.0)))
    return factor * grad_scale() ** 2


def draw_sharpness_energy_average(key, part):
    key = jax.random.fold_in(key, 20)
    factor = jnp.exp(jax.random.uniform(key, (HEAD_NUMBER,), jnp.float32, 0.0, math.log(4.0)))
    return factor * (5.0 * grad_scale()) ** 2


def draw_storage_position_map(key, part):
    key = jax.random.fold_in(key, 21)
    return jax.random.permutation(key, SLOTS)[:NBLK].astype(jnp.int32)


def levels(rng, shape, shards, smallest, high):
    factor_of, own = 1.0, jax.random.fold_in(rng, 6)
    for dim, parts in shards:
        steps = jnp.exp(jax.random.uniform(jax.random.fold_in(own, dim), (parts,), jnp.float32, smallest / len(shards), high / len(shards)))
        factor_of = factor_of * jnp.repeat(steps, shape[dim] // parts).reshape([-1 if axis == dim else 1 for axis in range(len(shape))])
    return factor_of


def gaussian(stream_key, extent, width, bound, cuts=(), kind=jnp.bfloat16):
    array = width * jax.random.normal(stream_key, extent, jnp.float32)
    if cuts:
        array = array * levels(stream_key, extent, cuts, -0.22, 0.18)
    return jnp.clip(array, -bound, bound).astype(kind)


def setup_inputs(seed: int = 0) -> dict:
    seeds = jax.random.split(jax.random.key(seed), 14)
    patch_embeddings = draw_patch_embeddings(jax.random.fold_in(seeds[13], 71), 0)
    view_side_tokens = draw_view_side_tokens(jax.random.fold_in(seeds[13], 71), 0)
    projection_masters = draw_projection_masters(jax.random.fold_in(seeds[13], 71), 0)
    channel_coefficients = draw_channel_coefficients(jax.random.fold_in(seeds[13], 71), 0)
    head_sharpness = jnp.clip(jax.random.uniform(seeds[4], (HEAD_NUMBER,), jnp.float32, 12.0, 24.0), 12.0, 24.0)
    output_adjoint = gaussian(seeds[5], (TOKENS, CHANNEL_DIM), 1.0, 6.0, ((0, 32),))
    leading_covariance = draw_leading_covariance(jax.random.fold_in(seeds[13], 71), 0)
    trailing_covariance = draw_trailing_covariance(jax.random.fold_in(seeds[13], 71), 0)
    leading_root_preconditioner = draw_leading_root_preconditioner(jax.random.fold_in(seeds[13], 71), 0)
    trailing_root_preconditioner = draw_trailing_root_preconditioner(jax.random.fold_in(seeds[13], 71), 0)
    channel_energy_average = draw_channel_energy_average(jax.random.fold_in(seeds[13], 71), 0)
    sharpness_energy_average = draw_sharpness_energy_average(jax.random.fold_in(seeds[13], 71), 0)
    storage_position_map = draw_storage_position_map(jax.random.fold_in(seeds[13], 71), 0)
    return {"patch_embeddings": patch_embeddings, "view_side_tokens": view_side_tokens, "projection_masters": projection_masters, "channel_coefficients": channel_coefficients, "head_sharpness": head_sharpness, "output_adjoint": output_adjoint, "leading_covariance": leading_covariance, "trailing_covariance": trailing_covariance, "leading_root_preconditioner": leading_root_preconditioner, "trailing_root_preconditioner": trailing_root_preconditioner, "channel_energy_average": channel_energy_average, "sharpness_energy_average": sharpness_energy_average, "storage_position_map": storage_position_map}


@jax.custom_vjp
def low(v):
    return lax.optimization_barrier(v.astype(jnp.bfloat16)).astype(jnp.float32)

@jax.custom_vjp
def low_back(v):
    return v

def low_keep(v):
    return (low(v), None)

def low_pass(kept, grad):
    return (grad,)

def back_keep(v):
    return (v, None)

def back_low(kept, grad):
    return (low(grad),)
low.defvjp(low_keep, low_pass)
low_back.defvjp(back_keep, back_low)
exact_multiply = lax.Precision.HIGHEST
norm_epsilon = 1e-06
batch_epsilon = 1e-05
attention_epsilon = 1e-06
covariance_forgetting = 0.5
weight_rate = 0.5
vector_rate = 0.1
sharpness_step_size = 2.0
energy_epsilon = 1e-08

def crop_layout(view_sides_sequence, tok_rows):
    crop_total = view_sides_sequence.shape[0]
    crop_cells = (view_sides_sequence * view_sides_sequence).astype(jnp.int32)
    crop_ends = jnp.cumsum(crop_cells).astype(jnp.int32)
    crop_starts = (crop_ends - crop_cells).astype(jnp.int32)
    position = jnp.arange(GSIDE * GSIDE, dtype=jnp.int32)
    grid_row = position // GSIDE
    grid_column = position % GSIDE
    inside = (grid_row[None, :] < view_sides_sequence[:, None]) & (grid_column[None, :] < view_sides_sequence[:, None])
    incoming_tensor = jnp.where(inside, crop_starts[:, None] + grid_row[None, :] * view_sides_sequence[:, None] + grid_column[None, :], tok_rows).astype(jnp.int32)
    row_index = jnp.arange(tok_rows, dtype=jnp.int32)
    crop_index = lax.optimization_barrier(jnp.sum((crop_ends[None, :] <= row_index[:, None]).astype(jnp.int32), axis=1)).astype(jnp.int32)
    live_rows = row_index < crop_ends[-1]
    crop_safe = jnp.minimum(crop_index, crop_total - 1).astype(jnp.int32)
    crop_match = crop_safe[:, None] == jnp.arange(crop_total, dtype=jnp.int32)[None, :]
    row_side = lax.optimization_barrier(jnp.sum(jnp.where(crop_match, view_sides_sequence[None, :], 0), axis=1)).astype(jnp.int32)
    row_start = lax.optimization_barrier(jnp.sum(jnp.where(crop_match, crop_starts[None, :], 0), axis=1)).astype(jnp.int32)
    offset = row_index - row_start
    target = jnp.where(live_rows, crop_safe * (GSIDE * GSIDE) + offset // row_side * GSIDE + offset % row_side, crop_total * GSIDE * GSIDE).astype(jnp.int32)
    return (inside, incoming_tensor, target, live_rows)

def regroup_into_grid(values, incoming_tensor):
    padded = jnp.concatenate([values, jnp.zeros((1, values.shape[1]), values.dtype)], axis=0)
    return jnp.take(padded, incoming_tensor, axis=0)

def into_rows(grid_cells, target):
    flattened = grid_cells.reshape(-1, grid_cells.shape[-1])
    padded = jnp.concatenate([flattened, jnp.zeros((1, flattened.shape[1]), flattened.dtype)], axis=0)
    return jnp.take(padded, target, axis=0)

def layer_norm(skip_path_sum, norm_gain, norm_bias):
    center = lax.optimization_barrier(jnp.mean(skip_path_sum, axis=-1, keepdims=True))
    shifted = skip_path_sum - center
    spread = lax.optimization_barrier(jnp.mean(shifted * shifted, axis=-1, keepdims=True))
    return shifted * lax.rsqrt(spread + norm_epsilon) * norm_gain + norm_bias

def exact_gelu(values):
    return jax.nn.gelu(values, approximate=False)

def depthwise(grid_cells, tap_table):
    grid_side = grid_cells.shape[1]
    padded = jnp.pad(grid_cells, ((0, 0), (1, 1), (1, 1), (0, 0)))
    result = jnp.zeros_like(grid_cells)
    for row_shift in range(3):
        for column_shift in range(3):
            result = result + padded[:, row_shift:row_shift + grid_side, column_shift:column_shift + grid_side, :] * tap_table[3 * row_shift + column_shift]
    return result

def channel_covariance_mixing(asking_grid, lookup_grid, content_grid, head_sharpness):
    crop_count, place_count, feature_count = asking_grid.shape
    split_shape = (crop_count, place_count, HEAD_NUMBER, HDIM)
    query_heads = asking_grid.reshape(split_shape)
    key_heads = lookup_grid.reshape(split_shape)
    value_heads = content_grid.reshape(split_shape)
    asking_unit_lines = query_heads * lax.rsqrt(lax.optimization_barrier(jnp.sum(query_heads * query_heads, axis=1, keepdims=True)) + attention_epsilon)
    lookup_unit_lines = key_heads * lax.rsqrt(lax.optimization_barrier(jnp.sum(key_heads * key_heads, axis=1, keepdims=True)) + attention_epsilon)
    affinity_grid = jnp.einsum('xpom,xpoy->xomy', asking_unit_lines, lookup_unit_lines, precision=exact_multiply) * head_sharpness[None, :, None, None]
    row_max = lax.optimization_barrier(jnp.max(affinity_grid, axis=-1, keepdims=True))
    exp_scores = jnp.exp(affinity_grid - row_max)
    attention = exp_scores / lax.optimization_barrier(jnp.sum(exp_scores, axis=-1, keepdims=True))
    mixed = jnp.einsum('chij,cphj->cphi', attention, value_heads, precision=exact_multiply)
    return mixed.reshape(crop_count, place_count, feature_count)

def mixing_share(skip_path_sum, view_sides_sequence, layer_collection, coefficient_catalog, head_sharpness):
    inside, incoming_tensor, target, live_rows = crop_layout(view_sides_sequence, skip_path_sum.shape[0])
    first_norm = low(layer_norm(skip_path_sum, coefficient_catalog[0], coefficient_catalog[1]))
    mapped_lines = low_back(jnp.einsum('td,sde->tse', first_norm, layer_collection[0:3], precision=exact_multiply))
    combined_grid = channel_covariance_mixing(regroup_into_grid(mapped_lines[:, 0], incoming_tensor), regroup_into_grid(mapped_lines[:, 1], incoming_tensor), regroup_into_grid(mapped_lines[:, 2], incoming_tensor), head_sharpness)
    mixed_rows = low(into_rows(combined_grid, target))
    attention_out = low_back(jnp.dot(mixed_rows, layer_collection[3], precision=exact_multiply))
    after_attention = skip_path_sum + coefficient_catalog[2] * attention_out
    second_norm = layer_norm(after_attention, coefficient_catalog[3], coefficient_catalog[4])
    conv_grid = regroup_into_grid(second_norm, incoming_tensor).reshape(view_sides_sequence.shape[0], GSIDE, GSIDE, skip_path_sum.shape[1])
    activated = exact_gelu(depthwise(conv_grid, coefficient_catalog[11:20]))
    return (after_attention, activated)

def mix_part(after_attention, activated, view_sides_sequence, layer_collection, coefficient_catalog, batch_center, batch_scale):
    inside, incoming_tensor, target, live_rows = crop_layout(view_sides_sequence, after_attention.shape[0])
    valid_mask = inside.astype(jnp.float32).reshape(view_sides_sequence.shape[0], GSIDE, GSIDE, 1)
    batch_out = ((activated - batch_center) * batch_scale * coefficient_catalog[5] + coefficient_catalog[6]) * valid_mask
    conv_second = depthwise(batch_out, coefficient_catalog[20:29])
    local_out = into_rows(conv_second.reshape(view_sides_sequence.shape[0], GSIDE * GSIDE, after_attention.shape[1]), target)
    after_local = after_attention + coefficient_catalog[7] * local_out
    third_norm = low(layer_norm(after_local, coefficient_catalog[8], coefficient_catalog[9]))
    expand = MLP // CHANNEL_DIM
    hidden_pre = low_back(jnp.einsum('td,rde->tre', third_norm, layer_collection[4:4 + expand], precision=exact_multiply))
    hidden_low = low(exact_gelu(hidden_pre))
    feed_out = low_back(jnp.einsum('trd,rde->te', hidden_low, layer_collection[4 + expand:], precision=exact_multiply))
    return (after_local + coefficient_catalog[10] * feed_out) * live_rows.astype(jnp.float32)[:, None]

def complete_layer(skip_path_sum, view_sides_sequence, layer_collection, coefficient_catalog, head_sharpness):
    layer_collection = low(layer_collection)
    coefficient_catalog = low(coefficient_catalog)

    def first_pass(couple_bundle):
        return mixing_share(couple_bundle[0], couple_bundle[1], layer_collection, coefficient_catalog, head_sharpness)
    after_attention, activated = lax.map(jax.checkpoint(first_pass), (skip_path_sum, view_sides_sequence))
    valid_all = lax.map(lambda sides_in: crop_layout(sides_in, TOK_DEV)[0], view_sides_sequence)
    valid_mask = valid_all.astype(jnp.float32).reshape(activated.shape[0], activated.shape[1], GSIDE, GSIDE, 1)
    cell_count = jnp.sum(valid_mask)
    masked = activated * valid_mask
    batch_center = lax.optimization_barrier(jnp.sum(masked, axis=(0, 1, 2, 3))) / cell_count
    batch_scale = lax.rsqrt(lax.optimization_barrier(jnp.sum(masked * activated, axis=(0, 1, 2, 3))) / cell_count - batch_center * batch_center + batch_epsilon)

    def second_pass(trio):
        return mix_part(trio[0], trio[1], trio[2], layer_collection, coefficient_catalog, batch_center, batch_scale)
    return lax.map(jax.checkpoint(second_pass), (after_attention, activated, view_sides_sequence))

def reference(patch_embeddings, view_side_tokens, projection_masters, channel_coefficients, head_sharpness, output_adjoint, leading_covariance, trailing_covariance, leading_root_preconditioner, trailing_root_preconditioner, channel_energy_average, sharpness_energy_average, storage_position_map):
    device_count = patch_embeddings.shape[0] // TOK_DEV
    skip_path_sum = patch_embeddings.astype(jnp.float32).reshape(device_count, TOK_DEV, CHANNEL_DIM)
    view_sides_sequence = view_side_tokens.reshape(device_count, CROPS_DEV)
    incoming_entry = output_adjoint.astype(jnp.float32).reshape(device_count, TOK_DEV, CHANNEL_DIM)

    def evaluate_layer(residual_in, blocks_in, table_in, temper_in):
        return complete_layer(residual_in, view_sides_sequence, blocks_in, table_in, temper_in)
    layer_output, backprop_rule = jax.vjp(evaluate_layer, skip_path_sum, projection_masters, channel_coefficients, head_sharpness)
    incoming_tokens_grad, projection_derivative_sum, channel_params_grad, sharpness_derivative = backprop_rule(incoming_entry)
    slot_index = jnp.arange(SLOTS, dtype=jnp.int32)
    slot_match = storage_position_map[None, :] == slot_index[:, None]
    slot_filled = jnp.any(slot_match, axis=1).astype(jnp.float32)[:, None, None]
    slot_block = lax.optimization_barrier(jnp.sum(jnp.where(slot_match, jnp.arange(NBLK, dtype=jnp.int32)[None, :], 0), axis=1)).astype(jnp.int32)
    owned_grad = jnp.take(projection_derivative_sum, slot_block, axis=0) * slot_filled
    leading_covariance_renewed = covariance_forgetting * leading_covariance + (1.0 - covariance_forgetting) * jnp.einsum('sij,skj->sik', owned_grad, owned_grad, precision=exact_multiply)
    trailing_covariance_renewed = covariance_forgetting * trailing_covariance + (1.0 - covariance_forgetting) * jnp.einsum('sji,sjk->sik', owned_grad, owned_grad, precision=exact_multiply)
    halfway = jnp.einsum('sij,sjk->sik', leading_root_preconditioner, owned_grad, precision=exact_multiply)
    conditioned = jnp.einsum('sij,sjk->sik', halfway, trailing_root_preconditioner, precision=exact_multiply)
    update = jnp.take(conditioned, storage_position_map, axis=0)
    projection_updated = projection_masters - weight_rate * update
    channel_energy_renewed = covariance_forgetting * channel_energy_average + (1.0 - covariance_forgetting) * channel_params_grad * channel_params_grad
    channel_params_updated = channel_coefficients - vector_rate * channel_params_grad / (jnp.sqrt(channel_energy_renewed) + energy_epsilon)
    sharpness_energy_renewed = covariance_forgetting * sharpness_energy_average + (1.0 - covariance_forgetting) * sharpness_derivative * sharpness_derivative
    sharpness_updated = head_sharpness - sharpness_step_size * sharpness_derivative / (jnp.sqrt(sharpness_energy_renewed) + energy_epsilon)
    return (layer_output.reshape(-1, CHANNEL_DIM).astype(jnp.bfloat16), incoming_tokens_grad.reshape(-1, CHANNEL_DIM).astype(jnp.bfloat16), projection_derivative_sum, leading_covariance_renewed, trailing_covariance_renewed, projection_updated, projection_updated.astype(jnp.bfloat16), channel_params_grad, channel_energy_renewed, channel_params_updated, sharpness_derivative, sharpness_energy_renewed, sharpness_updated)
```

```python
import functools

import jax
import jax.numpy as jnp
from jax import lax
from jax.experimental import pallas as pl
from jax.experimental.pallas import tpu as pltpu
from jax.sharding import PartitionSpec as P

HEAD_NUMBER = 8
HDIM = 48
HEAD_PAD = 64
LANES = 128
HEAD_PAIRS = HEAD_NUMBER // 2
PAD_WIDTH = HEAD_NUMBER * HEAD_PAD
HALF_WIDTH = PAD_WIDTH // 2
LEAD = 16
TAIL = 32
SMALL_WINDOW = 48
LARGE_WINDOW = 208
VMEM_LIMIT = 58 * 2**20

norm_epsilon = 1e-06
batch_epsilon = 1e-05
attention_epsilon = 1e-06
covariance_forgetting = 0.5
weight_rate = 0.5
vector_rate = 0.1
sharpness_step_size = 2.0
energy_epsilon = 1e-08

F32 = jnp.float32
BF16 = jnp.bfloat16
VMEM_SPEC = pl.BlockSpec(memory_space=pltpu.VMEM)
ANY_SPEC = pl.BlockSpec(memory_space=pl.ANY)
SMEM_SPEC = pl.BlockSpec(memory_space=pltpu.SMEM)


def dot(left, right):
    return lax.dot_general(left, right, (((1,), (0,)), ((), ())), preferred_element_type=F32)


def dot_rows(left, right):
    return lax.dot_general(left, right, (((0,), (0,)), ((), ())), preferred_element_type=F32)


def dot_lanes(left, right):
    return lax.dot_general(left, right, (((1,), (1,)), ((), ())), preferred_element_type=F32)


def split(values):
    high = values.astype(BF16)
    return high, (values - high.astype(F32)).astype(BF16)


def dot_split(product, left, right):
    return (
        product(left[0], right[0]) + product(left[0], right[1]) + product(left[1], right[0])
    )


def fold(values):
    total = values[0:8]
    for first in range(8, values.shape[0], 8):
        total = total + values[first : first + 8]
    return total


def gelu_parts(values):
    magnitude = jnp.abs(values) * 0.7071067811865476
    base = 1.0 + 0.3275911 * magnitude
    guess = pl.reciprocal(base, approx=True)
    slot = guess * (2.0 - base * guess)
    series = slot * (
        0.127414796
        + slot
        * (-0.142248368 + slot * (0.7107068705 + slot * (-0.7265760135 + slot * 0.5307027145)))
    )
    bell = jnp.exp(-0.5 * values * values)
    lower = series * bell
    return jnp.where(values >= 0, 1.0 - lower, lower), bell


def gelu_slope(values, share, bell):
    return share + values * bell * 0.3989422804014327


def head_map(dtype):
    feature = lax.broadcasted_iota(jnp.int32, (HEAD_NUMBER * HDIM, PAD_WIDTH), 0)
    lane = lax.broadcasted_iota(jnp.int32, (HEAD_NUMBER * HDIM, PAD_WIDTH), 1)
    inner = lane & (HEAD_PAD - 1)
    hit = (inner < HDIM) & ((lane >> 6) * HDIM + inner == feature)
    return hit.astype(F32).astype(dtype)


def centered(values):
    center = jnp.sum(values, axis=-1, keepdims=True) * (1.0 / values.shape[-1])
    shifted = values - center
    spread = jnp.sum(shifted * shifted, axis=-1, keepdims=True) * (1.0 / values.shape[-1])
    scale = lax.rsqrt(spread + norm_epsilon)
    return shifted * scale, scale


def norm_back(grad, unit, scale):
    size = 1.0 / grad.shape[-1]
    middle = jnp.sum(grad, axis=-1, keepdims=True) * size
    slope = jnp.sum(grad * unit, axis=-1, keepdims=True) * size
    return scale * (grad - middle - unit * slope)


def tile_rows(count):
    for parts in range(4, count // 16 + 1):
        if count % (16 * parts) == 0:
            return count // parts
    return count


def live_total(sides_ref):
    return lax.fori_loop(
        0, sides_ref.shape[0], lambda c, t: t + sides_ref[c] * sides_ref[c], jnp.int32(0)
    )


def row_mask(first, rows, width, limit):
    return lax.broadcasted_iota(jnp.int32, (rows, width), 0) + first < limit


def for_groups(sides_ref, step, carry):
    def crop_body(crop, state):
        start, carry = state
        side = sides_ref[crop]
        cells = side * side
        inverse = 1.0 / jnp.full((8, LANES), side, jnp.int32).astype(F32)
        lines = lax.broadcasted_iota(jnp.int32, (8, LANES), 0)

        def group_body(group, carry):
            for part in range(2):
                row = pl.multiple_of((group * 2 + part) * 8, 8)
                place = lines + (row - start)
                line = ((place.astype(F32) + 0.5) * inverse).astype(jnp.int32)
                column = place - line * side
                inside = (place >= 0) & (place < cells)
                masks = (
                    inside,
                    column >= 1,
                    column < side - 1,
                    place >= side,
                    place < cells - side,
                )
                carry = step(row, side, masks, carry)
            return carry

        carry = lax.fori_loop(start // 16, (start + cells + 15) // 16, group_body, carry)
        return start + cells, carry

    return lax.fori_loop(0, sides_ref.shape[0], crop_body, (jnp.int32(0), carry))[1]


def conv_forward(source, chunk, row, side, masks, taps):
    inside, left_ok, right_ok, up_ok, down_ok = masks
    total = None
    for shift in (-1, 0, 1):
        base = LEAD + row + shift * side
        middle = source[chunk, pl.ds(base, 8), :]
        left = jnp.where(left_ok, source[chunk, pl.ds(base - 1, 8), :], 0.0)
        right = jnp.where(right_ok, source[chunk, pl.ds(base + 1, 8), :], 0.0)
        first = 3 * (shift + 1)
        value = taps[first] * left + taps[first + 1] * middle + taps[first + 2] * right
        if shift == -1:
            value = jnp.where(up_ok, value, 0.0)
        if shift == 1:
            value = jnp.where(down_ok, value, 0.0)
        total = value if total is None else total + value
    return total


def conv_backward(source, chunk, row, side, masks, taps, own, tap_sums):
    inside, left_ok, right_ok, up_ok, down_ok = masks
    total = None
    tap_sums = list(tap_sums)
    for shift in (-1, 0, 1):
        base = LEAD + row + shift * side
        row_ok = {-1: up_ok, 0: None, 1: down_ok}[shift]
        for sway in (-1, 0, 1):
            column_ok = {-1: left_ok, 0: None, 1: right_ok}[sway]
            value = source[chunk, pl.ds(base + sway, 8), :]
            keep = inside
            if row_ok is not None:
                keep = keep & row_ok
            if column_ok is not None:
                keep = keep & column_ok
            value = jnp.where(keep, value, 0.0)
            index = 3 * (1 - shift) + (1 - sway)
            term = taps[index] * value
            total = term if total is None else total + term
            tap_sums[index] = tap_sums[index] + own * value
    return total, tuple(tap_sums)


def chunk_lanes(chunk):
    return slice(chunk * LANES, (chunk + 1) * LANES)


def tap_vectors(table_ref, first, chunk):
    return [
        jnp.broadcast_to(table_ref[first + k : first + k + 1, chunk_lanes(chunk)], (8, LANES))
        for k in range(9)
    ]


def for_crops(sides_ref, row_count, step):
    def crop_body(crop, start):
        side = sides_ref[crop]
        cells = side * side
        for window, fits in ((SMALL_WINDOW, side <= 6), (LARGE_WINDOW, side > 6)):

            @pl.when(fits)
            def _():
                first = pl.multiple_of(
                    jnp.minimum(start // 8, (row_count - window) // 8) * 8, 8
                )
                place = lax.broadcasted_iota(jnp.int32, (window, HALF_WIDTH), 0) + (first - start)
                step(crop, pl.ds(first, window), (place >= 0) & (place < cells))

        return start + cells

    lax.fori_loop(0, sides_ref.shape[0], crop_body, jnp.int32(0))


def pair_lanes():
    return lax.broadcasted_iota(jnp.int32, (HDIM, LANES), 1) < HEAD_PAD


def pair_part(block, pair):
    first = pair * LANES
    lanes = slice(first, first + LANES)
    return jnp.where(
        pair_lanes(),
        block[first : first + HDIM, lanes],
        block[first + HEAD_PAD : first + HEAD_PAD + HDIM, lanes],
    )


def spread_pair(target, half, pair, values):
    first = pair * LANES
    lanes = slice(first, first + LANES)
    parts = split(values)
    for index in range(2):
        value = parts[index].astype(F32)
        target[half, index, first : first + HDIM, lanes] = jnp.where(
            pair_lanes(), value, 0.0
        ).astype(BF16)
        target[half, index, first + HEAD_PAD : first + HEAD_PAD + HDIM, lanes] = jnp.where(
            pair_lanes(), 0.0, value
        ).astype(BF16)


def pair_sharpness(sharp_ref, pair):
    lane = lax.broadcasted_iota(jnp.int32, (1, LANES), 1)
    return jnp.where(lane < HEAD_PAD, sharp_ref[2 * pair], sharp_ref[2 * pair + 1])


def units(values):
    scale = lax.rsqrt(jnp.sum(values * values, axis=0, keepdims=True) + attention_epsilon)
    return values * scale, scale


def mixing_forward_kernel(
    sides_ref,
    sharp_ref,
    input_ref,
    weight_ref,
    table_ref,
    x1_ref,
    qkv_ref,
    mixed_ref,
    scores_ref,
    attention_ref,
    u_ref,
    e_ref,
    sums_ref,
    head_weights,
    out_weight,
    first_low,
    mixed,
    attention_out,
    conv_in,
    spread,
):
    row_count, width = input_ref.shape
    chunks = width // LANES
    tile = tile_rows(row_count)
    total_live = live_total(sides_ref)
    mapping = head_map(BF16)
    for part in range(3):
        head_weights[:, part * PAD_WIDTH : (part + 1) * PAD_WIDTH] = dot(
            weight_ref[part], mapping
        ).astype(BF16)
    spread[...] = jnp.zeros_like(spread)

    def first_norm(step, _):
        rows = pl.ds(pl.multiple_of(step * 32, 32), 32)
        unit, _ = centered(input_ref[rows, :].astype(F32))
        first_low[rows, :] = (unit * table_ref[0:1, :] + table_ref[1:2, :]).astype(BF16)
        mixed[rows, :] = jnp.zeros((32, PAD_WIDTH), F32)
        return 0

    lax.fori_loop(0, row_count // 32, first_norm, 0)

    @pl.loop(0, row_count // tile)
    def _(step):
        rows = pl.ds(pl.multiple_of(step * tile, 16), tile)
        for part in range(3):
            lanes = slice(part * PAD_WIDTH, (part + 1) * PAD_WIDTH)
            qkv_ref[rows, lanes] = dot(first_low[rows, :], head_weights[:, lanes])

    def crop_step(crop, rows, keep):
        for half in range(2):
            lanes = [
                slice(part * PAD_WIDTH + half * HALF_WIDTH, part * PAD_WIDTH + (half + 1) * HALF_WIDTH)
                for part in range(3)
            ]
            query = units(jnp.where(keep, qkv_ref[rows, lanes[0]], 0.0))[0]
            key = units(jnp.where(keep, qkv_ref[rows, lanes[1]], 0.0))[0]
            block = dot_split(dot_rows, split(key), split(query))
            for pair in range(2):
                scores = pair_part(block, pair)
                scores_ref[crop, 2 * half + pair] = scores
                scores = scores * pair_sharpness(sharp_ref, 2 * half + pair)
                scores = jnp.exp(scores - jnp.max(scores, axis=0, keepdims=True))
                shares = scores / jnp.sum(scores, axis=0, keepdims=True)
                attention_ref[crop, 2 * half + pair] = shares
                spread_pair(spread, half, pair, shares)
            result = dot_split(
                dot, split(qkv_ref[rows, lanes[2]]), (spread[half, 0], spread[half, 1])
            )
            mixed[rows, lanes[0]] = jnp.where(keep, result, mixed[rows, lanes[0]])

    for_crops(sides_ref, row_count, crop_step)

    out_weight[...] = dot_rows(mapping, weight_ref[3]).astype(BF16)

    @pl.loop(0, row_count // tile)
    def _(step):
        rows = pl.ds(pl.multiple_of(step * tile, 16), tile)
        low = mixed[rows, :].astype(BF16)
        mixed_ref[rows, :] = low
        attention_out[rows, :] = dot(low, out_weight[...])

    def second_norm(step, _):
        first = pl.multiple_of(step * 32, 32)
        rows = pl.ds(first, 32)
        value = input_ref[rows, :].astype(F32) + table_ref[2:3, :] * attention_out[rows, :]
        x1_ref[rows, :] = value
        unit, _ = centered(value)
        value = unit * table_ref[3:4, :] + table_ref[4:5, :]
        for chunk in range(chunks):
            conv_in[chunk, pl.ds(LEAD + first, 32), :] = value[:, chunk_lanes(chunk)]
            u_ref[chunk, rows, :] = jnp.zeros((32, LANES), F32)
            e_ref[chunk, rows, :] = jnp.zeros((32, LANES), F32)
        return 0

    lax.fori_loop(0, row_count // 32, second_norm, 0)

    zero = jnp.zeros((8, LANES), F32)
    sums_ref[...] = zero
    for chunk in range(chunks):
        taps = tap_vectors(table_ref, 11, chunk)

        def conv_step(row, side, masks, carry, chunk=chunk, taps=taps):
            value = conv_forward(conv_in, chunk, row, side, masks, taps)
            share, _ = gelu_parts(value)
            active = value * share
            rows = pl.ds(row, 8)
            u_ref[chunk, rows, :] = jnp.where(masks[0], value, u_ref[chunk, rows, :])
            e_ref[chunk, rows, :] = jnp.where(masks[0], active, e_ref[chunk, rows, :])
            active = jnp.where(masks[0], active, 0.0)
            return carry[0] + active, carry[1] + active * active

        plain, square = for_groups(sides_ref, conv_step, (zero, zero))
        sums_ref[chunk : chunk + 1, :] = jnp.sum(plain, axis=0, keepdims=True)
        sums_ref[chunks + chunk : chunks + chunk + 1, :] = jnp.sum(square, axis=0, keepdims=True)
    sums_ref[2 * chunks : 2 * chunks + 1, :] = jnp.full((1, LANES), total_live, jnp.int32).astype(F32)


def mixing_forward(sides, sharpness, inputs, weights, table):
    row_count, width = inputs.shape
    crops = sides.shape[0]
    chunks = width // LANES
    shape = jax.ShapeDtypeStruct
    return pl.pallas_call(
        mixing_forward_kernel,
        out_shape=(
            shape((row_count, width), F32),
            shape((row_count, 3 * PAD_WIDTH), F32),
            shape((row_count, PAD_WIDTH), BF16),
            shape((crops, HEAD_PAIRS, HDIM, LANES), F32),
            shape((crops, HEAD_PAIRS, HDIM, LANES), F32),
            shape((chunks, row_count, LANES), F32),
            shape((chunks, row_count, LANES), F32),
            shape((8, LANES), F32),
        ),
        in_specs=[SMEM_SPEC, SMEM_SPEC, VMEM_SPEC, VMEM_SPEC, VMEM_SPEC],
        out_specs=(VMEM_SPEC,) * 8,
        scratch_shapes=[
            pltpu.VMEM((width, 3 * PAD_WIDTH), BF16),
            pltpu.VMEM((PAD_WIDTH, width), BF16),
            pltpu.VMEM((row_count, width), BF16),
            pltpu.VMEM((row_count, PAD_WIDTH), F32),
            pltpu.VMEM((row_count, width), F32),
            pltpu.VMEM((chunks, LEAD + row_count + TAIL, LANES), F32),
            pltpu.VMEM((2, 2, HALF_WIDTH, HALF_WIDTH), BF16),
        ],
        compiler_params=pltpu.CompilerParams(vmem_limit_bytes=VMEM_LIMIT),
        name="mixing_forward",
    )(sides, sharpness, inputs, weights, table)


def batch_vectors(bn_ref, chunk, chunks):
    count = bn_ref[2 * chunks : 2 * chunks + 1, :]
    mean = bn_ref[chunk : chunk + 1, :] / count
    scale = lax.rsqrt(bn_ref[chunks + chunk : chunks + chunk + 1, :] / count - mean * mean + batch_epsilon)
    return mean, scale


def feed_kernel(
    sides_ref,
    x1_ref,
    e_ref,
    bn_ref,
    weight_ref,
    table_ref,
    adjoint_ref,
    out_ref,
    dx2_ref,
    dn_ref,
    up_grad_ref,
    down_grad_ref,
    grads_ref,
    n_ref,
    z_ref,
    dw_ref,
    x2,
    unit,
    spread,
    third_low,
    pre,
    hidden_low,
    feed,
    feed_grad,
    pre_grad,
    grads,
):
    row_count, width = x1_ref.shape
    chunks = width // LANES
    expand = weight_ref.shape[0] // 2
    tile = tile_rows(row_count)
    total_live = live_total(sides_ref)
    batch = [batch_vectors(bn_ref, chunk, chunks) for chunk in range(chunks)]
    zero = jnp.zeros((8, LANES), F32)

    def normalize(step, _):
        first = pl.multiple_of(step * 32, 32)
        rows = pl.ds(first, 32)
        live = row_mask(first, 32, LANES, total_live)
        for chunk in range(chunks):
            lanes = chunk_lanes(chunk)
            mean, scale = batch[chunk]
            value = (e_ref[chunk, rows, :] - mean) * scale
            value = value * table_ref[5:6, lanes] + table_ref[6:7, lanes]
            n_ref[chunk, pl.ds(LEAD + first, 32), :] = jnp.where(live, value, 0.0)
            z_ref[chunk, rows, :] = jnp.zeros((32, LANES), F32)
            dn_ref[chunk, rows, :] = jnp.zeros((32, LANES), F32)
        return 0

    lax.fori_loop(0, row_count // 32, normalize, 0)

    for chunk in range(chunks):
        taps = tap_vectors(table_ref, 20, chunk)

        def conv_step(row, side, masks, carry, chunk=chunk, taps=taps):
            value = conv_forward(n_ref, chunk, row, side, masks, taps)
            rows = pl.ds(row, 8)
            z_ref[chunk, rows, :] = jnp.where(masks[0], value, z_ref[chunk, rows, :])
            return carry

        for_groups(sides_ref, conv_step, 0)

    up_grad_ref[...] = jnp.zeros_like(up_grad_ref)
    down_grad_ref[...] = jnp.zeros_like(down_grad_ref)
    grads[...] = jnp.zeros_like(grads)

    def z_rows(rows):
        return jnp.concatenate([z_ref[chunk, rows, :] for chunk in range(chunks)], axis=1)

    @pl.loop(0, row_count // tile)
    def _(step):
        base = pl.multiple_of(step * tile, 16)

        def before(sub, _):
            inner = pl.multiple_of(sub * 16, 16)
            near, rows = pl.ds(inner, 16), pl.ds(base + inner, 16)
            value = x1_ref[rows, :] + table_ref[7:8, :] * z_rows(rows)
            x2[near, :] = value
            value, scale = centered(value)
            unit[near, :] = value
            spread[near, :] = jnp.broadcast_to(scale, (16, LANES))
            third_low[near, :] = (value * table_ref[8:9, :] + table_ref[9:10, :]).astype(BF16)
            return 0

        lax.fori_loop(0, tile // 16, before, 0)
        for part in range(expand):
            lanes = slice(part * width, (part + 1) * width)
            pre[:, lanes] = dot(third_low[...], weight_ref[part])

        def activate(sub, _):
            near = pl.ds(pl.multiple_of(sub * 16, 16), 16)
            for part in range(expand):
                lanes = slice(part * width, (part + 1) * width)
                value = pre[near, lanes]
                share, bell = gelu_parts(value)
                hidden_low[near, lanes] = (value * share).astype(BF16)
                pre[near, lanes] = gelu_slope(value, share, bell)
            return 0

        lax.fori_loop(0, tile // 16, activate, 0)
        total = None
        for part in range(expand):
            lanes = slice(part * width, (part + 1) * width)
            term = dot(hidden_low[:, lanes], weight_ref[expand + part])
            total = term if total is None else total + term
        feed[...] = total

        def output(sub, carry):
            inner = pl.multiple_of(sub * 16, 16)
            near, rows = pl.ds(inner, 16), pl.ds(base + inner, 16)
            live = row_mask(base + inner, 16, width, total_live)
            value = x2[near, :] + table_ref[10:11, :] * feed[near, :]
            out_ref[rows, :] = jnp.where(live, value, 0.0).astype(BF16)
            entry = jnp.where(live, adjoint_ref[rows, :].astype(F32), 0.0)
            feed_grad[near, :] = (entry * table_ref[10:11, :]).astype(BF16)
            return carry + fold(entry * feed[near, :])

        grads[0] += lax.fori_loop(0, tile // 16, output, jnp.zeros((8, width), F32))
        for part in range(expand):
            lanes = slice(part * width, (part + 1) * width)
            hidden_grad = dot_lanes(feed_grad[...], weight_ref[expand + part])
            pre_grad[:, lanes] = (hidden_grad * pre[:, lanes]).astype(BF16)
        for part in range(expand):
            lanes = slice(part * width, (part + 1) * width)
            down_grad_ref[part] += dot_rows(hidden_low[:, lanes], feed_grad[...])
            up_grad_ref[part] += dot_rows(third_low[...], pre_grad[:, lanes])
        total = None
        for part in range(expand):
            lanes = slice(part * width, (part + 1) * width)
            term = dot_lanes(pre_grad[:, lanes], weight_ref[part])
            total = term if total is None else total + term
        feed[...] = total

        def after(sub, carry):
            inner = pl.multiple_of(sub * 16, 16)
            near, rows = pl.ds(inner, 16), pl.ds(base + inner, 16)
            live = row_mask(base + inner, 16, width, total_live)
            entry = jnp.where(live, adjoint_ref[rows, :].astype(F32), 0.0)
            grad = feed[near, :]
            value = unit[near, :]
            total = entry + norm_back(grad * table_ref[8:9, :], value, spread[near, 0:1])
            dx2_ref[rows, :] = total
            scaled = total * table_ref[7:8, :]
            for chunk in range(chunks):
                dw_ref[chunk, pl.ds(LEAD + base + inner, 16), :] = scaled[:, chunk_lanes(chunk)]
            return (
                carry[0] + fold(total * z_rows(rows)),
                carry[1] + fold(grad * value),
                carry[2] + fold(grad),
            )

        wide = jnp.zeros((8, width), F32)
        sums = lax.fori_loop(0, tile // 16, after, (wide, wide, wide))
        for index in range(3):
            grads[1 + index] += sums[index]

    for index, source in enumerate((1, 2, 3, 0)):
        grads_ref[index : index + 1, :] = jnp.sum(grads[source], axis=0, keepdims=True)
    for chunk in range(chunks):
        taps = tap_vectors(table_ref, 20, chunk)
        mean, scale = batch[chunk]

        def back_step(row, side, masks, carry, chunk=chunk, taps=taps, mean=mean, scale=scale):
            own = jnp.where(masks[0], n_ref[chunk, pl.ds(LEAD + row, 8), :], 0.0)
            total, tap_sums = conv_backward(dw_ref, chunk, row, side, masks, taps, own, carry[0])
            rows = pl.ds(row, 8)
            dn_ref[chunk, rows, :] = jnp.where(masks[0], total, dn_ref[chunk, rows, :])
            total = jnp.where(masks[0], total, 0.0)
            standard = (e_ref[chunk, rows, :] - mean) * scale
            return tap_sums, carry[1] + total * standard, carry[2] + total

        tap_sums, gamma, beta = for_groups(sides_ref, back_step, ((zero,) * 9, zero, zero))
        lanes = chunk_lanes(chunk)
        for index, value in enumerate((*tap_sums, gamma, beta)):
            grads_ref[4 + index : 5 + index, lanes] = jnp.sum(value, axis=0, keepdims=True)


def feed_forward(sides, x1, e, batch_sums, weights, table, adjoint):
    row_count, width = x1.shape
    chunks = width // LANES
    expand = weights.shape[0] // 2
    tile = tile_rows(row_count)
    shape = jax.ShapeDtypeStruct
    return pl.pallas_call(
        feed_kernel,
        out_shape=(
            shape((row_count, width), BF16),
            shape((row_count, width), F32),
            shape((chunks, row_count, LANES), F32),
            shape((expand, width, width), F32),
            shape((expand, width, width), F32),
            shape((16, width), F32),
        ),
        in_specs=[SMEM_SPEC] + [VMEM_SPEC] * 6,
        out_specs=(VMEM_SPEC,) * 6,
        scratch_shapes=[
            pltpu.VMEM((chunks, LEAD + row_count + TAIL, LANES), F32),
            pltpu.VMEM((chunks, row_count, LANES), F32),
            pltpu.VMEM((chunks, LEAD + row_count + TAIL, LANES), F32),
            pltpu.VMEM((tile, width), F32),
            pltpu.VMEM((tile, width), F32),
            pltpu.VMEM((tile, LANES), F32),
            pltpu.VMEM((tile, width), BF16),
            pltpu.VMEM((tile, expand * width), F32),
            pltpu.VMEM((tile, expand * width), BF16),
            pltpu.VMEM((tile, width), F32),
            pltpu.VMEM((tile, width), BF16),
            pltpu.VMEM((tile, expand * width), BF16),
            pltpu.VMEM((4, 8, width), F32),
        ],
        compiler_params=pltpu.CompilerParams(vmem_limit_bytes=VMEM_LIMIT),
        name="feed_forward",
    )(sides, x1, e, batch_sums, weights, table, adjoint)


def mixing_backward_kernel(
    sides_ref,
    sharp_ref,
    input_ref,
    weight_ref,
    table_ref,
    x1_ref,
    qkv_ref,
    mixed_ref,
    scores_ref,
    attention_ref,
    u_hbm,
    bn_ref,
    dx2_ref,
    dn_hbm,
    back_ref,
    out_ref,
    head_grad_ref,
    out_grad_ref,
    grads_ref,
    sharp_grad_ref,
    head_weights,
    out_weight,
    pool,
    conv_grad,
    dx1,
    mixed_grad,
    low_rows,
    head_low,
    spread,
    out_sum,
    load_sems,
):
    row_count, width = input_ref.shape
    chunks = width // LANES
    u_ref, dn_ref = pool.at[0:chunks], pool.at[chunks : 2 * chunks]
    conv_in, attention_out = pool.at[2 * chunks : 3 * chunks], pool.at[3 * chunks : 4 * chunks]
    loads = [
        pltpu.make_async_copy(u_hbm, u_ref, load_sems.at[0]),
        pltpu.make_async_copy(dn_hbm, dn_ref, load_sems.at[1]),
    ]
    for load in loads:
        load.start()
    tile = tile_rows(row_count)
    total_live = live_total(sides_ref)
    batch = [batch_vectors(bn_ref, chunk, chunks) for chunk in range(chunks)]
    zero = jnp.zeros((8, LANES), F32)
    wide = jnp.zeros((8, width), F32)
    mapping = head_map(BF16)
    for part in range(3):
        head_weights[:, part * PAD_WIDTH : (part + 1) * PAD_WIDTH] = dot(
            weight_ref[part], mapping
        ).astype(BF16)
    out_weight[...] = dot_rows(mapping, weight_ref[3]).astype(BF16)
    spread[...] = jnp.zeros_like(spread)

    for load in loads:
        load.wait()

    def batch_back(step, _):
        first = pl.multiple_of(step * 32, 32)
        rows = pl.ds(first, 32)
        live = row_mask(first, 32, LANES, total_live)
        unit, _ = centered(x1_ref[rows, :])
        value = unit * table_ref[3:4, :] + table_ref[4:5, :]
        for chunk in range(chunks):
            lanes = chunk_lanes(chunk)
            mean, scale = batch[chunk]
            count = bn_ref[2 * chunks : 2 * chunks + 1, :]
            u = u_ref[chunk, rows, :]
            share, bell = gelu_parts(u)
            standard = (u * share - mean) * scale
            inner = (
                back_ref[chunk : chunk + 1, :]
                + standard * back_ref[chunks + chunk : chunks + chunk + 1, :]
            ) / count
            grad = scale * table_ref[5:6, lanes] * (dn_ref[chunk, rows, :] - inner)
            grad = grad * gelu_slope(u, share, bell)
            conv_grad[chunk, pl.ds(LEAD + first, 32), :] = jnp.where(live, grad, 0.0)
            conv_in[chunk, pl.ds(first, 32), :] = value[:, lanes]
        return 0

    lax.fori_loop(0, row_count // 32, batch_back, 0)

    for chunk in range(chunks):
        taps = tap_vectors(table_ref, 11, chunk)

        def back_step(row, side, masks, carry, chunk=chunk, taps=taps):
            rows = pl.ds(row, 8)
            held = conv_in[chunk, rows, :]
            own = jnp.where(masks[0], held, 0.0)
            total, tap_sums = conv_backward(conv_grad, chunk, row, side, masks, taps, own, carry)
            conv_in[chunk, rows, :] = jnp.where(masks[0], total, held)
            return tap_sums

        tap_sums = for_groups(sides_ref, back_step, (zero,) * 9)
        for index, value in enumerate(tap_sums):
            grads_ref[5 + index : 6 + index, chunk_lanes(chunk)] = jnp.sum(
                value, axis=0, keepdims=True
            )

    @pl.loop(0, row_count // tile)
    def _(step):
        rows = pl.ds(pl.multiple_of(step * tile, 16), tile)
        result = dot(mixed_ref[rows, :], out_weight[...])
        for chunk in range(chunks):
            attention_out[chunk, rows, :] = result[:, chunk_lanes(chunk)]

    def second_back(step, carry):
        first = pl.multiple_of(step * 16, 16)
        rows = pl.ds(first, 16)
        live = row_mask(first, 16, width, total_live)
        grad = jnp.concatenate([conv_in[chunk, rows, :] for chunk in range(chunks)], axis=1)
        grad = jnp.where(live, grad, 0.0)
        unit, scale = centered(x1_ref[rows, :])
        total = dx2_ref[rows, :] + norm_back(grad * table_ref[3:4, :], unit, scale)
        dx1[rows, :] = total
        low_rows[rows, :] = (total * table_ref[2:3, :]).astype(BF16)
        held = jnp.concatenate([attention_out[chunk, rows, :] for chunk in range(chunks)], axis=1)
        return (
            carry[0] + fold(total * held),
            carry[1] + fold(grad * unit),
            carry[2] + fold(grad),
        )

    sums = lax.fori_loop(0, row_count // 16, second_back, (wide, wide, wide))
    for index in range(3):
        grads_ref[2 + index : 3 + index, :] = jnp.sum(sums[index], axis=0, keepdims=True)

    out_sum[...] = jnp.zeros_like(out_sum)

    @pl.loop(0, row_count // tile)
    def _(step):
        rows = pl.ds(pl.multiple_of(step * tile, 16), tile)
        mixed_grad[rows, :] = dot_lanes(low_rows[rows, :], out_weight[...])
        out_sum[...] += dot_rows(mixed_ref[rows, :], low_rows[rows, :])

    pool[...] = jnp.zeros_like(pool)

    low = out_sum[...].astype(BF16)
    out_grad_ref[...] = dot(mapping, low).astype(BF16)
    sharp_grad_ref[...] = jnp.zeros_like(sharp_grad_ref)

    def crop_step(crop, rows, keep):
        for half in range(2):
            lanes = [
                slice(part * PAD_WIDTH + half * HALF_WIDTH, part * PAD_WIDTH + (half + 1) * HALF_WIDTH)
                for part in range(3)
            ]
            query, query_scale = units(jnp.where(keep, qkv_ref[rows, lanes[0]], 0.0))
            key, key_scale = units(jnp.where(keep, qkv_ref[rows, lanes[1]], 0.0))
            value = split(jnp.where(keep, qkv_ref[rows, lanes[2]], 0.0))
            grad = split(jnp.where(keep, mixed_grad[rows, lanes[0]], 0.0))
            block = dot_split(dot_rows, value, grad)
            query_sums = []
            for pair in range(2):
                index = 2 * half + pair
                shares = attention_ref[crop, index]
                scores = scores_ref[crop, index]
                part = pair_part(block, pair)
                part = shares * (part - jnp.sum(part * shares, axis=0, keepdims=True))
                spread_pair(spread, half, pair, shares)
                sharp_grad_ref[index : index + 1, :] += jnp.sum(part * scores, axis=0, keepdims=True)
                part = part * pair_sharpness(sharp_ref, index)
                query_sums.append(jnp.sum(part * scores, axis=0, keepdims=True))
                spread_pair(spread, 2 + half, pair, part)
            shares = (spread[half, 0], spread[half, 1])
            slopes = (spread[2 + half, 0], spread[2 + half, 1])
            value_grad = dot_split(dot_lanes, grad, shares)
            query_grad = dot_split(dot, split(key), slopes)
            query_grad = query_scale * (query_grad - query * jnp.concatenate(query_sums, axis=1))
            key_grad = dot_split(dot_lanes, split(query), slopes)
            key_grad = key_scale * (
                key_grad - key * jnp.sum(key_grad * key, axis=0, keepdims=True)
            )
            for part, result in enumerate((query_grad, key_grad, value_grad)):
                for side in range(HALF_WIDTH // LANES):
                    chunk = (part * PAD_WIDTH + half * HALF_WIDTH) // LANES + side
                    pool[chunk, rows, :] = jnp.where(
                        keep[:, 0:LANES], result[:, chunk_lanes(side)], pool[chunk, rows, :]
                    )

    for_crops(sides_ref, row_count, crop_step)

    def first_norm(step, _):
        rows = pl.ds(pl.multiple_of(step * 32, 32), 32)
        unit, _ = centered(input_ref[rows, :].astype(F32))
        low_rows[rows, :] = (unit * table_ref[0:1, :] + table_ref[1:2, :]).astype(BF16)
        return 0

    lax.fori_loop(0, row_count // 32, first_norm, 0)

    for part in range(3):
        lanes = slice(part * PAD_WIDTH, (part + 1) * PAD_WIDTH)
        out_sum[...] = jnp.zeros_like(out_sum)

        @pl.loop(0, row_count // tile)
        def _(step, lanes=lanes, part=part):
            rows = pl.ds(pl.multiple_of(step * tile, 16), tile)
            first = part * PAD_WIDTH // LANES
            for chunk in range(PAD_WIDTH // LANES):
                head_low[rows, chunk_lanes(chunk)] = pool[first + chunk, rows, :].astype(BF16)
            term = dot_lanes(head_low[rows, :], head_weights[:, lanes])
            mixed_grad[rows, 0:width] = term if part == 0 else mixed_grad[rows, 0:width] + term

        @pl.loop(0, row_count // tile)
        def _(step, lanes=lanes):
            rows = pl.ds(pl.multiple_of(step * tile, 16), tile)
            out_sum[...] += dot_rows(head_low[rows, :], low_rows[rows, :])

        low = out_sum[...].astype(BF16)
        head_grad_ref[part] = lax.dot_general(
            low, mapping, (((0,), (1,)), ((), ())), preferred_element_type=F32
        ).astype(BF16)

    def first_back(step, carry):
        rows = pl.ds(pl.multiple_of(step * 16, 16), 16)
        unit, scale = centered(input_ref[rows, :].astype(F32))
        grad = mixed_grad[rows, 0:width]
        total = dx1[rows, :] + norm_back(grad * table_ref[0:1, :], unit, scale)
        out_ref[rows, :] = total.astype(BF16)
        return carry[0] + fold(grad * unit), carry[1] + fold(grad)

    sums = lax.fori_loop(0, row_count // 16, first_back, (wide, wide))
    for index in range(2):
        grads_ref[index : index + 1, :] = jnp.sum(sums[index], axis=0, keepdims=True)


def mixing_backward(sides, sharpness, inputs, weights, table, saved, batch_sums, dx2, dn, back_sums):
    row_count, width = inputs.shape
    chunks = width // LANES
    shape = jax.ShapeDtypeStruct
    x1, qkv, mixed, scores, attention, u = saved
    return pl.pallas_call(
        mixing_backward_kernel,
        out_shape=(
            shape((row_count, width), BF16),
            shape((3, width, width), BF16),
            shape((width, width), BF16),
            shape((16, width), F32),
            shape((HEAD_PAIRS, LANES), F32),
        ),
        in_specs=[SMEM_SPEC, SMEM_SPEC]
        + [VMEM_SPEC] * 8
        + [ANY_SPEC, VMEM_SPEC, VMEM_SPEC, ANY_SPEC, VMEM_SPEC],
        out_specs=(VMEM_SPEC,) * 5,
        scratch_shapes=[
            pltpu.VMEM((width, 3 * PAD_WIDTH), BF16),
            pltpu.VMEM((PAD_WIDTH, width), BF16),
            pltpu.VMEM((3 * PAD_WIDTH // LANES, row_count, LANES), F32),
            pltpu.VMEM((chunks, LEAD + row_count + TAIL, LANES), F32),
            pltpu.VMEM((row_count, width), F32),
            pltpu.VMEM((row_count, PAD_WIDTH), F32),
            pltpu.VMEM((row_count, width), BF16),
            pltpu.VMEM((row_count, PAD_WIDTH), BF16),
            pltpu.VMEM((4, 2, HALF_WIDTH, HALF_WIDTH), BF16),
            pltpu.VMEM((PAD_WIDTH, width), F32),
            pltpu.SemaphoreType.DMA((2,)),
        ],
        compiler_params=pltpu.CompilerParams(vmem_limit_bytes=VMEM_LIMIT),
        name="mixing_backward",
    )(
        sides,
        sharpness,
        inputs,
        weights,
        table,
        x1,
        qkv,
        mixed,
        scores,
        attention,
        u,
        batch_sums,
        dx2,
        dn,
        back_sums,
    )


def shards(
    patch_embeddings,
    view_side_tokens,
    projection_masters,
    channel_coefficients,
    head_sharpness,
    output_adjoint,
    leading_covariance,
    trailing_covariance,
    leading_root_preconditioner,
    trailing_root_preconditioner,
    channel_energy_average,
    sharpness_energy_average,
    storage_position_map,
):
    row_count, feature_count = patch_embeddings.shape
    chunks = feature_count // LANES
    block_count = projection_masters.shape[0]
    shard_rows = projection_masters.shape[1]
    slot_count = leading_covariance.shape[0]
    weight_low = projection_masters.astype(BF16)
    full_table = lax.all_gather(channel_coefficients.astype(BF16), "fsdp", axis=1, tiled=True)
    table = full_table.astype(F32)
    mixing_blocks = lax.all_gather(weight_low[:4], "fsdp", axis=1, tiled=True)
    feed_blocks = lax.all_gather(weight_low[4:], "fsdp", axis=1, tiled=True)
    x1, qkv, mixed, scores, attention, u, e, sums = mixing_forward(
        view_side_tokens, head_sharpness, patch_embeddings, mixing_blocks, table
    )
    batch_sums = lax.psum(sums, ("dp", "fsdp"))
    layer_output, dx2, dn, up_grad, down_grad, feed_table = feed_forward(
        view_side_tokens, x1, e, batch_sums, feed_blocks, table, output_adjoint
    )
    gamma_part, beta_part = feed_table[13], feed_table[14]
    back_sums = lax.psum(
        jnp.concatenate(
            [beta_part.reshape(chunks, LANES), gamma_part.reshape(chunks, LANES), jnp.zeros((8 - 2 * chunks, LANES), F32)]
        ),
        ("dp", "fsdp"),
    )
    incoming_tokens_grad, head_grad, out_grad, mixing_table, sharp_lanes = mixing_backward(
        view_side_tokens,
        head_sharpness,
        patch_embeddings,
        mixing_blocks,
        table,
        (x1, qkv, mixed, scores, attention, u),
        batch_sums,
        dx2,
        dn,
        back_sums,
    )
    sharpness_share = jnp.sum(sharp_lanes.reshape(HEAD_NUMBER, HEAD_PAD), axis=1)
    table_grad = jnp.concatenate(
        [
            mixing_table[0:5],
            feed_table[13:15],
            feed_table[0:4],
            mixing_table[5:14],
            feed_table[4:13],
        ],
        axis=0,
    )
    block_grad = jnp.concatenate(
        [head_grad.astype(F32), out_grad.astype(F32)[None], up_grad, down_grad], axis=0
    )
    denominator_sum = lax.axis_size("fsdp")
    tiled_part = jnp.broadcast_to(
        sharpness_share[None, :], (denominator_sum, sharpness_share.shape[0])
    )
    portion_derivative, catalog_portion, sharpness_normalizer = (
        lax.psum_scatter(block_grad, "fsdp", scatter_dimension=1, tiled=True),
        lax.psum_scatter(table_grad, "fsdp", scatter_dimension=1, tiled=True),
        lax.psum_scatter(tiled_part, "fsdp", scatter_dimension=0, tiled=True),
    )
    portion_derivative, catalog_portion, sharpness_normalizer = lax.psum(
        (portion_derivative, catalog_portion, sharpness_normalizer), "dp"
    )
    sharpness_derivative = sharpness_normalizer[0]
    shard_place = lax.axis_index("fsdp")
    slot_index = jnp.arange(denominator_sum * slot_count, dtype=jnp.int32)
    slot_match = storage_position_map[None, :] == slot_index[:, None]
    slot_filled = jnp.any(slot_match, axis=1).astype(jnp.float32)[:, None, None]
    slot_block = jnp.sum(
        jnp.where(slot_match, jnp.arange(block_count, dtype=jnp.int32)[None, :], 0), axis=1
    )
    my_filled = lax.dynamic_slice_in_dim(slot_filled, shard_place * slot_count, slot_count, 0)
    my_block = lax.dynamic_slice_in_dim(slot_block, shard_place * slot_count, slot_count, 0)
    whole_grad = lax.all_gather(portion_derivative, "fsdp", axis=1, tiled=True)
    owned_grad = jnp.take(whole_grad, my_block, axis=0) * my_filled
    leading_covariance_renewed = covariance_forgetting * leading_covariance + (
        1.0 - covariance_forgetting
    ) * jnp.einsum("sij,skj->sik", owned_grad, owned_grad, precision=lax.Precision.HIGHEST)
    trailing_covariance_renewed = covariance_forgetting * trailing_covariance + (
        1.0 - covariance_forgetting
    ) * jnp.einsum("sji,sjk->sik", owned_grad, owned_grad, precision=lax.Precision.HIGHEST)
    halfway = jnp.einsum(
        "sij,sjk->sik", leading_root_preconditioner, owned_grad, precision=lax.Precision.HIGHEST
    )
    conditioned = jnp.einsum(
        "sij,sjk->sik", halfway, trailing_root_preconditioner, precision=lax.Precision.HIGHEST
    )
    every_update = lax.all_gather(conditioned, "fsdp", axis=0, tiled=True)
    my_rows = lax.dynamic_slice_in_dim(every_update, shard_place * shard_rows, shard_rows, 1)
    update = jnp.take(my_rows, storage_position_map, axis=0)
    projection_updated = projection_masters - weight_rate * update
    channel_energy_renewed = (
        covariance_forgetting * channel_energy_average
        + (1.0 - covariance_forgetting) * catalog_portion * catalog_portion
    )
    channel_params_updated = channel_coefficients - vector_rate * catalog_portion / (
        jnp.sqrt(channel_energy_renewed) + energy_epsilon
    )
    sharpness_energy_renewed = (
        covariance_forgetting * sharpness_energy_average
        + (1.0 - covariance_forgetting) * sharpness_derivative * sharpness_derivative
    )
    sharpness_updated = head_sharpness - sharpness_step_size * sharpness_derivative / (
        jnp.sqrt(sharpness_energy_renewed) + energy_epsilon
    )
    return (
        layer_output,
        incoming_tokens_grad,
        portion_derivative,
        leading_covariance_renewed,
        trailing_covariance_renewed,
        projection_updated,
        projection_updated.astype(jnp.bfloat16),
        catalog_portion,
        channel_energy_renewed,
        channel_params_updated,
        sharpness_derivative,
        sharpness_energy_renewed,
        sharpness_updated,
    )


def solution(mesh):
    in_specs = (
        P(("dp", "fsdp"), None),
        P(("dp", "fsdp")),
        P(None, "fsdp", None),
        P(None, "fsdp"),
        P(),
        P(("dp", "fsdp"), None),
        P("fsdp", None, None),
        P("fsdp", None, None),
        P("fsdp", None, None),
        P("fsdp", None, None),
        P(None, "fsdp"),
        P(),
        P(),
    )
    out_specs = (
        P(("dp", "fsdp"), None),
        P(("dp", "fsdp"), None),
        P(None, "fsdp", None),
        P("fsdp", None, None),
        P("fsdp", None, None),
        P(None, "fsdp", None),
        P(None, "fsdp", None),
        P(None, "fsdp"),
        P(None, "fsdp"),
        P(None, "fsdp"),
        P(),
        P(),
        P(),
    )
    return jax.shard_map(shards, mesh=mesh, in_specs=in_specs, out_specs=out_specs, check_vma=False)
```

```python
import functools

import jax
import jax.numpy as jnp
from jax import lax
from jax.experimental import pallas as pl
from jax.experimental.pallas import tpu as pltpu
from jax.sharding import PartitionSpec as P

HEAD_NUMBER = 8
HDIM = 48
HEAD_PAD = 64
LANES = 128
HEAD_PAIRS = HEAD_NUMBER // 2
PAD_WIDTH = HEAD_NUMBER * HEAD_PAD
HALF_WIDTH = PAD_WIDTH // 2
LEAD = 16
TAIL = 32
SMALL_WINDOW = 48
LARGE_WINDOW = 208
VMEM_LIMIT = 58 * 2**20

norm_epsilon = 1e-06
batch_epsilon = 1e-05
attention_epsilon = 1e-06
covariance_forgetting = 0.5
weight_rate = 0.5
vector_rate = 0.1
sharpness_step_size = 2.0
energy_epsilon = 1e-08

F32 = jnp.float32
BF16 = jnp.bfloat16
VMEM_SPEC = pl.BlockSpec(memory_space=pltpu.VMEM)
ANY_SPEC = pl.BlockSpec(memory_space=pl.ANY)
SMEM_SPEC = pl.BlockSpec(memory_space=pltpu.SMEM)


def dot(left, right):
    return lax.dot_general(left, right, (((1,), (0,)), ((), ())), preferred_element_type=F32)


def dot_rows(left, right):
    return lax.dot_general(left, right, (((0,), (0,)), ((), ())), preferred_element_type=F32)


def dot_lanes(left, right):
    return lax.dot_general(left, right, (((1,), (1,)), ((), ())), preferred_element_type=F32)


def split(values):
    high = values.astype(BF16)
    return high, (values - high.astype(F32)).astype(BF16)


def dot_split(product, left, right):
    return (
        product(left[0], right[0]) + product(left[0], right[1]) + product(left[1], right[0])
    )


def fold(values):
    total = values[0:8]
    for first in range(8, values.shape[0], 8):
        total = total + values[first : first + 8]
    return total


def gelu_parts(values):
    magnitude = jnp.abs(values) * 0.7071067811865476
    base = 1.0 + 0.3275911 * magnitude
    guess = pl.reciprocal(base, approx=True)
    slot = guess * (2.0 - base * guess)
    series = slot * (
        0.127414796
        + slot
        * (-0.142248368 + slot * (0.7107068705 + slot * (-0.7265760135 + slot * 0.5307027145)))
    )
    bell = jnp.exp(-0.5 * values * values)
    lower = series * bell
    return jnp.where(values >= 0, 1.0 - lower, lower), bell


def gelu_slope(values, share, bell):
    return share + values * bell * 0.3989422804014327


def head_map(dtype):
    feature = lax.broadcasted_iota(jnp.int32, (HEAD_NUMBER * HDIM, PAD_WIDTH), 0)
    lane = lax.broadcasted_iota(jnp.int32, (HEAD_NUMBER * HDIM, PAD_WIDTH), 1)
    inner = lane & (HEAD_PAD - 1)
    hit = (inner < HDIM) & ((lane >> 6) * HDIM + inner == feature)
    return hit.astype(F32).astype(dtype)


def centered(values):
    center = jnp.sum(values, axis=-1, keepdims=True) * (1.0 / values.shape[-1])
    shifted = values - center
    spread = jnp.sum(shifted * shifted, axis=-1, keepdims=True) * (1.0 / values.shape[-1])
    scale = lax.rsqrt(spread + norm_epsilon)
    return shifted * scale, scale


def norm_back(grad, unit, scale):
    size = 1.0 / grad.shape[-1]
    middle = jnp.sum(grad, axis=-1, keepdims=True) * size
    slope = jnp.sum(grad * unit, axis=-1, keepdims=True) * size
    return scale * (grad - middle - unit * slope)


def tile_rows(count):
    for parts in range(4, count // 16 + 1):
        if count % (16 * parts) == 0:
            return count // parts
    return count


def live_total(sides_ref):
    return lax.fori_loop(
        0, sides_ref.shape[0], lambda c, t: t + sides_ref[c] * sides_ref[c], jnp.int32(0)
    )


def row_mask(first, rows, width, limit):
    return lax.broadcasted_iota(jnp.int32, (rows, width), 0) + first < limit


def for_groups(sides_ref, step, carry):
    def crop_body(crop, state):
        start, carry = state
        side = sides_ref[crop]
        cells = side * side
        inverse = 1.0 / jnp.full((8, LANES), side, jnp.int32).astype(F32)
        lines = lax.broadcasted_iota(jnp.int32, (8, LANES), 0)

        def group_body(group, carry):
            for part in range(2):
                row = pl.multiple_of((group * 2 + part) * 8, 8)
                place = lines + (row - start)
                line = ((place.astype(F32) + 0.5) * inverse).astype(jnp.int32)
                column = place - line * side
                inside = (place >= 0) & (place < cells)
                masks = (
                    inside,
                    column >= 1,
                    column < side - 1,
                    place >= side,
                    place < cells - side,
                )
                carry = step(row, side, masks, carry)
            return carry

        carry = lax.fori_loop(start // 16, (start + cells + 15) // 16, group_body, carry)
        return start + cells, carry

    return lax.fori_loop(0, sides_ref.shape[0], crop_body, (jnp.int32(0), carry))[1]


def conv_forward(source, chunk, row, side, masks, taps):
    inside, left_ok, right_ok, up_ok, down_ok = masks
    total = None
    for shift in (-1, 0, 1):
        base = LEAD + row + shift * side
        middle = source[chunk, pl.ds(base, 8), :]
        left = jnp.where(left_ok, source[chunk, pl.ds(base - 1, 8), :], 0.0)
        right = jnp.where(right_ok, source[chunk, pl.ds(base + 1, 8), :], 0.0)
        first = 3 * (shift + 1)
        value = taps[first] * left + taps[first + 1] * middle + taps[first + 2] * right
        if shift == -1:
            value = jnp.where(up_ok, value, 0.0)
        if shift == 1:
            value = jnp.where(down_ok, value, 0.0)
        total = value if total is None else total + value
    return total


def conv_backward(source, chunk, row, side, masks, taps, own, tap_sums):
    inside, left_ok, right_ok, up_ok, down_ok = masks
    total = None
    tap_sums = list(tap_sums)
    for shift in (-1, 0, 1):
        base = LEAD + row + shift * side
        row_ok = {-1: up_ok, 0: None, 1: down_ok}[shift]
        for sway in (-1, 0, 1):
            column_ok = {-1: left_ok, 0: None, 1: right_ok}[sway]
            value = source[chunk, pl.ds(base + sway, 8), :]
            keep = inside
            if row_ok is not None:
                keep = keep & row_ok
            if column_ok is not None:
                keep = keep & column_ok
            value = jnp.where(keep, value, 0.0)
            index = 3 * (1 - shift) + (1 - sway)
            term = taps[index] * value
            total = term if total is None else total + term
            tap_sums[index] = tap_sums[index] + own * value
    return total, tuple(tap_sums)


def chunk_lanes(chunk):
    return slice(chunk * LANES, (chunk + 1) * LANES)


def tap_vectors(table_ref, first, chunk):
    return [
        jnp.broadcast_to(table_ref[first + k : first + k + 1, chunk_lanes(chunk)], (8, LANES))
        for k in range(9)
    ]


def for_crops(sides_ref, row_count, step):
    def crop_body(crop, start):
        side = sides_ref[crop]
        cells = side * side
        for window, fits in ((SMALL_WINDOW, side <= 6), (LARGE_WINDOW, side > 6)):

            @pl.when(fits)
            def _():
                first = pl.multiple_of(
                    jnp.minimum(start // 8, (row_count - window) // 8) * 8, 8
                )
                place = lax.broadcasted_iota(jnp.int32, (window, HALF_WIDTH), 0) + (first - start)
                step(crop, pl.ds(first, window), (place >= 0) & (place < cells))

        return start + cells

    lax.fori_loop(0, sides_ref.shape[0], crop_body, jnp.int32(0))


def pair_lanes():
    return lax.broadcasted_iota(jnp.int32, (HDIM, LANES), 1) < HEAD_PAD


def pair_part(block, pair):
    first = pair * LANES
    lanes = slice(first, first + LANES)
    return jnp.where(
        pair_lanes(),
        block[first : first + HDIM, lanes],
        block[first + HEAD_PAD : first + HEAD_PAD + HDIM, lanes],
    )


def spread_pair(target, half, pair, values):
    first = pair * LANES
    lanes = slice(first, first + LANES)
    parts = split(values)
    for index in range(2):
        value = parts[index].astype(F32)
        target[half, index, first : first + HDIM, lanes] = jnp.where(
            pair_lanes(), value, 0.0
        ).astype(BF16)
        target[half, index, first + HEAD_PAD : first + HEAD_PAD + HDIM, lanes] = jnp.where(
            pair_lanes(), 0.0, value
        ).astype(BF16)


def pair_sharpness(sharp_ref, pair):
    lane = lax.broadcasted_iota(jnp.int32, (1, LANES), 1)
    return jnp.where(lane < HEAD_PAD, sharp_ref[2 * pair], sharp_ref[2 * pair + 1])


def units(values):
    scale = lax.rsqrt(jnp.sum(values * values, axis=0, keepdims=True) + attention_epsilon)
    return values * scale, scale


def mixing_forward_kernel(
    sides_ref,
    sharp_ref,
    input_ref,
    weight_ref,
    table_ref,
    x1_ref,
    qkv_ref,
    mixed_ref,
    scores_ref,
    attention_ref,
    u_ref,
    e_ref,
    sums_ref,
    head_weights,
    out_weight,
    first_low,
    mixed,
    attention_out,
    conv_in,
    spread,
):
    row_count, width = input_ref.shape
    chunks = width // LANES
    tile = tile_rows(row_count)
    total_live = live_total(sides_ref)
    mapping = head_map(BF16)
    for part in range(3):
        head_weights[:, part * PAD_WIDTH : (part + 1) * PAD_WIDTH] = dot(
            weight_ref[part], mapping
        ).astype(BF16)
    spread[...] = jnp.zeros_like(spread)

    def first_norm(step, _):
        rows = pl.ds(pl.multiple_of(step * 32, 32), 32)
        unit, _ = centered(input_ref[rows, :].astype(F32))
        first_low[rows, :] = (unit * table_ref[0:1, :] + table_ref[1:2, :]).astype(BF16)
        mixed[rows, :] = jnp.zeros((32, PAD_WIDTH), F32)
        return 0

    lax.fori_loop(0, row_count // 32, first_norm, 0)

    @pl.loop(0, row_count // tile)
    def _(step):
        rows = pl.ds(pl.multiple_of(step * tile, 16), tile)
        for part in range(3):
            lanes = slice(part * PAD_WIDTH, (part + 1) * PAD_WIDTH)
            qkv_ref[rows, lanes] = dot(first_low[rows, :], head_weights[:, lanes])

    def crop_step(crop, rows, keep):
        for half in range(2):
            lanes = [
                slice(part * PAD_WIDTH + half * HALF_WIDTH, part * PAD_WIDTH + (half + 1) * HALF_WIDTH)
                for part in range(3)
            ]
            query = units(jnp.where(keep, qkv_ref[rows, lanes[0]], 0.0))[0]
            key = units(jnp.where(keep, qkv_ref[rows, lanes[1]], 0.0))[0]
            block = dot_split(dot_rows, split(key), split(query))
            for pair in range(2):
                scores = pair_part(block, pair)
                scores_ref[crop, 2 * half + pair] = scores
                scores = scores * pair_sharpness(sharp_ref, 2 * half + pair)
                scores = jnp.exp(scores - jnp.max(scores, axis=0, keepdims=True))
                shares = scores / jnp.sum(scores, axis=0, keepdims=True)
                attention_ref[crop, 2 * half + pair] = shares
                spread_pair(spread, half, pair, shares)
            result = dot_split(
                dot, split(qkv_ref[rows, lanes[2]]), (spread[half, 0], spread[half, 1])
            )
            mixed[rows, lanes[0]] = jnp.where(keep, result, mixed[rows, lanes[0]])

    for_crops(sides_ref, row_count, crop_step)

    out_weight[...] = dot_rows(mapping, weight_ref[3]).astype(BF16)

    @pl.loop(0, row_count // tile)
    def _(step):
        rows = pl.ds(pl.multiple_of(step * tile, 16), tile)
        low = mixed[rows, :].astype(BF16)
        mixed_ref[rows, :] = low
        attention_out[rows, :] = dot(low, out_weight[...])

    def second_norm(step, _):
        first = pl.multiple_of(step * 32, 32)
        rows = pl.ds(first, 32)
        value = input_ref[rows, :].astype(F32) + table_ref[2:3, :] * attention_out[rows, :]
        x1_ref[rows, :] = value
        unit, _ = centered(value)
        value = unit * table_ref[3:4, :] + table_ref[4:5, :]
        for chunk in range(chunks):
            conv_in[chunk, pl.ds(LEAD + first, 32), :] = value[:, chunk_lanes(chunk)]
            u_ref[chunk, rows, :] = jnp.zeros((32, LANES), F32)
            e_ref[chunk, rows, :] = jnp.zeros((32, LANES), F32)
        return 0

    lax.fori_loop(0, row_count // 32, second_norm, 0)

    zero = jnp.zeros((8, LANES), F32)
    sums_ref[...] = zero
    for chunk in range(chunks):
        taps = tap_vectors(table_ref, 11, chunk)

        def conv_step(row, side, masks, carry, chunk=chunk, taps=taps):
            value = conv_forward(conv_in, chunk, row, side, masks, taps)
            share, _ = gelu_parts(value)
            active = value * share
            rows = pl.ds(row, 8)
            u_ref[chunk, rows, :] = jnp.where(masks[0], value, u_ref[chunk, rows, :])
            e_ref[chunk, rows, :] = jnp.where(masks[0], active, e_ref[chunk, rows, :])
            active = jnp.where(masks[0], active, 0.0)
            return carry[0] + active, carry[1] + active * active

        plain, square = for_groups(sides_ref, conv_step, (zero, zero))
        sums_ref[chunk : chunk + 1, :] = jnp.sum(plain, axis=0, keepdims=True)
        sums_ref[chunks + chunk : chunks + chunk + 1, :] = jnp.sum(square, axis=0, keepdims=True)
    sums_ref[2 * chunks : 2 * chunks + 1, :] = jnp.full((1, LANES), total_live, jnp.int32).astype(F32)


def mixing_forward(sides, sharpness, inputs, weights, table):
    row_count, width = inputs.shape
    crops = sides.shape[0]
    chunks = width // LANES
    shape = jax.ShapeDtypeStruct
    return pl.pallas_call(
        mixing_forward_kernel,
        out_shape=(
            shape((row_count, width), F32),
            shape((row_count, 3 * PAD_WIDTH), F32),
            shape((row_count, PAD_WIDTH), BF16),
            shape((crops, HEAD_PAIRS, HDIM, LANES), F32),
            shape((crops, HEAD_PAIRS, HDIM, LANES), F32),
            shape((chunks, row_count, LANES), F32),
            shape((chunks, row_count, LANES), F32),
            shape((8, LANES), F32),
        ),
        in_specs=[SMEM_SPEC, SMEM_SPEC, VMEM_SPEC, VMEM_SPEC, VMEM_SPEC],
        out_specs=(VMEM_SPEC,) * 8,
        scratch_shapes=[
            pltpu.VMEM((width, 3 * PAD_WIDTH), BF16),
            pltpu.VMEM((PAD_WIDTH, width), BF16),
            pltpu.VMEM((row_count, width), BF16),
            pltpu.VMEM((row_count, PAD_WIDTH), F32),
            pltpu.VMEM((row_count, width), F32),
            pltpu.VMEM((chunks, LEAD + row_count + TAIL, LANES), F32),
            pltpu.VMEM((2, 2, HALF_WIDTH, HALF_WIDTH), BF16),
        ],
        compiler_params=pltpu.CompilerParams(vmem_limit_bytes=VMEM_LIMIT),
        name="mixing_forward",
    )(sides, sharpness, inputs, weights, table)


def batch_vectors(bn_ref, chunk, chunks):
    count = bn_ref[2 * chunks : 2 * chunks + 1, :]
    mean = bn_ref[chunk : chunk + 1, :] / count
    scale = lax.rsqrt(bn_ref[chunks + chunk : chunks + chunk + 1, :] / count - mean * mean + batch_epsilon)
    return mean, scale


def feed_kernel(
    sides_ref,
    x1_ref,
    e_ref,
    bn_ref,
    weight_ref,
    table_ref,
    adjoint_ref,
    out_ref,
    dx2_ref,
    dn_ref,
    weight_grad_ref,
    grads_ref,
    back_sums_ref,
    n_ref,
    z_ref,
    dw_ref,
    x2,
    unit,
    spread,
    third_low,
    pre,
    hidden_low,
    feed,
    feed_grad,
    pre_grad,
    grads,
    weight_sums,
):
    row_count, width = x1_ref.shape
    chunks = width // LANES
    expand = weight_ref.shape[0] // 2
    tile = tile_rows(row_count)
    total_live = live_total(sides_ref)
    batch = [batch_vectors(bn_ref, chunk, chunks) for chunk in range(chunks)]
    zero = jnp.zeros((8, LANES), F32)

    def normalize(step, _):
        first = pl.multiple_of(step * 32, 32)
        rows = pl.ds(first, 32)
        live = row_mask(first, 32, LANES, total_live)
        for chunk in range(chunks):
            lanes = chunk_lanes(chunk)
            mean, scale = batch[chunk]
            value = (e_ref[chunk, rows, :] - mean) * scale
            value = value * table_ref[5:6, lanes] + table_ref[6:7, lanes]
            n_ref[chunk, pl.ds(LEAD + first, 32), :] = jnp.where(live, value, 0.0)
            z_ref[chunk, rows, :] = jnp.zeros((32, LANES), F32)
            dn_ref[chunk, rows, :] = jnp.zeros((32, LANES), F32)
        return 0

    lax.fori_loop(0, row_count // 32, normalize, 0)

    for chunk in range(chunks):
        taps = tap_vectors(table_ref, 20, chunk)

        def conv_step(row, side, masks, carry, chunk=chunk, taps=taps):
            value = conv_forward(n_ref, chunk, row, side, masks, taps)
            rows = pl.ds(row, 8)
            z_ref[chunk, rows, :] = jnp.where(masks[0], value, z_ref[chunk, rows, :])
            return carry

        for_groups(sides_ref, conv_step, 0)

    weight_sums[...] = jnp.zeros_like(weight_sums)
    grads[...] = jnp.zeros_like(grads)

    def z_rows(rows):
        return jnp.concatenate([z_ref[chunk, rows, :] for chunk in range(chunks)], axis=1)

    @pl.loop(0, row_count // tile)
    def _(step):
        base = pl.multiple_of(step * tile, 16)

        def before(sub, _):
            inner = pl.multiple_of(sub * 16, 16)
            near, rows = pl.ds(inner, 16), pl.ds(base + inner, 16)
            value = x1_ref[rows, :] + table_ref[7:8, :] * z_rows(rows)
            x2[near, :] = value
            value, scale = centered(value)
            unit[near, :] = value
            spread[near, :] = jnp.broadcast_to(scale, (16, LANES))
            third_low[near, :] = (value * table_ref[8:9, :] + table_ref[9:10, :]).astype(BF16)
            return 0

        lax.fori_loop(0, tile // 16, before, 0)
        for part in range(expand):
            lanes = slice(part * width, (part + 1) * width)
            pre[:, lanes] = dot(third_low[...], weight_ref[part])

        def activate(sub, _):
            near = pl.ds(pl.multiple_of(sub * 16, 16), 16)
            for part in range(expand):
                lanes = slice(part * width, (part + 1) * width)
                value = pre[near, lanes]
                share, bell = gelu_parts(value)
                hidden_low[near, lanes] = (value * share).astype(BF16)
                pre[near, lanes] = gelu_slope(value, share, bell)
            return 0

        lax.fori_loop(0, tile // 16, activate, 0)
        total = None
        for part in range(expand):
            lanes = slice(part * width, (part + 1) * width)
            term = dot(hidden_low[:, lanes], weight_ref[expand + part])
            total = term if total is None else total + term
        feed[...] = total

        def output(sub, carry):
            inner = pl.multiple_of(sub * 16, 16)
            near, rows = pl.ds(inner, 16), pl.ds(base + inner, 16)
            live = row_mask(base + inner, 16, width, total_live)
            value = x2[near, :] + table_ref[10:11, :] * feed[near, :]
            out_ref[rows, :] = jnp.where(live, value, 0.0).astype(BF16)
            entry = jnp.where(live, adjoint_ref[rows, :].astype(F32), 0.0)
            feed_grad[near, :] = (entry * table_ref[10:11, :]).astype(BF16)
            return carry + fold(entry * feed[near, :])

        grads[0] += lax.fori_loop(0, tile // 16, output, jnp.zeros((8, width), F32))
        for part in range(expand):
            lanes = slice(part * width, (part + 1) * width)
            hidden_grad = dot_lanes(feed_grad[...], weight_ref[expand + part])
            pre_grad[:, lanes] = (hidden_grad * pre[:, lanes]).astype(BF16)
        for part in range(expand):
            lanes = slice(part * width, (part + 1) * width)
            weight_sums[expand + part] += dot_rows(hidden_low[:, lanes], feed_grad[...])
            weight_sums[part] += dot_rows(third_low[...], pre_grad[:, lanes])
        total = None
        for part in range(expand):
            lanes = slice(part * width, (part + 1) * width)
            term = dot_lanes(pre_grad[:, lanes], weight_ref[part])
            total = term if total is None else total + term
        feed[...] = total

        def after(sub, carry):
            inner = pl.multiple_of(sub * 16, 16)
            near, rows = pl.ds(inner, 16), pl.ds(base + inner, 16)
            live = row_mask(base + inner, 16, width, total_live)
            entry = jnp.where(live, adjoint_ref[rows, :].astype(F32), 0.0)
            grad = feed[near, :]
            value = unit[near, :]
            total = entry + norm_back(grad * table_ref[8:9, :], value, spread[near, 0:1])
            dx2_ref[rows, :] = total
            scaled = total * table_ref[7:8, :]
            for chunk in range(chunks):
                dw_ref[chunk, pl.ds(LEAD + base + inner, 16), :] = scaled[:, chunk_lanes(chunk)]
            return (
                carry[0] + fold(total * z_rows(rows)),
                carry[1] + fold(grad * value),
                carry[2] + fold(grad),
            )

        wide = jnp.zeros((8, width), F32)
        sums = lax.fori_loop(0, tile // 16, after, (wide, wide, wide))
        for index in range(3):
            grads[1 + index] += sums[index]

    owners, pieces, shard, _ = weight_grad_ref.shape
    inner = width // shard
    for owner in range(owners):
        rows = slice(owner % inner * shard, (owner % inner + 1) * shard)
        for piece in range(pieces):
            weight_grad_ref[owner, piece] = weight_sums[
                owner // inner * pieces + piece, rows, :
            ].astype(BF16)

    back_sums_ref[...] = zero
    for index, source in enumerate((1, 2, 3, 0)):
        grads_ref[index : index + 1, :] = jnp.sum(grads[source], axis=0, keepdims=True)
    for chunk in range(chunks):
        taps = tap_vectors(table_ref, 20, chunk)
        mean, scale = batch[chunk]

        def back_step(row, side, masks, carry, chunk=chunk, taps=taps, mean=mean, scale=scale):
            own = jnp.where(masks[0], n_ref[chunk, pl.ds(LEAD + row, 8), :], 0.0)
            total, tap_sums = conv_backward(dw_ref, chunk, row, side, masks, taps, own, carry[0])
            rows = pl.ds(row, 8)
            dn_ref[chunk, rows, :] = jnp.where(masks[0], total, dn_ref[chunk, rows, :])
            total = jnp.where(masks[0], total, 0.0)
            standard = (e_ref[chunk, rows, :] - mean) * scale
            return tap_sums, carry[1] + total * standard, carry[2] + total

        tap_sums, gamma, beta = for_groups(sides_ref, back_step, ((zero,) * 9, zero, zero))
        lanes = chunk_lanes(chunk)
        for index, value in enumerate((*tap_sums, gamma, beta)):
            value = jnp.sum(value, axis=0, keepdims=True)
            grads_ref[4 + index : 5 + index, lanes] = value
            if index == 9:
                back_sums_ref[chunks + chunk : chunks + chunk + 1, :] = value
            if index == 10:
                back_sums_ref[chunk : chunk + 1, :] = value


def feed_forward(sides, x1, e, batch_sums, weights, table, adjoint, grad_shape):
    row_count, width = x1.shape
    chunks = width // LANES
    expand = weights.shape[0] // 2
    tile = tile_rows(row_count)
    shape = jax.ShapeDtypeStruct
    return pl.pallas_call(
        feed_kernel,
        out_shape=(
            shape((row_count, width), BF16),
            shape((row_count, width), F32),
            shape((chunks, row_count, LANES), F32),
            shape(grad_shape, BF16),
            shape((16, width), F32),
            shape((8, LANES), F32),
        ),
        in_specs=[SMEM_SPEC] + [VMEM_SPEC] * 6,
        out_specs=(VMEM_SPEC,) * 6,
        scratch_shapes=[
            pltpu.VMEM((chunks, LEAD + row_count + TAIL, LANES), F32),
            pltpu.VMEM((chunks, row_count, LANES), F32),
            pltpu.VMEM((chunks, LEAD + row_count + TAIL, LANES), F32),
            pltpu.VMEM((tile, width), F32),
            pltpu.VMEM((tile, width), F32),
            pltpu.VMEM((tile, LANES), F32),
            pltpu.VMEM((tile, width), BF16),
            pltpu.VMEM((tile, expand * width), F32),
            pltpu.VMEM((tile, expand * width), BF16),
            pltpu.VMEM((tile, width), F32),
            pltpu.VMEM((tile, width), BF16),
            pltpu.VMEM((tile, expand * width), BF16),
            pltpu.VMEM((4, 8, width), F32),
            pltpu.VMEM((2 * expand, width, width), F32),
        ],
        compiler_params=pltpu.CompilerParams(vmem_limit_bytes=VMEM_LIMIT),
        name="feed_forward",
    )(sides, x1, e, batch_sums, weights, table, adjoint)


def mixing_backward_kernel(
    sides_ref,
    sharp_ref,
    input_ref,
    weight_ref,
    table_ref,
    x1_ref,
    qkv_ref,
    mixed_ref,
    scores_ref,
    attention_ref,
    u_hbm,
    bn_ref,
    dx2_ref,
    dn_hbm,
    back_ref,
    out_ref,
    weight_grad_ref,
    grads_ref,
    head_weights,
    out_weight,
    pool,
    conv_grad,
    dx1,
    mixed_grad,
    low_rows,
    head_low,
    spread,
    out_sum,
    sharp_sums,
    load_sems,
):
    row_count, width = input_ref.shape
    chunks = width // LANES
    u_ref, dn_ref = pool.at[0:chunks], pool.at[chunks : 2 * chunks]
    conv_in, attention_out = pool.at[2 * chunks : 3 * chunks], pool.at[3 * chunks : 4 * chunks]
    loads = [
        pltpu.make_async_copy(u_hbm, u_ref, load_sems.at[0]),
        pltpu.make_async_copy(dn_hbm, dn_ref, load_sems.at[1]),
    ]
    for load in loads:
        load.start()
    tile = tile_rows(row_count)
    total_live = live_total(sides_ref)
    batch = [batch_vectors(bn_ref, chunk, chunks) for chunk in range(chunks)]
    zero = jnp.zeros((8, LANES), F32)
    wide = jnp.zeros((8, width), F32)
    mapping = head_map(BF16)
    for part in range(3):
        head_weights[:, part * PAD_WIDTH : (part + 1) * PAD_WIDTH] = dot(
            weight_ref[part], mapping
        ).astype(BF16)
    out_weight[...] = dot_rows(mapping, weight_ref[3]).astype(BF16)
    spread[...] = jnp.zeros_like(spread)

    for load in loads:
        load.wait()

    def batch_back(step, _):
        first = pl.multiple_of(step * 32, 32)
        rows = pl.ds(first, 32)
        live = row_mask(first, 32, LANES, total_live)
        unit, _ = centered(x1_ref[rows, :])
        value = unit * table_ref[3:4, :] + table_ref[4:5, :]
        for chunk in range(chunks):
            lanes = chunk_lanes(chunk)
            mean, scale = batch[chunk]
            count = bn_ref[2 * chunks : 2 * chunks + 1, :]
            u = u_ref[chunk, rows, :]
            share, bell = gelu_parts(u)
            standard = (u * share - mean) * scale
            inner = (
                back_ref[chunk : chunk + 1, :]
                + standard * back_ref[chunks + chunk : chunks + chunk + 1, :]
            ) / count
            grad = scale * table_ref[5:6, lanes] * (dn_ref[chunk, rows, :] - inner)
            grad = grad * gelu_slope(u, share, bell)
            conv_grad[chunk, pl.ds(LEAD + first, 32), :] = jnp.where(live, grad, 0.0)
            conv_in[chunk, pl.ds(first, 32), :] = value[:, lanes]
        return 0

    lax.fori_loop(0, row_count // 32, batch_back, 0)

    for chunk in range(chunks):
        taps = tap_vectors(table_ref, 11, chunk)

        def back_step(row, side, masks, carry, chunk=chunk, taps=taps):
            rows = pl.ds(row, 8)
            held = conv_in[chunk, rows, :]
            own = jnp.where(masks[0], held, 0.0)
            total, tap_sums = conv_backward(conv_grad, chunk, row, side, masks, taps, own, carry)
            conv_in[chunk, rows, :] = jnp.where(masks[0], total, held)
            return tap_sums

        tap_sums = for_groups(sides_ref, back_step, (zero,) * 9)
        for index, value in enumerate(tap_sums):
            grads_ref[5 + index : 6 + index, chunk_lanes(chunk)] = jnp.sum(
                value, axis=0, keepdims=True
            )

    @pl.loop(0, row_count // tile)
    def _(step):
        rows = pl.ds(pl.multiple_of(step * tile, 16), tile)
        result = dot(mixed_ref[rows, :], out_weight[...])
        for chunk in range(chunks):
            attention_out[chunk, rows, :] = result[:, chunk_lanes(chunk)]

    def second_back(step, carry):
        first = pl.multiple_of(step * 16, 16)
        rows = pl.ds(first, 16)
        live = row_mask(first, 16, width, total_live)
        grad = jnp.concatenate([conv_in[chunk, rows, :] for chunk in range(chunks)], axis=1)
        grad = jnp.where(live, grad, 0.0)
        unit, scale = centered(x1_ref[rows, :])
        total = dx2_ref[rows, :] + norm_back(grad * table_ref[3:4, :], unit, scale)
        dx1[rows, :] = total
        low_rows[rows, :] = (total * table_ref[2:3, :]).astype(BF16)
        held = jnp.concatenate([attention_out[chunk, rows, :] for chunk in range(chunks)], axis=1)
        return (
            carry[0] + fold(total * held),
            carry[1] + fold(grad * unit),
            carry[2] + fold(grad),
        )

    sums = lax.fori_loop(0, row_count // 16, second_back, (wide, wide, wide))
    for index in range(3):
        grads_ref[2 + index : 3 + index, :] = jnp.sum(sums[index], axis=0, keepdims=True)

    out_sum[...] = jnp.zeros_like(out_sum)

    @pl.loop(0, row_count // tile)
    def _(step):
        rows = pl.ds(pl.multiple_of(step * tile, 16), tile)
        mixed_grad[rows, :] = dot_lanes(low_rows[rows, :], out_weight[...])
        out_sum[...] += dot_rows(mixed_ref[rows, :], low_rows[rows, :])

    pool[...] = jnp.zeros_like(pool)

    low = out_sum[...].astype(BF16)
    weight_grad_ref[3] = dot(mapping, low).astype(BF16)
    sharp_sums[...] = jnp.zeros_like(sharp_sums)

    def crop_step(crop, rows, keep):
        for half in range(2):
            lanes = [
                slice(part * PAD_WIDTH + half * HALF_WIDTH, part * PAD_WIDTH + (half + 1) * HALF_WIDTH)
                for part in range(3)
            ]
            query, query_scale = units(jnp.where(keep, qkv_ref[rows, lanes[0]], 0.0))
            key, key_scale = units(jnp.where(keep, qkv_ref[rows, lanes[1]], 0.0))
            value = split(jnp.where(keep, qkv_ref[rows, lanes[2]], 0.0))
            grad = split(jnp.where(keep, mixed_grad[rows, lanes[0]], 0.0))
            block = dot_split(dot_rows, value, grad)
            query_sums = []
            for pair in range(2):
                index = 2 * half + pair
                shares = attention_ref[crop, index]
                scores = scores_ref[crop, index]
                part = pair_part(block, pair)
                part = shares * (part - jnp.sum(part * shares, axis=0, keepdims=True))
                spread_pair(spread, half, pair, shares)
                sharp_sums[index : index + 1, :] += jnp.sum(part * scores, axis=0, keepdims=True)
                part = part * pair_sharpness(sharp_ref, index)
                query_sums.append(jnp.sum(part * scores, axis=0, keepdims=True))
                spread_pair(spread, 2 + half, pair, part)
            shares = (spread[half, 0], spread[half, 1])
            slopes = (spread[2 + half, 0], spread[2 + half, 1])
            value_grad = dot_split(dot_lanes, grad, shares)
            query_grad = dot_split(dot, split(key), slopes)
            query_grad = query_scale * (query_grad - query * jnp.concatenate(query_sums, axis=1))
            key_grad = dot_split(dot_lanes, split(query), slopes)
            key_grad = key_scale * (
                key_grad - key * jnp.sum(key_grad * key, axis=0, keepdims=True)
            )
            for part, result in enumerate((query_grad, key_grad, value_grad)):
                for side in range(HALF_WIDTH // LANES):
                    chunk = (part * PAD_WIDTH + half * HALF_WIDTH) // LANES + side
                    pool[chunk, rows, :] = jnp.where(
                        keep[:, 0:LANES], result[:, chunk_lanes(side)], pool[chunk, rows, :]
                    )

    for_crops(sides_ref, row_count, crop_step)

    grads_ref[14:16, :] = jnp.zeros((2, width), F32)
    lane = lax.broadcasted_iota(jnp.int32, (1, LANES), 1)
    total = jnp.zeros((1, LANES), F32)
    for head in range(HEAD_NUMBER):
        row = sharp_sums[head // 2 : head // 2 + 1, :]
        row = jnp.where((lane >> 6) == head % 2, row, 0.0)
        total = jnp.where(lane == head, jnp.sum(row, axis=1, keepdims=True), total)
    grads_ref[14:15, 0:LANES] = total

    def first_norm(step, _):
        rows = pl.ds(pl.multiple_of(step * 32, 32), 32)
        unit, _ = centered(input_ref[rows, :].astype(F32))
        low_rows[rows, :] = (unit * table_ref[0:1, :] + table_ref[1:2, :]).astype(BF16)
        return 0

    lax.fori_loop(0, row_count // 32, first_norm, 0)

    for part in range(3):
        lanes = slice(part * PAD_WIDTH, (part + 1) * PAD_WIDTH)
        out_sum[...] = jnp.zeros_like(out_sum)

        @pl.loop(0, row_count // tile)
        def _(step, lanes=lanes, part=part):
            rows = pl.ds(pl.multiple_of(step * tile, 16), tile)
            first = part * PAD_WIDTH // LANES
            for chunk in range(PAD_WIDTH // LANES):
                head_low[rows, chunk_lanes(chunk)] = pool[first + chunk, rows, :].astype(BF16)
            term = dot_lanes(head_low[rows, :], head_weights[:, lanes])
            mixed_grad[rows, 0:width] = term if part == 0 else mixed_grad[rows, 0:width] + term

        @pl.loop(0, row_count // tile)
        def _(step, lanes=lanes):
            rows = pl.ds(pl.multiple_of(step * tile, 16), tile)
            out_sum[...] += dot_rows(head_low[rows, :], low_rows[rows, :])

        low = out_sum[...].astype(BF16)
        weight_grad_ref[part] = lax.dot_general(
            low, mapping, (((0,), (1,)), ((), ())), preferred_element_type=F32
        ).astype(BF16)

    def first_back(step, carry):
        rows = pl.ds(pl.multiple_of(step * 16, 16), 16)
        unit, scale = centered(input_ref[rows, :].astype(F32))
        grad = mixed_grad[rows, 0:width]
        total = dx1[rows, :] + norm_back(grad * table_ref[0:1, :], unit, scale)
        out_ref[rows, :] = total.astype(BF16)
        return carry[0] + fold(grad * unit), carry[1] + fold(grad)

    sums = lax.fori_loop(0, row_count // 16, first_back, (wide, wide))
    for index in range(2):
        grads_ref[index : index + 1, :] = jnp.sum(sums[index], axis=0, keepdims=True)


def mixing_backward(sides, sharpness, inputs, weights, table, saved, batch_sums, dx2, dn, back_sums):
    row_count, width = inputs.shape
    chunks = width // LANES
    shape = jax.ShapeDtypeStruct
    x1, qkv, mixed, scores, attention, u = saved
    return pl.pallas_call(
        mixing_backward_kernel,
        out_shape=(
            shape((row_count, width), BF16),
            shape((4, width, width), BF16),
            shape((16, width), F32),
        ),
        in_specs=[SMEM_SPEC, SMEM_SPEC]
        + [VMEM_SPEC] * 8
        + [ANY_SPEC, VMEM_SPEC, VMEM_SPEC, ANY_SPEC, VMEM_SPEC],
        out_specs=(VMEM_SPEC,) * 3,
        scratch_shapes=[
            pltpu.VMEM((width, 3 * PAD_WIDTH), BF16),
            pltpu.VMEM((PAD_WIDTH, width), BF16),
            pltpu.VMEM((3 * PAD_WIDTH // LANES, row_count, LANES), F32),
            pltpu.VMEM((chunks, LEAD + row_count + TAIL, LANES), F32),
            pltpu.VMEM((row_count, width), F32),
            pltpu.VMEM((row_count, PAD_WIDTH), F32),
            pltpu.VMEM((row_count, width), BF16),
            pltpu.VMEM((row_count, PAD_WIDTH), BF16),
            pltpu.VMEM((4, 2, HALF_WIDTH, HALF_WIDTH), BF16),
            pltpu.VMEM((PAD_WIDTH, width), F32),
            pltpu.VMEM((HEAD_PAIRS, LANES), F32),
            pltpu.SemaphoreType.DMA((2,)),
        ],
        compiler_params=pltpu.CompilerParams(vmem_limit_bytes=VMEM_LIMIT),
        name="mixing_backward",
    )(
        sides,
        sharpness,
        inputs,
        weights,
        table,
        x1,
        qkv,
        mixed,
        scores,
        attention,
        u,
        batch_sums,
        dx2,
        dn,
        back_sums,
    )


MESH = pl.DeviceIdType.MESH


def greet(peers):
    barrier = pltpu.get_barrier_semaphore()
    for peer in peers:
        pl.semaphore_signal(barrier, inc=1, device_id=peer, device_id_type=MESH)
    pl.semaphore_wait(barrier, len(peers))


def push(source, target, send, receive, peer):
    copy = pltpu.make_async_remote_copy(
        src_ref=source,
        dst_ref=target,
        send_sem=send,
        recv_sem=receive,
        device_id=peer,
        device_id_type=MESH,
    )
    copy.start()
    return copy


def turned(place, step, count):
    return lax.rem(place + step, count)


def ring_peers(axis, count):
    place = lax.axis_index(axis)
    return [{axis: turned(place, step, count)} for step in range(1, count)]


def comm_params(identity):
    return pltpu.CompilerParams(
        collective_id=identity, has_side_effects=True, vmem_limit_bytes=VMEM_LIMIT
    )


def sum_all_kernel(
    counts, part_ref, total_ref, outer, inner, middle, outer_send, outer_recv, inner_send, inner_recv
):
    n_dp, n_fsdp = counts
    dp, fsdp = lax.axis_index("dp"), lax.axis_index("fsdp")
    inner_peers, outer_peers = ring_peers("fsdp", n_fsdp), ring_peers("dp", n_dp)
    greet(inner_peers + outer_peers)
    inner[fsdp] = part_ref[...]
    copies = [
        push(part_ref, inner.at[fsdp], inner_send.at[k], inner_recv.at[k], peer)
        for k, peer in enumerate(inner_peers)
    ]
    for copy in copies:
        copy.wait()
    total = inner[0]
    for k in range(1, n_fsdp):
        total = total + inner[k]
    middle[...] = total
    outer[dp] = total
    copies = [
        push(middle, outer.at[dp], outer_send.at[k], outer_recv.at[k], peer)
        for k, peer in enumerate(outer_peers)
    ]
    for copy in copies:
        copy.wait()
    total = outer[0]
    for k in range(1, n_dp):
        total = total + outer[k]
    total_ref[...] = total


def sum_all(part, counts, identity):
    n_dp, n_fsdp = counts
    return pl.pallas_call(
        functools.partial(sum_all_kernel, counts),
        out_shape=jax.ShapeDtypeStruct(part.shape, F32),
        in_specs=[VMEM_SPEC],
        out_specs=VMEM_SPEC,
        scratch_shapes=[
            pltpu.VMEM((n_dp, *part.shape), F32),
            pltpu.VMEM((n_fsdp, *part.shape), F32),
            pltpu.VMEM(part.shape, F32),
            pltpu.SemaphoreType.DMA((n_dp - 1,)),
            pltpu.SemaphoreType.DMA((n_dp - 1,)),
            pltpu.SemaphoreType.DMA((n_fsdp - 1,)),
            pltpu.SemaphoreType.DMA((n_fsdp - 1,)),
        ],
        compiler_params=comm_params(identity),
        name="sum_all",
    )(part)


def gather_kernel(
    counts,
    masters_ref,
    table_ref,
    blocks_ref,
    full_table_ref,
    blocks,
    tables,
    stage,
    ring_send,
    ring_recv,
    table_send,
    table_recv,
    cross_send,
    cross_recv,
    pair_send,
    pair_recv,
):
    n_dp, n_fsdp = counts
    dp, fsdp = lax.axis_index("dp"), lax.axis_index("fsdp")
    shard, width = masters_ref.shape[1:]
    columns = table_ref.shape[1]
    across = lax.rem(dp + 2, 4)
    pair = dp + 1 - 2 * lax.rem(dp, 2)
    peers = ring_peers("fsdp", n_fsdp)
    greet(peers + [{"dp": across}, {"dp": pair}])

    def piece(block, owner):
        return blocks.at[block, pl.ds(pl.multiple_of(owner * shard, 16), shard), :]

    def origin(step):
        return lax.rem(fsdp + n_fsdp - step, n_fsdp)

    stage[...] = jnp.zeros_like(stage)
    stage[0 : table_ref.shape[0], 0:columns] = table_ref[...]
    tables[fsdp] = stage[...].astype(BF16)
    blocks[dp, pl.ds(pl.multiple_of(fsdp * shard, 16), shard), :] = masters_ref[dp].astype(BF16)
    own = piece(dp, fsdp)
    ring = [
        push(own, own, ring_send.at[k], ring_recv.at[k], peer) for k, peer in enumerate(peers)
    ]
    table_copies = [
        push(tables.at[fsdp], tables.at[fsdp], table_send.at[k], table_recv.at[k], peer)
        for k, peer in enumerate(peers)
    ]
    crossing, pairing = [], []
    for step in range(n_fsdp):
        if step:
            ring[step - 1].wait_recv()
        part = piece(dp, origin(step))
        crossing.append(push(part, part, cross_send.at[step], cross_recv.at[step], {"dp": across}))
        pairing.append(
            push(part, part, pair_send.at[0, step], pair_recv.at[0, step], {"dp": pair})
        )
    for step in range(n_fsdp):
        crossing[step].wait_recv()
        part = piece(across, origin(step))
        pairing.append(
            push(part, part, pair_send.at[1, step], pair_recv.at[1, step], {"dp": pair})
        )
    for copy in table_copies:
        copy.wait_recv()
    total = None
    for owner in range(n_fsdp):
        lane = lax.broadcasted_iota(jnp.int32, (LANES, width), 0)
        target = lax.broadcasted_iota(jnp.int32, (LANES, width), 1)
        hit = (lane < columns) & (lane + owner * columns == target)
        term = dot(tables[owner], hit.astype(F32).astype(BF16))
        total = term if total is None else total + term
    full_table_ref[...] = total
    for copy in pairing:
        copy.wait_recv()
    blocks_ref[...] = blocks[...]
    for copy in ring + table_copies + crossing + pairing:
        copy.wait_send()


def gather_start(masters, coefficients, counts, identity):
    n_dp, n_fsdp = counts
    width = masters.shape[2]
    shape = jax.ShapeDtypeStruct
    dma = pltpu.SemaphoreType.DMA
    return pl.pallas_call(
        functools.partial(gather_kernel, counts),
        out_shape=(shape((4, width, width), BF16), shape((32, width), F32)),
        in_specs=[VMEM_SPEC, VMEM_SPEC],
        out_specs=(VMEM_SPEC, VMEM_SPEC),
        scratch_shapes=[
            pltpu.VMEM((4, width, width), BF16),
            pltpu.VMEM((n_fsdp, 32, LANES), BF16),
            pltpu.VMEM((32, LANES), F32),
            dma((n_fsdp - 1,)),
            dma((n_fsdp - 1,)),
            dma((n_fsdp - 1,)),
            dma((n_fsdp - 1,)),
            dma((n_fsdp,)),
            dma((n_fsdp,)),
            dma((2, n_fsdp)),
            dma((2, n_fsdp)),
        ],
        compiler_params=comm_params(identity),
        name="gather_start",
    )(masters, coefficients)


def owner_rows(owner, shard):
    return pl.ds(pl.multiple_of(owner * shard, 16), shard)


def reduce_kernel(
    counts,
    place_ref,
    mix_ref,
    feed_ref,
    mix_table_ref,
    feed_table_ref,
    energy_ref,
    coefficient_ref,
    sharp_ref,
    grad_ref,
    slots_ref,
    table_grad_ref,
    energy_out_ref,
    coefficient_out_ref,
    sharp_out_ref,
    pair_buf,
    cross_out,
    cross_buf,
    ring_out,
    ring_buf,
    feed_buf,
    dp_buf,
    slot_out,
    slots,
    table_stage,
    table_out,
    table_buf,
    table_part,
    table_dp,
    pair_send,
    pair_recv,
    cross_send,
    cross_recv,
    ring_send,
    ring_recv,
    feed_send,
    feed_recv,
    dp_send,
    dp_recv,
    slot_send,
    slot_recv,
    twin_send,
    twin_recv,
    table_send,
    table_recv,
    table_dp_send,
    table_dp_recv,
):
    n_dp, n_fsdp = counts
    dp, fsdp = lax.axis_index("dp"), lax.axis_index("fsdp")
    width = mix_ref.shape[2]
    shard = width // n_fsdp
    core = lax.rem(dp, 2)
    across = lax.rem(dp + 2, 4)
    pair = dp + 1 - 2 * core
    pair_across = lax.rem(pair + 2, 4)
    peers, dp_peers = ring_peers("fsdp", n_fsdp), ring_peers("dp", n_dp)
    to_pair, to_across = {"dp": pair}, {"dp": across}
    greet(peers + dp_peers)

    parts = 4
    deep = width // parts
    pairing = []
    for part in range(parts):
        rows = pl.ds(part * deep, deep)
        for side, block in enumerate((pair_across, pair)):
            pairing.append(
                push(
                    mix_ref.at[block, rows],
                    pair_buf.at[side, rows],
                    pair_send.at[side, part],
                    pair_recv.at[side, part],
                    to_pair,
                )
            )
    feed_buf[dp] = feed_ref[...]
    feeding = [
        push(feed_ref, feed_buf.at[dp], feed_send.at[k], feed_recv.at[k], peer)
        for k, peer in enumerate(dp_peers)
    ]

    table_stage[...] = jnp.zeros_like(table_stage)
    for row, (source, first) in enumerate(TABLE_ROWS):
        ref = mix_table_ref if source == 0 else feed_table_ref
        table_stage[row : row + 1, :] = ref[first : first + 1, :]
    terms, rest = [], table_stage[...]
    for _ in range(3):
        term = rest.astype(BF16)
        terms.append(term)
        rest = rest - term.astype(F32)
    columns = width // n_fsdp
    sharp_row = lax.broadcasted_iota(jnp.int32, (32, LANES), 0) == 31
    sharp_values = jnp.broadcast_to(mix_table_ref[14:15, 0:LANES], (32, LANES))
    for owner in range(n_fsdp):
        lane = lax.broadcasted_iota(jnp.int32, (width, LANES), 1)
        source = lax.broadcasted_iota(jnp.int32, (width, LANES), 0)
        hit = ((lane < columns) & (lane + owner * columns == source)).astype(F32).astype(BF16)
        value = dot(terms[0], hit) + dot(terms[1], hit) + dot(terms[2], hit)
        table_out[owner] = jnp.where(sharp_row, sharp_values, value)
    table_buf[fsdp] = table_out[fsdp]
    tabling = [
        push(
            table_out.at[turned(fsdp, k + 1, n_fsdp)],
            table_buf.at[fsdp],
            table_send.at[k],
            table_recv.at[k],
            peer,
        )
        for k, peer in enumerate(peers)
    ]

    crossing = []
    for part in range(parts):
        rows = pl.ds(part * deep, deep)
        pairing[2 * part].wait_recv()
        cross_out[rows, :] = (
            mix_ref[across, rows, :].astype(F32) + pair_buf[0, rows, :].astype(F32)
        ).astype(BF16)
        crossing.append(
            push(
                cross_out.at[rows],
                cross_buf.at[rows],
                cross_send.at[part],
                cross_recv.at[part],
                to_across,
            )
        )
    for part in range(parts):
        rows = pl.ds(part * deep, deep)
        pairing[2 * part + 1].wait_recv()
        crossing[part].wait_recv()
        ring_out[rows, :] = (
            mix_ref[dp, rows, :].astype(F32)
            + pair_buf[1, rows, :].astype(F32)
            + cross_buf[rows, :].astype(F32)
        ).astype(BF16)
    ring = [
        push(
            ring_out.at[owner_rows(turned(fsdp, k + 1, n_fsdp), shard)],
            ring_buf.at[fsdp],
            ring_send.at[k],
            ring_recv.at[k],
            peer,
        )
        for k, peer in enumerate(peers)
    ]
    ring_buf[fsdp] = ring_out[owner_rows(fsdp, shard), :]

    for copy in tabling:
        copy.wait_recv()
    total = table_buf[0]
    for owner in range(1, n_fsdp):
        total = total + table_buf[owner]
    table_part[...] = total
    table_dp[dp] = total
    table_dps = [
        push(table_part, table_dp.at[dp], table_dp_send.at[k], table_dp_recv.at[k], peer)
        for k, peer in enumerate(dp_peers)
    ]

    for copy in ring:
        copy.wait_recv()
    total = ring_buf[0].astype(F32)
    for owner in range(1, n_fsdp):
        total = total + ring_buf[owner].astype(F32)
    dp_buf[dp] = total
    gathering = [
        push(dp_buf.at[dp], dp_buf.at[dp], dp_send.at[k], dp_recv.at[k], peer)
        for k, peer in enumerate(dp_peers)
    ]
    for copy in feeding:
        copy.wait_recv()
    pieces = feed_ref.shape[0]
    for place in range(n_dp):
        for piece in range(pieces):
            grad_ref[n_dp + place * pieces + piece] = feed_buf[place, piece].astype(F32)
    for copy in gathering:
        copy.wait_recv()
    for place in range(n_dp):
        grad_ref[place] = dp_buf[place]

    slot_count = 2 * n_fsdp
    block_count = grad_ref.shape[0]
    for slot in range(slot_count):
        block, filled = jnp.int32(0), jnp.int32(0)
        for index in range(block_count):
            here = place_ref[index] == slot
            block = jnp.where(here, index, block)
            filled = jnp.where(here, 1, filled)
        rows = grad_ref[block]
        slot_out[slot] = (rows * filled.astype(F32)).astype(BF16)
    slots[core, owner_rows(fsdp, shard), :] = slot_out[2 * fsdp + core]
    slotting = [
        push(
            slot_out.at[2 * turned(fsdp, k + 1, n_fsdp) + core],
            slots.at[core, owner_rows(fsdp, shard), :],
            slot_send.at[k],
            slot_recv.at[k],
            peer,
        )
        for k, peer in enumerate(peers)
    ]
    twins = []
    for step in range(n_fsdp):
        if step:
            slotting[step - 1].wait_recv()
        owner = lax.rem(fsdp + n_fsdp - step, n_fsdp)
        part = slots.at[core, owner_rows(owner, shard), :]
        twins.append(push(part, part, twin_send.at[step], twin_recv.at[step], to_pair))

    for copy in table_dps:
        copy.wait_recv()
    total = table_dp[0]
    for place in range(1, n_dp):
        total = total + table_dp[place]
    count = energy_ref.shape[0]
    grad = total[0:count, 0:columns]
    table_grad_ref[...] = grad
    energy = covariance_forgetting * energy_ref[...] + (1.0 - covariance_forgetting) * grad * grad
    energy_out_ref[...] = energy
    coefficient_out_ref[...] = coefficient_ref[...] - vector_rate * grad / (
        jnp.sqrt(energy) + energy_epsilon
    )
    grad = total[31:32, 0:HEAD_NUMBER]
    energy = (
        covariance_forgetting * sharp_ref[1:2, :] + (1.0 - covariance_forgetting) * grad * grad
    )
    sharp_out_ref[0:1, :] = grad
    sharp_out_ref[1:2, :] = energy
    sharp_out_ref[2:3, :] = sharp_ref[0:1, :] - sharpness_step_size * grad / (
        jnp.sqrt(energy) + energy_epsilon
    )
    for copy in twins:
        copy.wait_recv()
    slots_ref[...] = slots[...]
    for copy in (
        pairing + feeding + tabling + crossing + ring + table_dps + gathering + slotting + twins
    ):
        copy.wait_send()


TABLE_ROWS = (
    [(0, row) for row in range(5)]
    + [(1, 13), (1, 14)]
    + [(1, row) for row in range(4)]
    + [(0, row) for row in range(5, 14)]
    + [(1, row) for row in range(4, 13)]
)


def reduce_gradients(
    places, mix, feed, mix_table, feed_table, energy, coefficients, sharps, counts, identity
):
    n_dp, n_fsdp = counts
    width = mix.shape[2]
    shard = width // n_fsdp
    blocks = n_dp + feed.shape[0] * n_dp
    shape = jax.ShapeDtypeStruct
    dma = pltpu.SemaphoreType.DMA
    return pl.pallas_call(
        functools.partial(reduce_kernel, counts),
        out_shape=(
            shape((blocks, shard, width), F32),
            shape((2, width, width), BF16),
            shape(energy.shape, F32),
            shape(energy.shape, F32),
            shape(energy.shape, F32),
            shape((3, sharps.shape[1]), F32),
        ),
        in_specs=[SMEM_SPEC] + [VMEM_SPEC] * 7,
        out_specs=(VMEM_SPEC,) * 6,
        scratch_shapes=[
            pltpu.VMEM((2, width, width), BF16),
            pltpu.VMEM((width, width), BF16),
            pltpu.VMEM((width, width), BF16),
            pltpu.VMEM((width, width), BF16),
            pltpu.VMEM((n_fsdp, shard, width), BF16),
            pltpu.VMEM((n_dp, *feed.shape), BF16),
            pltpu.VMEM((n_dp, shard, width), F32),
            pltpu.VMEM((2 * n_fsdp, shard, width), BF16),
            pltpu.VMEM((2, width, width), BF16),
            pltpu.VMEM((32, width), F32),
            pltpu.VMEM((n_fsdp, 32, LANES), F32),
            pltpu.VMEM((n_fsdp, 32, LANES), F32),
            pltpu.VMEM((32, LANES), F32),
            pltpu.VMEM((n_dp, 32, LANES), F32),
            dma((2, 4)),
            dma((2, 4)),
            dma((4,)),
            dma((4,)),
            dma((n_fsdp - 1,)),
            dma((n_fsdp - 1,)),
            dma((n_dp - 1,)),
            dma((n_dp - 1,)),
            dma((n_dp - 1,)),
            dma((n_dp - 1,)),
            dma((n_fsdp - 1,)),
            dma((n_fsdp - 1,)),
            dma((n_fsdp,)),
            dma((n_fsdp,)),
            dma((n_fsdp - 1,)),
            dma((n_fsdp - 1,)),
            dma((n_dp - 1,)),
            dma((n_dp - 1,)),
        ],
        compiler_params=comm_params(identity),
        name="reduce_gradients",
    )(places, mix, feed, mix_table, feed_table, energy, coefficients, sharps)


def shampoo_kernel(grad_ref, left_ref, right_ref, left_root, right_root, left_out, right_out, step_ref):
    grad = grad_ref[...]
    left_out[...] = covariance_forgetting * left_ref[...] + (
        1.0 - covariance_forgetting
    ) * dot_lanes(grad, grad)
    right_out[...] = covariance_forgetting * right_ref[...] + (
        1.0 - covariance_forgetting
    ) * dot_rows(grad, grad)
    root = split(left_root[...])
    half = split(dot(root[0], grad) + dot(root[1], grad))
    step_ref[...] = dot_split(dot, half, split(right_root[...])).astype(BF16)


def shampoo(grads, left, right, left_root, right_root):
    slots, width, _ = grads.shape
    shape = jax.ShapeDtypeStruct
    spec = pl.BlockSpec((pl.Squeezed(), width, width), lambda slot: (slot, 0, 0))
    return pl.pallas_call(
        shampoo_kernel,
        grid=(slots,),
        out_shape=(
            shape(grads.shape, F32),
            shape(grads.shape, F32),
            shape(grads.shape, BF16),
        ),
        in_specs=[spec] * 5,
        out_specs=(spec,) * 3,
        compiler_params=pltpu.CompilerParams(vmem_limit_bytes=VMEM_LIMIT),
        name="shampoo",
    )(grads, left, right, left_root, right_root)


def return_kernel(
    counts, steps_ref, rows_ref, rows_buf, ring_send, ring_recv, twin_send, twin_recv
):
    n_dp, n_fsdp = counts
    dp, fsdp = lax.axis_index("dp"), lax.axis_index("fsdp")
    width = steps_ref.shape[2]
    shard = width // n_fsdp
    core = lax.rem(dp, 2)
    to_pair = {"dp": dp + 1 - 2 * core}
    peers = ring_peers("fsdp", n_fsdp)
    greet(peers + [to_pair])
    ring = [
        push(
            steps_ref.at[core, owner_rows(turned(fsdp, k + 1, n_fsdp), shard)],
            rows_buf.at[2 * fsdp + core],
            ring_send.at[k],
            ring_recv.at[k],
            peer,
        )
        for k, peer in enumerate(peers)
    ]
    rows_buf[2 * fsdp + core] = steps_ref[core, owner_rows(fsdp, shard), :]
    twins = []
    for step in range(n_fsdp):
        if step:
            ring[step - 1].wait_recv()
        owner = lax.rem(fsdp + n_fsdp - step, n_fsdp)
        part = rows_buf.at[2 * owner + core]
        twins.append(push(part, part, twin_send.at[step], twin_recv.at[step], to_pair))
    for copy in twins:
        copy.wait_recv()
    rows_ref[...] = rows_buf[...]
    for copy in ring + twins:
        copy.wait_send()


def return_steps(steps, counts, identity):
    n_dp, n_fsdp = counts
    width = steps.shape[2]
    shard = width // n_fsdp
    dma = pltpu.SemaphoreType.DMA
    return pl.pallas_call(
        functools.partial(return_kernel, counts),
        out_shape=jax.ShapeDtypeStruct((2 * n_fsdp, shard, width), BF16),
        in_specs=[VMEM_SPEC],
        out_specs=VMEM_SPEC,
        scratch_shapes=[
            pltpu.VMEM((2 * n_fsdp, shard, width), BF16),
            dma((n_fsdp - 1,)),
            dma((n_fsdp - 1,)),
            dma((n_fsdp,)),
            dma((n_fsdp,)),
        ],
        compiler_params=comm_params(identity),
        name="return_steps",
    )(steps)


def shards(
    patch_embeddings,
    view_side_tokens,
    projection_masters,
    channel_coefficients,
    head_sharpness,
    output_adjoint,
    leading_covariance,
    trailing_covariance,
    leading_root_preconditioner,
    trailing_root_preconditioner,
    channel_energy_average,
    sharpness_energy_average,
    storage_position_map,
):
    row_count, feature_count = patch_embeddings.shape
    block_count = projection_masters.shape[0]
    shard_rows = projection_masters.shape[1]
    slot_count = leading_covariance.shape[0]
    counts = (lax.axis_size("dp"), lax.axis_size("fsdp"))
    direct = counts[0] == 4 and slot_count == 2 and shard_rows % 16 == 0
    if direct:
        mixing_blocks, table = gather_start(projection_masters, channel_coefficients, counts, 0)
        grad_shape = (counts[0] * counts[1], (block_count - 4) // counts[0], shard_rows, feature_count)
    else:
        full_table = lax.all_gather(channel_coefficients.astype(BF16), "fsdp", axis=1, tiled=True)
        table = full_table.astype(F32)
        mixing_blocks = lax.all_gather(
            projection_masters[:4].astype(BF16), "fsdp", axis=1, tiled=True
        )
        grad_shape = (1, block_count - 4, feature_count, feature_count)
    feed_blocks = lax.all_gather(projection_masters[4:].astype(BF16), "fsdp", axis=1, tiled=True)

    def batch_total(part, identity):
        if direct:
            return sum_all(part, counts, identity)
        return lax.psum(part, ("dp", "fsdp"))

    x1, qkv, mixed, scores, attention, u, e, sums = mixing_forward(
        view_side_tokens, head_sharpness, patch_embeddings, mixing_blocks, table
    )
    batch_sums = batch_total(sums, 1)
    layer_output, dx2, dn, feed_grad, feed_table, back_part = feed_forward(
        view_side_tokens, x1, e, batch_sums, feed_blocks, table, output_adjoint, grad_shape
    )
    back_sums = batch_total(back_part, 2)
    incoming_tokens_grad, mixing_grad, mixing_table = mixing_backward(
        view_side_tokens,
        head_sharpness,
        patch_embeddings,
        mixing_blocks,
        table,
        (x1, qkv, mixed, scores, attention, u),
        batch_sums,
        dx2,
        dn,
        back_sums,
    )
    if direct:
        feed_grad = lax.psum_scatter(
            feed_grad, ("dp", "fsdp"), scatter_dimension=0, tiled=True
        )[0]
        (
            portion_derivative,
            owned_grad,
            catalog_portion,
            channel_energy_renewed,
            channel_params_updated,
            sharps,
        ) = reduce_gradients(
            storage_position_map,
            mixing_grad,
            feed_grad,
            mixing_table,
            feed_table,
            channel_energy_average,
            channel_coefficients,
            jnp.stack([head_sharpness, sharpness_energy_average]),
            counts,
            3,
        )
        leading_covariance_renewed, trailing_covariance_renewed, steps = shampoo(
            owned_grad,
            leading_covariance,
            trailing_covariance,
            leading_root_preconditioner,
            trailing_root_preconditioner,
        )
        my_rows = return_steps(steps, counts, 4)
        update = jnp.take(my_rows, storage_position_map, axis=0).astype(F32)
        projection_updated = projection_masters - weight_rate * update
        return (
            layer_output,
            incoming_tokens_grad,
            portion_derivative,
            leading_covariance_renewed,
            trailing_covariance_renewed,
            projection_updated,
            projection_updated.astype(BF16),
            catalog_portion,
            channel_energy_renewed,
            channel_params_updated,
            *sharps,
        )
    sharpness_share = mixing_table[14, 0:HEAD_NUMBER]
    table_grad = jnp.stack([(mixing_table, feed_table)[source][row] for source, row in TABLE_ROWS])
    block_grad = jnp.concatenate([mixing_grad, feed_grad[0]], axis=0).astype(F32)
    denominator_sum = lax.axis_size("fsdp")
    tiled_part = jnp.broadcast_to(
        sharpness_share[None, :], (denominator_sum, sharpness_share.shape[0])
    )
    portion_derivative, catalog_portion, sharpness_normalizer = (
        lax.psum_scatter(block_grad, "fsdp", scatter_dimension=1, tiled=True),
        lax.psum_scatter(table_grad, "fsdp", scatter_dimension=1, tiled=True),
        lax.psum_scatter(tiled_part, "fsdp", scatter_dimension=0, tiled=True),
    )
    portion_derivative, catalog_portion, sharpness_normalizer = lax.psum(
        (portion_derivative, catalog_portion, sharpness_normalizer), "dp"
    )
    sharpness_derivative = sharpness_normalizer[0]
    shard_place = lax.axis_index("fsdp")
    slot_index = jnp.arange(denominator_sum * slot_count, dtype=jnp.int32)
    slot_match = storage_position_map[None, :] == slot_index[:, None]
    slot_filled = jnp.any(slot_match, axis=1).astype(jnp.float32)[:, None, None]
    slot_block = jnp.sum(
        jnp.where(slot_match, jnp.arange(block_count, dtype=jnp.int32)[None, :], 0), axis=1
    )
    my_filled = lax.dynamic_slice_in_dim(slot_filled, shard_place * slot_count, slot_count, 0)
    my_block = lax.dynamic_slice_in_dim(slot_block, shard_place * slot_count, slot_count, 0)
    whole_grad = lax.all_gather(portion_derivative, "fsdp", axis=1, tiled=True)
    owned_grad = jnp.take(whole_grad, my_block, axis=0) * my_filled
    leading_covariance_renewed = covariance_forgetting * leading_covariance + (
        1.0 - covariance_forgetting
    ) * jnp.einsum("sij,skj->sik", owned_grad, owned_grad, precision=lax.Precision.HIGHEST)
    trailing_covariance_renewed = covariance_forgetting * trailing_covariance + (
        1.0 - covariance_forgetting
    ) * jnp.einsum("sji,sjk->sik", owned_grad, owned_grad, precision=lax.Precision.HIGHEST)
    halfway = jnp.einsum(
        "sij,sjk->sik", leading_root_preconditioner, owned_grad, precision=lax.Precision.HIGHEST
    )
    conditioned = jnp.einsum(
        "sij,sjk->sik", halfway, trailing_root_preconditioner, precision=lax.Precision.HIGHEST
    )
    every_update = lax.all_gather(conditioned, "fsdp", axis=0, tiled=True)
    my_rows = lax.dynamic_slice_in_dim(every_update, shard_place * shard_rows, shard_rows, 1)
    update = jnp.take(my_rows, storage_position_map, axis=0)
    projection_updated = projection_masters - weight_rate * update
    channel_energy_renewed = (
        covariance_forgetting * channel_energy_average
        + (1.0 - covariance_forgetting) * catalog_portion * catalog_portion
    )
    channel_params_updated = channel_coefficients - vector_rate * catalog_portion / (
        jnp.sqrt(channel_energy_renewed) + energy_epsilon
    )
    sharpness_energy_renewed = (
        covariance_forgetting * sharpness_energy_average
        + (1.0 - covariance_forgetting) * sharpness_derivative * sharpness_derivative
    )
    sharpness_updated = head_sharpness - sharpness_step_size * sharpness_derivative / (
        jnp.sqrt(sharpness_energy_renewed) + energy_epsilon
    )
    return (
        layer_output,
        incoming_tokens_grad,
        portion_derivative,
        leading_covariance_renewed,
        trailing_covariance_renewed,
        projection_updated,
        projection_updated.astype(jnp.bfloat16),
        catalog_portion,
        channel_energy_renewed,
        channel_params_updated,
        sharpness_derivative,
        sharpness_energy_renewed,
        sharpness_updated,
    )


def solution(mesh):
    in_specs = (
        P(("dp", "fsdp"), None),
        P(("dp", "fsdp")),
        P(None, "fsdp", None),
        P(None, "fsdp"),
        P(),
        P(("dp", "fsdp"), None),
        P("fsdp", None, None),
        P("fsdp", None, None),
        P("fsdp", None, None),
        P("fsdp", None, None),
        P(None, "fsdp"),
        P(),
        P(),
    )
    out_specs = (
        P(("dp", "fsdp"), None),
        P(("dp", "fsdp"), None),
        P(None, "fsdp", None),
        P("fsdp", None, None),
        P("fsdp", None, None),
        P(None, "fsdp", None),
        P(None, "fsdp", None),
        P(None, "fsdp"),
        P(None, "fsdp"),
        P(None, "fsdp"),
        P(),
        P(),
        P(),
    )
    return jax.shard_map(shards, mesh=mesh, in_specs=in_specs, out_specs=out_specs, check_vma=False)
```

```python
import functools

import jax
import jax.numpy as jnp
from jax import lax
from jax.experimental import pallas as pl
from jax.experimental.pallas import tpu as pltpu
from jax.sharding import PartitionSpec as P

HEAD_NUMBER = 8
HDIM = 48
HEAD_PAD = 64
LANES = 128
HEAD_PAIRS = HEAD_NUMBER // 2
PAD_WIDTH = HEAD_NUMBER * HEAD_PAD
HALF_WIDTH = PAD_WIDTH // 2
LEAD = 16
TAIL = 32
SMALL_WINDOW = 48
LARGE_WINDOW = 208
ROW_TILE = 464
GELU_TILE = 128
VMEM_LIMIT = 58 * 2**20

norm_epsilon = 1e-06
batch_epsilon = 1e-05
attention_epsilon = 1e-06
covariance_forgetting = 0.5
weight_rate = 0.5
vector_rate = 0.1
sharpness_step_size = 2.0
energy_epsilon = 1e-08

F32 = jnp.float32
BF16 = jnp.bfloat16
VMEM_SPEC = pl.BlockSpec(memory_space=pltpu.VMEM)
ANY_SPEC = pl.BlockSpec(memory_space=pl.ANY)
SMEM_SPEC = pl.BlockSpec(memory_space=pltpu.SMEM)


def dot(left, right):
    return lax.dot_general(left, right, (((1,), (0,)), ((), ())), preferred_element_type=F32)


def dot_rows(left, right):
    return lax.dot_general(left, right, (((0,), (0,)), ((), ())), preferred_element_type=F32)


def dot_lanes(left, right):
    return lax.dot_general(left, right, (((1,), (1,)), ((), ())), preferred_element_type=F32)


def split(values):
    high = values.astype(BF16)
    return high, (values - high.astype(F32)).astype(BF16)


def dot_split(product, left, right):
    return (
        product(left[0], right[0]) + product(left[0], right[1]) + product(left[1], right[0])
    )


def fold(values):
    total = values[0:8]
    for first in range(8, values.shape[0], 8):
        total = total + values[first : first + 8]
    return total


def gelu_parts(values):
    magnitude = jnp.abs(values) * 0.7071067811865476
    base = 1.0 + 0.3275911 * magnitude
    guess = pl.reciprocal(base, approx=True)
    slot = guess * (2.0 - base * guess)
    series = slot * (
        0.127414796
        + slot
        * (-0.142248368 + slot * (0.7107068705 + slot * (-0.7265760135 + slot * 0.5307027145)))
    )
    bell = jnp.exp(-0.5 * values * values)
    lower = series * bell
    return jnp.where(values >= 0, 1.0 - lower, lower), bell


def gelu_slope(values, share, bell):
    return share + values * bell * 0.3989422804014327


def head_map(dtype):
    feature = lax.broadcasted_iota(jnp.int32, (HEAD_NUMBER * HDIM, PAD_WIDTH), 0)
    lane = lax.broadcasted_iota(jnp.int32, (HEAD_NUMBER * HDIM, PAD_WIDTH), 1)
    inner = lane & (HEAD_PAD - 1)
    hit = (inner < HDIM) & ((lane >> 6) * HDIM + inner == feature)
    return hit.astype(F32).astype(dtype)


def centered(values):
    center = jnp.sum(values, axis=-1, keepdims=True) * (1.0 / values.shape[-1])
    shifted = values - center
    spread = jnp.sum(shifted * shifted, axis=-1, keepdims=True) * (1.0 / values.shape[-1])
    scale = lax.rsqrt(spread + norm_epsilon)
    return shifted * scale, scale


def norm_back(grad, unit, scale):
    size = 1.0 / grad.shape[-1]
    middle = jnp.sum(grad, axis=-1, keepdims=True) * size
    slope = jnp.sum(grad * unit, axis=-1, keepdims=True) * size
    return scale * (grad - middle - unit * slope)


def tile_rows(count):
    for parts in range(4, count // 16 + 1):
        if count % (16 * parts) == 0:
            return count // parts
    return count


def for_rows(count, tile, step, carry=0):
    def body(index, carry):
        return step(pl.multiple_of(index * tile, tile), tile, carry)

    carry = lax.fori_loop(0, count // tile, body, carry)
    if count % tile:
        carry = step(count - count % tile, count % tile, carry)
    return carry


def live_total(sides_ref):
    return lax.fori_loop(
        0, sides_ref.shape[0], lambda c, t: t + sides_ref[c] * sides_ref[c], jnp.int32(0)
    )


def row_mask(first, rows, width, limit):
    return lax.broadcasted_iota(jnp.int32, (rows, width), 0) + first < limit


def for_groups(sides_ref, step, carry):
    def crop_body(crop, state):
        start, carry = state
        side = sides_ref[crop]
        cells = side * side
        inverse = 1.0 / jnp.full((8, LANES), side, jnp.int32).astype(F32)
        lines = lax.broadcasted_iota(jnp.int32, (8, LANES), 0)

        def group_body(group, carry):
            for part in range(2):
                row = pl.multiple_of((group * 2 + part) * 8, 8)
                place = lines + (row - start)
                line = ((place.astype(F32) + 0.5) * inverse).astype(jnp.int32)
                column = place - line * side
                inside = (place >= 0) & (place < cells)
                masks = (
                    inside,
                    column >= 1,
                    column < side - 1,
                    place >= side,
                    place < cells - side,
                )
                carry = step(row, side, masks, carry)
            return carry

        carry = lax.fori_loop(start // 16, (start + cells + 15) // 16, group_body, carry)
        return start + cells, carry

    return lax.fori_loop(0, sides_ref.shape[0], crop_body, (jnp.int32(0), carry))[1]


def conv_forward(source, chunk, row, side, masks, taps):
    inside, left_ok, right_ok, up_ok, down_ok = masks
    total = None
    for shift in (-1, 0, 1):
        base = LEAD + row + shift * side
        middle = source[chunk, pl.ds(base, 8), :]
        left = jnp.where(left_ok, source[chunk, pl.ds(base - 1, 8), :], 0.0)
        right = jnp.where(right_ok, source[chunk, pl.ds(base + 1, 8), :], 0.0)
        first = 3 * (shift + 1)
        value = taps[first] * left + taps[first + 1] * middle + taps[first + 2] * right
        if shift == -1:
            value = jnp.where(up_ok, value, 0.0)
        if shift == 1:
            value = jnp.where(down_ok, value, 0.0)
        total = value if total is None else total + value
    return total


def conv_backward(source, chunk, row, side, masks, taps, own, tap_sums):
    inside, left_ok, right_ok, up_ok, down_ok = masks
    total = None
    tap_sums = list(tap_sums)
    for shift in (-1, 0, 1):
        base = LEAD + row + shift * side
        row_ok = {-1: up_ok, 0: None, 1: down_ok}[shift]
        for sway in (-1, 0, 1):
            column_ok = {-1: left_ok, 0: None, 1: right_ok}[sway]
            value = source[chunk, pl.ds(base + sway, 8), :]
            keep = inside
            if row_ok is not None:
                keep = keep & row_ok
            if column_ok is not None:
                keep = keep & column_ok
            value = jnp.where(keep, value, 0.0)
            index = 3 * (1 - shift) + (1 - sway)
            term = taps[index] * value
            total = term if total is None else total + term
            tap_sums[index] = tap_sums[index] + own * value
    return total, tuple(tap_sums)


def chunk_lanes(chunk):
    return slice(chunk * LANES, (chunk + 1) * LANES)


def tap_vectors(table_ref, first, chunk):
    return [
        jnp.broadcast_to(table_ref[first + k : first + k + 1, chunk_lanes(chunk)], (8, LANES))
        for k in range(9)
    ]


def for_crops(sides_ref, row_count, step):
    def crop_body(crop, start):
        side = sides_ref[crop]
        cells = side * side
        for window, fits in ((SMALL_WINDOW, side <= 6), (LARGE_WINDOW, side > 6)):

            @pl.when(fits)
            def _():
                first = pl.multiple_of(
                    jnp.minimum(start // 8, (row_count - window) // 8) * 8, 8
                )
                place = lax.broadcasted_iota(jnp.int32, (window, HALF_WIDTH), 0) + (first - start)
                step(crop, pl.ds(first, window), (place >= 0) & (place < cells))

        return start + cells

    lax.fori_loop(0, sides_ref.shape[0], crop_body, jnp.int32(0))


def pair_lanes():
    return lax.broadcasted_iota(jnp.int32, (HDIM, LANES), 1) < HEAD_PAD


def pair_part(block, pair):
    first = pair * LANES
    lanes = slice(first, first + LANES)
    return jnp.where(
        pair_lanes(),
        block[first : first + HDIM, lanes],
        block[first + HEAD_PAD : first + HEAD_PAD + HDIM, lanes],
    )


def spread_pair(target, half, pair, values):
    first = pair * LANES
    lanes = slice(first, first + LANES)
    parts = split(values)
    for index in range(2):
        value = parts[index].astype(F32)
        target[half, index, first : first + HDIM, lanes] = jnp.where(
            pair_lanes(), value, 0.0
        ).astype(BF16)
        target[half, index, first + HEAD_PAD : first + HEAD_PAD + HDIM, lanes] = jnp.where(
            pair_lanes(), 0.0, value
        ).astype(BF16)


def pair_sharpness(sharp_ref, pair):
    lane = lax.broadcasted_iota(jnp.int32, (1, LANES), 1)
    return jnp.where(lane < HEAD_PAD, sharp_ref[2 * pair], sharp_ref[2 * pair + 1])


def units(values):
    scale = lax.rsqrt(jnp.sum(values * values, axis=0, keepdims=True) + attention_epsilon)
    return values * scale, scale


def mixing_forward_kernel(
    sides_ref,
    sharp_ref,
    input_ref,
    weight_ref,
    table_ref,
    x1_ref,
    qkv_ref,
    mixed_ref,
    scores_ref,
    attention_ref,
    u_ref,
    e_ref,
    sums_ref,
    head_weights,
    out_weight,
    first_low,
    mixed,
    attention_out,
    conv_in,
    spread,
):
    row_count, width = input_ref.shape
    chunks = width // LANES
    tile = tile_rows(row_count)
    total_live = live_total(sides_ref)
    mapping = head_map(BF16)
    for part in range(3):
        head_weights[:, part * PAD_WIDTH : (part + 1) * PAD_WIDTH] = dot(
            weight_ref[part], mapping
        ).astype(BF16)
    spread[...] = jnp.zeros_like(spread)

    def first_norm(first, size, _):
        rows = pl.ds(first, size)
        unit, _ = centered(input_ref[rows, :].astype(F32))
        first_low[rows, :] = (unit * table_ref[0:1, :] + table_ref[1:2, :]).astype(BF16)
        mixed[rows, :] = jnp.zeros((size, PAD_WIDTH), F32)
        return 0

    for_rows(row_count, ROW_TILE, first_norm)

    @pl.loop(0, row_count // tile)
    def _(step):
        rows = pl.ds(pl.multiple_of(step * tile, 16), tile)
        for part in range(3):
            lanes = slice(part * PAD_WIDTH, (part + 1) * PAD_WIDTH)
            qkv_ref[rows, lanes] = dot(first_low[rows, :], head_weights[:, lanes])

    def crop_step(crop, rows, keep):
        for half in range(2):
            lanes = [
                slice(part * PAD_WIDTH + half * HALF_WIDTH, part * PAD_WIDTH + (half + 1) * HALF_WIDTH)
                for part in range(3)
            ]
            query = units(jnp.where(keep, qkv_ref[rows, lanes[0]], 0.0))[0]
            key = units(jnp.where(keep, qkv_ref[rows, lanes[1]], 0.0))[0]
            block = dot_split(dot_rows, split(key), split(query))
            for pair in range(2):
                scores = pair_part(block, pair)
                scores_ref[crop, 2 * half + pair] = scores
                scores = scores * pair_sharpness(sharp_ref, 2 * half + pair)
                scores = jnp.exp(scores - jnp.max(scores, axis=0, keepdims=True))
                shares = scores / jnp.sum(scores, axis=0, keepdims=True)
                attention_ref[crop, 2 * half + pair] = shares
                spread_pair(spread, half, pair, shares)
            result = dot_split(
                dot, split(qkv_ref[rows, lanes[2]]), (spread[half, 0], spread[half, 1])
            )
            mixed[rows, lanes[0]] = jnp.where(keep, result, mixed[rows, lanes[0]])

    for_crops(sides_ref, row_count, crop_step)

    out_weight[...] = dot_rows(mapping, weight_ref[3]).astype(BF16)

    @pl.loop(0, row_count // tile)
    def _(step):
        rows = pl.ds(pl.multiple_of(step * tile, 16), tile)
        low = mixed[rows, :].astype(BF16)
        mixed_ref[rows, :] = low
        attention_out[rows, :] = dot(low, out_weight[...])

    def second_norm(first, size, _):
        rows = pl.ds(first, size)
        value = input_ref[rows, :].astype(F32) + table_ref[2:3, :] * attention_out[rows, :]
        x1_ref[rows, :] = value
        unit, _ = centered(value)
        value = unit * table_ref[3:4, :] + table_ref[4:5, :]
        for chunk in range(chunks):
            conv_in[chunk, pl.ds(LEAD + first, size), :] = value[:, chunk_lanes(chunk)]
            u_ref[chunk, rows, :] = jnp.zeros((size, LANES), F32)
            e_ref[chunk, rows, :] = jnp.zeros((size, LANES), F32)
        return 0

    for_rows(row_count, ROW_TILE, second_norm)

    zero = jnp.zeros((8, LANES), F32)
    sums_ref[...] = zero
    taps = [tap_vectors(table_ref, 11, chunk) for chunk in range(chunks)]

    def conv_step(row, side, masks, carry):
        rows = pl.ds(row, 8)
        carry = list(carry)
        for chunk in range(chunks):
            value = conv_forward(conv_in, chunk, row, side, masks, taps[chunk])
            share, _ = gelu_parts(value)
            active = value * share
            u_ref[chunk, rows, :] = jnp.where(masks[0], value, u_ref[chunk, rows, :])
            e_ref[chunk, rows, :] = jnp.where(masks[0], active, e_ref[chunk, rows, :])
            active = jnp.where(masks[0], active, 0.0)
            carry[chunk] = carry[chunk] + active
            carry[chunks + chunk] = carry[chunks + chunk] + active * active
        return tuple(carry)

    sums = for_groups(sides_ref, conv_step, (zero,) * (2 * chunks))
    for index, value in enumerate(sums):
        sums_ref[index : index + 1, :] = jnp.sum(value, axis=0, keepdims=True)
    sums_ref[2 * chunks : 2 * chunks + 1, :] = jnp.full((1, LANES), total_live, jnp.int32).astype(F32)


def mixing_forward(sides, sharpness, inputs, weights, table):
    row_count, width = inputs.shape
    crops = sides.shape[0]
    chunks = width // LANES
    shape = jax.ShapeDtypeStruct
    return pl.pallas_call(
        mixing_forward_kernel,
        out_shape=(
            shape((row_count, width), F32),
            shape((row_count, 3 * PAD_WIDTH), F32),
            shape((row_count, PAD_WIDTH), BF16),
            shape((crops, HEAD_PAIRS, HDIM, LANES), F32),
            shape((crops, HEAD_PAIRS, HDIM, LANES), F32),
            shape((chunks, row_count, LANES), F32),
            shape((chunks, row_count, LANES), F32),
            shape((8, LANES), F32),
        ),
        in_specs=[SMEM_SPEC, SMEM_SPEC, VMEM_SPEC, VMEM_SPEC, VMEM_SPEC],
        out_specs=(VMEM_SPEC,) * 8,
        scratch_shapes=[
            pltpu.VMEM((width, 3 * PAD_WIDTH), BF16),
            pltpu.VMEM((PAD_WIDTH, width), BF16),
            pltpu.VMEM((row_count, width), BF16),
            pltpu.VMEM((row_count, PAD_WIDTH), F32),
            pltpu.VMEM((row_count, width), F32),
            pltpu.VMEM((chunks, LEAD + row_count + TAIL, LANES), F32),
            pltpu.VMEM((2, 2, HALF_WIDTH, HALF_WIDTH), BF16),
        ],
        compiler_params=pltpu.CompilerParams(vmem_limit_bytes=VMEM_LIMIT),
        name="mixing_forward",
    )(sides, sharpness, inputs, weights, table)


def batch_vectors(bn_ref, chunk, chunks):
    count = bn_ref[2 * chunks : 2 * chunks + 1, :]
    mean = bn_ref[chunk : chunk + 1, :] / count
    scale = lax.rsqrt(bn_ref[chunks + chunk : chunks + chunk + 1, :] / count - mean * mean + batch_epsilon)
    return mean, scale


def feed_kernel(
    sides_ref,
    x1_ref,
    e_ref,
    bn_ref,
    weight_ref,
    table_ref,
    adjoint_ref,
    out_ref,
    dx2_ref,
    dn_ref,
    weight_grad_ref,
    grads_ref,
    back_sums_ref,
    n_ref,
    z_ref,
    dw_ref,
    x2,
    unit,
    spread,
    third_low,
    pre,
    hidden_low,
    feed,
    feed_grad,
    pre_grad,
    grads,
    weight_sums,
):
    row_count, width = x1_ref.shape
    chunks = width // LANES
    expand = weight_ref.shape[0] // 2
    tile = tile_rows(row_count)
    total_live = live_total(sides_ref)
    batch = [batch_vectors(bn_ref, chunk, chunks) for chunk in range(chunks)]
    zero = jnp.zeros((8, LANES), F32)

    def normalize(first, size, _):
        rows = pl.ds(first, size)
        live = row_mask(first, size, LANES, total_live)
        for chunk in range(chunks):
            lanes = chunk_lanes(chunk)
            mean, scale = batch[chunk]
            value = (e_ref[chunk, rows, :] - mean) * scale
            value = value * table_ref[5:6, lanes] + table_ref[6:7, lanes]
            n_ref[chunk, pl.ds(LEAD + first, size), :] = jnp.where(live, value, 0.0)
            z_ref[chunk, rows, :] = jnp.zeros((size, LANES), F32)
            dn_ref[chunk, rows, :] = jnp.zeros((size, LANES), F32)
        return 0

    for_rows(row_count, ROW_TILE, normalize)

    taps = [tap_vectors(table_ref, 20, chunk) for chunk in range(chunks)]

    def conv_step(row, side, masks, carry):
        rows = pl.ds(row, 8)
        for chunk in range(chunks):
            value = conv_forward(n_ref, chunk, row, side, masks, taps[chunk])
            z_ref[chunk, rows, :] = jnp.where(masks[0], value, z_ref[chunk, rows, :])
        return carry

    for_groups(sides_ref, conv_step, 0)

    weight_sums[...] = jnp.zeros_like(weight_sums)
    grads[...] = jnp.zeros_like(grads)

    def z_rows(rows):
        return jnp.concatenate([z_ref[chunk, rows, :] for chunk in range(chunks)], axis=1)

    @pl.loop(0, row_count // tile)
    def _(step):
        base = pl.multiple_of(step * tile, 16)

        def before(inner, size, _):
            near, rows = pl.ds(inner, size), pl.ds(base + inner, size)
            value = x1_ref[rows, :] + table_ref[7:8, :] * z_rows(rows)
            x2[near, :] = value
            value, scale = centered(value)
            unit[near, :] = value
            spread[near, :] = jnp.broadcast_to(scale, (size, LANES))
            third_low[near, :] = (value * table_ref[8:9, :] + table_ref[9:10, :]).astype(BF16)
            return 0

        for_rows(tile, ROW_TILE, before)
        for part in range(expand):
            lanes = slice(part * width, (part + 1) * width)
            pre[:, lanes] = dot(third_low[...], weight_ref[part])

        def activate(inner, size, _):
            near = pl.ds(inner, size)
            for part in range(expand):
                lanes = slice(part * width, (part + 1) * width)
                value = pre[near, lanes]
                share, bell = gelu_parts(value)
                hidden_low[near, lanes] = (value * share).astype(BF16)
                pre[near, lanes] = gelu_slope(value, share, bell)
            return 0

        for_rows(tile, GELU_TILE, activate)
        total = None
        for part in range(expand):
            lanes = slice(part * width, (part + 1) * width)
            term = dot(hidden_low[:, lanes], weight_ref[expand + part])
            total = term if total is None else total + term
        feed[...] = total

        def output(inner, size, carry):
            near, rows = pl.ds(inner, size), pl.ds(base + inner, size)
            live = row_mask(base + inner, size, width, total_live)
            value = x2[near, :] + table_ref[10:11, :] * feed[near, :]
            out_ref[rows, :] = jnp.where(live, value, 0.0).astype(BF16)
            entry = jnp.where(live, adjoint_ref[rows, :].astype(F32), 0.0)
            feed_grad[near, :] = (entry * table_ref[10:11, :]).astype(BF16)
            return carry + fold(entry * feed[near, :])

        grads[0] += for_rows(tile, ROW_TILE, output, jnp.zeros((8, width), F32))
        for part in range(expand):
            lanes = slice(part * width, (part + 1) * width)
            hidden_grad = dot_lanes(feed_grad[...], weight_ref[expand + part])
            pre_grad[:, lanes] = (hidden_grad * pre[:, lanes]).astype(BF16)
        for part in range(expand):
            lanes = slice(part * width, (part + 1) * width)
            weight_sums[expand + part] += dot_rows(hidden_low[:, lanes], feed_grad[...])
            weight_sums[part] += dot_rows(third_low[...], pre_grad[:, lanes])
        total = None
        for part in range(expand):
            lanes = slice(part * width, (part + 1) * width)
            term = dot_lanes(pre_grad[:, lanes], weight_ref[part])
            total = term if total is None else total + term
        feed[...] = total

        def after(inner, size, carry):
            near, rows = pl.ds(inner, size), pl.ds(base + inner, size)
            live = row_mask(base + inner, size, width, total_live)
            entry = jnp.where(live, adjoint_ref[rows, :].astype(F32), 0.0)
            grad = feed[near, :]
            value = unit[near, :]
            total = entry + norm_back(grad * table_ref[8:9, :], value, spread[near, 0:1])
            dx2_ref[rows, :] = total
            scaled = total * table_ref[7:8, :]
            for chunk in range(chunks):
                dw_ref[chunk, pl.ds(LEAD + base + inner, size), :] = scaled[:, chunk_lanes(chunk)]
            return (
                carry[0] + fold(total * z_rows(rows)),
                carry[1] + fold(grad * value),
                carry[2] + fold(grad),
            )

        wide = jnp.zeros((8, width), F32)
        sums = for_rows(tile, ROW_TILE, after, (wide, wide, wide))
        for index in range(3):
            grads[1 + index] += sums[index]

    owners, pieces, shard, _ = weight_grad_ref.shape
    inner = width // shard
    for owner in range(owners):
        rows = slice(owner % inner * shard, (owner % inner + 1) * shard)
        for piece in range(pieces):
            weight_grad_ref[owner, piece] = weight_sums[
                owner // inner * pieces + piece, rows, :
            ].astype(BF16)

    back_sums_ref[...] = zero
    for index, source in enumerate((1, 2, 3, 0)):
        grads_ref[index : index + 1, :] = jnp.sum(grads[source], axis=0, keepdims=True)
    def back_step(row, side, masks, carry):
        rows = pl.ds(row, 8)
        result = []
        for chunk in range(chunks):
            mean, scale = batch[chunk]
            sums = carry[chunk]
            own = jnp.where(masks[0], n_ref[chunk, pl.ds(LEAD + row, 8), :], 0.0)
            total, tap_sums = conv_backward(
                dw_ref, chunk, row, side, masks, taps[chunk], own, sums[0:9]
            )
            dn_ref[chunk, rows, :] = jnp.where(masks[0], total, dn_ref[chunk, rows, :])
            total = jnp.where(masks[0], total, 0.0)
            standard = (e_ref[chunk, rows, :] - mean) * scale
            result.append((*tap_sums, sums[9] + total * standard, sums[10] + total))
        return tuple(result)

    sums = for_groups(sides_ref, back_step, ((zero,) * 11,) * chunks)
    for chunk in range(chunks):
        lanes = chunk_lanes(chunk)
        for index, value in enumerate(sums[chunk]):
            value = jnp.sum(value, axis=0, keepdims=True)
            grads_ref[4 + index : 5 + index, lanes] = value
            if index == 9:
                back_sums_ref[chunks + chunk : chunks + chunk + 1, :] = value
            if index == 10:
                back_sums_ref[chunk : chunk + 1, :] = value


def feed_forward(sides, x1, e, batch_sums, weights, table, adjoint, grad_shape):
    row_count, width = x1.shape
    chunks = width // LANES
    expand = weights.shape[0] // 2
    tile = tile_rows(row_count)
    shape = jax.ShapeDtypeStruct
    return pl.pallas_call(
        feed_kernel,
        out_shape=(
            shape((row_count, width), BF16),
            shape((row_count, width), F32),
            shape((chunks, row_count, LANES), F32),
            shape(grad_shape, BF16),
            shape((16, width), F32),
            shape((8, LANES), F32),
        ),
        in_specs=[SMEM_SPEC] + [VMEM_SPEC] * 6,
        out_specs=(VMEM_SPEC,) * 6,
        scratch_shapes=[
            pltpu.VMEM((chunks, LEAD + row_count + TAIL, LANES), F32),
            pltpu.VMEM((chunks, row_count, LANES), F32),
            pltpu.VMEM((chunks, LEAD + row_count + TAIL, LANES), F32),
            pltpu.VMEM((tile, width), F32),
            pltpu.VMEM((tile, width), F32),
            pltpu.VMEM((tile, LANES), F32),
            pltpu.VMEM((tile, width), BF16),
            pltpu.VMEM((tile, expand * width), F32),
            pltpu.VMEM((tile, expand * width), BF16),
            pltpu.VMEM((tile, width), F32),
            pltpu.VMEM((tile, width), BF16),
            pltpu.VMEM((tile, expand * width), BF16),
            pltpu.VMEM((4, 8, width), F32),
            pltpu.VMEM((2 * expand, width, width), F32),
        ],
        compiler_params=pltpu.CompilerParams(vmem_limit_bytes=VMEM_LIMIT),
        name="feed_forward",
    )(sides, x1, e, batch_sums, weights, table, adjoint)


def mixing_backward_kernel(
    sides_ref,
    sharp_ref,
    input_ref,
    weight_ref,
    table_ref,
    x1_ref,
    qkv_ref,
    mixed_ref,
    scores_ref,
    attention_ref,
    u_hbm,
    bn_ref,
    dx2_ref,
    dn_hbm,
    back_ref,
    out_ref,
    weight_grad_ref,
    grads_ref,
    head_weights,
    out_weight,
    pool,
    conv_grad,
    dx1,
    mixed_grad,
    low_rows,
    head_low,
    spread,
    out_sum,
    sharp_sums,
    load_sems,
):
    row_count, width = input_ref.shape
    chunks = width // LANES
    u_ref, dn_ref = pool.at[0:chunks], pool.at[chunks : 2 * chunks]
    conv_in, attention_out = pool.at[2 * chunks : 3 * chunks], pool.at[3 * chunks : 4 * chunks]
    loads = [
        pltpu.make_async_copy(u_hbm, u_ref, load_sems.at[0]),
        pltpu.make_async_copy(dn_hbm, dn_ref, load_sems.at[1]),
    ]
    for load in loads:
        load.start()
    tile = tile_rows(row_count)
    total_live = live_total(sides_ref)
    batch = [batch_vectors(bn_ref, chunk, chunks) for chunk in range(chunks)]
    zero = jnp.zeros((8, LANES), F32)
    wide = jnp.zeros((8, width), F32)
    mapping = head_map(BF16)
    for part in range(3):
        head_weights[:, part * PAD_WIDTH : (part + 1) * PAD_WIDTH] = dot(
            weight_ref[part], mapping
        ).astype(BF16)
    out_weight[...] = dot_rows(mapping, weight_ref[3]).astype(BF16)
    spread[...] = jnp.zeros_like(spread)

    for load in loads:
        load.wait()

    def batch_back(first, size, _):
        rows = pl.ds(first, size)
        live = row_mask(first, size, LANES, total_live)
        unit, _ = centered(x1_ref[rows, :])
        value = unit * table_ref[3:4, :] + table_ref[4:5, :]
        for chunk in range(chunks):
            lanes = chunk_lanes(chunk)
            mean, scale = batch[chunk]
            count = bn_ref[2 * chunks : 2 * chunks + 1, :]
            u = u_ref[chunk, rows, :]
            share, bell = gelu_parts(u)
            standard = (u * share - mean) * scale
            inner = (
                back_ref[chunk : chunk + 1, :]
                + standard * back_ref[chunks + chunk : chunks + chunk + 1, :]
            ) / count
            grad = scale * table_ref[5:6, lanes] * (dn_ref[chunk, rows, :] - inner)
            grad = grad * gelu_slope(u, share, bell)
            conv_grad[chunk, pl.ds(LEAD + first, size), :] = jnp.where(live, grad, 0.0)
            conv_in[chunk, pl.ds(first, size), :] = value[:, lanes]
        return 0

    for_rows(row_count, ROW_TILE, batch_back)

    taps = [tap_vectors(table_ref, 11, chunk) for chunk in range(chunks)]

    def back_step(row, side, masks, carry):
        rows = pl.ds(row, 8)
        result = []
        for chunk in range(chunks):
            held = conv_in[chunk, rows, :]
            own = jnp.where(masks[0], held, 0.0)
            total, tap_sums = conv_backward(
                conv_grad, chunk, row, side, masks, taps[chunk], own, carry[chunk]
            )
            conv_in[chunk, rows, :] = jnp.where(masks[0], total, held)
            result.append(tap_sums)
        return tuple(result)

    tap_sums = for_groups(sides_ref, back_step, ((zero,) * 9,) * chunks)
    for chunk in range(chunks):
        for index, value in enumerate(tap_sums[chunk]):
            grads_ref[5 + index : 6 + index, chunk_lanes(chunk)] = jnp.sum(
                value, axis=0, keepdims=True
            )

    @pl.loop(0, row_count // tile)
    def _(step):
        rows = pl.ds(pl.multiple_of(step * tile, 16), tile)
        result = dot(mixed_ref[rows, :], out_weight[...])
        for chunk in range(chunks):
            attention_out[chunk, rows, :] = result[:, chunk_lanes(chunk)]

    def second_back(first, size, carry):
        rows = pl.ds(first, size)
        live = row_mask(first, size, width, total_live)
        grad = jnp.concatenate([conv_in[chunk, rows, :] for chunk in range(chunks)], axis=1)
        grad = jnp.where(live, grad, 0.0)
        unit, scale = centered(x1_ref[rows, :])
        total = dx2_ref[rows, :] + norm_back(grad * table_ref[3:4, :], unit, scale)
        dx1[rows, :] = total
        low_rows[rows, :] = (total * table_ref[2:3, :]).astype(BF16)
        held = jnp.concatenate([attention_out[chunk, rows, :] for chunk in range(chunks)], axis=1)
        return (
            carry[0] + fold(total * held),
            carry[1] + fold(grad * unit),
            carry[2] + fold(grad),
        )

    sums = for_rows(row_count, ROW_TILE, second_back, (wide, wide, wide))
    for index in range(3):
        grads_ref[2 + index : 3 + index, :] = jnp.sum(sums[index], axis=0, keepdims=True)

    out_sum[...] = jnp.zeros_like(out_sum)

    @pl.loop(0, row_count // tile)
    def _(step):
        rows = pl.ds(pl.multiple_of(step * tile, 16), tile)
        mixed_grad[rows, :] = dot_lanes(low_rows[rows, :], out_weight[...])
        out_sum[...] += dot_rows(mixed_ref[rows, :], low_rows[rows, :])

    pool[...] = jnp.zeros_like(pool)

    low = out_sum[...].astype(BF16)
    weight_grad_ref[3] = dot(mapping, low).astype(BF16)
    sharp_sums[...] = jnp.zeros_like(sharp_sums)

    def crop_step(crop, rows, keep):
        for half in range(2):
            lanes = [
                slice(part * PAD_WIDTH + half * HALF_WIDTH, part * PAD_WIDTH + (half + 1) * HALF_WIDTH)
                for part in range(3)
            ]
            query, query_scale = units(jnp.where(keep, qkv_ref[rows, lanes[0]], 0.0))
            key, key_scale = units(jnp.where(keep, qkv_ref[rows, lanes[1]], 0.0))
            value = split(jnp.where(keep, qkv_ref[rows, lanes[2]], 0.0))
            grad = split(jnp.where(keep, mixed_grad[rows, lanes[0]], 0.0))
            block = dot_split(dot_rows, value, grad)
            query_sums = []
            for pair in range(2):
                index = 2 * half + pair
                shares = attention_ref[crop, index]
                scores = scores_ref[crop, index]
                part = pair_part(block, pair)
                part = shares * (part - jnp.sum(part * shares, axis=0, keepdims=True))
                spread_pair(spread, half, pair, shares)
                sharp_sums[index : index + 1, :] += jnp.sum(part * scores, axis=0, keepdims=True)
                part = part * pair_sharpness(sharp_ref, index)
                query_sums.append(jnp.sum(part * scores, axis=0, keepdims=True))
                spread_pair(spread, 2 + half, pair, part)
            shares = (spread[half, 0], spread[half, 1])
            slopes = (spread[2 + half, 0], spread[2 + half, 1])
            value_grad = dot_split(dot_lanes, grad, shares)
            query_grad = dot_split(dot, split(key), slopes)
            query_grad = query_scale * (query_grad - query * jnp.concatenate(query_sums, axis=1))
            key_grad = dot_split(dot_lanes, split(query), slopes)
            key_grad = key_scale * (
                key_grad - key * jnp.sum(key_grad * key, axis=0, keepdims=True)
            )
            for part, result in enumerate((query_grad, key_grad, value_grad)):
                for side in range(HALF_WIDTH // LANES):
                    chunk = (part * PAD_WIDTH + half * HALF_WIDTH) // LANES + side
                    pool[chunk, rows, :] = jnp.where(
                        keep[:, 0:LANES], result[:, chunk_lanes(side)], pool[chunk, rows, :]
                    )

    for_crops(sides_ref, row_count, crop_step)

    grads_ref[14:16, :] = jnp.zeros((2, width), F32)
    lane = lax.broadcasted_iota(jnp.int32, (1, LANES), 1)
    total = jnp.zeros((1, LANES), F32)
    for head in range(HEAD_NUMBER):
        row = sharp_sums[head // 2 : head // 2 + 1, :]
        row = jnp.where((lane >> 6) == head % 2, row, 0.0)
        total = jnp.where(lane == head, jnp.sum(row, axis=1, keepdims=True), total)
    grads_ref[14:15, 0:LANES] = total

    def first_norm(first, size, _):
        rows = pl.ds(first, size)
        unit, _ = centered(input_ref[rows, :].astype(F32))
        low_rows[rows, :] = (unit * table_ref[0:1, :] + table_ref[1:2, :]).astype(BF16)
        return 0

    for_rows(row_count, ROW_TILE, first_norm)

    for part in range(3):
        lanes = slice(part * PAD_WIDTH, (part + 1) * PAD_WIDTH)
        out_sum[...] = jnp.zeros_like(out_sum)

        @pl.loop(0, row_count // tile)
        def _(step, lanes=lanes, part=part):
            rows = pl.ds(pl.multiple_of(step * tile, 16), tile)
            first = part * PAD_WIDTH // LANES
            for chunk in range(PAD_WIDTH // LANES):
                head_low[rows, chunk_lanes(chunk)] = pool[first + chunk, rows, :].astype(BF16)
            term = dot_lanes(head_low[rows, :], head_weights[:, lanes])
            mixed_grad[rows, 0:width] = term if part == 0 else mixed_grad[rows, 0:width] + term

        @pl.loop(0, row_count // tile)
        def _(step, lanes=lanes):
            rows = pl.ds(pl.multiple_of(step * tile, 16), tile)
            out_sum[...] += dot_rows(head_low[rows, :], low_rows[rows, :])

        low = out_sum[...].astype(BF16)
        weight_grad_ref[part] = lax.dot_general(
            low, mapping, (((0,), (1,)), ((), ())), preferred_element_type=F32
        ).astype(BF16)

    def first_back(first, size, carry):
        rows = pl.ds(first, size)
        unit, scale = centered(input_ref[rows, :].astype(F32))
        grad = mixed_grad[rows, 0:width]
        total = dx1[rows, :] + norm_back(grad * table_ref[0:1, :], unit, scale)
        out_ref[rows, :] = total.astype(BF16)
        return carry[0] + fold(grad * unit), carry[1] + fold(grad)

    sums = for_rows(row_count, ROW_TILE, first_back, (wide, wide))
    for index in range(2):
        grads_ref[index : index + 1, :] = jnp.sum(sums[index], axis=0, keepdims=True)


def mixing_backward(sides, sharpness, inputs, weights, table, saved, batch_sums, dx2, dn, back_sums):
    row_count, width = inputs.shape
    chunks = width // LANES
    shape = jax.ShapeDtypeStruct
    x1, qkv, mixed, scores, attention, u = saved
    return pl.pallas_call(
        mixing_backward_kernel,
        out_shape=(
            shape((row_count, width), BF16),
            shape((4, width, width), BF16),
            shape((16, width), F32),
        ),
        in_specs=[SMEM_SPEC, SMEM_SPEC]
        + [VMEM_SPEC] * 8
        + [ANY_SPEC, VMEM_SPEC, VMEM_SPEC, ANY_SPEC, VMEM_SPEC],
        out_specs=(VMEM_SPEC,) * 3,
        scratch_shapes=[
            pltpu.VMEM((width, 3 * PAD_WIDTH), BF16),
            pltpu.VMEM((PAD_WIDTH, width), BF16),
            pltpu.VMEM((3 * PAD_WIDTH // LANES, row_count, LANES), F32),
            pltpu.VMEM((chunks, LEAD + row_count + TAIL, LANES), F32),
            pltpu.VMEM((row_count, width), F32),
            pltpu.VMEM((row_count, PAD_WIDTH), F32),
            pltpu.VMEM((row_count, width), BF16),
            pltpu.VMEM((row_count, PAD_WIDTH), BF16),
            pltpu.VMEM((4, 2, HALF_WIDTH, HALF_WIDTH), BF16),
            pltpu.VMEM((PAD_WIDTH, width), F32),
            pltpu.VMEM((HEAD_PAIRS, LANES), F32),
            pltpu.SemaphoreType.DMA((2,)),
        ],
        compiler_params=pltpu.CompilerParams(vmem_limit_bytes=VMEM_LIMIT),
        name="mixing_backward",
    )(
        sides,
        sharpness,
        inputs,
        weights,
        table,
        x1,
        qkv,
        mixed,
        scores,
        attention,
        u,
        batch_sums,
        dx2,
        dn,
        back_sums,
    )


MESH = pl.DeviceIdType.MESH


def greet(peers):
    barrier = pltpu.get_barrier_semaphore()
    for peer in peers:
        pl.semaphore_signal(barrier, inc=1, device_id=peer, device_id_type=MESH)
    pl.semaphore_wait(barrier, len(peers))


def push(source, target, send, receive, peer):
    copy = pltpu.make_async_remote_copy(
        src_ref=source,
        dst_ref=target,
        send_sem=send,
        recv_sem=receive,
        device_id=peer,
        device_id_type=MESH,
    )
    copy.start()
    return copy


def turned(place, step, count):
    return lax.rem(place + step, count)


def ring_peers(axis, count):
    place = lax.axis_index(axis)
    return [{axis: turned(place, step, count)} for step in range(1, count)]


def comm_params(identity):
    return pltpu.CompilerParams(
        collective_id=identity, has_side_effects=True, vmem_limit_bytes=VMEM_LIMIT
    )


def sum_all_kernel(
    counts, part_ref, total_ref, outer, inner, middle, outer_send, outer_recv, inner_send, inner_recv
):
    n_dp, n_fsdp = counts
    dp, fsdp = lax.axis_index("dp"), lax.axis_index("fsdp")
    inner_peers, outer_peers = ring_peers("fsdp", n_fsdp), ring_peers("dp", n_dp)
    greet(inner_peers + outer_peers)
    inner[fsdp] = part_ref[...]
    copies = [
        push(part_ref, inner.at[fsdp], inner_send.at[k], inner_recv.at[k], peer)
        for k, peer in enumerate(inner_peers)
    ]
    for copy in copies:
        copy.wait()
    total = inner[0]
    for k in range(1, n_fsdp):
        total = total + inner[k]
    middle[...] = total
    outer[dp] = total
    copies = [
        push(middle, outer.at[dp], outer_send.at[k], outer_recv.at[k], peer)
        for k, peer in enumerate(outer_peers)
    ]
    for copy in copies:
        copy.wait()
    total = outer[0]
    for k in range(1, n_dp):
        total = total + outer[k]
    total_ref[...] = total


def sum_all(part, counts, identity):
    n_dp, n_fsdp = counts
    return pl.pallas_call(
        functools.partial(sum_all_kernel, counts),
        out_shape=jax.ShapeDtypeStruct(part.shape, F32),
        in_specs=[VMEM_SPEC],
        out_specs=VMEM_SPEC,
        scratch_shapes=[
            pltpu.VMEM((n_dp, *part.shape), F32),
            pltpu.VMEM((n_fsdp, *part.shape), F32),
            pltpu.VMEM(part.shape, F32),
            pltpu.SemaphoreType.DMA((n_dp - 1,)),
            pltpu.SemaphoreType.DMA((n_dp - 1,)),
            pltpu.SemaphoreType.DMA((n_fsdp - 1,)),
            pltpu.SemaphoreType.DMA((n_fsdp - 1,)),
        ],
        compiler_params=comm_params(identity),
        name="sum_all",
    )(part)


def gather_kernel(
    counts,
    masters_ref,
    table_ref,
    blocks_ref,
    full_table_ref,
    blocks,
    tables,
    stage,
    ring_send,
    ring_recv,
    table_send,
    table_recv,
    cross_send,
    cross_recv,
    pair_send,
    pair_recv,
):
    n_dp, n_fsdp = counts
    dp, fsdp = lax.axis_index("dp"), lax.axis_index("fsdp")
    shard, width = masters_ref.shape[1:]
    columns = table_ref.shape[1]
    across = lax.rem(dp + 2, 4)
    pair = dp + 1 - 2 * lax.rem(dp, 2)
    peers = ring_peers("fsdp", n_fsdp)
    greet(peers + [{"dp": across}, {"dp": pair}])

    def piece(block, owner):
        return blocks.at[block, pl.ds(pl.multiple_of(owner * shard, 16), shard), :]

    def origin(step):
        return lax.rem(fsdp + n_fsdp - step, n_fsdp)

    stage[...] = jnp.zeros_like(stage)
    stage[0 : table_ref.shape[0], 0:columns] = table_ref[...]
    tables[fsdp] = stage[...].astype(BF16)
    blocks[dp, pl.ds(pl.multiple_of(fsdp * shard, 16), shard), :] = masters_ref[dp].astype(BF16)
    own = piece(dp, fsdp)
    ring = [
        push(own, own, ring_send.at[k], ring_recv.at[k], peer) for k, peer in enumerate(peers)
    ]
    table_copies = [
        push(tables.at[fsdp], tables.at[fsdp], table_send.at[k], table_recv.at[k], peer)
        for k, peer in enumerate(peers)
    ]
    crossing, pairing = [], []
    for step in range(n_fsdp):
        if step:
            ring[step - 1].wait_recv()
        part = piece(dp, origin(step))
        crossing.append(push(part, part, cross_send.at[step], cross_recv.at[step], {"dp": across}))
        pairing.append(
            push(part, part, pair_send.at[0, step], pair_recv.at[0, step], {"dp": pair})
        )
    for step in range(n_fsdp):
        crossing[step].wait_recv()
        part = piece(across, origin(step))
        pairing.append(
            push(part, part, pair_send.at[1, step], pair_recv.at[1, step], {"dp": pair})
        )
    for copy in table_copies:
        copy.wait_recv()
    total = None
    for owner in range(n_fsdp):
        lane = lax.broadcasted_iota(jnp.int32, (LANES, width), 0)
        target = lax.broadcasted_iota(jnp.int32, (LANES, width), 1)
        hit = (lane < columns) & (lane + owner * columns == target)
        term = dot(tables[owner], hit.astype(F32).astype(BF16))
        total = term if total is None else total + term
    full_table_ref[...] = total
    for copy in pairing:
        copy.wait_recv()
    blocks_ref[...] = blocks[...]
    for copy in ring + table_copies + crossing + pairing:
        copy.wait_send()


def gather_start(masters, coefficients, counts, identity):
    n_dp, n_fsdp = counts
    width = masters.shape[2]
    shape = jax.ShapeDtypeStruct
    dma = pltpu.SemaphoreType.DMA
    return pl.pallas_call(
        functools.partial(gather_kernel, counts),
        out_shape=(shape((4, width, width), BF16), shape((32, width), F32)),
        in_specs=[VMEM_SPEC, VMEM_SPEC],
        out_specs=(VMEM_SPEC, VMEM_SPEC),
        scratch_shapes=[
            pltpu.VMEM((4, width, width), BF16),
            pltpu.VMEM((n_fsdp, 32, LANES), BF16),
            pltpu.VMEM((32, LANES), F32),
            dma((n_fsdp - 1,)),
            dma((n_fsdp - 1,)),
            dma((n_fsdp - 1,)),
            dma((n_fsdp - 1,)),
            dma((n_fsdp,)),
            dma((n_fsdp,)),
            dma((2, n_fsdp)),
            dma((2, n_fsdp)),
        ],
        compiler_params=comm_params(identity),
        name="gather_start",
    )(masters, coefficients)


def owner_rows(owner, shard):
    return pl.ds(pl.multiple_of(owner * shard, 16), shard)


def reduce_kernel(
    counts,
    place_ref,
    mix_ref,
    feed_ref,
    mix_table_ref,
    feed_table_ref,
    energy_ref,
    coefficient_ref,
    sharp_ref,
    grad_ref,
    slots_ref,
    table_grad_ref,
    energy_out_ref,
    coefficient_out_ref,
    sharp_out_ref,
    pair_buf,
    cross_out,
    cross_buf,
    ring_out,
    ring_buf,
    feed_buf,
    dp_buf,
    slot_out,
    slots,
    table_stage,
    table_out,
    table_buf,
    table_part,
    table_dp,
    pair_send,
    pair_recv,
    cross_send,
    cross_recv,
    ring_send,
    ring_recv,
    feed_send,
    feed_recv,
    dp_send,
    dp_recv,
    slot_send,
    slot_recv,
    twin_send,
    twin_recv,
    table_send,
    table_recv,
    table_dp_send,
    table_dp_recv,
):
    n_dp, n_fsdp = counts
    dp, fsdp = lax.axis_index("dp"), lax.axis_index("fsdp")
    width = mix_ref.shape[2]
    shard = width // n_fsdp
    core = lax.rem(dp, 2)
    across = lax.rem(dp + 2, 4)
    pair = dp + 1 - 2 * core
    pair_across = lax.rem(pair + 2, 4)
    peers, dp_peers = ring_peers("fsdp", n_fsdp), ring_peers("dp", n_dp)
    to_pair, to_across = {"dp": pair}, {"dp": across}
    greet(peers + dp_peers)

    parts = 4
    deep = width // parts
    pairing = []
    for part in range(parts):
        rows = pl.ds(part * deep, deep)
        for side, block in enumerate((pair_across, pair)):
            pairing.append(
                push(
                    mix_ref.at[block, rows],
                    pair_buf.at[side, rows],
                    pair_send.at[side, part],
                    pair_recv.at[side, part],
                    to_pair,
                )
            )
    feed_buf[dp] = feed_ref[...]
    feeding = [
        push(feed_ref, feed_buf.at[dp], feed_send.at[k], feed_recv.at[k], peer)
        for k, peer in enumerate(dp_peers)
    ]

    table_stage[...] = jnp.zeros_like(table_stage)
    for row, (source, first) in enumerate(TABLE_ROWS):
        ref = mix_table_ref if source == 0 else feed_table_ref
        table_stage[row : row + 1, :] = ref[first : first + 1, :]
    terms, rest = [], table_stage[...]
    for _ in range(3):
        term = rest.astype(BF16)
        terms.append(term)
        rest = rest - term.astype(F32)
    columns = width // n_fsdp
    sharp_row = lax.broadcasted_iota(jnp.int32, (32, LANES), 0) == 31
    sharp_values = jnp.broadcast_to(mix_table_ref[14:15, 0:LANES], (32, LANES))
    for owner in range(n_fsdp):
        lane = lax.broadcasted_iota(jnp.int32, (width, LANES), 1)
        source = lax.broadcasted_iota(jnp.int32, (width, LANES), 0)
        hit = ((lane < columns) & (lane + owner * columns == source)).astype(F32).astype(BF16)
        value = dot(terms[0], hit) + dot(terms[1], hit) + dot(terms[2], hit)
        table_out[owner] = jnp.where(sharp_row, sharp_values, value)
    table_buf[fsdp] = table_out[fsdp]
    tabling = [
        push(
            table_out.at[turned(fsdp, k + 1, n_fsdp)],
            table_buf.at[fsdp],
            table_send.at[k],
            table_recv.at[k],
            peer,
        )
        for k, peer in enumerate(peers)
    ]

    crossing = []
    for part in range(parts):
        rows = pl.ds(part * deep, deep)
        pairing[2 * part].wait_recv()
        cross_out[rows, :] = (
            mix_ref[across, rows, :].astype(F32) + pair_buf[0, rows, :].astype(F32)
        ).astype(BF16)
        crossing.append(
            push(
                cross_out.at[rows],
                cross_buf.at[rows],
                cross_send.at[part],
                cross_recv.at[part],
                to_across,
            )
        )
    for part in range(parts):
        rows = pl.ds(part * deep, deep)
        pairing[2 * part + 1].wait_recv()
        crossing[part].wait_recv()
        ring_out[rows, :] = (
            mix_ref[dp, rows, :].astype(F32)
            + pair_buf[1, rows, :].astype(F32)
            + cross_buf[rows, :].astype(F32)
        ).astype(BF16)
    ring = [
        push(
            ring_out.at[owner_rows(turned(fsdp, k + 1, n_fsdp), shard)],
            ring_buf.at[fsdp],
            ring_send.at[k],
            ring_recv.at[k],
            peer,
        )
        for k, peer in enumerate(peers)
    ]
    ring_buf[fsdp] = ring_out[owner_rows(fsdp, shard), :]

    for copy in tabling:
        copy.wait_recv()
    total = table_buf[0]
    for owner in range(1, n_fsdp):
        total = total + table_buf[owner]
    table_part[...] = total
    table_dp[dp] = total
    table_dps = [
        push(table_part, table_dp.at[dp], table_dp_send.at[k], table_dp_recv.at[k], peer)
        for k, peer in enumerate(dp_peers)
    ]

    for copy in ring:
        copy.wait_recv()
    total = ring_buf[0].astype(F32)
    for owner in range(1, n_fsdp):
        total = total + ring_buf[owner].astype(F32)
    dp_buf[dp] = total
    gathering = [
        push(dp_buf.at[dp], dp_buf.at[dp], dp_send.at[k], dp_recv.at[k], peer)
        for k, peer in enumerate(dp_peers)
    ]
    for copy in feeding:
        copy.wait_recv()
    pieces = feed_ref.shape[0]
    for place in range(n_dp):
        for piece in range(pieces):
            grad_ref[n_dp + place * pieces + piece] = feed_buf[place, piece].astype(F32)
    for copy in gathering:
        copy.wait_recv()
    for place in range(n_dp):
        grad_ref[place] = dp_buf[place]

    slot_count = 2 * n_fsdp
    block_count = grad_ref.shape[0]
    for slot in range(slot_count):
        block, filled = jnp.int32(0), jnp.int32(0)
        for index in range(block_count):
            here = place_ref[index] == slot
            block = jnp.where(here, index, block)
            filled = jnp.where(here, 1, filled)
        rows = grad_ref[block]
        slot_out[slot] = (rows * filled.astype(F32)).astype(BF16)
    slots[core, owner_rows(fsdp, shard), :] = slot_out[2 * fsdp + core]
    slotting = [
        push(
            slot_out.at[2 * turned(fsdp, k + 1, n_fsdp) + core],
            slots.at[core, owner_rows(fsdp, shard), :],
            slot_send.at[k],
            slot_recv.at[k],
            peer,
        )
        for k, peer in enumerate(peers)
    ]
    twins = []
    for step in range(n_fsdp):
        if step:
            slotting[step - 1].wait_recv()
        owner = lax.rem(fsdp + n_fsdp - step, n_fsdp)
        part = slots.at[core, owner_rows(owner, shard), :]
        twins.append(push(part, part, twin_send.at[step], twin_recv.at[step], to_pair))

    for copy in table_dps:
        copy.wait_recv()
    total = table_dp[0]
    for place in range(1, n_dp):
        total = total + table_dp[place]
    count = energy_ref.shape[0]
    grad = total[0:count, 0:columns]
    table_grad_ref[...] = grad
    energy = covariance_forgetting * energy_ref[...] + (1.0 - covariance_forgetting) * grad * grad
    energy_out_ref[...] = energy
    coefficient_out_ref[...] = coefficient_ref[...] - vector_rate * grad / (
        jnp.sqrt(energy) + energy_epsilon
    )
    grad = total[31:32, 0:HEAD_NUMBER]
    energy = (
        covariance_forgetting * sharp_ref[1:2, :] + (1.0 - covariance_forgetting) * grad * grad
    )
    sharp_out_ref[0:1, :] = grad
    sharp_out_ref[1:2, :] = energy
    sharp_out_ref[2:3, :] = sharp_ref[0:1, :] - sharpness_step_size * grad / (
        jnp.sqrt(energy) + energy_epsilon
    )
    for copy in twins:
        copy.wait_recv()
    slots_ref[...] = slots[...]
    for copy in (
        pairing + feeding + tabling + crossing + ring + table_dps + gathering + slotting + twins
    ):
        copy.wait_send()


TABLE_ROWS = (
    [(0, row) for row in range(5)]
    + [(1, 13), (1, 14)]
    + [(1, row) for row in range(4)]
    + [(0, row) for row in range(5, 14)]
    + [(1, row) for row in range(4, 13)]
)


def reduce_gradients(
    places, mix, feed, mix_table, feed_table, energy, coefficients, sharps, counts, identity
):
    n_dp, n_fsdp = counts
    width = mix.shape[2]
    shard = width // n_fsdp
    blocks = n_dp + feed.shape[0] * n_dp
    shape = jax.ShapeDtypeStruct
    dma = pltpu.SemaphoreType.DMA
    return pl.pallas_call(
        functools.partial(reduce_kernel, counts),
        out_shape=(
            shape((blocks, shard, width), F32),
            shape((2, width, width), BF16),
            shape(energy.shape, F32),
            shape(energy.shape, F32),
            shape(energy.shape, F32),
            shape((3, sharps.shape[1]), F32),
        ),
        in_specs=[SMEM_SPEC] + [VMEM_SPEC] * 7,
        out_specs=(VMEM_SPEC,) * 6,
        scratch_shapes=[
            pltpu.VMEM((2, width, width), BF16),
            pltpu.VMEM((width, width), BF16),
            pltpu.VMEM((width, width), BF16),
            pltpu.VMEM((width, width), BF16),
            pltpu.VMEM((n_fsdp, shard, width), BF16),
            pltpu.VMEM((n_dp, *feed.shape), BF16),
            pltpu.VMEM((n_dp, shard, width), F32),
            pltpu.VMEM((2 * n_fsdp, shard, width), BF16),
            pltpu.VMEM((2, width, width), BF16),
            pltpu.VMEM((32, width), F32),
            pltpu.VMEM((n_fsdp, 32, LANES), F32),
            pltpu.VMEM((n_fsdp, 32, LANES), F32),
            pltpu.VMEM((32, LANES), F32),
            pltpu.VMEM((n_dp, 32, LANES), F32),
            dma((2, 4)),
            dma((2, 4)),
            dma((4,)),
            dma((4,)),
            dma((n_fsdp - 1,)),
            dma((n_fsdp - 1,)),
            dma((n_dp - 1,)),
            dma((n_dp - 1,)),
            dma((n_dp - 1,)),
            dma((n_dp - 1,)),
            dma((n_fsdp - 1,)),
            dma((n_fsdp - 1,)),
            dma((n_fsdp,)),
            dma((n_fsdp,)),
            dma((n_fsdp - 1,)),
            dma((n_fsdp - 1,)),
            dma((n_dp - 1,)),
            dma((n_dp - 1,)),
        ],
        compiler_params=comm_params(identity),
        name="reduce_gradients",
    )(places, mix, feed, mix_table, feed_table, energy, coefficients, sharps)


def shampoo_kernel(grad_ref, left_ref, right_ref, left_root, right_root, left_out, right_out, step_ref):
    grad = grad_ref[...]
    left_out[...] = covariance_forgetting * left_ref[...] + (
        1.0 - covariance_forgetting
    ) * dot_lanes(grad, grad)
    right_out[...] = covariance_forgetting * right_ref[...] + (
        1.0 - covariance_forgetting
    ) * dot_rows(grad, grad)
    root = split(left_root[...])
    half = split(dot(root[0], grad) + dot(root[1], grad))
    step_ref[...] = dot_split(dot, half, split(right_root[...])).astype(BF16)


def shampoo(grads, left, right, left_root, right_root):
    slots, width, _ = grads.shape
    shape = jax.ShapeDtypeStruct
    spec = pl.BlockSpec((pl.Squeezed(), width, width), lambda slot: (slot, 0, 0))
    return pl.pallas_call(
        shampoo_kernel,
        grid=(slots,),
        out_shape=(
            shape(grads.shape, F32),
            shape(grads.shape, F32),
            shape(grads.shape, BF16),
        ),
        in_specs=[spec] * 5,
        out_specs=(spec,) * 3,
        compiler_params=pltpu.CompilerParams(vmem_limit_bytes=VMEM_LIMIT),
        name="shampoo",
    )(grads, left, right, left_root, right_root)


def return_kernel(
    counts, steps_ref, rows_ref, rows_buf, ring_send, ring_recv, twin_send, twin_recv
):
    n_dp, n_fsdp = counts
    dp, fsdp = lax.axis_index("dp"), lax.axis_index("fsdp")
    width = steps_ref.shape[2]
    shard = width // n_fsdp
    core = lax.rem(dp, 2)
    to_pair = {"dp": dp + 1 - 2 * core}
    peers = ring_peers("fsdp", n_fsdp)
    greet(peers + [to_pair])
    ring = [
        push(
            steps_ref.at[core, owner_rows(turned(fsdp, k + 1, n_fsdp), shard)],
            rows_buf.at[2 * fsdp + core],
            ring_send.at[k],
            ring_recv.at[k],
            peer,
        )
        for k, peer in enumerate(peers)
    ]
    rows_buf[2 * fsdp + core] = steps_ref[core, owner_rows(fsdp, shard), :]
    twins = []
    for step in range(n_fsdp):
        if step:
            ring[step - 1].wait_recv()
        owner = lax.rem(fsdp + n_fsdp - step, n_fsdp)
        part = rows_buf.at[2 * owner + core]
        twins.append(push(part, part, twin_send.at[step], twin_recv.at[step], to_pair))
    for copy in twins:
        copy.wait_recv()
    rows_ref[...] = rows_buf[...]
    for copy in ring + twins:
        copy.wait_send()


def return_steps(steps, counts, identity):
    n_dp, n_fsdp = counts
    width = steps.shape[2]
    shard = width // n_fsdp
    dma = pltpu.SemaphoreType.DMA
    return pl.pallas_call(
        functools.partial(return_kernel, counts),
        out_shape=jax.ShapeDtypeStruct((2 * n_fsdp, shard, width), BF16),
        in_specs=[VMEM_SPEC],
        out_specs=VMEM_SPEC,
        scratch_shapes=[
            pltpu.VMEM((2 * n_fsdp, shard, width), BF16),
            dma((n_fsdp - 1,)),
            dma((n_fsdp - 1,)),
            dma((n_fsdp,)),
            dma((n_fsdp,)),
        ],
        compiler_params=comm_params(identity),
        name="return_steps",
    )(steps)


def shards(
    patch_embeddings,
    view_side_tokens,
    projection_masters,
    channel_coefficients,
    head_sharpness,
    output_adjoint,
    leading_covariance,
    trailing_covariance,
    leading_root_preconditioner,
    trailing_root_preconditioner,
    channel_energy_average,
    sharpness_energy_average,
    storage_position_map,
):
    row_count, feature_count = patch_embeddings.shape
    block_count = projection_masters.shape[0]
    shard_rows = projection_masters.shape[1]
    slot_count = leading_covariance.shape[0]
    counts = (lax.axis_size("dp"), lax.axis_size("fsdp"))
    direct = counts[0] == 4 and slot_count == 2 and shard_rows % 16 == 0
    if direct:
        mixing_blocks, table = gather_start(projection_masters, channel_coefficients, counts, 0)
        grad_shape = (counts[0] * counts[1], (block_count - 4) // counts[0], shard_rows, feature_count)
    else:
        full_table = lax.all_gather(channel_coefficients.astype(BF16), "fsdp", axis=1, tiled=True)
        table = full_table.astype(F32)
        mixing_blocks = lax.all_gather(
            projection_masters[:4].astype(BF16), "fsdp", axis=1, tiled=True
        )
        grad_shape = (1, block_count - 4, feature_count, feature_count)
    feed_blocks = lax.all_gather(projection_masters[4:].astype(BF16), "fsdp", axis=1, tiled=True)

    def batch_total(part, identity):
        if direct:
            return sum_all(part, counts, identity)
        return lax.psum(part, ("dp", "fsdp"))

    x1, qkv, mixed, scores, attention, u, e, sums = mixing_forward(
        view_side_tokens, head_sharpness, patch_embeddings, mixing_blocks, table
    )
    batch_sums = batch_total(sums, 1)
    layer_output, dx2, dn, feed_grad, feed_table, back_part = feed_forward(
        view_side_tokens, x1, e, batch_sums, feed_blocks, table, output_adjoint, grad_shape
    )
    back_sums = batch_total(back_part, 2)
    incoming_tokens_grad, mixing_grad, mixing_table = mixing_backward(
        view_side_tokens,
        head_sharpness,
        patch_embeddings,
        mixing_blocks,
        table,
        (x1, qkv, mixed, scores, attention, u),
        batch_sums,
        dx2,
        dn,
        back_sums,
    )
    if direct:
        feed_grad = lax.psum_scatter(
            feed_grad, ("dp", "fsdp"), scatter_dimension=0, tiled=True
        )[0]
        (
            portion_derivative,
            owned_grad,
            catalog_portion,
            channel_energy_renewed,
            channel_params_updated,
            sharps,
        ) = reduce_gradients(
            storage_position_map,
            mixing_grad,
            feed_grad,
            mixing_table,
            feed_table,
            channel_energy_average,
            channel_coefficients,
            jnp.stack([head_sharpness, sharpness_energy_average]),
            counts,
            3,
        )
        leading_covariance_renewed, trailing_covariance_renewed, steps = shampoo(
            owned_grad,
            leading_covariance,
            trailing_covariance,
            leading_root_preconditioner,
            trailing_root_preconditioner,
        )
        my_rows = return_steps(steps, counts, 4)
        update = jnp.take(my_rows, storage_position_map, axis=0).astype(F32)
        projection_updated = projection_masters - weight_rate * update
        return (
            layer_output,
            incoming_tokens_grad,
            portion_derivative,
            leading_covariance_renewed,
            trailing_covariance_renewed,
            projection_updated,
            projection_updated.astype(BF16),
            catalog_portion,
            channel_energy_renewed,
            channel_params_updated,
            *sharps,
        )
    sharpness_share = mixing_table[14, 0:HEAD_NUMBER]
    table_grad = jnp.stack([(mixing_table, feed_table)[source][row] for source, row in TABLE_ROWS])
    block_grad = jnp.concatenate([mixing_grad, feed_grad[0]], axis=0).astype(F32)
    denominator_sum = lax.axis_size("fsdp")
    tiled_part = jnp.broadcast_to(
        sharpness_share[None, :], (denominator_sum, sharpness_share.shape[0])
    )
    portion_derivative, catalog_portion, sharpness_normalizer = (
        lax.psum_scatter(block_grad, "fsdp", scatter_dimension=1, tiled=True),
        lax.psum_scatter(table_grad, "fsdp", scatter_dimension=1, tiled=True),
        lax.psum_scatter(tiled_part, "fsdp", scatter_dimension=0, tiled=True),
    )
    portion_derivative, catalog_portion, sharpness_normalizer = lax.psum(
        (portion_derivative, catalog_portion, sharpness_normalizer), "dp"
    )
    sharpness_derivative = sharpness_normalizer[0]
    shard_place = lax.axis_index("fsdp")
    slot_index = jnp.arange(denominator_sum * slot_count, dtype=jnp.int32)
    slot_match = storage_position_map[None, :] == slot_index[:, None]
    slot_filled = jnp.any(slot_match, axis=1).astype(jnp.float32)[:, None, None]
    slot_block = jnp.sum(
        jnp.where(slot_match, jnp.arange(block_count, dtype=jnp.int32)[None, :], 0), axis=1
    )
    my_filled = lax.dynamic_slice_in_dim(slot_filled, shard_place * slot_count, slot_count, 0)
    my_block = lax.dynamic_slice_in_dim(slot_block, shard_place * slot_count, slot_count, 0)
    whole_grad = lax.all_gather(portion_derivative, "fsdp", axis=1, tiled=True)
    owned_grad = jnp.take(whole_grad, my_block, axis=0) * my_filled
    leading_covariance_renewed = covariance_forgetting * leading_covariance + (
        1.0 - covariance_forgetting
    ) * jnp.einsum("sij,skj->sik", owned_grad, owned_grad, precision=lax.Precision.HIGHEST)
    trailing_covariance_renewed = covariance_forgetting * trailing_covariance + (
        1.0 - covariance_forgetting
    ) * jnp.einsum("sji,sjk->sik", owned_grad, owned_grad, precision=lax.Precision.HIGHEST)
    halfway = jnp.einsum(
        "sij,sjk->sik", leading_root_preconditioner, owned_grad, precision=lax.Precision.HIGHEST
    )
    conditioned = jnp.einsum(
        "sij,sjk->sik", halfway, trailing_root_preconditioner, precision=lax.Precision.HIGHEST
    )
    every_update = lax.all_gather(conditioned, "fsdp", axis=0, tiled=True)
    my_rows = lax.dynamic_slice_in_dim(every_update, shard_place * shard_rows, shard_rows, 1)
    update = jnp.take(my_rows, storage_position_map, axis=0)
    projection_updated = projection_masters - weight_rate * update
    channel_energy_renewed = (
        covariance_forgetting * channel_energy_average
        + (1.0 - covariance_forgetting) * catalog_portion * catalog_portion
    )
    channel_params_updated = channel_coefficients - vector_rate * catalog_portion / (
        jnp.sqrt(channel_energy_renewed) + energy_epsilon
    )
    sharpness_energy_renewed = (
        covariance_forgetting * sharpness_energy_average
        + (1.0 - covariance_forgetting) * sharpness_derivative * sharpness_derivative
    )
    sharpness_updated = head_sharpness - sharpness_step_size * sharpness_derivative / (
        jnp.sqrt(sharpness_energy_renewed) + energy_epsilon
    )
    return (
        layer_output,
        incoming_tokens_grad,
        portion_derivative,
        leading_covariance_renewed,
        trailing_covariance_renewed,
        projection_updated,
        projection_updated.astype(jnp.bfloat16),
        catalog_portion,
        channel_energy_renewed,
        channel_params_updated,
        sharpness_derivative,
        sharpness_energy_renewed,
        sharpness_updated,
    )


def solution(mesh):
    in_specs = (
        P(("dp", "fsdp"), None),
        P(("dp", "fsdp")),
        P(None, "fsdp", None),
        P(None, "fsdp"),
        P(),
        P(("dp", "fsdp"), None),
        P("fsdp", None, None),
        P("fsdp", None, None),
        P("fsdp", None, None),
        P("fsdp", None, None),
        P(None, "fsdp"),
        P(),
        P(),
    )
    out_specs = (
        P(("dp", "fsdp"), None),
        P(("dp", "fsdp"), None),
        P(None, "fsdp", None),
        P("fsdp", None, None),
        P("fsdp", None, None),
        P(None, "fsdp", None),
        P(None, "fsdp", None),
        P(None, "fsdp"),
        P(None, "fsdp"),
        P(None, "fsdp"),
        P(),
        P(),
        P(),
    )
    return jax.shard_map(shards, mesh=mesh, in_specs=in_specs, out_specs=out_specs, check_vma=False)
```

```python
import functools

import jax
import jax.numpy as jnp
from jax import lax
from jax.experimental import pallas as pl
from jax.experimental.pallas import tpu as pltpu
from jax.sharding import PartitionSpec as P

HEAD_NUMBER = 8
HDIM = 48
HEAD_PAD = 64
LANES = 128
HEAD_PAIRS = HEAD_NUMBER // 2
PAD_WIDTH = HEAD_NUMBER * HEAD_PAD
HALF_WIDTH = PAD_WIDTH // 2
LEAD = 16
TAIL = 32
SMALL_SIDE = 6
SMALL_WINDOW = 48
LARGE_WINDOW = 208
CROP_GROUP = 2
ROW_TILE = 464
GELU_TILE = 128
VMEM_LIMIT = 58 * 2**20

norm_epsilon = 1e-06
batch_epsilon = 1e-05
attention_epsilon = 1e-06
covariance_forgetting = 0.5
weight_rate = 0.5
vector_rate = 0.1
sharpness_step_size = 2.0
energy_epsilon = 1e-08

F32 = jnp.float32
BF16 = jnp.bfloat16
VMEM_SPEC = pl.BlockSpec(memory_space=pltpu.VMEM)
ANY_SPEC = pl.BlockSpec(memory_space=pl.ANY)
SMEM_SPEC = pl.BlockSpec(memory_space=pltpu.SMEM)


def dot(left, right):
    return lax.dot_general(left, right, (((1,), (0,)), ((), ())), preferred_element_type=F32)


def dot_rows(left, right):
    return lax.dot_general(left, right, (((0,), (0,)), ((), ())), preferred_element_type=F32)


def dot_lanes(left, right):
    return lax.dot_general(left, right, (((1,), (1,)), ((), ())), preferred_element_type=F32)


def split(values):
    high = values.astype(BF16)
    return high, (values - high.astype(F32)).astype(BF16)


def dot_split(product, left, right):
    if product is dot_rows:
        return product(
            jnp.concatenate([left[0], left[0], left[1]], axis=0),
            jnp.concatenate([right[0], right[1], right[0]], axis=0),
        )
    rows = left[0].shape[0]
    both = product(jnp.concatenate(left, axis=0), right[0])
    return both[:rows] + both[rows:] + product(left[0], right[1])


def fold(values):
    total = values[0:8]
    for first in range(8, values.shape[0], 8):
        total = total + values[first : first + 8]
    return total


def gelu_parts(values):
    magnitude = jnp.abs(values) * 0.7071067811865476
    base = 1.0 + 0.3275911 * magnitude
    guess = pl.reciprocal(base, approx=True)
    slot = guess * (2.0 - base * guess)
    series = slot * (
        0.127414796
        + slot
        * (-0.142248368 + slot * (0.7107068705 + slot * (-0.7265760135 + slot * 0.5307027145)))
    )
    bell = jnp.exp(-0.5 * values * values)
    lower = series * bell
    return jnp.where(values >= 0, 1.0 - lower, lower), bell


def gelu_slope(values, share, bell):
    return share + values * bell * 0.3989422804014327


def head_map(dtype):
    feature = lax.broadcasted_iota(jnp.int32, (HEAD_NUMBER * HDIM, PAD_WIDTH), 0)
    lane = lax.broadcasted_iota(jnp.int32, (HEAD_NUMBER * HDIM, PAD_WIDTH), 1)
    inner = lane & (HEAD_PAD - 1)
    hit = (inner < HDIM) & ((lane >> 6) * HDIM + inner == feature)
    return hit.astype(F32).astype(dtype)


def centered(values):
    center = jnp.sum(values, axis=-1, keepdims=True) * (1.0 / values.shape[-1])
    shifted = values - center
    spread = jnp.sum(shifted * shifted, axis=-1, keepdims=True) * (1.0 / values.shape[-1])
    scale = lax.rsqrt(spread + norm_epsilon)
    return shifted * scale, scale


def norm_back(grad, unit, scale):
    size = 1.0 / grad.shape[-1]
    middle = jnp.sum(grad, axis=-1, keepdims=True) * size
    slope = jnp.sum(grad * unit, axis=-1, keepdims=True) * size
    return scale * (grad - middle - unit * slope)


def tile_rows(count, least):
    for parts in range(least, count // 16 + 1):
        if count % (16 * parts) == 0:
            return count // parts
    return count


def for_rows(count, tile, step, carry=0):
    def body(index, carry):
        return step(pl.multiple_of(index * tile, tile), tile, carry)

    if count // tile == 1:
        carry = step(0, tile, carry)
    else:
        carry = lax.fori_loop(0, count // tile, body, carry)
    if count % tile:
        carry = step(count - count % tile, count % tile, carry)
    return carry


def live_total(sides_ref):
    return lax.fori_loop(
        0, sides_ref.shape[0], lambda c, t: t + sides_ref[c] * sides_ref[c], jnp.int32(0)
    )


def row_mask(first, rows, width, limit):
    return lax.broadcasted_iota(jnp.int32, (rows, width), 0) + first < limit


def for_groups(sides_ref, step, carry):
    def crop_body(crop, state):
        start, carry = state
        side = sides_ref[crop]
        cells = side * side
        inverse = 1.0 / jnp.full((8, LANES), side, jnp.int32).astype(F32)
        lines = lax.broadcasted_iota(jnp.int32, (8, LANES), 0)

        def group_body(group, carry):
            for part in range(2):
                row = pl.multiple_of((group * 2 + part) * 8, 8)
                place = lines + (row - start)
                line = ((place.astype(F32) + 0.5) * inverse).astype(jnp.int32)
                column = place - line * side
                inside = (place >= 0) & (place < cells)
                masks = (
                    inside,
                    column >= 1,
                    column < side - 1,
                    place >= side,
                    place < cells - side,
                )
                carry = step(row, side, masks, carry)
            return carry

        carry = lax.fori_loop(start // 16, (start + cells + 15) // 16, group_body, carry)
        return start + cells, carry

    return lax.fori_loop(0, sides_ref.shape[0], crop_body, (jnp.int32(0), carry))[1]


def conv_forward(source, chunk, row, side, masks, taps):
    inside, left_ok, right_ok, up_ok, down_ok = masks
    total = None
    for shift in (-1, 0, 1):
        base = LEAD + row + shift * side
        middle = source[chunk, pl.ds(base, 8), :]
        left = jnp.where(left_ok, source[chunk, pl.ds(base - 1, 8), :], 0.0)
        right = jnp.where(right_ok, source[chunk, pl.ds(base + 1, 8), :], 0.0)
        first = 3 * (shift + 1)
        value = taps[first] * left + taps[first + 1] * middle + taps[first + 2] * right
        if shift == -1:
            value = jnp.where(up_ok, value, 0.0)
        if shift == 1:
            value = jnp.where(down_ok, value, 0.0)
        total = value if total is None else total + value
    return total


def conv_backward(source, chunk, row, side, masks, taps, own, tap_sums):
    inside, left_ok, right_ok, up_ok, down_ok = masks
    total = None
    tap_sums = list(tap_sums)
    for shift in (-1, 0, 1):
        base = LEAD + row + shift * side
        row_ok = {-1: up_ok, 0: None, 1: down_ok}[shift]
        for sway in (-1, 0, 1):
            column_ok = {-1: left_ok, 0: None, 1: right_ok}[sway]
            value = source[chunk, pl.ds(base + sway, 8), :]
            keep = inside
            if row_ok is not None:
                keep = keep & row_ok
            if column_ok is not None:
                keep = keep & column_ok
            value = jnp.where(keep, value, 0.0)
            index = 3 * (1 - shift) + (1 - sway)
            term = taps[index] * value
            total = term if total is None else total + term
            tap_sums[index] = tap_sums[index] + own * value
    return total, tuple(tap_sums)


def chunk_lanes(chunk):
    return slice(chunk * LANES, (chunk + 1) * LANES)


def tap_vectors(table_ref, first, chunk):
    return [
        jnp.broadcast_to(table_ref[first + k : first + k + 1, chunk_lanes(chunk)], (8, LANES))
        for k in range(9)
    ]


def for_crops(sides_ref, row_count, order_ref, start_ref, step):
    crops = sides_ref.shape[0]

    def scan(crop, state):
        start, large, small = state
        side = sides_ref[crop]
        start_ref[crop] = start
        is_small = side <= SMALL_SIDE
        order_ref[jnp.where(is_small, crops + small, large)] = crop
        return (
            start + side * side,
            large + jnp.where(is_small, 0, 1),
            small + jnp.where(is_small, 1, 0),
        )

    zero = jnp.int32(0)
    _, large, small = lax.fori_loop(0, crops, scan, (zero, zero, zero))
    for window, first, count in ((LARGE_WINDOW, 0, large), (SMALL_WINDOW, crops, small)):

        def group_body(group, _, window=window, first=first, count=count):
            members = []
            for member in range(CROP_GROUP):
                crop = order_ref[first + jnp.minimum(group * CROP_GROUP + member, count - 1)]
                start = start_ref[crop]
                side = sides_ref[crop]
                row = pl.multiple_of(jnp.minimum(start // 8, (row_count - window) // 8) * 8, 8)
                place = lax.broadcasted_iota(jnp.int32, (window, HALF_WIDTH), 0) + (row - start)
                members.append((crop, pl.ds(row, window), (place >= 0) & (place < side * side)))
            step(members)
            return 0

        lax.fori_loop(0, (count + CROP_GROUP - 1) // CROP_GROUP, group_body, 0)


def half_lanes(half):
    starts = [part * PAD_WIDTH + half * HALF_WIDTH for part in range(3)]
    return [slice(start, start + HALF_WIDTH) for start in starts]


def pair_lanes():
    return lax.broadcasted_iota(jnp.int32, (HDIM, LANES), 1) < HEAD_PAD


def pair_part(block, pair):
    first = pair * LANES
    lanes = slice(first, first + LANES)
    return jnp.where(
        pair_lanes(),
        block[first : first + HDIM, lanes],
        block[first + HEAD_PAD : first + HEAD_PAD + HDIM, lanes],
    )


def spread_pair(target, member, half, pair, values):
    first = pair * LANES
    lanes = slice(first, first + LANES)
    parts = split(values)
    for index in range(2):
        value = parts[index].astype(F32)
        target[member, half, index, first : first + HDIM, lanes] = jnp.where(
            pair_lanes(), value, 0.0
        ).astype(BF16)
        target[member, half, index, first + HEAD_PAD : first + HEAD_PAD + HDIM, lanes] = jnp.where(
            pair_lanes(), 0.0, value
        ).astype(BF16)


def pair_sharpness(sharp_ref, pair):
    lane = lax.broadcasted_iota(jnp.int32, (1, LANES), 1)
    return jnp.where(lane < HEAD_PAD, sharp_ref[2 * pair], sharp_ref[2 * pair + 1])


def units(values):
    scale = lax.rsqrt(jnp.sum(values * values, axis=0, keepdims=True) + attention_epsilon)
    return values * scale, scale


def mixing_forward_kernel(
    sides_ref,
    sharp_ref,
    input_ref,
    weight_ref,
    table_ref,
    x1_hbm,
    qkv_hbm,
    mixed_hbm,
    scores_hbm,
    attention_hbm,
    u_hbm,
    e_hbm,
    sums_ref,
    x1_ref,
    qkv_ref,
    mixed_ref,
    scores_ref,
    attention_ref,
    u_ref,
    e_ref,
    head_weights,
    out_weight,
    first_low,
    mixed,
    attention_out,
    conv_in,
    spread,
    order_ref,
    start_ref,
    sems,
):
    row_count, width = input_ref.shape
    chunks = width // LANES
    tile = tile_rows(row_count, 2)
    saves = [
        pltpu.make_async_copy(source, target, sems.at[index])
        for index, (source, target) in enumerate(
            (
                (qkv_ref, qkv_hbm),
                (scores_ref, scores_hbm),
                (attention_ref, attention_hbm),
                (mixed_ref, mixed_hbm),
                (x1_ref, x1_hbm),
                (u_ref, u_hbm),
                (e_ref, e_hbm),
            )
        )
    ]
    total_live = live_total(sides_ref)
    mapping = head_map(BF16)
    for part in range(3):
        head_weights[:, part * PAD_WIDTH : (part + 1) * PAD_WIDTH] = dot(
            weight_ref[part], mapping
        ).astype(BF16)
    spread[...] = jnp.zeros_like(spread)

    def first_norm(first, size, _):
        rows = pl.ds(first, size)
        unit, _ = centered(input_ref[rows, :].astype(F32))
        first_low[rows, :] = (unit * table_ref[0:1, :] + table_ref[1:2, :]).astype(BF16)
        mixed[rows, :] = jnp.zeros((size, PAD_WIDTH), F32)
        return 0

    for_rows(row_count, ROW_TILE, first_norm)

    @pl.loop(0, row_count // tile)
    def _(step):
        rows = pl.ds(pl.multiple_of(step * tile, 16), tile)
        for part in range(3):
            lanes = slice(part * PAD_WIDTH, (part + 1) * PAD_WIDTH)
            qkv_ref[rows, lanes] = dot(first_low[rows, :], head_weights[:, lanes])

    saves[0].start()

    def crop_step(members):
        units_of = [(member, half) for member in range(len(members)) for half in range(2)]
        blocks, results = [], []
        for member, half in units_of:
            crop, rows, keep = members[member]
            lanes = half_lanes(half)
            query = units(jnp.where(keep, qkv_ref[rows, lanes[0]], 0.0))[0]
            key = units(jnp.where(keep, qkv_ref[rows, lanes[1]], 0.0))[0]
            blocks.append(dot_split(dot_rows, split(key), split(query)))
        for (member, half), block in zip(units_of, blocks):
            crop = members[member][0]
            for pair in range(2):
                scores = pair_part(block, pair)
                scores_ref[crop, 2 * half + pair] = scores
                scores = scores * pair_sharpness(sharp_ref, 2 * half + pair)
                scores = jnp.exp(scores - jnp.max(scores, axis=0, keepdims=True))
                shares = scores / jnp.sum(scores, axis=0, keepdims=True)
                attention_ref[crop, 2 * half + pair] = shares
                spread_pair(spread, member, half, pair, shares)
        for member, half in units_of:
            rows = members[member][1]
            shares = (spread[member, half, 0], spread[member, half, 1])
            results.append(dot_split(dot, split(qkv_ref[rows, half_lanes(half)[2]]), shares))
        for (member, half), result in zip(units_of, results):
            _, rows, keep = members[member]
            lanes = half_lanes(half)[0]
            mixed[rows, lanes] = jnp.where(keep, result, mixed[rows, lanes])

    for_crops(sides_ref, row_count, order_ref, start_ref, crop_step)

    saves[1].start()
    saves[2].start()
    out_weight[...] = dot_rows(mapping, weight_ref[3]).astype(BF16)

    @pl.loop(0, row_count // tile)
    def _(step):
        rows = pl.ds(pl.multiple_of(step * tile, 16), tile)
        low = mixed[rows, :].astype(BF16)
        mixed_ref[rows, :] = low
        attention_out[rows, :] = dot(low, out_weight[...])

    saves[3].start()

    def second_norm(first, size, _):
        rows = pl.ds(first, size)
        value = input_ref[rows, :].astype(F32) + table_ref[2:3, :] * attention_out[rows, :]
        x1_ref[rows, :] = value
        unit, _ = centered(value)
        value = unit * table_ref[3:4, :] + table_ref[4:5, :]
        for chunk in range(chunks):
            conv_in[chunk, pl.ds(LEAD + first, size), :] = value[:, chunk_lanes(chunk)]
            u_ref[chunk, rows, :] = jnp.zeros((size, LANES), F32)
            e_ref[chunk, rows, :] = jnp.zeros((size, LANES), F32)
        return 0

    for_rows(row_count, ROW_TILE, second_norm)
    saves[4].start()

    zero = jnp.zeros((8, LANES), F32)
    sums_ref[...] = zero
    taps = [tap_vectors(table_ref, 11, chunk) for chunk in range(chunks)]

    def conv_step(row, side, masks, carry):
        rows = pl.ds(row, 8)
        carry = list(carry)
        for chunk in range(chunks):
            value = conv_forward(conv_in, chunk, row, side, masks, taps[chunk])
            share, _ = gelu_parts(value)
            active = value * share
            u_ref[chunk, rows, :] = jnp.where(masks[0], value, u_ref[chunk, rows, :])
            e_ref[chunk, rows, :] = jnp.where(masks[0], active, e_ref[chunk, rows, :])
            active = jnp.where(masks[0], active, 0.0)
            carry[chunk] = carry[chunk] + active
            carry[chunks + chunk] = carry[chunks + chunk] + active * active
        return tuple(carry)

    sums = for_groups(sides_ref, conv_step, (zero,) * (2 * chunks))
    saves[5].start()
    saves[6].start()
    for index, value in enumerate(sums):
        sums_ref[index : index + 1, :] = jnp.sum(value, axis=0, keepdims=True)
    sums_ref[2 * chunks : 2 * chunks + 1, :] = jnp.full((1, LANES), total_live, jnp.int32).astype(F32)
    for save in saves:
        save.wait()


def mixing_forward(sides, sharpness, inputs, weights, table):
    row_count, width = inputs.shape
    crops = sides.shape[0]
    chunks = width // LANES
    shape = jax.ShapeDtypeStruct
    return pl.pallas_call(
        mixing_forward_kernel,
        out_shape=(
            shape((row_count, width), F32),
            shape((row_count, 3 * PAD_WIDTH), F32),
            shape((row_count, PAD_WIDTH), BF16),
            shape((crops, HEAD_PAIRS, HDIM, LANES), F32),
            shape((crops, HEAD_PAIRS, HDIM, LANES), F32),
            shape((chunks, row_count, LANES), F32),
            shape((chunks, row_count, LANES), F32),
            shape((8, LANES), F32),
        ),
        in_specs=[SMEM_SPEC, SMEM_SPEC, VMEM_SPEC, VMEM_SPEC, VMEM_SPEC],
        out_specs=(ANY_SPEC,) * 7 + (VMEM_SPEC,),
        scratch_shapes=[
            pltpu.VMEM((row_count, width), F32),
            pltpu.VMEM((row_count, 3 * PAD_WIDTH), F32),
            pltpu.VMEM((row_count, PAD_WIDTH), BF16),
            pltpu.VMEM((crops, HEAD_PAIRS, HDIM, LANES), F32),
            pltpu.VMEM((crops, HEAD_PAIRS, HDIM, LANES), F32),
            pltpu.VMEM((chunks, row_count, LANES), F32),
            pltpu.VMEM((chunks, row_count, LANES), F32),
            pltpu.VMEM((width, 3 * PAD_WIDTH), BF16),
            pltpu.VMEM((PAD_WIDTH, width), BF16),
            pltpu.VMEM((row_count, width), BF16),
            pltpu.VMEM((row_count, PAD_WIDTH), F32),
            pltpu.VMEM((row_count, width), F32),
            pltpu.VMEM((chunks, LEAD + row_count + TAIL, LANES), F32),
            pltpu.VMEM((CROP_GROUP, 2, 2, HALF_WIDTH, HALF_WIDTH), BF16),
            pltpu.SMEM((2 * crops,), jnp.int32),
            pltpu.SMEM((crops,), jnp.int32),
            pltpu.SemaphoreType.DMA((7,)),
        ],
        compiler_params=pltpu.CompilerParams(vmem_limit_bytes=VMEM_LIMIT),
        name="mixing_forward",
    )(sides, sharpness, inputs, weights, table)


def batch_vectors(bn_ref, chunk, chunks):
    count = bn_ref[2 * chunks : 2 * chunks + 1, :]
    mean = bn_ref[chunk : chunk + 1, :] / count
    scale = lax.rsqrt(bn_ref[chunks + chunk : chunks + chunk + 1, :] / count - mean * mean + batch_epsilon)
    return mean, scale


def feed_kernel(
    sides_ref,
    x1_hbm,
    e_hbm,
    bn_ref,
    weight_hbm,
    table_ref,
    adjoint_hbm,
    out_hbm,
    dx2_hbm,
    dn_hbm,
    weight_grad_hbm,
    grads_ref,
    back_sums_ref,
    e_ref,
    x1_ref,
    weight_ref,
    adjoint_ref,
    out_ref,
    dx2_ref,
    dn_ref,
    weight_grad_ref,
    up_weight,
    n_ref,
    z_ref,
    dw_ref,
    x2,
    unit,
    spread,
    third_low,
    pre,
    hidden_low,
    feed,
    feed_grad,
    pre_grad,
    grads,
    weight_sums,
    sems,
):
    loads = [
        pltpu.make_async_copy(source, target, sems.at[index])
        for index, (source, target) in enumerate(
            (
                (e_hbm, e_ref),
                (x1_hbm, x1_ref),
                (weight_hbm, weight_ref),
                (adjoint_hbm, adjoint_ref),
            )
        )
    ]
    saves = [
        pltpu.make_async_copy(source, target, sems.at[4 + index])
        for index, (source, target) in enumerate(
            (
                (out_ref, out_hbm),
                (dx2_ref, dx2_hbm),
                (weight_grad_ref, weight_grad_hbm),
                (dn_ref, dn_hbm),
            )
        )
    ]
    for load in loads:
        load.start()
    row_count, width = x1_ref.shape
    chunks = width // LANES
    expand = weight_ref.shape[0] // 2
    tile = tile_rows(row_count, 4)
    total_live = live_total(sides_ref)
    hidden = expand * width
    batch = [batch_vectors(bn_ref, chunk, chunks) for chunk in range(chunks)]
    zero = jnp.zeros((8, LANES), F32)

    def down_weight():
        return weight_ref[expand : 2 * expand].reshape(hidden, width)

    def normalize(first, size, _):
        rows = pl.ds(first, size)
        live = row_mask(first, size, LANES, total_live)
        for chunk in range(chunks):
            lanes = chunk_lanes(chunk)
            mean, scale = batch[chunk]
            value = (e_ref[chunk, rows, :] - mean) * scale
            value = value * table_ref[5:6, lanes] + table_ref[6:7, lanes]
            n_ref[chunk, pl.ds(LEAD + first, size), :] = jnp.where(live, value, 0.0)
            z_ref[chunk, rows, :] = jnp.zeros((size, LANES), F32)
            dn_ref[chunk, rows, :] = jnp.zeros((size, LANES), F32)
        return 0

    loads[0].wait()
    for_rows(row_count, ROW_TILE, normalize)

    taps = [tap_vectors(table_ref, 20, chunk) for chunk in range(chunks)]

    def conv_step(row, side, masks, carry):
        rows = pl.ds(row, 8)
        for chunk in range(chunks):
            value = conv_forward(n_ref, chunk, row, side, masks, taps[chunk])
            z_ref[chunk, rows, :] = jnp.where(masks[0], value, z_ref[chunk, rows, :])
        return carry

    for_groups(sides_ref, conv_step, 0)

    for load in loads[1:]:
        load.wait()
    for part in range(expand):
        up_weight[:, part * width : (part + 1) * width] = weight_ref[part]
    weight_sums[...] = jnp.zeros_like(weight_sums)
    grads[...] = jnp.zeros_like(grads)

    def z_rows(rows):
        return jnp.concatenate([z_ref[chunk, rows, :] for chunk in range(chunks)], axis=1)

    @pl.loop(0, row_count // tile)
    def _(step):
        base = pl.multiple_of(step * tile, 16)

        def before(inner, size, _):
            near, rows = pl.ds(inner, size), pl.ds(base + inner, size)
            value = x1_ref[rows, :] + table_ref[7:8, :] * z_rows(rows)
            x2[near, :] = value
            value, scale = centered(value)
            unit[near, :] = value
            spread[near, :] = jnp.broadcast_to(scale, (size, LANES))
            third_low[near, :] = (value * table_ref[8:9, :] + table_ref[9:10, :]).astype(BF16)
            return 0

        for_rows(tile, ROW_TILE, before)
        for part in range(2):
            lanes = slice(part * hidden // 2, (part + 1) * hidden // 2)
            value = dot(third_low[...], up_weight[:, lanes])
            share, bell = gelu_parts(value)
            hidden_low[:, lanes] = (value * share).astype(BF16)
            pre[:, lanes] = gelu_slope(value, share, bell)
        feed[...] = dot(hidden_low[...], down_weight())

        def output(inner, size, carry):
            near, rows = pl.ds(inner, size), pl.ds(base + inner, size)
            live = row_mask(base + inner, size, width, total_live)
            value = x2[near, :] + table_ref[10:11, :] * feed[near, :]
            out_ref[rows, :] = jnp.where(live, value, 0.0).astype(BF16)
            entry = jnp.where(live, adjoint_ref[rows, :].astype(F32), 0.0)
            feed_grad[near, :] = (entry * table_ref[10:11, :]).astype(BF16)
            return carry + fold(entry * feed[near, :])

        grads[0] += for_rows(tile, ROW_TILE, output, jnp.zeros((8, width), F32))
        pre_grad[...] = (dot_lanes(feed_grad[...], down_weight()) * pre[...]).astype(BF16)
        weight_sums[expand : 2 * expand] += dot_rows(hidden_low[...], feed_grad[...]).reshape(
            expand, width, width
        )
        up_grad = dot_rows(third_low[...], pre_grad[...])
        for part in range(expand):
            weight_sums[part] += up_grad[:, part * width : (part + 1) * width]
        feed[...] = dot_lanes(pre_grad[...], up_weight[...])

        def after(inner, size, carry):
            near, rows = pl.ds(inner, size), pl.ds(base + inner, size)
            live = row_mask(base + inner, size, width, total_live)
            entry = jnp.where(live, adjoint_ref[rows, :].astype(F32), 0.0)
            grad = feed[near, :]
            value = unit[near, :]
            total = entry + norm_back(grad * table_ref[8:9, :], value, spread[near, 0:1])
            dx2_ref[rows, :] = total
            scaled = total * table_ref[7:8, :]
            for chunk in range(chunks):
                dw_ref[chunk, pl.ds(LEAD + base + inner, size), :] = scaled[:, chunk_lanes(chunk)]
            return (
                carry[0] + fold(total * z_rows(rows)),
                carry[1] + fold(grad * value),
                carry[2] + fold(grad),
            )

        wide = jnp.zeros((8, width), F32)
        sums = for_rows(tile, ROW_TILE, after, (wide, wide, wide))
        for index in range(3):
            grads[1 + index] += sums[index]

    saves[0].start()
    saves[1].start()

    owners, pieces, shard, _ = weight_grad_ref.shape
    inner = width // shard
    for owner in range(owners):
        rows = slice(owner % inner * shard, (owner % inner + 1) * shard)
        for piece in range(pieces):
            weight_grad_ref[owner, piece] = weight_sums[
                owner // inner * pieces + piece, rows, :
            ].astype(BF16)

    saves[2].start()

    back_sums_ref[...] = zero
    for index, source in enumerate((1, 2, 3, 0)):
        grads_ref[index : index + 1, :] = jnp.sum(grads[source], axis=0, keepdims=True)
    def back_step(row, side, masks, carry):
        rows = pl.ds(row, 8)
        result = []
        for chunk in range(chunks):
            mean, scale = batch[chunk]
            sums = carry[chunk]
            own = jnp.where(masks[0], n_ref[chunk, pl.ds(LEAD + row, 8), :], 0.0)
            total, tap_sums = conv_backward(
                dw_ref, chunk, row, side, masks, taps[chunk], own, sums[0:9]
            )
            dn_ref[chunk, rows, :] = jnp.where(masks[0], total, dn_ref[chunk, rows, :])
            total = jnp.where(masks[0], total, 0.0)
            standard = (e_ref[chunk, rows, :] - mean) * scale
            result.append((*tap_sums, sums[9] + total * standard, sums[10] + total))
        return tuple(result)

    sums = for_groups(sides_ref, back_step, ((zero,) * 11,) * chunks)
    saves[3].start()
    for chunk in range(chunks):
        lanes = chunk_lanes(chunk)
        for index, value in enumerate(sums[chunk]):
            value = jnp.sum(value, axis=0, keepdims=True)
            grads_ref[4 + index : 5 + index, lanes] = value
            if index == 9:
                back_sums_ref[chunks + chunk : chunks + chunk + 1, :] = value
            if index == 10:
                back_sums_ref[chunk : chunk + 1, :] = value
    for save in saves:
        save.wait()


def feed_forward(sides, x1, e, batch_sums, weights, table, adjoint, grad_shape):
    row_count, width = x1.shape
    chunks = width // LANES
    expand = weights.shape[0] // 2
    tile = tile_rows(row_count, 4)
    shape = jax.ShapeDtypeStruct
    return pl.pallas_call(
        feed_kernel,
        out_shape=(
            shape((row_count, width), BF16),
            shape((row_count, width), F32),
            shape((chunks, row_count, LANES), F32),
            shape(grad_shape, BF16),
            shape((16, width), F32),
            shape((8, LANES), F32),
        ),
        in_specs=[SMEM_SPEC, ANY_SPEC, ANY_SPEC, VMEM_SPEC, ANY_SPEC, VMEM_SPEC, ANY_SPEC],
        out_specs=(ANY_SPEC,) * 4 + (VMEM_SPEC,) * 2,
        scratch_shapes=[
            pltpu.VMEM((chunks, row_count, LANES), F32),
            pltpu.VMEM((row_count, width), F32),
            pltpu.VMEM(weights.shape, BF16),
            pltpu.VMEM((row_count, width), BF16),
            pltpu.VMEM((row_count, width), BF16),
            pltpu.VMEM((row_count, width), F32),
            pltpu.VMEM((chunks, row_count, LANES), F32),
            pltpu.VMEM(grad_shape, BF16),
            pltpu.VMEM((width, expand * width), BF16),
            pltpu.VMEM((chunks, LEAD + row_count + TAIL, LANES), F32),
            pltpu.VMEM((chunks, row_count, LANES), F32),
            pltpu.VMEM((chunks, LEAD + row_count + TAIL, LANES), F32),
            pltpu.VMEM((tile, width), F32),
            pltpu.VMEM((tile, width), F32),
            pltpu.VMEM((tile, LANES), F32),
            pltpu.VMEM((tile, width), BF16),
            pltpu.VMEM((tile, expand * width), F32),
            pltpu.VMEM((tile, expand * width), BF16),
            pltpu.VMEM((tile, width), F32),
            pltpu.VMEM((tile, width), BF16),
            pltpu.VMEM((tile, expand * width), BF16),
            pltpu.VMEM((4, 8, width), F32),
            pltpu.VMEM((2 * expand, width, width), F32),
            pltpu.SemaphoreType.DMA((8,)),
        ],
        compiler_params=pltpu.CompilerParams(vmem_limit_bytes=VMEM_LIMIT),
        name="feed_forward",
    )(sides, x1, e, batch_sums, weights, table, adjoint)


def mixing_backward_kernel(
    sides_ref,
    sharp_ref,
    input_ref,
    weight_ref,
    table_ref,
    x1_hbm,
    qkv_hbm,
    mixed_hbm,
    scores_hbm,
    attention_hbm,
    u_hbm,
    bn_ref,
    dx2_hbm,
    dn_hbm,
    back_ref,
    out_ref,
    weight_grad_ref,
    grads_ref,
    x1_ref,
    qkv_ref,
    mixed_ref,
    scores_ref,
    attention_ref,
    dx2_ref,
    head_weights,
    out_weight,
    pool,
    conv_grad,
    dx1,
    mixed_grad,
    low_rows,
    head_low,
    spread,
    out_sum,
    sharp_sums,
    order_ref,
    start_ref,
    load_sems,
):
    row_count, width = input_ref.shape
    chunks = width // LANES
    u_ref, dn_ref = pool.at[0:chunks], pool.at[chunks : 2 * chunks]
    conv_in, attention_out = pool.at[2 * chunks : 3 * chunks], pool.at[3 * chunks : 4 * chunks]
    loads = [
        pltpu.make_async_copy(source, target, load_sems.at[index])
        for index, (source, target) in enumerate(
            (
                (x1_hbm, x1_ref),
                (u_hbm, u_ref),
                (dn_hbm, dn_ref),
                (mixed_hbm, mixed_ref),
                (dx2_hbm, dx2_ref),
                (qkv_hbm, qkv_ref),
                (scores_hbm, scores_ref),
                (attention_hbm, attention_ref),
            )
        )
    ]
    for load in loads:
        load.start()
    tile = tile_rows(row_count, 2)
    total_live = live_total(sides_ref)
    batch = [batch_vectors(bn_ref, chunk, chunks) for chunk in range(chunks)]
    zero = jnp.zeros((8, LANES), F32)
    wide = jnp.zeros((8, width), F32)
    mapping = head_map(BF16)
    for part in range(3):
        head_weights[:, part * PAD_WIDTH : (part + 1) * PAD_WIDTH] = dot(
            weight_ref[part], mapping
        ).astype(BF16)
    out_weight[...] = dot_rows(mapping, weight_ref[3]).astype(BF16)
    spread[...] = jnp.zeros_like(spread)

    for load in loads[0:3]:
        load.wait()

    def batch_back(first, size, _):
        rows = pl.ds(first, size)
        live = row_mask(first, size, LANES, total_live)
        unit, _ = centered(x1_ref[rows, :])
        value = unit * table_ref[3:4, :] + table_ref[4:5, :]
        for chunk in range(chunks):
            lanes = chunk_lanes(chunk)
            mean, scale = batch[chunk]
            count = bn_ref[2 * chunks : 2 * chunks + 1, :]
            u = u_ref[chunk, rows, :]
            share, bell = gelu_parts(u)
            standard = (u * share - mean) * scale
            inner = (
                back_ref[chunk : chunk + 1, :]
                + standard * back_ref[chunks + chunk : chunks + chunk + 1, :]
            ) / count
            grad = scale * table_ref[5:6, lanes] * (dn_ref[chunk, rows, :] - inner)
            grad = grad * gelu_slope(u, share, bell)
            conv_grad[chunk, pl.ds(LEAD + first, size), :] = jnp.where(live, grad, 0.0)
            conv_in[chunk, pl.ds(first, size), :] = value[:, lanes]
        return 0

    for_rows(row_count, ROW_TILE, batch_back)

    taps = [tap_vectors(table_ref, 11, chunk) for chunk in range(chunks)]

    def back_step(row, side, masks, carry):
        rows = pl.ds(row, 8)
        result = []
        for chunk in range(chunks):
            held = conv_in[chunk, rows, :]
            own = jnp.where(masks[0], held, 0.0)
            total, tap_sums = conv_backward(
                conv_grad, chunk, row, side, masks, taps[chunk], own, carry[chunk]
            )
            conv_in[chunk, rows, :] = jnp.where(masks[0], total, held)
            result.append(tap_sums)
        return tuple(result)

    tap_sums = for_groups(sides_ref, back_step, ((zero,) * 9,) * chunks)
    for chunk in range(chunks):
        for index, value in enumerate(tap_sums[chunk]):
            grads_ref[5 + index : 6 + index, chunk_lanes(chunk)] = jnp.sum(
                value, axis=0, keepdims=True
            )

    for load in loads[3:5]:
        load.wait()

    @pl.loop(0, row_count // tile)
    def _(step):
        rows = pl.ds(pl.multiple_of(step * tile, 16), tile)
        result = dot(mixed_ref[rows, :], out_weight[...])
        for chunk in range(chunks):
            attention_out[chunk, rows, :] = result[:, chunk_lanes(chunk)]

    def second_back(first, size, carry):
        rows = pl.ds(first, size)
        live = row_mask(first, size, width, total_live)
        grad = jnp.concatenate([conv_in[chunk, rows, :] for chunk in range(chunks)], axis=1)
        grad = jnp.where(live, grad, 0.0)
        unit, scale = centered(x1_ref[rows, :])
        total = dx2_ref[rows, :] + norm_back(grad * table_ref[3:4, :], unit, scale)
        dx1[rows, :] = total
        low_rows[rows, :] = (total * table_ref[2:3, :]).astype(BF16)
        held = jnp.concatenate([attention_out[chunk, rows, :] for chunk in range(chunks)], axis=1)
        return (
            carry[0] + fold(total * held),
            carry[1] + fold(grad * unit),
            carry[2] + fold(grad),
        )

    sums = for_rows(row_count, ROW_TILE, second_back, (wide, wide, wide))
    for index in range(3):
        grads_ref[2 + index : 3 + index, :] = jnp.sum(sums[index], axis=0, keepdims=True)

    out_sum[...] = jnp.zeros_like(out_sum)

    @pl.loop(0, row_count // tile)
    def _(step):
        rows = pl.ds(pl.multiple_of(step * tile, 16), tile)
        mixed_grad[rows, :] = dot_lanes(low_rows[rows, :], out_weight[...])
        out_sum[...] += dot_rows(mixed_ref[rows, :], low_rows[rows, :])

    pool[...] = jnp.zeros_like(pool)

    low = out_sum[...].astype(BF16)
    weight_grad_ref[3] = dot(mapping, low).astype(BF16)
    sharp_sums[...] = jnp.zeros_like(sharp_sums)

    for load in loads[5:]:
        load.wait()

    def crop_step(members):
        units_of = [(member, half) for member in range(len(members)) for half in range(2)]
        grads, blocks, sums, results = [], [], [], []
        for member, half in units_of:
            crop, rows, keep = members[member]
            lanes = half_lanes(half)
            value = split(jnp.where(keep, qkv_ref[rows, lanes[2]], 0.0))
            grad = split(jnp.where(keep, mixed_grad[rows, lanes[0]], 0.0))
            grads.append(grad)
            blocks.append(dot_split(dot_rows, value, grad))
        for (member, half), block in zip(units_of, blocks):
            crop = members[member][0]
            query_sums = []
            for pair in range(2):
                index = 2 * half + pair
                shares = attention_ref[crop, index]
                scores = scores_ref[crop, index]
                part = pair_part(block, pair)
                part = shares * (part - jnp.sum(part * shares, axis=0, keepdims=True))
                spread_pair(spread, member, half, pair, shares)
                total = jnp.sum(part * scores, axis=0, keepdims=True)
                sharp_sums[index, pl.ds(crop, 1), :] = total
                sharpness = pair_sharpness(sharp_ref, index)
                query_sums.append(total * sharpness)
                spread_pair(spread, member, 2 + half, pair, part * sharpness)
            sums.append(jnp.concatenate(query_sums, axis=1))
        for index, (member, half) in enumerate(units_of):
            crop, rows, keep = members[member]
            lanes = half_lanes(half)
            query, query_scale = units(jnp.where(keep, qkv_ref[rows, lanes[0]], 0.0))
            key, key_scale = units(jnp.where(keep, qkv_ref[rows, lanes[1]], 0.0))
            shares = (spread[member, half, 0], spread[member, half, 1])
            slopes = (spread[member, 2 + half, 0], spread[member, 2 + half, 1])
            value_grad = dot_split(dot_lanes, grads[index], shares)
            query_grad = dot_split(dot, split(key), slopes)
            query_grad = query_scale * (query_grad - query * sums[index])
            key_grad = dot_split(dot_lanes, split(query), slopes)
            key_grad = key_scale * (
                key_grad - key * jnp.sum(key_grad * key, axis=0, keepdims=True)
            )
            results.append((query_grad, key_grad, value_grad))
        for (member, half), grads in zip(units_of, results):
            _, rows, keep = members[member]
            for part, result in enumerate(grads):
                for side in range(HALF_WIDTH // LANES):
                    chunk = (part * PAD_WIDTH + half * HALF_WIDTH) // LANES + side
                    pool[chunk, rows, :] = jnp.where(
                        keep[:, 0:LANES], result[:, chunk_lanes(side)], pool[chunk, rows, :]
                    )

    for_crops(sides_ref, row_count, order_ref, start_ref, crop_step)

    grads_ref[14:16, :] = jnp.zeros((2, width), F32)
    lane = lax.broadcasted_iota(jnp.int32, (1, LANES), 1)
    total = jnp.zeros((1, LANES), F32)
    for head in range(HEAD_NUMBER):
        row = jnp.sum(sharp_sums[head // 2], axis=0, keepdims=True)
        row = jnp.where((lane >> 6) == head % 2, row, 0.0)
        total = jnp.where(lane == head, jnp.sum(row, axis=1, keepdims=True), total)
    grads_ref[14:15, 0:LANES] = total

    def first_norm(first, size, _):
        rows = pl.ds(first, size)
        unit, _ = centered(input_ref[rows, :].astype(F32))
        low_rows[rows, :] = (unit * table_ref[0:1, :] + table_ref[1:2, :]).astype(BF16)
        return 0

    for_rows(row_count, ROW_TILE, first_norm)

    for part in range(3):
        lanes = slice(part * PAD_WIDTH, (part + 1) * PAD_WIDTH)
        out_sum[...] = jnp.zeros_like(out_sum)

        @pl.loop(0, row_count // tile)
        def _(step, lanes=lanes, part=part):
            rows = pl.ds(pl.multiple_of(step * tile, 16), tile)
            first = part * PAD_WIDTH // LANES
            for chunk in range(PAD_WIDTH // LANES):
                head_low[rows, chunk_lanes(chunk)] = pool[first + chunk, rows, :].astype(BF16)
            term = dot_lanes(head_low[rows, :], head_weights[:, lanes])
            mixed_grad[rows, 0:width] = term if part == 0 else mixed_grad[rows, 0:width] + term

        @pl.loop(0, row_count // tile)
        def _(step, lanes=lanes):
            rows = pl.ds(pl.multiple_of(step * tile, 16), tile)
            out_sum[...] += dot_rows(head_low[rows, :], low_rows[rows, :])

        low = out_sum[...].astype(BF16)
        weight_grad_ref[part] = lax.dot_general(
            low, mapping, (((0,), (1,)), ((), ())), preferred_element_type=F32
        ).astype(BF16)

    def first_back(first, size, carry):
        rows = pl.ds(first, size)
        unit, scale = centered(input_ref[rows, :].astype(F32))
        grad = mixed_grad[rows, 0:width]
        total = dx1[rows, :] + norm_back(grad * table_ref[0:1, :], unit, scale)
        out_ref[rows, :] = total.astype(BF16)
        return carry[0] + fold(grad * unit), carry[1] + fold(grad)

    sums = for_rows(row_count, ROW_TILE, first_back, (wide, wide))
    for index in range(2):
        grads_ref[index : index + 1, :] = jnp.sum(sums[index], axis=0, keepdims=True)


def mixing_backward(sides, sharpness, inputs, weights, table, saved, batch_sums, dx2, dn, back_sums):
    row_count, width = inputs.shape
    chunks = width // LANES
    crops = sides.shape[0]
    shape = jax.ShapeDtypeStruct
    x1, qkv, mixed, scores, attention, u = saved
    return pl.pallas_call(
        mixing_backward_kernel,
        out_shape=(
            shape((row_count, width), BF16),
            shape((4, width, width), BF16),
            shape((16, width), F32),
        ),
        in_specs=[SMEM_SPEC, SMEM_SPEC]
        + [VMEM_SPEC] * 3
        + [ANY_SPEC] * 6
        + [VMEM_SPEC, ANY_SPEC, ANY_SPEC, VMEM_SPEC],
        out_specs=(VMEM_SPEC,) * 3,
        scratch_shapes=[
            pltpu.VMEM((row_count, width), F32),
            pltpu.VMEM((row_count, 3 * PAD_WIDTH), F32),
            pltpu.VMEM((row_count, PAD_WIDTH), BF16),
            pltpu.VMEM((crops, HEAD_PAIRS, HDIM, LANES), F32),
            pltpu.VMEM((crops, HEAD_PAIRS, HDIM, LANES), F32),
            pltpu.VMEM((row_count, width), F32),
            pltpu.VMEM((width, 3 * PAD_WIDTH), BF16),
            pltpu.VMEM((PAD_WIDTH, width), BF16),
            pltpu.VMEM((3 * PAD_WIDTH // LANES, row_count, LANES), F32),
            pltpu.VMEM((chunks, LEAD + row_count + TAIL, LANES), F32),
            pltpu.VMEM((row_count, width), F32),
            pltpu.VMEM((row_count, PAD_WIDTH), F32),
            pltpu.VMEM((row_count, width), BF16),
            pltpu.VMEM((row_count, PAD_WIDTH), BF16),
            pltpu.VMEM((CROP_GROUP, 4, 2, HALF_WIDTH, HALF_WIDTH), BF16),
            pltpu.VMEM((PAD_WIDTH, width), F32),
            pltpu.VMEM((HEAD_PAIRS, crops, LANES), F32),
            pltpu.SMEM((2 * crops,), jnp.int32),
            pltpu.SMEM((crops,), jnp.int32),
            pltpu.SemaphoreType.DMA((8,)),
        ],
        compiler_params=pltpu.CompilerParams(vmem_limit_bytes=VMEM_LIMIT),
        name="mixing_backward",
    )(
        sides,
        sharpness,
        inputs,
        weights,
        table,
        x1,
        qkv,
        mixed,
        scores,
        attention,
        u,
        batch_sums,
        dx2,
        dn,
        back_sums,
    )


MESH = pl.DeviceIdType.MESH


def greet(peers):
    barrier = pltpu.get_barrier_semaphore()
    for peer in peers:
        pl.semaphore_signal(barrier, inc=1, device_id=peer, device_id_type=MESH)
    pl.semaphore_wait(barrier, len(peers))


def push(source, target, send, receive, peer):
    copy = pltpu.make_async_remote_copy(
        src_ref=source,
        dst_ref=target,
        send_sem=send,
        recv_sem=receive,
        device_id=peer,
        device_id_type=MESH,
    )
    copy.start()
    return copy


def turned(place, step, count):
    return lax.rem(place + step, count)


def ring_peers(axis, count):
    place = lax.axis_index(axis)
    return [{axis: turned(place, step, count)} for step in range(1, count)]


def comm_params(identity):
    return pltpu.CompilerParams(
        collective_id=identity, has_side_effects=True, vmem_limit_bytes=VMEM_LIMIT
    )


def flip(value, bits):
    for bit in (1, 2, 4):
        if bits & bit:
            value = value + bit - 2 * bit * lax.rem(lax.div(value, bit), 2)
    return value


def flip_peers(axis, count):
    place = lax.axis_index(axis)
    return [{axis: flip(place, bits)} for bits in range(1, count)]


def sum_all_kernel(counts, part_ref, total_ref, parts, send, receive):
    n_dp, n_fsdp = counts
    dp, fsdp = lax.axis_index("dp"), lax.axis_index("fsdp")
    place = dp * n_fsdp + fsdp
    peers = [
        {"dp": flip(dp, outer), "fsdp": flip(fsdp, inner)}
        for inner in reversed(range(n_fsdp))
        for outer in reversed(range(n_dp))
        if inner or outer
    ]
    greet(peers)
    parts[place] = part_ref[...]
    copies = [
        push(part_ref, parts.at[place], send.at[k], receive.at[k], peer)
        for k, peer in enumerate(peers)
    ]
    for copy in copies:
        copy.wait()
    total = parts[0]
    for k in range(1, n_dp * n_fsdp):
        total = total + parts[k]
    total_ref[...] = total


def sum_all(part, counts, identity):
    size = counts[0] * counts[1]
    return pl.pallas_call(
        functools.partial(sum_all_kernel, counts),
        out_shape=jax.ShapeDtypeStruct(part.shape, F32),
        in_specs=[VMEM_SPEC],
        out_specs=VMEM_SPEC,
        scratch_shapes=[
            pltpu.VMEM((size, *part.shape), F32),
            pltpu.SemaphoreType.DMA((size - 1,)),
            pltpu.SemaphoreType.DMA((size - 1,)),
        ],
        compiler_params=comm_params(identity),
        name="sum_all",
    )(part)


def gather_kernel(
    counts,
    masters_ref,
    table_ref,
    blocks_ref,
    full_table_ref,
    blocks,
    tables,
    stage,
    ring_send,
    ring_recv,
    table_send,
    table_recv,
    cross_send,
    cross_recv,
    pair_send,
    pair_recv,
):
    n_dp, n_fsdp = counts
    dp, fsdp = lax.axis_index("dp"), lax.axis_index("fsdp")
    shard, width = masters_ref.shape[1:]
    columns = table_ref.shape[1]
    across = lax.rem(dp + 2, 4)
    pair = dp + 1 - 2 * lax.rem(dp, 2)
    peers = flip_peers("fsdp", n_fsdp)
    greet(peers + [{"dp": across}, {"dp": pair}])

    def piece(block, owner):
        return blocks.at[block, pl.ds(pl.multiple_of(owner * shard, 16), shard), :]

    def origin(step):
        return flip(fsdp, step)

    stage[...] = jnp.zeros_like(stage)
    stage[0 : table_ref.shape[0], 0:columns] = table_ref[...]
    tables[fsdp] = stage[...].astype(BF16)
    blocks[dp, pl.ds(pl.multiple_of(fsdp * shard, 16), shard), :] = masters_ref[dp].astype(BF16)
    own = piece(dp, fsdp)
    ring = [
        push(own, own, ring_send.at[k], ring_recv.at[k], peer) for k, peer in enumerate(peers)
    ]
    table_copies = [
        push(tables.at[fsdp], tables.at[fsdp], table_send.at[k], table_recv.at[k], peer)
        for k, peer in enumerate(peers)
    ]
    crossing, pairing = [], []
    for step in range(n_fsdp):
        if step:
            ring[step - 1].wait_recv()
        part = piece(dp, origin(step))
        crossing.append(push(part, part, cross_send.at[step], cross_recv.at[step], {"dp": across}))
        pairing.append(
            push(part, part, pair_send.at[0, step], pair_recv.at[0, step], {"dp": pair})
        )
    for step in range(n_fsdp):
        crossing[step].wait_recv()
        part = piece(across, origin(step))
        pairing.append(
            push(part, part, pair_send.at[1, step], pair_recv.at[1, step], {"dp": pair})
        )
    for copy in table_copies:
        copy.wait_recv()
    total = None
    for owner in range(n_fsdp):
        lane = lax.broadcasted_iota(jnp.int32, (LANES, width), 0)
        target = lax.broadcasted_iota(jnp.int32, (LANES, width), 1)
        hit = (lane < columns) & (lane + owner * columns == target)
        term = dot(tables[owner], hit.astype(F32).astype(BF16))
        total = term if total is None else total + term
    full_table_ref[...] = total
    for copy in pairing:
        copy.wait_recv()
    blocks_ref[...] = blocks[...]
    for copy in ring + table_copies + crossing + pairing:
        copy.wait_send()


def gather_start(masters, coefficients, counts, identity):
    n_dp, n_fsdp = counts
    width = masters.shape[2]
    shape = jax.ShapeDtypeStruct
    dma = pltpu.SemaphoreType.DMA
    return pl.pallas_call(
        functools.partial(gather_kernel, counts),
        out_shape=(shape((4, width, width), BF16), shape((32, width), F32)),
        in_specs=[VMEM_SPEC, VMEM_SPEC],
        out_specs=(VMEM_SPEC, VMEM_SPEC),
        scratch_shapes=[
            pltpu.VMEM((4, width, width), BF16),
            pltpu.VMEM((n_fsdp, 32, LANES), BF16),
            pltpu.VMEM((32, LANES), F32),
            dma((n_fsdp - 1,)),
            dma((n_fsdp - 1,)),
            dma((n_fsdp - 1,)),
            dma((n_fsdp - 1,)),
            dma((n_fsdp,)),
            dma((n_fsdp,)),
            dma((2, n_fsdp)),
            dma((2, n_fsdp)),
        ],
        compiler_params=comm_params(identity),
        name="gather_start",
    )(masters, coefficients)


def owner_rows(owner, shard):
    return pl.ds(pl.multiple_of(owner * shard, 16), shard)


TABLE_ROWS = (
    [(0, row) for row in range(5)]
    + [(1, 13), (1, 14)]
    + [(1, row) for row in range(4)]
    + [(0, row) for row in range(5, 14)]
    + [(1, row) for row in range(4, 13)]
)


def settle_kernel(
    counts,
    place_ref,
    mix_ref,
    feed_ref,
    mix_table_ref,
    feed_table_ref,
    left_hbm,
    right_hbm,
    grad_ref,
    slots_ref,
    rows_ref,
    table_ref,
    left,
    right,
    pair_buf,
    cross_out,
    cross_buf,
    ring_out,
    ring_buf,
    feed_in,
    feed_buf,
    dp_buf,
    slot_out,
    slots,
    steps,
    rows_buf,
    table_stage,
    table_out,
    table_buf,
    table_part,
    table_dp,
    load_sems,
    pair_send,
    pair_recv,
    cross_send,
    cross_recv,
    ring_send,
    ring_recv,
    feed_in_send,
    feed_in_recv,
    feed_send,
    feed_recv,
    dp_send,
    dp_recv,
    slot_send,
    slot_recv,
    twin_send,
    twin_recv,
    back_send,
    back_recv,
    last_send,
    last_recv,
    table_send,
    table_recv,
    table_dp_send,
    table_dp_recv,
):
    n_dp, n_fsdp = counts
    dp, fsdp = lax.axis_index("dp"), lax.axis_index("fsdp")
    width = mix_ref.shape[2]
    shard = width // n_fsdp
    core = lax.rem(dp, 2)
    across, pair, pair_across = flip(dp, 2), flip(dp, 1), flip(dp, 3)
    peers, dp_peers = flip_peers("fsdp", n_fsdp), flip_peers("dp", n_dp)
    to_pair, to_across = {"dp": pair}, {"dp": across}
    loads = [
        pltpu.make_async_copy(left_hbm.at[core], left, load_sems.at[0]),
        pltpu.make_async_copy(right_hbm.at[core], right, load_sems.at[1]),
    ]
    for load in loads:
        load.start()
    greet(peers + dp_peers)

    parts = list(reversed(range(n_fsdp // 2)))
    deep = 2 * shard

    def part_rows(part):
        first = lax.div(flip(fsdp, 2 * part), 2)
        return pl.ds(pl.multiple_of(first * deep, 16), deep)

    def owner_rows(owner):
        return pl.ds(pl.multiple_of(owner * shard, 16), shard)

    pairing = {}
    for part in parts:
        rows = part_rows(part)
        for side, block in enumerate((pair_across, pair)):
            pairing[part, side] = push(
                mix_ref.at[block, rows],
                pair_buf.at[side, rows],
                pair_send.at[side, part],
                pair_recv.at[side, part],
                to_pair,
            )
    pieces = feed_ref.shape[0] // n_dp
    feeding = [
        push(
            feed_ref.at[pl.ds(flip(dp, k + 1) * pieces, pieces)],
            feed_in.at[k],
            feed_in_send.at[k],
            feed_in_recv.at[k],
            peer,
        )
        for k, peer in enumerate(dp_peers)
    ]
    crossing = {}
    for part in parts:
        rows = part_rows(part)
        pairing[part, 0].wait_recv()
        cross_out[rows, :] = (
            mix_ref[across, rows, :].astype(F32) + pair_buf[0, rows, :].astype(F32)
        ).astype(BF16)
        crossing[part] = push(
            cross_out.at[rows],
            cross_buf.at[rows],
            cross_send.at[part],
            cross_recv.at[part],
            to_across,
        )
    ring = {}
    for part in parts:
        rows = part_rows(part)
        pairing[part, 1].wait_recv()
        crossing[part].wait_recv()
        ring_out[rows, :] = (
            mix_ref[dp, rows, :].astype(F32)
            + pair_buf[1, rows, :].astype(F32)
            + cross_buf[rows, :].astype(F32)
        ).astype(BF16)
        for bits in (2 * part + 1, 2 * part):
            if bits:
                ring[bits] = push(
                    ring_out.at[owner_rows(flip(fsdp, bits))],
                    ring_buf.at[bits],
                    ring_send.at[bits - 1],
                    ring_recv.at[bits - 1],
                    peers[bits - 1],
                )

    for copy in feeding:
        copy.wait_recv()
    total = feed_ref[pl.ds(dp * pieces, pieces)].astype(F32)
    for k in range(n_dp - 1):
        total = total + feed_in[k].astype(F32)
    feed_buf[dp] = total.astype(BF16)
    feeds = [
        push(feed_buf.at[dp], feed_buf.at[dp], feed_send.at[k], feed_recv.at[k], peer)
        for k, peer in enumerate(dp_peers)
    ]

    table_stage[...] = jnp.zeros_like(table_stage)
    for row, (source, first) in enumerate(TABLE_ROWS):
        ref = mix_table_ref if source == 0 else feed_table_ref
        table_stage[row : row + 1, :] = ref[first : first + 1, :]
    terms, rest = [], table_stage[...]
    for _ in range(3):
        term = rest.astype(BF16)
        terms.append(term)
        rest = rest - term.astype(F32)
    terms = jnp.concatenate(terms, axis=0)
    columns = width // n_fsdp
    sharp_row = lax.broadcasted_iota(jnp.int32, (32, LANES), 0) == 31
    sharp_values = jnp.broadcast_to(mix_table_ref[14:15, 0:LANES], (32, LANES))
    for owner in range(n_fsdp):
        lane = lax.broadcasted_iota(jnp.int32, (width, LANES), 1)
        source = lax.broadcasted_iota(jnp.int32, (width, LANES), 0)
        hit = ((lane < columns) & (lane + owner * columns == source)).astype(F32).astype(BF16)
        value = dot(terms, hit)
        value = value[0:32] + value[32:64] + value[64:96]
        table_out[owner] = jnp.where(sharp_row, sharp_values, value)
    table_buf[fsdp] = table_out[fsdp]
    tabling = [
        push(
            table_out.at[flip(fsdp, k + 1)],
            table_buf.at[fsdp],
            table_send.at[k],
            table_recv.at[k],
            peer,
        )
        for k, peer in enumerate(peers)
    ]

    total = ring_out[owner_rows(fsdp), :].astype(F32)
    for bits in range(1, n_fsdp):
        ring[bits].wait_recv()
        total = total + ring_buf[bits].astype(F32)
    dp_buf[dp] = total
    gathering = [
        push(dp_buf.at[dp], dp_buf.at[dp], dp_send.at[k], dp_recv.at[k], peer)
        for k, peer in enumerate(dp_peers)
    ]
    for copy in tabling:
        copy.wait_recv()
    total = table_buf[0]
    for owner in range(1, n_fsdp):
        total = total + table_buf[owner]
    table_part[...] = total
    table_dp[dp] = total
    table_dps = [
        push(table_part, table_dp.at[dp], table_dp_send.at[k], table_dp_recv.at[k], peer)
        for k, peer in enumerate(dp_peers)
    ]
    for copy in feeds:
        copy.wait_recv()
    for place in range(n_dp):
        for piece in range(pieces):
            grad_ref[n_dp + place * pieces + piece] = feed_buf[place, piece].astype(F32)
    for copy in gathering:
        copy.wait_recv()
    for place in range(n_dp):
        grad_ref[place] = dp_buf[place]

    slotting = {}
    for bits in reversed(range(n_fsdp)):
        slot = 2 * flip(fsdp, bits) + core
        block, filled = jnp.int32(0), jnp.int32(0)
        for index in range(grad_ref.shape[0]):
            here = place_ref[index] == slot
            block = jnp.where(here, index, block)
            filled = jnp.where(here, 1, filled)
        value = (grad_ref[block] * filled.astype(F32)).astype(BF16)
        if bits:
            slot_out[bits - 1] = value
            slotting[bits] = push(
                slot_out.at[bits - 1],
                slots.at[core, owner_rows(fsdp), :],
                slot_send.at[bits - 1],
                slot_recv.at[bits - 1],
                peers[bits - 1],
            )
        else:
            slots[core, owner_rows(fsdp), :] = value
    for load in loads:
        load.wait()
    left_parts, right_parts = split(left[...]), split(right[...])
    twins = []
    for bits in range(n_fsdp):
        if bits:
            slotting[bits].wait_recv()
        part = slots.at[core, owner_rows(flip(fsdp, bits)), :]
        twins.append(push(part, part, twin_send.at[bits], twin_recv.at[bits], to_pair))

    grad = slots[core]
    half = split(dot(left_parts[0], grad) + dot(left_parts[1], grad))
    steps[...] = dot_split(dot, half, right_parts).astype(BF16)
    back = {}
    for bits in reversed(range(1, n_fsdp)):
        back[bits] = push(
            steps.at[owner_rows(flip(fsdp, bits))],
            rows_buf.at[2 * fsdp + core],
            back_send.at[bits - 1],
            back_recv.at[bits - 1],
            peers[bits - 1],
        )
    rows_buf[2 * fsdp + core] = steps[owner_rows(fsdp), :]
    for copy in table_dps:
        copy.wait_recv()
    total = table_dp[0]
    for place in range(1, n_dp):
        total = total + table_dp[place]
    table_ref[...] = total
    lasts = []
    for bits in range(n_fsdp):
        if bits:
            back[bits].wait_recv()
        part = rows_buf.at[2 * flip(fsdp, bits) + core]
        lasts.append(push(part, part, last_send.at[bits], last_recv.at[bits], to_pair))
    for copy in twins:
        copy.wait_recv()
    slots_ref[...] = slots[...]
    for copy in lasts:
        copy.wait_recv()
    rows_ref[...] = rows_buf[...]
    copies = [*pairing.values(), *crossing.values(), *ring.values(), *slotting.values()]
    copies += [*back.values(), *feeding, *feeds, *tabling, *table_dps, *gathering]
    for copy in copies + twins + lasts:
        copy.wait_send()


def settle(places, mix, feed, mix_table, feed_table, left, right, counts, identity):
    n_dp, n_fsdp = counts
    width = mix.shape[2]
    shard = width // n_fsdp
    blocks = n_dp + feed.shape[0]
    pieces = feed.shape[0] // n_dp
    inner, outer = n_fsdp - 1, n_dp - 1
    shape = jax.ShapeDtypeStruct
    dma = pltpu.SemaphoreType.DMA
    sizes = [(2, n_fsdp // 2), (n_fsdp // 2,), (inner,), (outer,), (outer,), (outer,)]
    sizes += [(inner,), (n_fsdp,), (inner,), (n_fsdp,), (inner,), (outer,)]
    return pl.pallas_call(
        functools.partial(settle_kernel, counts),
        out_shape=(
            shape((blocks, shard, width), F32),
            shape((2, width, width), BF16),
            shape((2 * n_fsdp, shard, width), BF16),
            shape((32, LANES), F32),
        ),
        in_specs=[SMEM_SPEC] + [VMEM_SPEC] * 4 + [ANY_SPEC] * 2,
        out_specs=(VMEM_SPEC,) * 4,
        scratch_shapes=[
            pltpu.VMEM((width, width), F32),
            pltpu.VMEM((width, width), F32),
            pltpu.VMEM((2, width, width), BF16),
            pltpu.VMEM((width, width), BF16),
            pltpu.VMEM((width, width), BF16),
            pltpu.VMEM((width, width), BF16),
            pltpu.VMEM((n_fsdp, shard, width), BF16),
            pltpu.VMEM((outer, pieces, shard, width), BF16),
            pltpu.VMEM((n_dp, pieces, shard, width), BF16),
            pltpu.VMEM((n_dp, shard, width), F32),
            pltpu.VMEM((inner, shard, width), BF16),
            pltpu.VMEM((2, width, width), BF16),
            pltpu.VMEM((width, width), BF16),
            pltpu.VMEM((2 * n_fsdp, shard, width), BF16),
            pltpu.VMEM((32, width), F32),
            pltpu.VMEM((n_fsdp, 32, LANES), F32),
            pltpu.VMEM((n_fsdp, 32, LANES), F32),
            pltpu.VMEM((32, LANES), F32),
            pltpu.VMEM((n_dp, 32, LANES), F32),
            dma((2,)),
        ]
        + [dma(size) for size in sizes for _ in range(2)],
        compiler_params=comm_params(identity),
        name="settle",
    )(places, mix, feed, mix_table, feed_table, left, right)


def finish_kernel(
    place_ref,
    grad_ref,
    slots_ref,
    rows_ref,
    table_ref,
    energy_ref,
    coefficient_ref,
    sharp_ref,
    left_hbm,
    right_hbm,
    masters_hbm,
    grad_hbm,
    left_out_hbm,
    right_out_hbm,
    masters_out_hbm,
    low_hbm,
    table_grad_ref,
    energy_out_ref,
    coefficient_out_ref,
    sharp_out_ref,
    left,
    right,
    masters,
    low,
    sems,
):
    slot_count = slots_ref.shape[0]
    load_left = pltpu.make_async_copy(left_hbm, left, sems.at[0])
    load_right = pltpu.make_async_copy(right_hbm, right, sems.at[1])
    load_masters = pltpu.make_async_copy(masters_hbm, masters, sems.at[2])
    saves = [
        pltpu.make_async_copy(source, target, sems.at[3 + index])
        for index, (source, target) in enumerate(
            (
                (grad_ref, grad_hbm),
                (left, left_out_hbm),
                (right, right_out_hbm),
                (masters, masters_out_hbm),
                (low, low_hbm),
            )
        )
    ]
    load_left.start()
    load_right.start()
    load_masters.start()
    saves[0].start()
    load_left.wait()
    for slot in range(slot_count):
        grad = slots_ref[slot]
        left[slot] = (
            covariance_forgetting * left[slot]
            + (1.0 - covariance_forgetting) * dot_lanes(grad, grad)
        )
    saves[1].start()
    load_right.wait()
    for slot in range(slot_count):
        grad = slots_ref[slot]
        right[slot] = (
            covariance_forgetting * right[slot]
            + (1.0 - covariance_forgetting) * dot_rows(grad, grad)
        )
    saves[2].start()
    load_masters.wait()
    for block in range(masters.shape[0]):
        value = masters[block] - weight_rate * rows_ref[place_ref[block]].astype(F32)
        masters[block] = value
        low[block] = value.astype(BF16)
    saves[3].start()
    saves[4].start()
    count, columns = energy_ref.shape
    grad = table_ref[0:count, 0:columns]
    table_grad_ref[...] = grad
    energy = covariance_forgetting * energy_ref[...] + (1.0 - covariance_forgetting) * grad * grad
    energy_out_ref[...] = energy
    coefficient_out_ref[...] = coefficient_ref[...] - vector_rate * grad / (
        jnp.sqrt(energy) + energy_epsilon
    )
    grad = table_ref[31:32, 0:HEAD_NUMBER]
    energy = (
        covariance_forgetting * sharp_ref[1:2, :] + (1.0 - covariance_forgetting) * grad * grad
    )
    sharp_out_ref[0:1, :] = grad
    sharp_out_ref[1:2, :] = energy
    sharp_out_ref[2:3, :] = sharp_ref[0:1, :] - sharpness_step_size * grad / (
        jnp.sqrt(energy) + energy_epsilon
    )
    for save in saves:
        save.wait()


def finish(places, grads, slots, rows, table, energy, coefficients, sharps, left, right, masters):
    shape = jax.ShapeDtypeStruct
    return pl.pallas_call(
        finish_kernel,
        out_shape=(
            shape(grads.shape, F32),
            shape(left.shape, F32),
            shape(right.shape, F32),
            shape(masters.shape, F32),
            shape(masters.shape, BF16),
            shape(energy.shape, F32),
            shape(energy.shape, F32),
            shape(energy.shape, F32),
            shape((3, sharps.shape[1]), F32),
        ),
        in_specs=[SMEM_SPEC] + [VMEM_SPEC] * 7 + [ANY_SPEC] * 3,
        out_specs=(ANY_SPEC,) * 5 + (VMEM_SPEC,) * 4,
        scratch_shapes=[
            pltpu.VMEM(left.shape, F32),
            pltpu.VMEM(right.shape, F32),
            pltpu.VMEM(masters.shape, F32),
            pltpu.VMEM(masters.shape, BF16),
            pltpu.SemaphoreType.DMA((8,)),
        ],
        compiler_params=pltpu.CompilerParams(vmem_limit_bytes=VMEM_LIMIT),
        name="finish",
    )(places, grads, slots, rows, table, energy, coefficients, sharps, left, right, masters)


def shards(
    patch_embeddings,
    view_side_tokens,
    projection_masters,
    channel_coefficients,
    head_sharpness,
    output_adjoint,
    leading_covariance,
    trailing_covariance,
    leading_root_preconditioner,
    trailing_root_preconditioner,
    channel_energy_average,
    sharpness_energy_average,
    storage_position_map,
):
    row_count, feature_count = patch_embeddings.shape
    block_count = projection_masters.shape[0]
    shard_rows = projection_masters.shape[1]
    slot_count = leading_covariance.shape[0]
    counts = (lax.axis_size("dp"), lax.axis_size("fsdp"))
    direct = counts[0] == 4 and slot_count == 2 and shard_rows % 16 == 0
    if direct:
        mixing_blocks, table = gather_start(projection_masters, channel_coefficients, counts, 0)
        grad_shape = (counts[1], block_count - 4, shard_rows, feature_count)
    else:
        full_table = lax.all_gather(channel_coefficients.astype(BF16), "fsdp", axis=1, tiled=True)
        table = full_table.astype(F32)
        mixing_blocks = lax.all_gather(
            projection_masters[:4].astype(BF16), "fsdp", axis=1, tiled=True
        )
        grad_shape = (1, block_count - 4, feature_count, feature_count)
    feed_blocks = lax.all_gather(projection_masters[4:].astype(BF16), "fsdp", axis=1, tiled=True)

    def batch_total(part, identity):
        if direct:
            return sum_all(part, counts, identity)
        return lax.psum(part, ("dp", "fsdp"))

    x1, qkv, mixed, scores, attention, u, e, sums = mixing_forward(
        view_side_tokens, head_sharpness, patch_embeddings, mixing_blocks, table
    )
    batch_sums = batch_total(sums, 1)
    layer_output, dx2, dn, feed_grad, feed_table, back_part = feed_forward(
        view_side_tokens, x1, e, batch_sums, feed_blocks, table, output_adjoint, grad_shape
    )
    back_sums = batch_total(back_part, 2)
    incoming_tokens_grad, mixing_grad, mixing_table = mixing_backward(
        view_side_tokens,
        head_sharpness,
        patch_embeddings,
        mixing_blocks,
        table,
        (x1, qkv, mixed, scores, attention, u),
        batch_sums,
        dx2,
        dn,
        back_sums,
    )
    if direct:
        feed_grad = lax.psum_scatter(feed_grad, "fsdp", scatter_dimension=0, tiled=True)[0]
        grads, owned_grad, my_rows, table_total = settle(
            storage_position_map,
            mixing_grad,
            feed_grad,
            mixing_table,
            feed_table,
            leading_root_preconditioner,
            trailing_root_preconditioner,
            counts,
            3,
        )
        *results, sharps = finish(
            storage_position_map,
            grads,
            owned_grad,
            my_rows,
            table_total,
            channel_energy_average,
            channel_coefficients,
            jnp.stack([head_sharpness, sharpness_energy_average]),
            leading_covariance,
            trailing_covariance,
            projection_masters,
        )
        return (layer_output, incoming_tokens_grad, *results, *sharps)
    sharpness_share = mixing_table[14, 0:HEAD_NUMBER]
    table_grad = jnp.stack([(mixing_table, feed_table)[source][row] for source, row in TABLE_ROWS])
    block_grad = jnp.concatenate([mixing_grad, feed_grad[0]], axis=0).astype(F32)
    denominator_sum = lax.axis_size("fsdp")
    tiled_part = jnp.broadcast_to(
        sharpness_share[None, :], (denominator_sum, sharpness_share.shape[0])
    )
    portion_derivative, catalog_portion, sharpness_normalizer = (
        lax.psum_scatter(block_grad, "fsdp", scatter_dimension=1, tiled=True),
        lax.psum_scatter(table_grad, "fsdp", scatter_dimension=1, tiled=True),
        lax.psum_scatter(tiled_part, "fsdp", scatter_dimension=0, tiled=True),
    )
    portion_derivative, catalog_portion, sharpness_normalizer = lax.psum(
        (portion_derivative, catalog_portion, sharpness_normalizer), "dp"
    )
    sharpness_derivative = sharpness_normalizer[0]
    shard_place = lax.axis_index("fsdp")
    slot_index = jnp.arange(denominator_sum * slot_count, dtype=jnp.int32)
    slot_match = storage_position_map[None, :] == slot_index[:, None]
    slot_filled = jnp.any(slot_match, axis=1).astype(jnp.float32)[:, None, None]
    slot_block = jnp.sum(
        jnp.where(slot_match, jnp.arange(block_count, dtype=jnp.int32)[None, :], 0), axis=1
    )
    my_filled = lax.dynamic_slice_in_dim(slot_filled, shard_place * slot_count, slot_count, 0)
    my_block = lax.dynamic_slice_in_dim(slot_block, shard_place * slot_count, slot_count, 0)
    whole_grad = lax.all_gather(portion_derivative, "fsdp", axis=1, tiled=True)
    owned_grad = jnp.take(whole_grad, my_block, axis=0) * my_filled
    leading_covariance_renewed = covariance_forgetting * leading_covariance + (
        1.0 - covariance_forgetting
    ) * jnp.einsum("sij,skj->sik", owned_grad, owned_grad, precision=lax.Precision.HIGHEST)
    trailing_covariance_renewed = covariance_forgetting * trailing_covariance + (
        1.0 - covariance_forgetting
    ) * jnp.einsum("sji,sjk->sik", owned_grad, owned_grad, precision=lax.Precision.HIGHEST)
    halfway = jnp.einsum(
        "sij,sjk->sik", leading_root_preconditioner, owned_grad, precision=lax.Precision.HIGHEST
    )
    conditioned = jnp.einsum(
        "sij,sjk->sik", halfway, trailing_root_preconditioner, precision=lax.Precision.HIGHEST
    )
    every_update = lax.all_gather(conditioned, "fsdp", axis=0, tiled=True)
    my_rows = lax.dynamic_slice_in_dim(every_update, shard_place * shard_rows, shard_rows, 1)
    update = jnp.take(my_rows, storage_position_map, axis=0)
    projection_updated = projection_masters - weight_rate * update
    channel_energy_renewed = (
        covariance_forgetting * channel_energy_average
        + (1.0 - covariance_forgetting) * catalog_portion * catalog_portion
    )
    channel_params_updated = channel_coefficients - vector_rate * catalog_portion / (
        jnp.sqrt(channel_energy_renewed) + energy_epsilon
    )
    sharpness_energy_renewed = (
        covariance_forgetting * sharpness_energy_average
        + (1.0 - covariance_forgetting) * sharpness_derivative * sharpness_derivative
    )
    sharpness_updated = head_sharpness - sharpness_step_size * sharpness_derivative / (
        jnp.sqrt(sharpness_energy_renewed) + energy_epsilon
    )
    return (
        layer_output,
        incoming_tokens_grad,
        portion_derivative,
        leading_covariance_renewed,
        trailing_covariance_renewed,
        projection_updated,
        projection_updated.astype(jnp.bfloat16),
        catalog_portion,
        channel_energy_renewed,
        channel_params_updated,
        sharpness_derivative,
        sharpness_energy_renewed,
        sharpness_updated,
    )


def solution(mesh):
    in_specs = (
        P(("dp", "fsdp"), None),
        P(("dp", "fsdp")),
        P(None, "fsdp", None),
        P(None, "fsdp"),
        P(),
        P(("dp", "fsdp"), None),
        P("fsdp", None, None),
        P("fsdp", None, None),
        P("fsdp", None, None),
        P("fsdp", None, None),
        P(None, "fsdp"),
        P(),
        P(),
    )
    out_specs = (
        P(("dp", "fsdp"), None),
        P(("dp", "fsdp"), None),
        P(None, "fsdp", None),
        P("fsdp", None, None),
        P("fsdp", None, None),
        P(None, "fsdp", None),
        P(None, "fsdp", None),
        P(None, "fsdp"),
        P(None, "fsdp"),
        P(None, "fsdp"),
        P(),
        P(),
        P(),
    )
    return jax.shard_map(shards, mesh=mesh, in_specs=in_specs, out_specs=out_specs, check_vma=False)
```

```python
import functools

import jax
import jax.numpy as jnp
from jax import lax
from jax.experimental import pallas as pl
from jax.experimental.pallas import tpu as pltpu
from jax.sharding import PartitionSpec as P

HEAD_NUMBER = 8
HDIM = 48
HEAD_PAD = 64
LANES = 128
HEAD_PAIRS = HEAD_NUMBER // 2
PAD_WIDTH = HEAD_NUMBER * HEAD_PAD
HALF_WIDTH = PAD_WIDTH // 2
LEAD = 16
TAIL = 32
SMALL_SIDE = 6
SMALL_WINDOW = 48
LARGE_WINDOW = 208
CROP_GROUP = 2
ROW_TILE = 464
HIDDEN_PARTS = 6
VMEM_LIMIT = 60 * 2**20

norm_epsilon = 1e-06
batch_epsilon = 1e-05
attention_epsilon = 1e-06
covariance_forgetting = 0.5
weight_rate = 0.5
vector_rate = 0.1
sharpness_step_size = 2.0
energy_epsilon = 1e-08

F32 = jnp.float32
BF16 = jnp.bfloat16
VMEM_SPEC = pl.BlockSpec(memory_space=pltpu.VMEM)
ANY_SPEC = pl.BlockSpec(memory_space=pl.ANY)
SMEM_SPEC = pl.BlockSpec(memory_space=pltpu.SMEM)


def dot(left, right):
    return lax.dot_general(left, right, (((1,), (0,)), ((), ())), preferred_element_type=F32)


def dot_rows(left, right):
    return lax.dot_general(left, right, (((0,), (0,)), ((), ())), preferred_element_type=F32)


def dot_lanes(left, right):
    return lax.dot_general(left, right, (((1,), (1,)), ((), ())), preferred_element_type=F32)


def split(values):
    high = values.astype(BF16)
    return high, (values - high.astype(F32)).astype(BF16)


def dot_split(product, left, right):
    if product is dot_rows:
        return product(
            jnp.concatenate([left[0], left[0], left[1]], axis=0),
            jnp.concatenate([right[0], right[1], right[0]], axis=0),
        )
    rows = left[0].shape[0]
    both = product(jnp.concatenate(left, axis=0), right[0])
    return both[:rows] + both[rows:] + product(left[0], right[1])


def fold(values):
    total = values[0:8]
    for first in range(8, values.shape[0], 8):
        total = total + values[first : first + 8]
    return total


def gelu_parts(values):
    magnitude = jnp.abs(values) * 0.7071067811865476
    base = 1.0 + 0.3275911 * magnitude
    guess = pl.reciprocal(base, approx=True)
    slot = guess * (2.0 - base * guess)
    series = slot * (
        0.127414796
        + slot
        * (-0.142248368 + slot * (0.7107068705 + slot * (-0.7265760135 + slot * 0.5307027145)))
    )
    bell = jnp.exp(-0.5 * values * values)
    lower = series * bell
    return jnp.where(values >= 0, 1.0 - lower, lower), bell


def gelu_slope(values, share, bell):
    return share + values * bell * 0.3989422804014327


def head_map(dtype):
    feature = lax.broadcasted_iota(jnp.int32, (HEAD_NUMBER * HDIM, PAD_WIDTH), 0)
    lane = lax.broadcasted_iota(jnp.int32, (HEAD_NUMBER * HDIM, PAD_WIDTH), 1)
    inner = lane & (HEAD_PAD - 1)
    hit = (inner < HDIM) & ((lane >> 6) * HDIM + inner == feature)
    return hit.astype(F32).astype(dtype)


def centered(values):
    center = jnp.sum(values, axis=-1, keepdims=True) * (1.0 / values.shape[-1])
    shifted = values - center
    spread = jnp.sum(shifted * shifted, axis=-1, keepdims=True) * (1.0 / values.shape[-1])
    scale = lax.rsqrt(spread + norm_epsilon)
    return shifted * scale, scale


def norm_back(grad, unit, scale):
    size = 1.0 / grad.shape[-1]
    middle = jnp.sum(grad, axis=-1, keepdims=True) * size
    slope = jnp.sum(grad * unit, axis=-1, keepdims=True) * size
    return scale * (grad - middle - unit * slope)


def tile_rows(count, least):
    for parts in range(least, count // 16 + 1):
        if count % (16 * parts) == 0:
            return count // parts
    return count


def for_rows(count, tile, step, carry=0):
    def body(index, carry):
        return step(pl.multiple_of(index * tile, tile), tile, carry)

    if count // tile == 1:
        carry = step(0, tile, carry)
    else:
        carry = lax.fori_loop(0, count // tile, body, carry)
    if count % tile:
        carry = step(count - count % tile, count % tile, carry)
    return carry


def live_total(sides_ref):
    return lax.fori_loop(
        0, sides_ref.shape[0], lambda c, t: t + sides_ref[c] * sides_ref[c], jnp.int32(0)
    )


def row_mask(first, rows, width, limit):
    return lax.broadcasted_iota(jnp.int32, (rows, width), 0) + first < limit


def for_groups(sides_ref, step, carry):
    def crop_body(crop, state):
        start, carry = state
        side = sides_ref[crop]
        cells = side * side
        inverse = 1.0 / jnp.full((8, LANES), side, jnp.int32).astype(F32)
        lines = lax.broadcasted_iota(jnp.int32, (8, LANES), 0)

        def group_body(group, carry):
            for part in range(2):
                row = pl.multiple_of((group * 2 + part) * 8, 8)
                place = lines + (row - start)
                line = ((place.astype(F32) + 0.5) * inverse).astype(jnp.int32)
                column = place - line * side
                inside = (place >= 0) & (place < cells)
                masks = (
                    inside,
                    column >= 1,
                    column < side - 1,
                    place >= side,
                    place < cells - side,
                )
                carry = step(row, side, masks, carry)
            return carry

        carry = lax.fori_loop(start // 16, (start + cells + 15) // 16, group_body, carry)
        return start + cells, carry

    return lax.fori_loop(0, sides_ref.shape[0], crop_body, (jnp.int32(0), carry))[1]


def conv_forward(source, chunk, row, side, masks, taps):
    inside, left_ok, right_ok, up_ok, down_ok = masks
    total = None
    for shift in (-1, 0, 1):
        base = LEAD + row + shift * side
        middle = source[chunk, pl.ds(base, 8), :]
        left = jnp.where(left_ok, source[chunk, pl.ds(base - 1, 8), :], 0.0)
        right = jnp.where(right_ok, source[chunk, pl.ds(base + 1, 8), :], 0.0)
        first = 3 * (shift + 1)
        value = taps[first] * left + taps[first + 1] * middle + taps[first + 2] * right
        if shift == -1:
            value = jnp.where(up_ok, value, 0.0)
        if shift == 1:
            value = jnp.where(down_ok, value, 0.0)
        total = value if total is None else total + value
    return total


def conv_backward(source, chunk, row, side, masks, taps, own, tap_sums):
    inside, left_ok, right_ok, up_ok, down_ok = masks
    total = None
    tap_sums = list(tap_sums)
    for shift in (-1, 0, 1):
        base = LEAD + row + shift * side
        row_ok = {-1: up_ok, 0: None, 1: down_ok}[shift]
        for sway in (-1, 0, 1):
            column_ok = {-1: left_ok, 0: None, 1: right_ok}[sway]
            value = source[chunk, pl.ds(base + sway, 8), :]
            keep = inside
            if row_ok is not None:
                keep = keep & row_ok
            if column_ok is not None:
                keep = keep & column_ok
            value = jnp.where(keep, value, 0.0)
            index = 3 * (1 - shift) + (1 - sway)
            term = taps[index] * value
            total = term if total is None else total + term
            tap_sums[index] = tap_sums[index] + own * value
    return total, tuple(tap_sums)


def chunk_lanes(chunk):
    return slice(chunk * LANES, (chunk + 1) * LANES)


def tap_vectors(table_ref, first, chunk):
    return [
        jnp.broadcast_to(table_ref[first + k : first + k + 1, chunk_lanes(chunk)], (8, LANES))
        for k in range(9)
    ]


def for_crops(sides_ref, row_count, order_ref, start_ref, step):
    crops = sides_ref.shape[0]

    def scan(crop, state):
        start, large, small = state
        side = sides_ref[crop]
        start_ref[crop] = start
        is_small = side <= SMALL_SIDE
        order_ref[jnp.where(is_small, crops + small, large)] = crop
        return (
            start + side * side,
            large + jnp.where(is_small, 0, 1),
            small + jnp.where(is_small, 1, 0),
        )

    zero = jnp.int32(0)
    _, large, small = lax.fori_loop(0, crops, scan, (zero, zero, zero))
    for window, first, count in ((LARGE_WINDOW, 0, large), (SMALL_WINDOW, crops, small)):

        def group_body(group, _, window=window, first=first, count=count):
            members = []
            for member in range(CROP_GROUP):
                crop = order_ref[first + jnp.minimum(group * CROP_GROUP + member, count - 1)]
                start = start_ref[crop]
                side = sides_ref[crop]
                row = pl.multiple_of(jnp.minimum(start // 8, (row_count - window) // 8) * 8, 8)
                place = lax.broadcasted_iota(jnp.int32, (window, HALF_WIDTH), 0) + (row - start)
                members.append((crop, pl.ds(row, window), (place >= 0) & (place < side * side)))
            step(members)
            return 0

        lax.fori_loop(0, (count + CROP_GROUP - 1) // CROP_GROUP, group_body, 0)


def half_lanes(half):
    starts = [part * PAD_WIDTH + half * HALF_WIDTH for part in range(3)]
    return [slice(start, start + HALF_WIDTH) for start in starts]


def pair_lanes():
    return lax.broadcasted_iota(jnp.int32, (HDIM, LANES), 1) < HEAD_PAD


def pair_part(block, pair):
    first = pair * LANES
    lanes = slice(first, first + LANES)
    return jnp.where(
        pair_lanes(),
        block[first : first + HDIM, lanes],
        block[first + HEAD_PAD : first + HEAD_PAD + HDIM, lanes],
    )


def spread_pair(target, member, half, pair, values):
    first = pair * LANES
    lanes = slice(first, first + LANES)
    parts = split(values)
    for index in range(2):
        value = parts[index].astype(F32)
        target[member, half, index, first : first + HDIM, lanes] = jnp.where(
            pair_lanes(), value, 0.0
        ).astype(BF16)
        target[member, half, index, first + HEAD_PAD : first + HEAD_PAD + HDIM, lanes] = jnp.where(
            pair_lanes(), 0.0, value
        ).astype(BF16)


def pair_sharpness(sharp_ref, pair):
    lane = lax.broadcasted_iota(jnp.int32, (1, LANES), 1)
    return jnp.where(lane < HEAD_PAD, sharp_ref[2 * pair], sharp_ref[2 * pair + 1])


def units(values):
    scale = lax.rsqrt(jnp.sum(values * values, axis=0, keepdims=True) + attention_epsilon)
    return values * scale, scale


def mixing_forward_kernel(
    sides_ref,
    sharp_ref,
    input_ref,
    weight_ref,
    table_ref,
    x1_hbm,
    qkv_hbm,
    mixed_hbm,
    scores_hbm,
    attention_hbm,
    slope_hbm,
    e_hbm,
    sums_ref,
    x1_ref,
    qkv_ref,
    mixed_ref,
    scores_ref,
    attention_ref,
    slope_ref,
    e_ref,
    head_weights,
    out_weight,
    first_low,
    mixed,
    attention_out,
    conv_in,
    spread,
    order_ref,
    start_ref,
    sems,
):
    row_count, width = input_ref.shape
    chunks = width // LANES
    tile = tile_rows(row_count, 2)
    saves = [
        pltpu.make_async_copy(source, target, sems.at[index])
        for index, (source, target) in enumerate(
            (
                (qkv_ref, qkv_hbm),
                (scores_ref, scores_hbm),
                (attention_ref, attention_hbm),
                (mixed_ref, mixed_hbm),
                (x1_ref, x1_hbm),
                (slope_ref, slope_hbm),
                (e_ref, e_hbm),
            )
        )
    ]
    total_live = live_total(sides_ref)
    mapping = head_map(BF16)
    for part in range(3):
        head_weights[:, part * PAD_WIDTH : (part + 1) * PAD_WIDTH] = dot(
            weight_ref[part], mapping
        ).astype(BF16)
    spread[...] = jnp.zeros_like(spread)

    def first_norm(first, size, _):
        rows = pl.ds(first, size)
        unit, _ = centered(input_ref[rows, :].astype(F32))
        first_low[rows, :] = (unit * table_ref[0:1, :] + table_ref[1:2, :]).astype(BF16)
        mixed[rows, :] = jnp.zeros((size, PAD_WIDTH), F32)
        return 0

    for_rows(row_count, ROW_TILE, first_norm)

    @pl.loop(0, row_count // tile)
    def _(step):
        rows = pl.ds(pl.multiple_of(step * tile, 16), tile)
        for part in range(3):
            lanes = slice(part * PAD_WIDTH, (part + 1) * PAD_WIDTH)
            qkv_ref[rows, lanes] = dot(first_low[rows, :], head_weights[:, lanes])

    saves[0].start()

    def crop_step(members):
        units_of = [(member, half) for member in range(len(members)) for half in range(2)]
        blocks, results = [], []
        for member, half in units_of:
            crop, rows, keep = members[member]
            lanes = half_lanes(half)
            query = units(jnp.where(keep, qkv_ref[rows, lanes[0]], 0.0))[0]
            key = units(jnp.where(keep, qkv_ref[rows, lanes[1]], 0.0))[0]
            blocks.append(dot_split(dot_rows, split(key), split(query)))
        for (member, half), block in zip(units_of, blocks):
            crop = members[member][0]
            for pair in range(2):
                scores = pair_part(block, pair)
                scores_ref[crop, 2 * half + pair] = scores
                scores = scores * pair_sharpness(sharp_ref, 2 * half + pair)
                scores = jnp.exp(scores - jnp.max(scores, axis=0, keepdims=True))
                shares = scores / jnp.sum(scores, axis=0, keepdims=True)
                attention_ref[crop, 2 * half + pair] = shares
                spread_pair(spread, member, half, pair, shares)
        for member, half in units_of:
            rows = members[member][1]
            shares = (spread[member, half, 0], spread[member, half, 1])
            results.append(dot_split(dot, split(qkv_ref[rows, half_lanes(half)[2]]), shares))
        for (member, half), result in zip(units_of, results):
            _, rows, keep = members[member]
            lanes = half_lanes(half)[0]
            mixed[rows, lanes] = jnp.where(keep, result, mixed[rows, lanes])

    for_crops(sides_ref, row_count, order_ref, start_ref, crop_step)

    saves[1].start()
    saves[2].start()
    out_weight[...] = dot_rows(mapping, weight_ref[3]).astype(BF16)

    @pl.loop(0, row_count // tile)
    def _(step):
        rows = pl.ds(pl.multiple_of(step * tile, 16), tile)
        low = mixed[rows, :].astype(BF16)
        mixed_ref[rows, :] = low
        attention_out[rows, :] = dot(low, out_weight[...])

    saves[3].start()

    def second_norm(first, size, _):
        rows = pl.ds(first, size)
        value = input_ref[rows, :].astype(F32) + table_ref[2:3, :] * attention_out[rows, :]
        x1_ref[rows, :] = value
        unit, _ = centered(value)
        value = unit * table_ref[3:4, :] + table_ref[4:5, :]
        for chunk in range(chunks):
            conv_in[chunk, pl.ds(LEAD + first, size), :] = value[:, chunk_lanes(chunk)]
            slope_ref[chunk, rows, :] = jnp.zeros((size, LANES), F32)
            e_ref[chunk, rows, :] = jnp.zeros((size, LANES), F32)
        return 0

    for_rows(row_count, ROW_TILE, second_norm)
    saves[4].start()

    zero = jnp.zeros((8, LANES), F32)
    sums_ref[...] = zero
    taps = [tap_vectors(table_ref, 11, chunk) for chunk in range(chunks)]

    def conv_step(row, side, masks, carry):
        rows = pl.ds(row, 8)
        carry = list(carry)
        for chunk in range(chunks):
            value = conv_forward(conv_in, chunk, row, side, masks, taps[chunk])
            share, bell = gelu_parts(value)
            active = value * share
            slope = gelu_slope(value, share, bell)
            slope_ref[chunk, rows, :] = jnp.where(masks[0], slope, slope_ref[chunk, rows, :])
            e_ref[chunk, rows, :] = jnp.where(masks[0], active, e_ref[chunk, rows, :])
            active = jnp.where(masks[0], active, 0.0)
            carry[chunk] = carry[chunk] + active
            carry[chunks + chunk] = carry[chunks + chunk] + active * active
        return tuple(carry)

    sums = for_groups(sides_ref, conv_step, (zero,) * (2 * chunks))
    saves[5].start()
    saves[6].start()
    for index, value in enumerate(sums):
        sums_ref[index : index + 1, :] = jnp.sum(value, axis=0, keepdims=True)
    sums_ref[2 * chunks : 2 * chunks + 1, :] = jnp.full((1, LANES), total_live, jnp.int32).astype(F32)
    for save in saves:
        save.wait()


def mixing_forward(sides, sharpness, inputs, weights, table):
    row_count, width = inputs.shape
    crops = sides.shape[0]
    chunks = width // LANES
    shape = jax.ShapeDtypeStruct
    return pl.pallas_call(
        mixing_forward_kernel,
        out_shape=(
            shape((row_count, width), F32),
            shape((row_count, 3 * PAD_WIDTH), F32),
            shape((row_count, PAD_WIDTH), BF16),
            shape((crops, HEAD_PAIRS, HDIM, LANES), F32),
            shape((crops, HEAD_PAIRS, HDIM, LANES), F32),
            shape((chunks, row_count, LANES), F32),
            shape((chunks, row_count, LANES), F32),
            shape((8, LANES), F32),
        ),
        in_specs=[SMEM_SPEC, SMEM_SPEC, VMEM_SPEC, VMEM_SPEC, VMEM_SPEC],
        out_specs=(ANY_SPEC,) * 7 + (VMEM_SPEC,),
        scratch_shapes=[
            pltpu.VMEM((row_count, width), F32),
            pltpu.VMEM((row_count, 3 * PAD_WIDTH), F32),
            pltpu.VMEM((row_count, PAD_WIDTH), BF16),
            pltpu.VMEM((crops, HEAD_PAIRS, HDIM, LANES), F32),
            pltpu.VMEM((crops, HEAD_PAIRS, HDIM, LANES), F32),
            pltpu.VMEM((chunks, row_count, LANES), F32),
            pltpu.VMEM((chunks, row_count, LANES), F32),
            pltpu.VMEM((width, 3 * PAD_WIDTH), BF16),
            pltpu.VMEM((PAD_WIDTH, width), BF16),
            pltpu.VMEM((row_count, width), BF16),
            pltpu.VMEM((row_count, PAD_WIDTH), F32),
            pltpu.VMEM((row_count, width), F32),
            pltpu.VMEM((chunks, LEAD + row_count + TAIL, LANES), F32),
            pltpu.VMEM((CROP_GROUP, 2, 2, HALF_WIDTH, HALF_WIDTH), BF16),
            pltpu.SMEM((2 * crops,), jnp.int32),
            pltpu.SMEM((crops,), jnp.int32),
            pltpu.SemaphoreType.DMA((7,)),
        ],
        compiler_params=pltpu.CompilerParams(vmem_limit_bytes=VMEM_LIMIT),
        name="mixing_forward",
    )(sides, sharpness, inputs, weights, table)


def batch_vectors(bn_ref, chunk, chunks):
    count = bn_ref[2 * chunks : 2 * chunks + 1, :]
    mean = bn_ref[chunk : chunk + 1, :] / count
    scale = lax.rsqrt(bn_ref[chunks + chunk : chunks + chunk + 1, :] / count - mean * mean + batch_epsilon)
    return mean, scale


def feed_kernel(
    sides_ref,
    x1_hbm,
    e_hbm,
    bn_ref,
    weight_hbm,
    table_ref,
    adjoint_hbm,
    out_hbm,
    dx2_hbm,
    dn_hbm,
    weight_grad_hbm,
    grads_ref,
    back_sums_ref,
    e_ref,
    x1_ref,
    weight_ref,
    adjoint_ref,
    out_ref,
    dx2_ref,
    dn_ref,
    weight_grad_ref,
    up_weight,
    n_ref,
    z_ref,
    dw_ref,
    x2,
    unit,
    spread,
    third_low,
    hidden_low,
    feed,
    third_grad,
    feed_grad,
    pre_grad,
    grads,
    weight_sums,
    sems,
):
    loads = [
        pltpu.make_async_copy(source, target, sems.at[index])
        for index, (source, target) in enumerate(
            (
                (e_hbm, e_ref),
                (x1_hbm, x1_ref),
                (weight_hbm, weight_ref),
                (adjoint_hbm, adjoint_ref),
            )
        )
    ]
    saves = [
        pltpu.make_async_copy(source, target, sems.at[4 + index])
        for index, (source, target) in enumerate(
            (
                (out_ref, out_hbm),
                (dx2_ref, dx2_hbm),
                (weight_grad_ref, weight_grad_hbm),
                (dn_ref, dn_hbm),
            )
        )
    ]
    for load in loads:
        load.start()
    row_count, width = x1_ref.shape
    chunks = width // LANES
    expand = weight_ref.shape[0] // 2
    tile = tile_rows(row_count, 4)
    total_live = live_total(sides_ref)
    hidden = expand * width
    batch = [batch_vectors(bn_ref, chunk, chunks) for chunk in range(chunks)]
    zero = jnp.zeros((8, LANES), F32)

    def down_weight():
        return weight_ref[expand : 2 * expand].reshape(hidden, width)

    def normalize(first, size, _):
        rows = pl.ds(first, size)
        live = row_mask(first, size, LANES, total_live)
        for chunk in range(chunks):
            lanes = chunk_lanes(chunk)
            mean, scale = batch[chunk]
            value = (e_ref[chunk, rows, :] - mean) * scale
            value = value * table_ref[5:6, lanes] + table_ref[6:7, lanes]
            n_ref[chunk, pl.ds(LEAD + first, size), :] = jnp.where(live, value, 0.0)
            z_ref[chunk, rows, :] = jnp.zeros((size, LANES), F32)
            dn_ref[chunk, rows, :] = jnp.zeros((size, LANES), F32)
        return 0

    loads[0].wait()
    for_rows(row_count, ROW_TILE, normalize)

    taps = [tap_vectors(table_ref, 20, chunk) for chunk in range(chunks)]

    def conv_step(row, side, masks, carry):
        rows = pl.ds(row, 8)
        for chunk in range(chunks):
            value = conv_forward(n_ref, chunk, row, side, masks, taps[chunk])
            z_ref[chunk, rows, :] = jnp.where(masks[0], value, z_ref[chunk, rows, :])
        return carry

    for_groups(sides_ref, conv_step, 0)

    for load in loads[1:]:
        load.wait()
    for part in range(expand):
        up_weight[:, part * width : (part + 1) * width] = weight_ref[part]
    weight_sums[...] = jnp.zeros_like(weight_sums)
    grads[...] = jnp.zeros_like(grads)

    def z_rows(rows):
        return jnp.concatenate([z_ref[chunk, rows, :] for chunk in range(chunks)], axis=1)

    def before(base):
        rows = pl.ds(base, tile)
        value = x1_ref[rows, :] + table_ref[7:8, :] * z_rows(rows)
        x2[...] = value
        value, scale = centered(value)
        unit[...] = value
        spread[...] = jnp.broadcast_to(scale, (tile, LANES))
        third_low[...] = (value * table_ref[8:9, :] + table_ref[9:10, :]).astype(BF16)
        feed_grad[...] = (entry_rows(base) * table_ref[10:11, :]).astype(BF16)

    def entry_rows(base):
        live = row_mask(base, tile, width, total_live)
        return jnp.where(live, adjoint_ref[pl.ds(base, tile), :].astype(F32), 0.0)

    @pl.loop(0, row_count // tile)
    def _(step):
        base = pl.multiple_of(step * tile, 16)
        rows = pl.ds(base, tile)
        before(base)

        def hidden_lanes(part):
            return slice(part * hidden // HIDDEN_PARTS, (part + 1) * hidden // HIDDEN_PARTS)

        def products(part):
            lanes = hidden_lanes(part)
            return (
                dot(third_low[...], up_weight[:, lanes]),
                dot_lanes(feed_grad[...], down_weight()[lanes]),
            )

        ahead = products(0)
        for part in range(HIDDEN_PARTS):
            lanes = hidden_lanes(part)
            value, hidden_grad = ahead
            if part + 1 < HIDDEN_PARTS:
                ahead = products(part + 1)
            share, bell = gelu_parts(value)
            hidden_low[:, lanes] = (value * share).astype(BF16)
            pre_grad[:, lanes] = (hidden_grad * gelu_slope(value, share, bell)).astype(BF16)
        feed[...] = dot(hidden_low[...], down_weight())
        third_grad[...] = dot_lanes(pre_grad[...], up_weight[...])
        weight_sums[expand : 2 * expand] += dot_rows(hidden_low[...], feed_grad[...]).reshape(
            expand, width, width
        )
        up_grad = dot_rows(third_low[...], pre_grad[...])
        for part in range(expand):
            weight_sums[part] += up_grad[:, part * width : (part + 1) * width]

        value = x2[...] + table_ref[10:11, :] * feed[...]
        live = row_mask(base, tile, width, total_live)
        out_ref[rows, :] = jnp.where(live, value, 0.0).astype(BF16)
        entry = entry_rows(base)
        grads[0] += fold(entry * feed[...])
        grad = third_grad[...]
        value = unit[...]
        total = entry + norm_back(grad * table_ref[8:9, :], value, spread[:, 0:1])
        dx2_ref[rows, :] = total
        scaled = total * table_ref[7:8, :]
        for chunk in range(chunks):
            dw_ref[chunk, pl.ds(LEAD + base, tile), :] = scaled[:, chunk_lanes(chunk)]
        grads[1] += fold(total * z_rows(rows))
        grads[2] += fold(grad * value)
        grads[3] += fold(grad)

    saves[0].start()
    saves[1].start()

    owners, pieces, shard, _ = weight_grad_ref.shape
    inner = width // shard
    for owner in range(owners):
        rows = slice(owner % inner * shard, (owner % inner + 1) * shard)
        for piece in range(pieces):
            weight_grad_ref[owner, piece] = weight_sums[
                owner // inner * pieces + piece, rows, :
            ].astype(BF16)

    saves[2].start()

    back_sums_ref[...] = zero
    for index, source in enumerate((1, 2, 3, 0)):
        grads_ref[index : index + 1, :] = jnp.sum(grads[source], axis=0, keepdims=True)
    def back_step(row, side, masks, carry):
        rows = pl.ds(row, 8)
        result = []
        for chunk in range(chunks):
            mean, scale = batch[chunk]
            sums = carry[chunk]
            own = jnp.where(masks[0], n_ref[chunk, pl.ds(LEAD + row, 8), :], 0.0)
            total, tap_sums = conv_backward(
                dw_ref, chunk, row, side, masks, taps[chunk], own, sums[0:9]
            )
            dn_ref[chunk, rows, :] = jnp.where(masks[0], total, dn_ref[chunk, rows, :])
            total = jnp.where(masks[0], total, 0.0)
            standard = (e_ref[chunk, rows, :] - mean) * scale
            result.append((*tap_sums, sums[9] + total * standard, sums[10] + total))
        return tuple(result)

    sums = for_groups(sides_ref, back_step, ((zero,) * 11,) * chunks)
    saves[3].start()
    for chunk in range(chunks):
        lanes = chunk_lanes(chunk)
        for index, value in enumerate(sums[chunk]):
            value = jnp.sum(value, axis=0, keepdims=True)
            grads_ref[4 + index : 5 + index, lanes] = value
            if index == 9:
                back_sums_ref[chunks + chunk : chunks + chunk + 1, :] = value
            if index == 10:
                back_sums_ref[chunk : chunk + 1, :] = value
    for save in saves:
        save.wait()


def feed_forward(sides, x1, e, batch_sums, weights, table, adjoint, grad_shape):
    row_count, width = x1.shape
    chunks = width // LANES
    expand = weights.shape[0] // 2
    tile = tile_rows(row_count, 4)
    shape = jax.ShapeDtypeStruct
    return pl.pallas_call(
        feed_kernel,
        out_shape=(
            shape((row_count, width), BF16),
            shape((row_count, width), F32),
            shape((chunks, row_count, LANES), F32),
            shape(grad_shape, BF16),
            shape((16, width), F32),
            shape((8, LANES), F32),
        ),
        in_specs=[SMEM_SPEC, ANY_SPEC, ANY_SPEC, VMEM_SPEC, ANY_SPEC, VMEM_SPEC, ANY_SPEC],
        out_specs=(ANY_SPEC,) * 4 + (VMEM_SPEC,) * 2,
        scratch_shapes=[
            pltpu.VMEM((chunks, row_count, LANES), F32),
            pltpu.VMEM((row_count, width), F32),
            pltpu.VMEM(weights.shape, BF16),
            pltpu.VMEM((row_count, width), BF16),
            pltpu.VMEM((row_count, width), BF16),
            pltpu.VMEM((row_count, width), F32),
            pltpu.VMEM((chunks, row_count, LANES), F32),
            pltpu.VMEM(grad_shape, BF16),
            pltpu.VMEM((width, expand * width), BF16),
            pltpu.VMEM((chunks, LEAD + row_count + TAIL, LANES), F32),
            pltpu.VMEM((chunks, row_count, LANES), F32),
            pltpu.VMEM((chunks, LEAD + row_count + TAIL, LANES), F32),
            pltpu.VMEM((tile, width), F32),
            pltpu.VMEM((tile, width), F32),
            pltpu.VMEM((tile, LANES), F32),
            pltpu.VMEM((tile, width), BF16),
            pltpu.VMEM((tile, expand * width), BF16),
            pltpu.VMEM((tile, width), F32),
            pltpu.VMEM((tile, width), F32),
            pltpu.VMEM((tile, width), BF16),
            pltpu.VMEM((tile, expand * width), BF16),
            pltpu.VMEM((4, 8, width), F32),
            pltpu.VMEM((2 * expand, width, width), F32),
            pltpu.SemaphoreType.DMA((8,)),
        ],
        compiler_params=pltpu.CompilerParams(vmem_limit_bytes=VMEM_LIMIT),
        name="feed_forward",
    )(sides, x1, e, batch_sums, weights, table, adjoint)


def mixing_backward_kernel(
    sides_ref,
    sharp_ref,
    input_hbm,
    weight_ref,
    table_ref,
    x1_hbm,
    qkv_hbm,
    mixed_hbm,
    scores_hbm,
    attention_hbm,
    slope_hbm,
    e_hbm,
    bn_ref,
    dx2_hbm,
    dn_hbm,
    back_ref,
    head_low_hbm,
    dx1_hbm,
    head_weights_hbm,
    weight_grad_ref,
    grads_ref,
    x1_ref,
    qkv_ref,
    mixed_ref,
    scores_ref,
    attention_ref,
    dx2_ref,
    head_weights,
    out_weight,
    pool,
    conv_grad,
    mixed_grad,
    first_low,
    head_low,
    spread,
    out_sum,
    sharp_sums,
    order_ref,
    start_ref,
    load_sems,
):
    row_count, width = input_hbm.shape
    low_rows, input_ref = head_low.at[0, :, 0:width], head_low.at[1, :, 0:width]
    input_load = pltpu.make_async_copy(input_hbm, input_ref, load_sems.at[14])
    input_load.start()
    chunks = width // LANES
    slope_ref, e_ref = pool.at[0:chunks], pool.at[chunks : 2 * chunks]
    dn_ref, conv_in = pool.at[2 * chunks : 3 * chunks], pool.at[3 * chunks : 4 * chunks]
    attention_out = slope_ref
    loads = [
        pltpu.make_async_copy(source, target, load_sems.at[index])
        for index, (source, target) in enumerate(
            (
                (x1_hbm, x1_ref),
                (slope_hbm, slope_ref),
                (e_hbm, e_ref),
                (dn_hbm, dn_ref),
                (mixed_hbm, mixed_ref),
                (dx2_hbm, dx2_ref),
                (qkv_hbm, qkv_ref),
                (scores_hbm, scores_ref),
                (attention_hbm, attention_ref),
            )
        )
    ]
    saves = [
        pltpu.make_async_copy(source, target, load_sems.at[len(loads) + index])
        for index, (source, target) in enumerate(
            (
                (head_weights, head_weights_hbm),
                (dx2_ref, dx1_hbm),
                (head_low.at[0], head_low_hbm.at[0]),
                (head_low.at[1], head_low_hbm.at[1]),
                (head_low.at[2], head_low_hbm.at[2]),
            )
        )
    ]
    for load in loads:
        load.start()
    tile = tile_rows(row_count, 2)
    total_live = live_total(sides_ref)
    batch = [batch_vectors(bn_ref, chunk, chunks) for chunk in range(chunks)]
    zero = jnp.zeros((8, LANES), F32)
    wide = jnp.zeros((8, width), F32)
    mapping = head_map(BF16)
    for part in range(3):
        head_weights[:, part * PAD_WIDTH : (part + 1) * PAD_WIDTH] = dot(
            weight_ref[part], mapping
        ).astype(BF16)
    saves[0].start()
    out_weight[...] = dot_rows(mapping, weight_ref[3]).astype(BF16)
    spread[...] = jnp.zeros_like(spread)

    def first_norm(first, size, _):
        rows = pl.ds(first, size)
        unit, _ = centered(input_ref[rows, :].astype(F32))
        first_low[rows, :] = (unit * table_ref[0:1, :] + table_ref[1:2, :]).astype(BF16)
        return 0

    input_load.wait()
    for_rows(row_count, ROW_TILE, first_norm)

    for load in loads[0:4]:
        load.wait()

    def batch_back(first, size, _):
        rows = pl.ds(first, size)
        live = row_mask(first, size, LANES, total_live)
        unit, _ = centered(x1_ref[rows, :])
        value = unit * table_ref[3:4, :] + table_ref[4:5, :]
        for chunk in range(chunks):
            lanes = chunk_lanes(chunk)
            mean, scale = batch[chunk]
            count = bn_ref[2 * chunks : 2 * chunks + 1, :]
            standard = (e_ref[chunk, rows, :] - mean) * scale
            inner = (
                back_ref[chunk : chunk + 1, :]
                + standard * back_ref[chunks + chunk : chunks + chunk + 1, :]
            ) / count
            grad = scale * table_ref[5:6, lanes] * (dn_ref[chunk, rows, :] - inner)
            grad = grad * slope_ref[chunk, rows, :]
            conv_grad[chunk, pl.ds(LEAD + first, size), :] = jnp.where(live, grad, 0.0)
            conv_in[chunk, pl.ds(first, size), :] = value[:, lanes]
        return 0

    for_rows(row_count, ROW_TILE, batch_back)

    taps = [tap_vectors(table_ref, 11, chunk) for chunk in range(chunks)]

    def back_step(row, side, masks, carry):
        rows = pl.ds(row, 8)
        result = []
        for chunk in range(chunks):
            held = conv_in[chunk, rows, :]
            own = jnp.where(masks[0], held, 0.0)
            total, tap_sums = conv_backward(
                conv_grad, chunk, row, side, masks, taps[chunk], own, carry[chunk]
            )
            conv_in[chunk, rows, :] = jnp.where(masks[0], total, held)
            result.append(tap_sums)
        return tuple(result)

    tap_sums = for_groups(sides_ref, back_step, ((zero,) * 9,) * chunks)
    for chunk in range(chunks):
        for index, value in enumerate(tap_sums[chunk]):
            grads_ref[5 + index : 6 + index, chunk_lanes(chunk)] = jnp.sum(
                value, axis=0, keepdims=True
            )

    for load in loads[4:6]:
        load.wait()

    @pl.loop(0, row_count // tile)
    def _(step):
        rows = pl.ds(pl.multiple_of(step * tile, 16), tile)
        result = dot(mixed_ref[rows, :], out_weight[...])
        for chunk in range(chunks):
            attention_out[chunk, rows, :] = result[:, chunk_lanes(chunk)]

    def second_back(first, size, carry):
        rows = pl.ds(first, size)
        live = row_mask(first, size, width, total_live)
        grad = jnp.concatenate([conv_in[chunk, rows, :] for chunk in range(chunks)], axis=1)
        grad = jnp.where(live, grad, 0.0)
        unit, scale = centered(x1_ref[rows, :])
        total = dx2_ref[rows, :] + norm_back(grad * table_ref[3:4, :], unit, scale)
        dx2_ref[rows, :] = total
        low_rows[rows, :] = (total * table_ref[2:3, :]).astype(BF16)
        held = jnp.concatenate([attention_out[chunk, rows, :] for chunk in range(chunks)], axis=1)
        return (
            carry[0] + fold(total * held),
            carry[1] + fold(grad * unit),
            carry[2] + fold(grad),
        )

    sums = for_rows(row_count, ROW_TILE, second_back, (wide, wide, wide))
    saves[1].start()
    for index in range(3):
        grads_ref[2 + index : 3 + index, :] = jnp.sum(sums[index], axis=0, keepdims=True)

    out_sum[...] = jnp.zeros_like(out_sum)

    @pl.loop(0, row_count // tile)
    def _(step):
        rows = pl.ds(pl.multiple_of(step * tile, 16), tile)
        mixed_grad[rows, :] = dot_lanes(low_rows[rows, :], out_weight[...])
        out_sum[...] += dot_rows(mixed_ref[rows, :], low_rows[rows, :])

    pool[...] = jnp.zeros_like(pool)

    low = out_sum[...].astype(BF16)
    weight_grad_ref[3] = dot(mapping, low).astype(BF16)
    sharp_sums[...] = jnp.zeros_like(sharp_sums)

    for load in loads[6:]:
        load.wait()

    def crop_step(members):
        units_of = [(member, half) for member in range(len(members)) for half in range(2)]
        grads, blocks, sums, results = [], [], [], []
        for member, half in units_of:
            crop, rows, keep = members[member]
            lanes = half_lanes(half)
            value = split(jnp.where(keep, qkv_ref[rows, lanes[2]], 0.0))
            grad = split(jnp.where(keep, mixed_grad[rows, lanes[0]], 0.0))
            grads.append(grad)
            blocks.append(dot_split(dot_rows, value, grad))
        for (member, half), block in zip(units_of, blocks):
            crop = members[member][0]
            query_sums = []
            for pair in range(2):
                index = 2 * half + pair
                shares = attention_ref[crop, index]
                scores = scores_ref[crop, index]
                part = pair_part(block, pair)
                part = shares * (part - jnp.sum(part * shares, axis=0, keepdims=True))
                spread_pair(spread, member, half, pair, shares)
                total = jnp.sum(part * scores, axis=0, keepdims=True)
                sharp_sums[index, pl.ds(crop, 1), :] = total
                sharpness = pair_sharpness(sharp_ref, index)
                query_sums.append(total * sharpness)
                spread_pair(spread, member, 2 + half, pair, part * sharpness)
            sums.append(jnp.concatenate(query_sums, axis=1))
        for index, (member, half) in enumerate(units_of):
            crop, rows, keep = members[member]
            lanes = half_lanes(half)
            query, query_scale = units(jnp.where(keep, qkv_ref[rows, lanes[0]], 0.0))
            key, key_scale = units(jnp.where(keep, qkv_ref[rows, lanes[1]], 0.0))
            shares = (spread[member, half, 0], spread[member, half, 1])
            slopes = (spread[member, 2 + half, 0], spread[member, 2 + half, 1])
            value_grad = dot_split(dot_lanes, grads[index], shares)
            query_grad = dot_split(dot, split(key), slopes)
            query_grad = query_scale * (query_grad - query * sums[index])
            key_grad = dot_split(dot_lanes, split(query), slopes)
            key_grad = key_scale * (
                key_grad - key * jnp.sum(key_grad * key, axis=0, keepdims=True)
            )
            results.append((query_grad, key_grad, value_grad))
        for (member, half), grads in zip(units_of, results):
            _, rows, keep = members[member]
            for part, result in enumerate(grads):
                for side in range(HALF_WIDTH // LANES):
                    chunk = (part * PAD_WIDTH + half * HALF_WIDTH) // LANES + side
                    pool[chunk, rows, :] = jnp.where(
                        keep[:, 0:LANES], result[:, chunk_lanes(side)], pool[chunk, rows, :]
                    )

    for_crops(sides_ref, row_count, order_ref, start_ref, crop_step)

    grads_ref[0:2, :] = jnp.zeros((2, width), F32)
    grads_ref[14:16, :] = jnp.zeros((2, width), F32)
    lane = lax.broadcasted_iota(jnp.int32, (1, LANES), 1)
    total = jnp.zeros((1, LANES), F32)
    for head in range(HEAD_NUMBER):
        row = jnp.sum(sharp_sums[head // 2], axis=0, keepdims=True)
        row = jnp.where((lane >> 6) == head % 2, row, 0.0)
        total = jnp.where(lane == head, jnp.sum(row, axis=1, keepdims=True), total)
    grads_ref[14:15, 0:LANES] = total

    for part in range(3):
        out_sum[...] = jnp.zeros_like(out_sum)

        @pl.loop(0, row_count // tile)
        def _(step, part=part):
            rows = pl.ds(pl.multiple_of(step * tile, 16), tile)
            first = part * PAD_WIDTH // LANES
            for chunk in range(PAD_WIDTH // LANES):
                head_low[part, rows, chunk_lanes(chunk)] = pool[first + chunk, rows, :].astype(BF16)
            out_sum[...] += dot_rows(head_low[part, rows, :], first_low[rows, :])

        saves[2 + part].start()
        low = out_sum[...].astype(BF16)
        weight_grad_ref[part] = lax.dot_general(
            low, mapping, (((0,), (1,)), ((), ())), preferred_element_type=F32
        ).astype(BF16)
    for save in saves:
        save.wait()


def mixing_backward(sides, sharpness, inputs, weights, table, saved, batch_sums, dx2, dn, back_sums):
    row_count, width = inputs.shape
    chunks = width // LANES
    crops = sides.shape[0]
    shape = jax.ShapeDtypeStruct
    x1, qkv, mixed, scores, attention, slope, e = saved
    return pl.pallas_call(
        mixing_backward_kernel,
        out_shape=(
            shape((3, row_count, PAD_WIDTH), BF16),
            shape((row_count, width), F32),
            shape((width, 3 * PAD_WIDTH), BF16),
            shape((4, width, width), BF16),
            shape((16, width), F32),
        ),
        in_specs=[SMEM_SPEC, SMEM_SPEC]
        + [ANY_SPEC, VMEM_SPEC, VMEM_SPEC]
        + [ANY_SPEC] * 7
        + [VMEM_SPEC, ANY_SPEC, ANY_SPEC, VMEM_SPEC],
        out_specs=(ANY_SPEC,) * 3 + (VMEM_SPEC,) * 2,
        scratch_shapes=[
            pltpu.VMEM((row_count, width), F32),
            pltpu.VMEM((row_count, 3 * PAD_WIDTH), F32),
            pltpu.VMEM((row_count, PAD_WIDTH), BF16),
            pltpu.VMEM((crops, HEAD_PAIRS, HDIM, LANES), F32),
            pltpu.VMEM((crops, HEAD_PAIRS, HDIM, LANES), F32),
            pltpu.VMEM((row_count, width), F32),
            pltpu.VMEM((width, 3 * PAD_WIDTH), BF16),
            pltpu.VMEM((PAD_WIDTH, width), BF16),
            pltpu.VMEM((3 * PAD_WIDTH // LANES, row_count, LANES), F32),
            pltpu.VMEM((chunks, LEAD + row_count + TAIL, LANES), F32),
            pltpu.VMEM((row_count, PAD_WIDTH), F32),
            pltpu.VMEM((row_count, width), BF16),
            pltpu.VMEM((3, row_count, PAD_WIDTH), BF16),
            pltpu.VMEM((CROP_GROUP, 4, 2, HALF_WIDTH, HALF_WIDTH), BF16),
            pltpu.VMEM((PAD_WIDTH, width), F32),
            pltpu.VMEM((HEAD_PAIRS, crops, LANES), F32),
            pltpu.SMEM((2 * crops,), jnp.int32),
            pltpu.SMEM((crops,), jnp.int32),
            pltpu.SemaphoreType.DMA((15,)),
        ],
        compiler_params=pltpu.CompilerParams(vmem_limit_bytes=VMEM_LIMIT),
        name="mixing_backward",
    )(
        sides,
        sharpness,
        inputs,
        weights,
        table,
        x1,
        qkv,
        mixed,
        scores,
        attention,
        slope,
        e,
        batch_sums,
        dx2,
        dn,
        back_sums,
    )


MESH = pl.DeviceIdType.MESH


def greet(peers):
    barrier = pltpu.get_barrier_semaphore()
    for peer in peers:
        pl.semaphore_signal(barrier, inc=1, device_id=peer, device_id_type=MESH)
    pl.semaphore_wait(barrier, len(peers))


def push(source, target, send, receive, peer):
    copy = pltpu.make_async_remote_copy(
        src_ref=source,
        dst_ref=target,
        send_sem=send,
        recv_sem=receive,
        device_id=peer,
        device_id_type=MESH,
    )
    copy.start()
    return copy


def turned(place, step, count):
    return lax.rem(place + step, count)


def ring_peers(axis, count):
    place = lax.axis_index(axis)
    return [{axis: turned(place, step, count)} for step in range(1, count)]


def comm_params(identity):
    return pltpu.CompilerParams(
        collective_id=identity, has_side_effects=True, vmem_limit_bytes=VMEM_LIMIT
    )


def flip(value, bits):
    for bit in (1, 2, 4):
        if bits & bit:
            value = value + bit - 2 * bit * lax.rem(lax.div(value, bit), 2)
    return value


def flip_peers(axis, count):
    place = lax.axis_index(axis)
    return [{axis: flip(place, bits)} for bits in range(1, count)]


def sum_all_kernel(counts, part_ref, total_ref, parts, send, receive):
    n_dp, n_fsdp = counts
    dp, fsdp = lax.axis_index("dp"), lax.axis_index("fsdp")
    place = dp * n_fsdp + fsdp
    peers = [
        {"dp": flip(dp, outer), "fsdp": flip(fsdp, inner)}
        for inner in reversed(range(n_fsdp))
        for outer in reversed(range(n_dp))
        if inner or outer
    ]
    greet(peers)
    parts[place] = part_ref[...]
    copies = [
        push(part_ref, parts.at[place], send.at[k], receive.at[k], peer)
        for k, peer in enumerate(peers)
    ]
    for copy in copies:
        copy.wait()
    total = parts[0]
    for k in range(1, n_dp * n_fsdp):
        total = total + parts[k]
    total_ref[...] = total


def sum_all(part, counts, identity):
    size = counts[0] * counts[1]
    return pl.pallas_call(
        functools.partial(sum_all_kernel, counts),
        out_shape=jax.ShapeDtypeStruct(part.shape, F32),
        in_specs=[VMEM_SPEC],
        out_specs=VMEM_SPEC,
        scratch_shapes=[
            pltpu.VMEM((size, *part.shape), F32),
            pltpu.SemaphoreType.DMA((size - 1,)),
            pltpu.SemaphoreType.DMA((size - 1,)),
        ],
        compiler_params=comm_params(identity),
        name="sum_all",
    )(part)


def sum_pair_kernel(
    counts, part_ref, blocks_hbm, total_ref, sums_ref, parts, own, other, send, receive, sems
):
    n_dp, n_fsdp = counts
    dp, fsdp = lax.axis_index("dp"), lax.axis_index("fsdp")
    core = lax.rem(dp, 2)
    place = dp * n_fsdp + fsdp
    peers = [
        {"dp": flip(dp, outer), "fsdp": flip(fsdp, inner)}
        for inner in reversed(range(n_fsdp))
        for outer in reversed(range(n_dp))
        if inner or outer
    ]
    load = pltpu.make_async_copy(blocks_hbm.at[pl.ds(core * n_fsdp, n_fsdp)], own, sems.at[0])
    load.start()
    greet(peers)
    parts[place] = part_ref[...]
    copies = [
        push(part_ref, parts.at[place], send.at[k], receive.at[k], peer)
        for k, peer in enumerate(peers)
    ]
    blocks = push(
        blocks_hbm.at[pl.ds((1 - core) * n_fsdp, n_fsdp)],
        other,
        sems.at[1],
        sems.at[2],
        {"dp": flip(dp, 1)},
    )
    load.wait()
    blocks.wait_recv()
    for owner in range(n_fsdp):
        sums_ref[owner] = (own[owner].astype(F32) + other[owner].astype(F32)).astype(BF16)
    for copy in copies:
        copy.wait()
    total = parts[0]
    for k in range(1, n_dp * n_fsdp):
        total = total + parts[k]
    total_ref[...] = total
    blocks.wait_send()


def sum_pair(part, blocks, counts, identity):
    size = counts[0] * counts[1]
    half = (counts[1], *blocks.shape[1:])
    shape = jax.ShapeDtypeStruct
    return pl.pallas_call(
        functools.partial(sum_pair_kernel, counts),
        out_shape=(shape(part.shape, F32), shape(half, BF16)),
        in_specs=[VMEM_SPEC, ANY_SPEC],
        out_specs=(VMEM_SPEC, VMEM_SPEC),
        scratch_shapes=[
            pltpu.VMEM((size, *part.shape), F32),
            pltpu.VMEM(half, BF16),
            pltpu.VMEM(half, BF16),
            pltpu.SemaphoreType.DMA((size - 1,)),
            pltpu.SemaphoreType.DMA((size - 1,)),
            pltpu.SemaphoreType.DMA((3,)),
        ],
        compiler_params=comm_params(identity),
        name="sum_pair",
    )(part, blocks)


def gather_kernel(
    counts,
    masters_ref,
    table_ref,
    blocks_ref,
    full_table_ref,
    blocks,
    tables,
    stage,
    ring_send,
    ring_recv,
    table_send,
    table_recv,
    cross_send,
    cross_recv,
    pair_send,
    pair_recv,
):
    n_dp, n_fsdp = counts
    dp, fsdp = lax.axis_index("dp"), lax.axis_index("fsdp")
    shard, width = masters_ref.shape[1:]
    columns = table_ref.shape[1]
    across = lax.rem(dp + 2, 4)
    pair = dp + 1 - 2 * lax.rem(dp, 2)
    peers = flip_peers("fsdp", n_fsdp)
    greet(peers + [{"dp": across}, {"dp": pair}])

    def piece(block, owner):
        return blocks.at[block, pl.ds(pl.multiple_of(owner * shard, 16), shard), :]

    def origin(step):
        return flip(fsdp, step)

    stage[...] = jnp.zeros_like(stage)
    stage[0 : table_ref.shape[0], 0:columns] = table_ref[...]
    tables[fsdp] = stage[...].astype(BF16)
    blocks[dp, pl.ds(pl.multiple_of(fsdp * shard, 16), shard), :] = masters_ref[dp].astype(BF16)
    own = piece(dp, fsdp)
    ring = [
        push(own, own, ring_send.at[k], ring_recv.at[k], peer) for k, peer in enumerate(peers)
    ]
    table_copies = [
        push(tables.at[fsdp], tables.at[fsdp], table_send.at[k], table_recv.at[k], peer)
        for k, peer in enumerate(peers)
    ]
    crossing, pairing = [], []
    for step in range(n_fsdp):
        if step:
            ring[step - 1].wait_recv()
        part = piece(dp, origin(step))
        crossing.append(push(part, part, cross_send.at[step], cross_recv.at[step], {"dp": across}))
        pairing.append(
            push(part, part, pair_send.at[0, step], pair_recv.at[0, step], {"dp": pair})
        )
    for step in range(n_fsdp):
        crossing[step].wait_recv()
        part = piece(across, origin(step))
        pairing.append(
            push(part, part, pair_send.at[1, step], pair_recv.at[1, step], {"dp": pair})
        )
    for copy in table_copies:
        copy.wait_recv()
    total = None
    for owner in range(n_fsdp):
        lane = lax.broadcasted_iota(jnp.int32, (LANES, width), 0)
        target = lax.broadcasted_iota(jnp.int32, (LANES, width), 1)
        hit = (lane < columns) & (lane + owner * columns == target)
        term = dot(tables[owner], hit.astype(F32).astype(BF16))
        total = term if total is None else total + term
    full_table_ref[...] = total
    for copy in pairing:
        copy.wait_recv()
    blocks_ref[...] = blocks[...]
    for copy in ring + table_copies + crossing + pairing:
        copy.wait_send()


def gather_start(masters, coefficients, counts, identity):
    n_dp, n_fsdp = counts
    width = masters.shape[2]
    shape = jax.ShapeDtypeStruct
    dma = pltpu.SemaphoreType.DMA
    return pl.pallas_call(
        functools.partial(gather_kernel, counts),
        out_shape=(shape((4, width, width), BF16), shape((32, width), F32)),
        in_specs=[VMEM_SPEC, VMEM_SPEC],
        out_specs=(VMEM_SPEC, VMEM_SPEC),
        scratch_shapes=[
            pltpu.VMEM((4, width, width), BF16),
            pltpu.VMEM((n_fsdp, 32, LANES), BF16),
            pltpu.VMEM((32, LANES), F32),
            dma((n_fsdp - 1,)),
            dma((n_fsdp - 1,)),
            dma((n_fsdp - 1,)),
            dma((n_fsdp - 1,)),
            dma((n_fsdp,)),
            dma((n_fsdp,)),
            dma((2, n_fsdp)),
            dma((2, n_fsdp)),
        ],
        compiler_params=comm_params(identity),
        name="gather_start",
    )(masters, coefficients)


def owner_rows(owner, shard):
    return pl.ds(pl.multiple_of(owner * shard, 16), shard)


TABLE_ROWS = (
    [(0, row) for row in range(5)]
    + [(1, 13), (1, 14)]
    + [(1, row) for row in range(4)]
    + [(0, row) for row in range(5, 14)]
    + [(1, row) for row in range(4, 13)]
)


def settle_kernel(
    counts,
    place_ref,
    mix_ref,
    feed_ref,
    mix_table_ref,
    feed_table_ref,
    left_hbm,
    right_hbm,
    head_low_hbm,
    dx1_hbm,
    input_hbm,
    head_weights_hbm,
    coefficient_ref,
    grad_ref,
    slots_ref,
    rows_ref,
    table_ref,
    out_hbm,
    left,
    right,
    head_low,
    dx1,
    inputs,
    head_weights,
    out,
    first_sums,
    pair_buf,
    cross_out,
    cross_buf,
    ring_out,
    ring_buf,
    feed_in,
    feed_buf,
    dp_buf,
    slot_out,
    slots,
    steps,
    rows_buf,
    table_stage,
    table_out,
    table_buf,
    table_part,
    table_dp,
    feed_sum,
    load_sems,
    pair_send,
    pair_recv,
    cross_send,
    cross_recv,
    ring_send,
    ring_recv,
    feed_in_send,
    feed_in_recv,
    feed_send,
    feed_recv,
    dp_send,
    dp_recv,
    slot_send,
    slot_recv,
    twin_send,
    twin_recv,
    back_send,
    back_recv,
    last_send,
    last_recv,
    table_send,
    table_recv,
    table_dp_send,
    table_dp_recv,
):
    n_dp, n_fsdp = counts
    dp, fsdp = lax.axis_index("dp"), lax.axis_index("fsdp")
    width = mix_ref.shape[2]
    shard = width // n_fsdp
    core = lax.rem(dp, 2)
    across, pair, pair_across = flip(dp, 2), flip(dp, 1), flip(dp, 3)
    peers, dp_peers = flip_peers("fsdp", n_fsdp), flip_peers("dp", n_dp)
    to_pair, to_across = {"dp": pair}, {"dp": across}
    loads = [
        pltpu.make_async_copy(left_hbm.at[core], left, load_sems.at[0]),
        pltpu.make_async_copy(right_hbm.at[core], right, load_sems.at[1]),
    ]
    row_count = dx1.shape[0]
    tile = tile_rows(row_count, 4)
    tiles = row_count // tile
    weight_load = pltpu.make_async_copy(head_weights_hbm, head_weights, load_sems.at[2])
    weight_load.start()
    tile_loads, tile_saves = [], []
    for step in range(tiles):
        rows = pl.ds(step * tile, tile)
        sems = [load_sems.at[3 + 6 * step + index] for index in range(6)]
        tile_loads.append(
            [
                pltpu.make_async_copy(head_low_hbm.at[part, rows], head_low.at[part, rows], sems[part])
                for part in range(3)
            ]
            + [
                pltpu.make_async_copy(dx1_hbm.at[rows], dx1.at[rows], sems[3]),
                pltpu.make_async_copy(input_hbm.at[rows], inputs.at[rows], sems[4]),
            ]
        )
        tile_saves.append(pltpu.make_async_copy(out.at[rows], out_hbm.at[rows], sems[5]))
        for load in tile_loads[step]:
            load.start()
    for load in loads:
        load.start()
    first_sums[...] = jnp.zeros_like(first_sums)

    def first_back(step):
        rows = pl.ds(step * tile, tile)
        if step == 0:
            weight_load.wait()
        for load in tile_loads[step]:
            load.wait()
        grad = None
        for part in range(3):
            lanes = slice(part * PAD_WIDTH, (part + 1) * PAD_WIDTH)
            term = dot_lanes(head_low[part, rows, :], head_weights[:, lanes])
            grad = term if grad is None else grad + term
        unit, scale = centered(inputs[rows, :].astype(F32))
        total = dx1[rows, :] + norm_back(grad * coefficient_ref[0:1, :], unit, scale)
        out[rows, :] = total.astype(BF16)
        tile_saves[step].start()
        first_sums[0] += fold(grad * unit)
        first_sums[1] += fold(grad)

    greet(peers + dp_peers)

    parts = list(reversed(range(n_fsdp // 2)))
    deep = 2 * shard

    def part_rows(part):
        first = lax.div(flip(fsdp, 2 * part), 2)
        return pl.ds(pl.multiple_of(first * deep, 16), deep)

    def owner_rows(owner):
        return pl.ds(pl.multiple_of(owner * shard, 16), shard)

    pairing = {}
    for part in parts:
        rows = part_rows(part)
        for side, block in enumerate((pair_across, pair)):
            pairing[part, side] = push(
                mix_ref.at[block, rows],
                pair_buf.at[side, rows],
                pair_send.at[side, part],
                pair_recv.at[side, part],
                to_pair,
            )
    crossing = {}
    for part in parts:
        rows = part_rows(part)
        pairing[part, 0].wait_recv()
        cross_out[rows, :] = (
            mix_ref[across, rows, :].astype(F32) + pair_buf[0, rows, :].astype(F32)
        ).astype(BF16)
        crossing[part] = push(
            cross_out.at[rows],
            cross_buf.at[rows],
            cross_send.at[part],
            cross_recv.at[part],
            to_across,
        )
    ring = {}
    for part in parts:
        rows = part_rows(part)
        pairing[part, 1].wait_recv()
        crossing[part].wait_recv()
        ring_out[rows, :] = (
            mix_ref[dp, rows, :].astype(F32)
            + pair_buf[1, rows, :].astype(F32)
            + cross_buf[rows, :].astype(F32)
        ).astype(BF16)
        for bits in (2 * part + 1, 2 * part):
            if bits:
                ring[bits] = push(
                    ring_out.at[owner_rows(flip(fsdp, bits))],
                    ring_buf.at[bits],
                    ring_send.at[bits - 1],
                    ring_recv.at[bits - 1],
                    peers[bits - 1],
                )

    pieces = feed_sum.shape[0] // 2
    side = lax.div(dp, 2)
    for piece in range(2 * pieces):
        total = feed_ref[0, piece].astype(F32)
        for owner in range(1, n_fsdp):
            total = total + feed_ref[owner, piece].astype(F32)
        feed_sum[piece] = total.astype(BF16)
    feeding = push(
        feed_sum.at[pl.ds((1 - side) * pieces, pieces)],
        feed_in,
        feed_in_send.at[0],
        feed_in_recv.at[0],
        to_across,
    )
    for step in range(tiles - tiles // 2):
        first_back(step)
    feeding.wait_recv()
    total = feed_sum[pl.ds(side * pieces, pieces)].astype(F32) + feed_in[...].astype(F32)
    feed_buf[dp] = total.astype(BF16)
    feeds = [
        push(feed_buf.at[dp], feed_buf.at[dp], feed_send.at[k], feed_recv.at[k], peer)
        for k, peer in enumerate(dp_peers)
    ]

    total = ring_out[owner_rows(fsdp), :].astype(F32)
    for bits in range(1, n_fsdp):
        ring[bits].wait_recv()
        total = total + ring_buf[bits].astype(F32)
    dp_buf[dp] = total
    gathering = [
        push(dp_buf.at[dp], dp_buf.at[dp], dp_send.at[k], dp_recv.at[k], peer)
        for k, peer in enumerate(dp_peers)
    ]
    for step in range(tiles - tiles // 2, tiles - tiles // 4):
        first_back(step)
    for copy in feeds:
        copy.wait_recv()
    for place in range(n_dp):
        for piece in range(pieces):
            block = n_dp + (place % 2 * 2 + place // 2) * pieces + piece
            grad_ref[block] = feed_buf[place, piece].astype(F32)
    for copy in gathering:
        copy.wait_recv()
    for place in range(n_dp):
        grad_ref[place] = dp_buf[place]

    slotting = {}
    for bits in reversed(range(n_fsdp)):
        slot = 2 * flip(fsdp, bits) + core
        block, filled = jnp.int32(0), jnp.int32(0)
        for index in range(grad_ref.shape[0]):
            here = place_ref[index] == slot
            block = jnp.where(here, index, block)
            filled = jnp.where(here, 1, filled)
        value = (grad_ref[block] * filled.astype(F32)).astype(BF16)
        if bits:
            slot_out[bits - 1] = value
            slotting[bits] = push(
                slot_out.at[bits - 1],
                slots.at[core, owner_rows(fsdp), :],
                slot_send.at[bits - 1],
                slot_recv.at[bits - 1],
                peers[bits - 1],
            )
        else:
            slots[core, owner_rows(fsdp), :] = value
    for step in range(tiles - tiles // 4, tiles):
        first_back(step)
    table_stage[...] = jnp.zeros_like(table_stage)
    for row, (source, first) in enumerate(TABLE_ROWS):
        ref = mix_table_ref if source == 0 else feed_table_ref
        table_stage[row : row + 1, :] = ref[first : first + 1, :]
    for row in range(2):
        table_stage[row : row + 1, :] = jnp.sum(first_sums[row], axis=0, keepdims=True)
    terms, rest = [], table_stage[...]
    for _ in range(3):
        term = rest.astype(BF16)
        terms.append(term)
        rest = rest - term.astype(F32)
    terms = jnp.concatenate(terms, axis=0)
    columns = width // n_fsdp
    sharp_row = lax.broadcasted_iota(jnp.int32, (32, LANES), 0) == 31
    sharp_values = jnp.broadcast_to(mix_table_ref[14:15, 0:LANES], (32, LANES))
    for owner in range(n_fsdp):
        lane = lax.broadcasted_iota(jnp.int32, (width, LANES), 1)
        source = lax.broadcasted_iota(jnp.int32, (width, LANES), 0)
        hit = ((lane < columns) & (lane + owner * columns == source)).astype(F32).astype(BF16)
        value = dot(terms, hit)
        value = value[0:32] + value[32:64] + value[64:96]
        table_out[owner] = jnp.where(sharp_row, sharp_values, value)
    table_buf[fsdp] = table_out[fsdp]
    tabling = [
        push(
            table_out.at[flip(fsdp, k + 1)],
            table_buf.at[fsdp],
            table_send.at[k],
            table_recv.at[k],
            peer,
        )
        for k, peer in enumerate(peers)
    ]

    for load in loads:
        load.wait()
    left_parts, right_parts = split(left[...]), split(right[...])
    twins = []
    for bits in range(n_fsdp):
        if bits:
            slotting[bits].wait_recv()
        part = slots.at[core, owner_rows(flip(fsdp, bits)), :]
        twins.append(push(part, part, twin_send.at[bits], twin_recv.at[bits], to_pair))

    grad = slots[core]
    half = split(dot(left_parts[0], grad) + dot(left_parts[1], grad))
    steps[...] = dot_split(dot, half, right_parts).astype(BF16)
    back = {}
    for bits in reversed(range(1, n_fsdp)):
        back[bits] = push(
            steps.at[owner_rows(flip(fsdp, bits))],
            rows_buf.at[2 * fsdp + core],
            back_send.at[bits - 1],
            back_recv.at[bits - 1],
            peers[bits - 1],
        )
    rows_buf[2 * fsdp + core] = steps[owner_rows(fsdp), :]
    for copy in tabling:
        copy.wait_recv()
    total = table_buf[0]
    for owner in range(1, n_fsdp):
        total = total + table_buf[owner]
    table_part[...] = total
    table_dp[dp] = total
    table_dps = [
        push(table_part, table_dp.at[dp], table_dp_send.at[k], table_dp_recv.at[k], peer)
        for k, peer in enumerate(dp_peers)
    ]
    lasts = []
    for bits in range(n_fsdp):
        if bits:
            back[bits].wait_recv()
        part = rows_buf.at[2 * flip(fsdp, bits) + core]
        lasts.append(push(part, part, last_send.at[bits], last_recv.at[bits], to_pair))
    for copy in table_dps:
        copy.wait_recv()
    total = table_dp[0]
    for place in range(1, n_dp):
        total = total + table_dp[place]
    table_ref[...] = total
    for copy in twins:
        copy.wait_recv()
    slots_ref[...] = slots[...]
    for copy in lasts:
        copy.wait_recv()
    rows_ref[...] = rows_buf[...]
    copies = [*pairing.values(), *crossing.values(), *ring.values(), *slotting.values()]
    copies += [*back.values(), feeding, *feeds, *tabling, *table_dps, *gathering]
    for copy in copies + twins + lasts:
        copy.wait_send()
    for save in tile_saves:
        save.wait()


def settle(
    places, mix, feed, mix_table, feed_table, left, right, back, coefficients, counts, identity
):
    head_low, dx1, inputs, head_weights = back
    row_count = dx1.shape[0]
    tiles = row_count // tile_rows(row_count, 4)
    n_dp, n_fsdp = counts
    width = mix.shape[2]
    shard = width // n_fsdp
    blocks = n_dp + 2 * feed.shape[1]
    pieces = feed.shape[1] // 2
    inner, outer = n_fsdp - 1, n_dp - 1
    shape = jax.ShapeDtypeStruct
    dma = pltpu.SemaphoreType.DMA
    sizes = [(2, n_fsdp // 2), (n_fsdp // 2,), (inner,), (1,), (outer,), (outer,)]
    sizes += [(inner,), (n_fsdp,), (inner,), (n_fsdp,), (inner,), (outer,)]
    return pl.pallas_call(
        functools.partial(settle_kernel, counts),
        out_shape=(
            shape((blocks, shard, width), F32),
            shape((2, width, width), BF16),
            shape((2 * n_fsdp, shard, width), BF16),
            shape((32, LANES), F32),
            shape(inputs.shape, BF16),
        ),
        in_specs=[SMEM_SPEC] + [VMEM_SPEC] * 4 + [ANY_SPEC] * 6 + [VMEM_SPEC],
        out_specs=(VMEM_SPEC,) * 4 + (ANY_SPEC,),
        scratch_shapes=[
            pltpu.VMEM((width, width), F32),
            pltpu.VMEM((width, width), F32),
            pltpu.VMEM(head_low.shape, BF16),
            pltpu.VMEM(dx1.shape, F32),
            pltpu.VMEM(inputs.shape, BF16),
            pltpu.VMEM(head_weights.shape, BF16),
            pltpu.VMEM(inputs.shape, BF16),
            pltpu.VMEM((2, 8, width), F32),
            pltpu.VMEM((2, width, width), BF16),
            pltpu.VMEM((width, width), BF16),
            pltpu.VMEM((width, width), BF16),
            pltpu.VMEM((width, width), BF16),
            pltpu.VMEM((n_fsdp, shard, width), BF16),
            pltpu.VMEM((pieces, shard, width), BF16),
            pltpu.VMEM((n_dp, pieces, shard, width), BF16),
            pltpu.VMEM((n_dp, shard, width), F32),
            pltpu.VMEM((inner, shard, width), BF16),
            pltpu.VMEM((2, width, width), BF16),
            pltpu.VMEM((width, width), BF16),
            pltpu.VMEM((2 * n_fsdp, shard, width), BF16),
            pltpu.VMEM((32, width), F32),
            pltpu.VMEM((n_fsdp, 32, LANES), F32),
            pltpu.VMEM((n_fsdp, 32, LANES), F32),
            pltpu.VMEM((32, LANES), F32),
            pltpu.VMEM((n_dp, 32, LANES), F32),
            pltpu.VMEM(feed.shape[1:], BF16),
            dma((3 + 6 * tiles,)),
        ]
        + [dma(size) for size in sizes for _ in range(2)],
        compiler_params=comm_params(identity),
        name="settle",
    )(places, mix, feed, mix_table, feed_table, left, right, *back, coefficients)


def finish_kernel(
    place_ref,
    grad_ref,
    slots_ref,
    rows_ref,
    table_ref,
    energy_ref,
    coefficient_ref,
    sharp_ref,
    left_hbm,
    right_hbm,
    masters_hbm,
    tokens_hbm,
    grad_hbm,
    left_out_hbm,
    right_out_hbm,
    masters_out_hbm,
    low_hbm,
    tokens_out_hbm,
    table_grad_ref,
    energy_out_ref,
    coefficient_out_ref,
    sharp_out_ref,
    left,
    right,
    masters,
    low,
    tokens,
    sems,
):
    slot_count = slots_ref.shape[0]
    load_left = pltpu.make_async_copy(left_hbm, left, sems.at[0])
    load_right = pltpu.make_async_copy(right_hbm, right, sems.at[1])
    load_masters = pltpu.make_async_copy(masters_hbm, masters, sems.at[2])
    saves = [
        pltpu.make_async_copy(source, target, sems.at[3 + index])
        for index, (source, target) in enumerate(
            (
                (grad_ref, grad_hbm),
                (left, left_out_hbm),
                (right, right_out_hbm),
                (masters, masters_out_hbm),
                (low, low_hbm),
                (tokens, tokens_out_hbm),
            )
        )
    ]
    load_left.start()
    load_right.start()
    load_masters.start()
    load_tokens = pltpu.make_async_copy(tokens_hbm, tokens, sems.at[9])
    load_tokens.start()
    saves[0].start()
    load_left.wait()
    for slot in range(slot_count):
        grad = slots_ref[slot]
        left[slot] = (
            covariance_forgetting * left[slot]
            + (1.0 - covariance_forgetting) * dot_lanes(grad, grad)
        )
    saves[1].start()
    load_right.wait()
    for slot in range(slot_count):
        grad = slots_ref[slot]
        right[slot] = (
            covariance_forgetting * right[slot]
            + (1.0 - covariance_forgetting) * dot_rows(grad, grad)
        )
    saves[2].start()
    load_tokens.wait()
    saves[5].start()
    load_masters.wait()
    for block in range(masters.shape[0]):
        value = masters[block] - weight_rate * rows_ref[place_ref[block]].astype(F32)
        masters[block] = value
        low[block] = value.astype(BF16)
    saves[3].start()
    saves[4].start()
    count, columns = energy_ref.shape
    grad = table_ref[0:count, 0:columns]
    table_grad_ref[...] = grad
    energy = covariance_forgetting * energy_ref[...] + (1.0 - covariance_forgetting) * grad * grad
    energy_out_ref[...] = energy
    coefficient_out_ref[...] = coefficient_ref[...] - vector_rate * grad / (
        jnp.sqrt(energy) + energy_epsilon
    )
    grad = table_ref[31:32, 0:HEAD_NUMBER]
    energy = (
        covariance_forgetting * sharp_ref[1:2, :] + (1.0 - covariance_forgetting) * grad * grad
    )
    sharp_out_ref[0:1, :] = grad
    sharp_out_ref[1:2, :] = energy
    sharp_out_ref[2:3, :] = sharp_ref[0:1, :] - sharpness_step_size * grad / (
        jnp.sqrt(energy) + energy_epsilon
    )
    for save in saves:
        save.wait()


def finish(
    places, grads, slots, rows, table, energy, coefficients, sharps, left, right, masters, tokens
):
    shape = jax.ShapeDtypeStruct
    return pl.pallas_call(
        finish_kernel,
        out_shape=(
            shape(grads.shape, F32),
            shape(left.shape, F32),
            shape(right.shape, F32),
            shape(masters.shape, F32),
            shape(masters.shape, BF16),
            shape(tokens.shape, BF16),
            shape(energy.shape, F32),
            shape(energy.shape, F32),
            shape(energy.shape, F32),
            shape((3, sharps.shape[1]), F32),
        ),
        in_specs=[SMEM_SPEC] + [VMEM_SPEC] * 7 + [ANY_SPEC] * 4,
        out_specs=(ANY_SPEC,) * 6 + (VMEM_SPEC,) * 4,
        scratch_shapes=[
            pltpu.VMEM(left.shape, F32),
            pltpu.VMEM(right.shape, F32),
            pltpu.VMEM(masters.shape, F32),
            pltpu.VMEM(masters.shape, BF16),
            pltpu.VMEM(tokens.shape, BF16),
            pltpu.SemaphoreType.DMA((10,)),
        ],
        compiler_params=pltpu.CompilerParams(vmem_limit_bytes=VMEM_LIMIT),
        name="finish",
    )(places, grads, slots, rows, table, energy, coefficients, sharps, left, right, masters, tokens)


def shards(
    patch_embeddings,
    view_side_tokens,
    projection_masters,
    channel_coefficients,
    head_sharpness,
    output_adjoint,
    leading_covariance,
    trailing_covariance,
    leading_root_preconditioner,
    trailing_root_preconditioner,
    channel_energy_average,
    sharpness_energy_average,
    storage_position_map,
):
    row_count, feature_count = patch_embeddings.shape
    block_count = projection_masters.shape[0]
    shard_rows = projection_masters.shape[1]
    slot_count = leading_covariance.shape[0]
    counts = (lax.axis_size("dp"), lax.axis_size("fsdp"))
    direct = counts[0] == 4 and slot_count == 2 and shard_rows % 16 == 0
    if direct:
        mixing_blocks, table = gather_start(projection_masters, channel_coefficients, counts, 0)
        grad_shape = (2 * counts[1], (block_count - 4) // 2, shard_rows, feature_count)
    else:
        full_table = lax.all_gather(channel_coefficients.astype(BF16), "fsdp", axis=1, tiled=True)
        table = full_table.astype(F32)
        mixing_blocks = lax.all_gather(
            projection_masters[:4].astype(BF16), "fsdp", axis=1, tiled=True
        )
        grad_shape = (1, block_count - 4, feature_count, feature_count)
    feed_blocks = lax.all_gather(projection_masters[4:].astype(BF16), "fsdp", axis=1, tiled=True)

    x1, qkv, mixed, scores, attention, slope, e, sums = mixing_forward(
        view_side_tokens, head_sharpness, patch_embeddings, mixing_blocks, table
    )
    batch_sums = sum_all(sums, counts, 1) if direct else lax.psum(sums, ("dp", "fsdp"))
    layer_output, dx2, dn, feed_grad, feed_table, back_part = feed_forward(
        view_side_tokens, x1, e, batch_sums, feed_blocks, table, output_adjoint, grad_shape
    )
    if direct:
        back_sums, feed_grad = sum_pair(back_part, feed_grad, counts, 2)
        feed_grad = lax.all_to_all(feed_grad, "fsdp", 0, 0, tiled=True)
    else:
        back_sums = lax.psum(back_part, ("dp", "fsdp"))
    head_low, dx1, head_weights, mixing_grad, mixing_table = mixing_backward(
        view_side_tokens,
        head_sharpness,
        patch_embeddings,
        mixing_blocks,
        table,
        (x1, qkv, mixed, scores, attention, slope, e),
        batch_sums,
        dx2,
        dn,
        back_sums,
    )
    if direct:
        grads, owned_grad, my_rows, table_total, tokens_grad = settle(
            storage_position_map,
            mixing_grad,
            feed_grad,
            mixing_table,
            feed_table,
            leading_root_preconditioner,
            trailing_root_preconditioner,
            (head_low, dx1, patch_embeddings, head_weights),
            table,
            counts,
            3,
        )
        *results, sharps = finish(
            storage_position_map,
            grads,
            owned_grad,
            my_rows,
            table_total,
            channel_energy_average,
            channel_coefficients,
            jnp.stack([head_sharpness, sharpness_energy_average]),
            leading_covariance,
            trailing_covariance,
            projection_masters,
            tokens_grad,
        )
        tokens_grad = results.pop(5)
        return (layer_output, tokens_grad, *results, *sharps)
    first_grad = jnp.einsum(
        "stl,dsl->td",
        head_low,
        head_weights.reshape(feature_count, 3, PAD_WIDTH),
        preferred_element_type=F32,
    )
    unit, scale = centered(patch_embeddings.astype(F32))
    incoming_tokens_grad = (dx1 + norm_back(first_grad * table[0], unit, scale)).astype(BF16)
    mixing_table = mixing_table.at[0].set(jnp.sum(first_grad * unit, axis=0))
    mixing_table = mixing_table.at[1].set(jnp.sum(first_grad, axis=0))
    sharpness_share = mixing_table[14, 0:HEAD_NUMBER]
    table_grad = jnp.stack([(mixing_table, feed_table)[source][row] for source, row in TABLE_ROWS])
    block_grad = jnp.concatenate([mixing_grad, feed_grad[0]], axis=0).astype(F32)
    denominator_sum = lax.axis_size("fsdp")
    tiled_part = jnp.broadcast_to(
        sharpness_share[None, :], (denominator_sum, sharpness_share.shape[0])
    )
    portion_derivative, catalog_portion, sharpness_normalizer = (
        lax.psum_scatter(block_grad, "fsdp", scatter_dimension=1, tiled=True),
        lax.psum_scatter(table_grad, "fsdp", scatter_dimension=1, tiled=True),
        lax.psum_scatter(tiled_part, "fsdp", scatter_dimension=0, tiled=True),
    )
    portion_derivative, catalog_portion, sharpness_normalizer = lax.psum(
        (portion_derivative, catalog_portion, sharpness_normalizer), "dp"
    )
    sharpness_derivative = sharpness_normalizer[0]
    shard_place = lax.axis_index("fsdp")
    slot_index = jnp.arange(denominator_sum * slot_count, dtype=jnp.int32)
    slot_match = storage_position_map[None, :] == slot_index[:, None]
    slot_filled = jnp.any(slot_match, axis=1).astype(jnp.float32)[:, None, None]
    slot_block = jnp.sum(
        jnp.where(slot_match, jnp.arange(block_count, dtype=jnp.int32)[None, :], 0), axis=1
    )
    my_filled = lax.dynamic_slice_in_dim(slot_filled, shard_place * slot_count, slot_count, 0)
    my_block = lax.dynamic_slice_in_dim(slot_block, shard_place * slot_count, slot_count, 0)
    whole_grad = lax.all_gather(portion_derivative, "fsdp", axis=1, tiled=True)
    owned_grad = jnp.take(whole_grad, my_block, axis=0) * my_filled
    leading_covariance_renewed = covariance_forgetting * leading_covariance + (
        1.0 - covariance_forgetting
    ) * jnp.einsum("sij,skj->sik", owned_grad, owned_grad, precision=lax.Precision.HIGHEST)
    trailing_covariance_renewed = covariance_forgetting * trailing_covariance + (
        1.0 - covariance_forgetting
    ) * jnp.einsum("sji,sjk->sik", owned_grad, owned_grad, precision=lax.Precision.HIGHEST)
    halfway = jnp.einsum(
        "sij,sjk->sik", leading_root_preconditioner, owned_grad, precision=lax.Precision.HIGHEST
    )
    conditioned = jnp.einsum(
        "sij,sjk->sik", halfway, trailing_root_preconditioner, precision=lax.Precision.HIGHEST
    )
    every_update = lax.all_gather(conditioned, "fsdp", axis=0, tiled=True)
    my_rows = lax.dynamic_slice_in_dim(every_update, shard_place * shard_rows, shard_rows, 1)
    update = jnp.take(my_rows, storage_position_map, axis=0)
    projection_updated = projection_masters - weight_rate * update
    channel_energy_renewed = (
        covariance_forgetting * channel_energy_average
        + (1.0 - covariance_forgetting) * catalog_portion * catalog_portion
    )
    channel_params_updated = channel_coefficients - vector_rate * catalog_portion / (
        jnp.sqrt(channel_energy_renewed) + energy_epsilon
    )
    sharpness_energy_renewed = (
        covariance_forgetting * sharpness_energy_average
        + (1.0 - covariance_forgetting) * sharpness_derivative * sharpness_derivative
    )
    sharpness_updated = head_sharpness - sharpness_step_size * sharpness_derivative / (
        jnp.sqrt(sharpness_energy_renewed) + energy_epsilon
    )
    return (
        layer_output,
        incoming_tokens_grad,
        portion_derivative,
        leading_covariance_renewed,
        trailing_covariance_renewed,
        projection_updated,
        projection_updated.astype(jnp.bfloat16),
        catalog_portion,
        channel_energy_renewed,
        channel_params_updated,
        sharpness_derivative,
        sharpness_energy_renewed,
        sharpness_updated,
    )


def solution(mesh):
    in_specs = (
        P(("dp", "fsdp"), None),
        P(("dp", "fsdp")),
        P(None, "fsdp", None),
        P(None, "fsdp"),
        P(),
        P(("dp", "fsdp"), None),
        P("fsdp", None, None),
        P("fsdp", None, None),
        P("fsdp", None, None),
        P("fsdp", None, None),
        P(None, "fsdp"),
        P(),
        P(),
    )
    out_specs = (
        P(("dp", "fsdp"), None),
        P(("dp", "fsdp"), None),
        P(None, "fsdp", None),
        P("fsdp", None, None),
        P("fsdp", None, None),
        P(None, "fsdp", None),
        P(None, "fsdp", None),
        P(None, "fsdp"),
        P(None, "fsdp"),
        P(None, "fsdp"),
        P(),
        P(),
        P(),
    )
    return jax.shard_map(shards, mesh=mesh, in_specs=in_specs, out_specs=out_specs, check_vma=False)
```

```python
import functools

import jax
import jax.numpy as jnp
from jax import lax
from jax.experimental import pallas as pl
from jax.experimental.pallas import tpu as pltpu
from jax.sharding import PartitionSpec as P

HEAD_NUMBER = 8
HDIM = 48
HEAD_PAD = 64
LANES = 128
HEAD_PAIRS = HEAD_NUMBER // 2
PAD_WIDTH = HEAD_NUMBER * HEAD_PAD
HALF_WIDTH = PAD_WIDTH // 2
LEAD = 16
TAIL = 32
SMALL_SIDE = 6
SMALL_WINDOW = 48
LARGE_WINDOW = 208
CROP_GROUP = 2
ROW_TILE = 464
HIDDEN_PARTS = 6
VMEM_LIMIT = 60 * 2**20

norm_epsilon = 1e-06
batch_epsilon = 1e-05
attention_epsilon = 1e-06
covariance_forgetting = 0.5
weight_rate = 0.5
vector_rate = 0.1
sharpness_step_size = 2.0
energy_epsilon = 1e-08

F32 = jnp.float32
BF16 = jnp.bfloat16
VMEM_SPEC = pl.BlockSpec(memory_space=pltpu.VMEM)
ANY_SPEC = pl.BlockSpec(memory_space=pl.ANY)
SMEM_SPEC = pl.BlockSpec(memory_space=pltpu.SMEM)


def dot(left, right):
    return lax.dot_general(left, right, (((1,), (0,)), ((), ())), preferred_element_type=F32)


def dot_rows(left, right):
    return lax.dot_general(left, right, (((0,), (0,)), ((), ())), preferred_element_type=F32)


def dot_lanes(left, right):
    return lax.dot_general(left, right, (((1,), (1,)), ((), ())), preferred_element_type=F32)


def split(values):
    high = values.astype(BF16)
    return high, (values - high.astype(F32)).astype(BF16)


def dot_split(product, left, right):
    if product is dot_rows:
        return product(
            jnp.concatenate([left[0], left[0], left[1]], axis=0),
            jnp.concatenate([right[0], right[1], right[0]], axis=0),
        )
    rows = left[0].shape[0]
    both = product(jnp.concatenate(left, axis=0), right[0])
    return both[:rows] + both[rows:] + product(left[0], right[1])


def fold(values):
    total = values[0:8]
    for first in range(8, values.shape[0], 8):
        total = total + values[first : first + 8]
    return total


def gelu_parts(values):
    magnitude = jnp.abs(values) * 0.7071067811865476
    base = 1.0 + 0.3275911 * magnitude
    guess = pl.reciprocal(base, approx=True)
    slot = guess * (2.0 - base * guess)
    series = slot * (
        0.127414796
        + slot
        * (-0.142248368 + slot * (0.7107068705 + slot * (-0.7265760135 + slot * 0.5307027145)))
    )
    bell = jnp.exp(-0.5 * values * values)
    lower = series * bell
    return jnp.where(values >= 0, 1.0 - lower, lower), bell


def gelu_slope(values, share, bell):
    return share + values * bell * 0.3989422804014327


def head_map(dtype):
    feature = lax.broadcasted_iota(jnp.int32, (HEAD_NUMBER * HDIM, PAD_WIDTH), 0)
    lane = lax.broadcasted_iota(jnp.int32, (HEAD_NUMBER * HDIM, PAD_WIDTH), 1)
    inner = lane & (HEAD_PAD - 1)
    hit = (inner < HDIM) & ((lane >> 6) * HDIM + inner == feature)
    return hit.astype(F32).astype(dtype)


def centered(values):
    center = jnp.sum(values, axis=-1, keepdims=True) * (1.0 / values.shape[-1])
    shifted = values - center
    spread = jnp.sum(shifted * shifted, axis=-1, keepdims=True) * (1.0 / values.shape[-1])
    scale = lax.rsqrt(spread + norm_epsilon)
    return shifted * scale, scale


def norm_back(grad, unit, scale):
    size = 1.0 / grad.shape[-1]
    middle = jnp.sum(grad, axis=-1, keepdims=True) * size
    slope = jnp.sum(grad * unit, axis=-1, keepdims=True) * size
    return scale * (grad - middle - unit * slope)


def tile_rows(count, least):
    for parts in range(least, count // 16 + 1):
        if count % (16 * parts) == 0:
            return count // parts
    return count


def for_rows(count, tile, step, carry=0):
    def body(index, carry):
        return step(pl.multiple_of(index * tile, tile), tile, carry)

    if count // tile == 1:
        carry = step(0, tile, carry)
    else:
        carry = lax.fori_loop(0, count // tile, body, carry)
    if count % tile:
        carry = step(count - count % tile, count % tile, carry)
    return carry


def live_total(sides_ref):
    return lax.fori_loop(
        0, sides_ref.shape[0], lambda c, t: t + sides_ref[c] * sides_ref[c], jnp.int32(0)
    )


def row_mask(first, rows, width, limit):
    return lax.broadcasted_iota(jnp.int32, (rows, width), 0) + first < limit


def for_groups(sides_ref, step, carry):
    def crop_body(crop, state):
        start, carry = state
        side = sides_ref[crop]
        cells = side * side
        inverse = 1.0 / jnp.full((8, LANES), side, jnp.int32).astype(F32)
        lines = lax.broadcasted_iota(jnp.int32, (8, LANES), 0)

        def group_body(group, carry):
            for part in range(2):
                row = pl.multiple_of((group * 2 + part) * 8, 8)
                place = lines + (row - start)
                line = ((place.astype(F32) + 0.5) * inverse).astype(jnp.int32)
                column = place - line * side
                inside = (place >= 0) & (place < cells)
                masks = (
                    inside,
                    column >= 1,
                    column < side - 1,
                    place >= side,
                    place < cells - side,
                )
                carry = step(row, side, masks, carry)
            return carry

        carry = lax.fori_loop(start // 16, (start + cells + 15) // 16, group_body, carry)
        return start + cells, carry

    return lax.fori_loop(0, sides_ref.shape[0], crop_body, (jnp.int32(0), carry))[1]


def conv_forward(source, chunk, row, side, masks, taps):
    inside, left_ok, right_ok, up_ok, down_ok = masks
    total = None
    for shift in (-1, 0, 1):
        base = LEAD + row + shift * side
        middle = source[chunk, pl.ds(base, 8), :]
        left = jnp.where(left_ok, source[chunk, pl.ds(base - 1, 8), :], 0.0)
        right = jnp.where(right_ok, source[chunk, pl.ds(base + 1, 8), :], 0.0)
        first = 3 * (shift + 1)
        value = taps[first] * left + taps[first + 1] * middle + taps[first + 2] * right
        if shift == -1:
            value = jnp.where(up_ok, value, 0.0)
        if shift == 1:
            value = jnp.where(down_ok, value, 0.0)
        total = value if total is None else total + value
    return total


def conv_backward(source, chunk, row, side, masks, taps, own, tap_sums):
    inside, left_ok, right_ok, up_ok, down_ok = masks
    total = None
    tap_sums = list(tap_sums)
    for shift in (-1, 0, 1):
        base = LEAD + row + shift * side
        row_ok = {-1: up_ok, 0: None, 1: down_ok}[shift]
        for sway in (-1, 0, 1):
            column_ok = {-1: left_ok, 0: None, 1: right_ok}[sway]
            value = source[chunk, pl.ds(base + sway, 8), :]
            keep = inside
            if row_ok is not None:
                keep = keep & row_ok
            if column_ok is not None:
                keep = keep & column_ok
            value = jnp.where(keep, value, 0.0)
            index = 3 * (1 - shift) + (1 - sway)
            term = taps[index] * value
            total = term if total is None else total + term
            tap_sums[index] = tap_sums[index] + own * value
    return total, tuple(tap_sums)


def chunk_lanes(chunk):
    return slice(chunk * LANES, (chunk + 1) * LANES)


def tap_vectors(table_ref, first, chunk):
    return [
        jnp.broadcast_to(table_ref[first + k : first + k + 1, chunk_lanes(chunk)], (8, LANES))
        for k in range(9)
    ]


def for_crops(sides_ref, row_count, order_ref, start_ref, step):
    crops = sides_ref.shape[0]

    def scan(crop, state):
        start, large, small = state
        side = sides_ref[crop]
        start_ref[crop] = start
        is_small = side <= SMALL_SIDE
        order_ref[jnp.where(is_small, crops + small, large)] = crop
        return (
            start + side * side,
            large + jnp.where(is_small, 0, 1),
            small + jnp.where(is_small, 1, 0),
        )

    zero = jnp.int32(0)
    _, large, small = lax.fori_loop(0, crops, scan, (zero, zero, zero))
    for window, first, count in ((LARGE_WINDOW, 0, large), (SMALL_WINDOW, crops, small)):

        def group_body(group, _, window=window, first=first, count=count):
            members = []
            for member in range(CROP_GROUP):
                crop = order_ref[first + jnp.minimum(group * CROP_GROUP + member, count - 1)]
                start = start_ref[crop]
                side = sides_ref[crop]
                row = pl.multiple_of(jnp.minimum(start // 8, (row_count - window) // 8) * 8, 8)
                place = lax.broadcasted_iota(jnp.int32, (window, HALF_WIDTH), 0) + (row - start)
                members.append((crop, pl.ds(row, window), (place >= 0) & (place < side * side)))
            step(members)
            return 0

        lax.fori_loop(0, (count + CROP_GROUP - 1) // CROP_GROUP, group_body, 0)


def half_lanes(half):
    starts = [part * PAD_WIDTH + half * HALF_WIDTH for part in range(3)]
    return [slice(start, start + HALF_WIDTH) for start in starts]


def pair_lanes():
    return lax.broadcasted_iota(jnp.int32, (HDIM, LANES), 1) < HEAD_PAD


def pair_part(block, pair):
    first = pair * LANES
    lanes = slice(first, first + LANES)
    return jnp.where(
        pair_lanes(),
        block[first : first + HDIM, lanes],
        block[first + HEAD_PAD : first + HEAD_PAD + HDIM, lanes],
    )


def spread_pair(target, member, half, pair, values):
    first = pair * LANES
    lanes = slice(first, first + LANES)
    parts = split(values)
    for index in range(2):
        value = parts[index].astype(F32)
        target[member, half, index, first : first + HDIM, lanes] = jnp.where(
            pair_lanes(), value, 0.0
        ).astype(BF16)
        target[member, half, index, first + HEAD_PAD : first + HEAD_PAD + HDIM, lanes] = jnp.where(
            pair_lanes(), 0.0, value
        ).astype(BF16)


def pair_sharpness(sharp_ref, pair):
    lane = lax.broadcasted_iota(jnp.int32, (1, LANES), 1)
    return jnp.where(lane < HEAD_PAD, sharp_ref[2 * pair], sharp_ref[2 * pair + 1])


def units(values):
    scale = lax.rsqrt(jnp.sum(values * values, axis=0, keepdims=True) + attention_epsilon)
    return values * scale, scale


def mixing_forward_kernel(
    sides_ref,
    sharp_ref,
    input_ref,
    weight_ref,
    table_ref,
    x1_hbm,
    qkv_hbm,
    mixed_hbm,
    scores_hbm,
    attention_hbm,
    slope_hbm,
    e_hbm,
    sums_ref,
    x1_ref,
    qkv_ref,
    mixed_ref,
    scores_ref,
    attention_ref,
    slope_ref,
    e_ref,
    head_weights,
    out_weight,
    first_low,
    mixed,
    attention_out,
    conv_in,
    spread,
    order_ref,
    start_ref,
    sems,
):
    row_count, width = input_ref.shape
    chunks = width // LANES
    tile = tile_rows(row_count, 2)
    saves = [
        pltpu.make_async_copy(source, target, sems.at[index])
        for index, (source, target) in enumerate(
            (
                (qkv_ref, qkv_hbm),
                (scores_ref, scores_hbm),
                (attention_ref, attention_hbm),
                (mixed_ref, mixed_hbm),
                (x1_ref, x1_hbm),
                (slope_ref, slope_hbm),
                (e_ref, e_hbm),
            )
        )
    ]
    total_live = live_total(sides_ref)
    mapping = head_map(BF16)
    for part in range(3):
        head_weights[:, part * PAD_WIDTH : (part + 1) * PAD_WIDTH] = dot(
            weight_ref[part], mapping
        ).astype(BF16)
    spread[...] = jnp.zeros_like(spread)

    def first_norm(first, size, _):
        rows = pl.ds(first, size)
        unit, _ = centered(input_ref[rows, :].astype(F32))
        first_low[rows, :] = (unit * table_ref[0:1, :] + table_ref[1:2, :]).astype(BF16)
        mixed[rows, :] = jnp.zeros((size, PAD_WIDTH), F32)
        return 0

    for_rows(row_count, ROW_TILE, first_norm)

    @pl.loop(0, row_count // tile)
    def _(step):
        rows = pl.ds(pl.multiple_of(step * tile, 16), tile)
        for part in range(3):
            lanes = slice(part * PAD_WIDTH, (part + 1) * PAD_WIDTH)
            qkv_ref[rows, lanes] = dot(first_low[rows, :], head_weights[:, lanes])

    saves[0].start()

    def crop_step(members):
        units_of = [(member, half) for member in range(len(members)) for half in range(2)]
        blocks, results = [], []
        for member, half in units_of:
            crop, rows, keep = members[member]
            lanes = half_lanes(half)
            query = units(jnp.where(keep, qkv_ref[rows, lanes[0]], 0.0))[0]
            key = units(jnp.where(keep, qkv_ref[rows, lanes[1]], 0.0))[0]
            blocks.append(dot_split(dot_rows, split(key), split(query)))
        for (member, half), block in zip(units_of, blocks):
            crop = members[member][0]
            for pair in range(2):
                scores = pair_part(block, pair)
                scores_ref[crop, 2 * half + pair] = scores
                scores = scores * pair_sharpness(sharp_ref, 2 * half + pair)
                scores = jnp.exp(scores - jnp.max(scores, axis=0, keepdims=True))
                shares = scores / jnp.sum(scores, axis=0, keepdims=True)
                attention_ref[crop, 2 * half + pair] = shares
                spread_pair(spread, member, half, pair, shares)
        for member, half in units_of:
            rows = members[member][1]
            shares = (spread[member, half, 0], spread[member, half, 1])
            results.append(dot_split(dot, split(qkv_ref[rows, half_lanes(half)[2]]), shares))
        for (member, half), result in zip(units_of, results):
            _, rows, keep = members[member]
            lanes = half_lanes(half)[0]
            mixed[rows, lanes] = jnp.where(keep, result, mixed[rows, lanes])

    for_crops(sides_ref, row_count, order_ref, start_ref, crop_step)

    saves[1].start()
    saves[2].start()
    out_weight[...] = dot_rows(mapping, weight_ref[3]).astype(BF16)

    @pl.loop(0, row_count // tile)
    def _(step):
        rows = pl.ds(pl.multiple_of(step * tile, 16), tile)
        low = mixed[rows, :].astype(BF16)
        mixed_ref[rows, :] = low
        attention_out[rows, :] = dot(low, out_weight[...])

    saves[3].start()

    def second_norm(first, size, _):
        rows = pl.ds(first, size)
        value = input_ref[rows, :].astype(F32) + table_ref[2:3, :] * attention_out[rows, :]
        x1_ref[rows, :] = value
        unit, _ = centered(value)
        value = unit * table_ref[3:4, :] + table_ref[4:5, :]
        for chunk in range(chunks):
            conv_in[chunk, pl.ds(LEAD + first, size), :] = value[:, chunk_lanes(chunk)]
            slope_ref[chunk, rows, :] = jnp.zeros((size, LANES), F32)
            e_ref[chunk, rows, :] = jnp.zeros((size, LANES), F32)
        return 0

    for_rows(row_count, ROW_TILE, second_norm)
    saves[4].start()

    zero = jnp.zeros((8, LANES), F32)
    sums_ref[...] = zero
    taps = [tap_vectors(table_ref, 11, chunk) for chunk in range(chunks)]

    def conv_step(row, side, masks, carry):
        rows = pl.ds(row, 8)
        carry = list(carry)
        for chunk in range(chunks):
            value = conv_forward(conv_in, chunk, row, side, masks, taps[chunk])
            share, bell = gelu_parts(value)
            active = value * share
            slope = gelu_slope(value, share, bell)
            slope_ref[chunk, rows, :] = jnp.where(masks[0], slope, slope_ref[chunk, rows, :])
            e_ref[chunk, rows, :] = jnp.where(masks[0], active, e_ref[chunk, rows, :])
            active = jnp.where(masks[0], active, 0.0)
            carry[chunk] = carry[chunk] + active
            carry[chunks + chunk] = carry[chunks + chunk] + active * active
        return tuple(carry)

    sums = for_groups(sides_ref, conv_step, (zero,) * (2 * chunks))
    saves[5].start()
    saves[6].start()
    for index, value in enumerate(sums):
        sums_ref[index : index + 1, :] = jnp.sum(value, axis=0, keepdims=True)
    sums_ref[2 * chunks : 2 * chunks + 1, :] = jnp.full((1, LANES), total_live, jnp.int32).astype(F32)
    for save in saves:
        save.wait()


def mixing_forward(sides, sharpness, inputs, weights, table):
    row_count, width = inputs.shape
    crops = sides.shape[0]
    chunks = width // LANES
    shape = jax.ShapeDtypeStruct
    return pl.pallas_call(
        mixing_forward_kernel,
        out_shape=(
            shape((row_count, width), F32),
            shape((row_count, 3 * PAD_WIDTH), F32),
            shape((row_count, PAD_WIDTH), BF16),
            shape((crops, HEAD_PAIRS, HDIM, LANES), F32),
            shape((crops, HEAD_PAIRS, HDIM, LANES), F32),
            shape((chunks, row_count, LANES), F32),
            shape((chunks, row_count, LANES), F32),
            shape((8, LANES), F32),
        ),
        in_specs=[SMEM_SPEC, SMEM_SPEC, VMEM_SPEC, VMEM_SPEC, VMEM_SPEC],
        out_specs=(ANY_SPEC,) * 7 + (VMEM_SPEC,),
        scratch_shapes=[
            pltpu.VMEM((row_count, width), F32),
            pltpu.VMEM((row_count, 3 * PAD_WIDTH), F32),
            pltpu.VMEM((row_count, PAD_WIDTH), BF16),
            pltpu.VMEM((crops, HEAD_PAIRS, HDIM, LANES), F32),
            pltpu.VMEM((crops, HEAD_PAIRS, HDIM, LANES), F32),
            pltpu.VMEM((chunks, row_count, LANES), F32),
            pltpu.VMEM((chunks, row_count, LANES), F32),
            pltpu.VMEM((width, 3 * PAD_WIDTH), BF16),
            pltpu.VMEM((PAD_WIDTH, width), BF16),
            pltpu.VMEM((row_count, width), BF16),
            pltpu.VMEM((row_count, PAD_WIDTH), F32),
            pltpu.VMEM((row_count, width), F32),
            pltpu.VMEM((chunks, LEAD + row_count + TAIL, LANES), F32),
            pltpu.VMEM((CROP_GROUP, 2, 2, HALF_WIDTH, HALF_WIDTH), BF16),
            pltpu.SMEM((2 * crops,), jnp.int32),
            pltpu.SMEM((crops,), jnp.int32),
            pltpu.SemaphoreType.DMA((7,)),
        ],
        compiler_params=pltpu.CompilerParams(vmem_limit_bytes=VMEM_LIMIT),
        name="mixing_forward",
    )(sides, sharpness, inputs, weights, table)


def batch_vectors(bn_ref, chunk, chunks):
    count = bn_ref[2 * chunks : 2 * chunks + 1, :]
    mean = bn_ref[chunk : chunk + 1, :] / count
    scale = lax.rsqrt(bn_ref[chunks + chunk : chunks + chunk + 1, :] / count - mean * mean + batch_epsilon)
    return mean, scale


def feed_kernel(
    sides_ref,
    x1_hbm,
    e_hbm,
    bn_ref,
    weight_hbm,
    table_ref,
    adjoint_hbm,
    out_hbm,
    dx2_hbm,
    dn_hbm,
    weight_grad_hbm,
    grads_ref,
    back_sums_ref,
    e_ref,
    x1_ref,
    weight_ref,
    adjoint_ref,
    out_ref,
    dx2_ref,
    dn_ref,
    weight_grad_ref,
    up_weight,
    n_ref,
    z_ref,
    dw_ref,
    x2,
    unit,
    spread,
    third_low,
    hidden_low,
    feed,
    third_grad,
    feed_grad,
    pre_grad,
    grads,
    weight_sums,
    sems,
):
    loads = [
        pltpu.make_async_copy(source, target, sems.at[index])
        for index, (source, target) in enumerate(
            (
                (e_hbm, e_ref),
                (x1_hbm, x1_ref),
                (weight_hbm, weight_ref),
                (adjoint_hbm, adjoint_ref),
            )
        )
    ]
    saves = [
        pltpu.make_async_copy(source, target, sems.at[4 + index])
        for index, (source, target) in enumerate(
            (
                (out_ref, out_hbm),
                (dx2_ref, dx2_hbm),
                (weight_grad_ref, weight_grad_hbm),
                (dn_ref, dn_hbm),
            )
        )
    ]
    for load in loads:
        load.start()
    row_count, width = x1_ref.shape
    chunks = width // LANES
    expand = weight_ref.shape[0] // 2
    tile = tile_rows(row_count, 4)
    total_live = live_total(sides_ref)
    hidden = expand * width
    batch = [batch_vectors(bn_ref, chunk, chunks) for chunk in range(chunks)]
    zero = jnp.zeros((8, LANES), F32)

    def down_weight():
        return weight_ref[expand : 2 * expand].reshape(hidden, width)

    def normalize(first, size, _):
        rows = pl.ds(first, size)
        live = row_mask(first, size, LANES, total_live)
        for chunk in range(chunks):
            lanes = chunk_lanes(chunk)
            mean, scale = batch[chunk]
            value = (e_ref[chunk, rows, :] - mean) * scale
            value = value * table_ref[5:6, lanes] + table_ref[6:7, lanes]
            n_ref[chunk, pl.ds(LEAD + first, size), :] = jnp.where(live, value, 0.0)
            z_ref[chunk, rows, :] = jnp.zeros((size, LANES), F32)
            dn_ref[chunk, rows, :] = jnp.zeros((size, LANES), F32)
        return 0

    loads[0].wait()
    for_rows(row_count, ROW_TILE, normalize)

    taps = [tap_vectors(table_ref, 20, chunk) for chunk in range(chunks)]

    def conv_step(row, side, masks, carry):
        rows = pl.ds(row, 8)
        for chunk in range(chunks):
            value = conv_forward(n_ref, chunk, row, side, masks, taps[chunk])
            z_ref[chunk, rows, :] = jnp.where(masks[0], value, z_ref[chunk, rows, :])
        return carry

    for_groups(sides_ref, conv_step, 0)

    for load in loads[1:]:
        load.wait()
    for part in range(expand):
        up_weight[:, part * width : (part + 1) * width] = weight_ref[part]
    weight_sums[...] = jnp.zeros_like(weight_sums)
    grads[...] = jnp.zeros_like(grads)

    def z_rows(rows):
        return jnp.concatenate([z_ref[chunk, rows, :] for chunk in range(chunks)], axis=1)

    def before(base):
        rows = pl.ds(base, tile)
        value = x1_ref[rows, :] + table_ref[7:8, :] * z_rows(rows)
        x2[...] = value
        value, scale = centered(value)
        unit[...] = value
        spread[...] = jnp.broadcast_to(scale, (tile, LANES))
        third_low[...] = (value * table_ref[8:9, :] + table_ref[9:10, :]).astype(BF16)
        feed_grad[...] = (entry_rows(base) * table_ref[10:11, :]).astype(BF16)

    def entry_rows(base):
        live = row_mask(base, tile, width, total_live)
        return jnp.where(live, adjoint_ref[pl.ds(base, tile), :].astype(F32), 0.0)

    @pl.loop(0, row_count // tile)
    def _(step):
        base = pl.multiple_of(step * tile, 16)
        rows = pl.ds(base, tile)
        before(base)

        def hidden_lanes(part):
            return slice(part * hidden // HIDDEN_PARTS, (part + 1) * hidden // HIDDEN_PARTS)

        def products(part):
            lanes = hidden_lanes(part)
            return (
                dot(third_low[...], up_weight[:, lanes]),
                dot_lanes(feed_grad[...], down_weight()[lanes]),
            )

        ahead = products(0)
        for part in range(HIDDEN_PARTS):
            lanes = hidden_lanes(part)
            value, hidden_grad = ahead
            if part + 1 < HIDDEN_PARTS:
                ahead = products(part + 1)
            share, bell = gelu_parts(value)
            hidden_low[:, lanes] = (value * share).astype(BF16)
            pre_grad[:, lanes] = (hidden_grad * gelu_slope(value, share, bell)).astype(BF16)
        feed[...] = dot(hidden_low[...], down_weight())
        third_grad[...] = dot_lanes(pre_grad[...], up_weight[...])
        weight_sums[expand : 2 * expand] += dot_rows(hidden_low[...], feed_grad[...]).reshape(
            expand, width, width
        )
        up_grad = dot_rows(third_low[...], pre_grad[...])
        for part in range(expand):
            weight_sums[part] += up_grad[:, part * width : (part + 1) * width]

        value = x2[...] + table_ref[10:11, :] * feed[...]
        live = row_mask(base, tile, width, total_live)
        out_ref[rows, :] = jnp.where(live, value, 0.0).astype(BF16)
        entry = entry_rows(base)
        grads[0] += fold(entry * feed[...])
        grad = third_grad[...]
        value = unit[...]
        total = entry + norm_back(grad * table_ref[8:9, :], value, spread[:, 0:1])
        dx2_ref[rows, :] = total
        scaled = total * table_ref[7:8, :]
        for chunk in range(chunks):
            dw_ref[chunk, pl.ds(LEAD + base, tile), :] = scaled[:, chunk_lanes(chunk)]
        grads[1] += fold(total * z_rows(rows))
        grads[2] += fold(grad * value)
        grads[3] += fold(grad)

    saves[0].start()
    saves[1].start()

    owners, pieces, shard, _ = weight_grad_ref.shape
    inner = width // shard
    for owner in range(owners):
        rows = slice(owner % inner * shard, (owner % inner + 1) * shard)
        for piece in range(pieces):
            weight_grad_ref[owner, piece] = weight_sums[
                owner // inner * pieces + piece, rows, :
            ].astype(BF16)

    saves[2].start()

    back_sums_ref[...] = zero
    for index, source in enumerate((1, 2, 3, 0)):
        grads_ref[index : index + 1, :] = jnp.sum(grads[source], axis=0, keepdims=True)
    def back_step(row, side, masks, carry):
        rows = pl.ds(row, 8)
        result = []
        for chunk in range(chunks):
            mean, scale = batch[chunk]
            sums = carry[chunk]
            own = jnp.where(masks[0], n_ref[chunk, pl.ds(LEAD + row, 8), :], 0.0)
            total, tap_sums = conv_backward(
                dw_ref, chunk, row, side, masks, taps[chunk], own, sums[0:9]
            )
            dn_ref[chunk, rows, :] = jnp.where(masks[0], total, dn_ref[chunk, rows, :])
            total = jnp.where(masks[0], total, 0.0)
            standard = (e_ref[chunk, rows, :] - mean) * scale
            result.append((*tap_sums, sums[9] + total * standard, sums[10] + total))
        return tuple(result)

    sums = for_groups(sides_ref, back_step, ((zero,) * 11,) * chunks)
    saves[3].start()
    for chunk in range(chunks):
        lanes = chunk_lanes(chunk)
        for index, value in enumerate(sums[chunk]):
            value = jnp.sum(value, axis=0, keepdims=True)
            grads_ref[4 + index : 5 + index, lanes] = value
            if index == 9:
                back_sums_ref[chunks + chunk : chunks + chunk + 1, :] = value
            if index == 10:
                back_sums_ref[chunk : chunk + 1, :] = value
    for save in saves:
        save.wait()


def feed_forward(sides, x1, e, batch_sums, weights, table, adjoint, grad_shape):
    row_count, width = x1.shape
    chunks = width // LANES
    expand = weights.shape[0] // 2
    tile = tile_rows(row_count, 4)
    shape = jax.ShapeDtypeStruct
    return pl.pallas_call(
        feed_kernel,
        out_shape=(
            shape((row_count, width), BF16),
            shape((row_count, width), F32),
            shape((chunks, row_count, LANES), F32),
            shape(grad_shape, BF16),
            shape((16, width), F32),
            shape((8, LANES), F32),
        ),
        in_specs=[SMEM_SPEC, ANY_SPEC, ANY_SPEC, VMEM_SPEC, ANY_SPEC, VMEM_SPEC, ANY_SPEC],
        out_specs=(ANY_SPEC,) * 4 + (VMEM_SPEC,) * 2,
        scratch_shapes=[
            pltpu.VMEM((chunks, row_count, LANES), F32),
            pltpu.VMEM((row_count, width), F32),
            pltpu.VMEM(weights.shape, BF16),
            pltpu.VMEM((row_count, width), BF16),
            pltpu.VMEM((row_count, width), BF16),
            pltpu.VMEM((row_count, width), F32),
            pltpu.VMEM((chunks, row_count, LANES), F32),
            pltpu.VMEM(grad_shape, BF16),
            pltpu.VMEM((width, expand * width), BF16),
            pltpu.VMEM((chunks, LEAD + row_count + TAIL, LANES), F32),
            pltpu.VMEM((chunks, row_count, LANES), F32),
            pltpu.VMEM((chunks, LEAD + row_count + TAIL, LANES), F32),
            pltpu.VMEM((tile, width), F32),
            pltpu.VMEM((tile, width), F32),
            pltpu.VMEM((tile, LANES), F32),
            pltpu.VMEM((tile, width), BF16),
            pltpu.VMEM((tile, expand * width), BF16),
            pltpu.VMEM((tile, width), F32),
            pltpu.VMEM((tile, width), F32),
            pltpu.VMEM((tile, width), BF16),
            pltpu.VMEM((tile, expand * width), BF16),
            pltpu.VMEM((4, 8, width), F32),
            pltpu.VMEM((2 * expand, width, width), F32),
            pltpu.SemaphoreType.DMA((8,)),
        ],
        compiler_params=pltpu.CompilerParams(vmem_limit_bytes=VMEM_LIMIT),
        name="feed_forward",
    )(sides, x1, e, batch_sums, weights, table, adjoint)


def mixing_backward_kernel(
    sides_ref,
    sharp_ref,
    input_hbm,
    weight_ref,
    table_ref,
    x1_hbm,
    qkv_hbm,
    mixed_hbm,
    scores_hbm,
    attention_hbm,
    slope_hbm,
    e_hbm,
    bn_ref,
    dx2_hbm,
    dn_hbm,
    back_ref,
    head_low_hbm,
    dx1_hbm,
    head_weights_hbm,
    weight_grad_ref,
    grads_ref,
    x1_ref,
    qkv_ref,
    mixed_ref,
    scores_ref,
    attention_ref,
    dx2_ref,
    head_weights,
    out_weight,
    pool,
    conv_grad,
    mixed_grad,
    first_low,
    head_low,
    spread,
    out_sum,
    head_sum,
    sharp_sums,
    order_ref,
    start_ref,
    load_sems,
):
    row_count, width = input_hbm.shape
    low_rows, input_ref = head_low.at[:, 0:width], head_low.at[:, PAD_WIDTH : PAD_WIDTH + width]
    tile = tile_rows(row_count, 2)
    input_load = pltpu.make_async_copy(input_hbm, input_ref, load_sems.at[11 + row_count // tile])
    input_load.start()
    chunks = width // LANES
    slope_ref, e_ref = pool.at[0:chunks], pool.at[chunks : 2 * chunks]
    dn_ref, conv_in = pool.at[2 * chunks : 3 * chunks], pool.at[3 * chunks : 4 * chunks]
    attention_out = slope_ref
    loads = [
        pltpu.make_async_copy(source, target, load_sems.at[index])
        for index, (source, target) in enumerate(
            (
                (x1_hbm, x1_ref),
                (slope_hbm, slope_ref),
                (e_hbm, e_ref),
                (dn_hbm, dn_ref),
                (mixed_hbm, mixed_ref),
                (dx2_hbm, dx2_ref),
                (qkv_hbm, qkv_ref),
                (scores_hbm, scores_ref),
                (attention_hbm, attention_ref),
            )
        )
    ]
    saves = [
        pltpu.make_async_copy(source, target, load_sems.at[len(loads) + index])
        for index, (source, target) in enumerate(
            (
                (head_weights, head_weights_hbm),
                (dx2_ref, dx1_hbm),
            )
        )
    ]
    for step in range(row_count // tile):
        rows = pl.ds(step * tile, tile)
        saves.append(
            pltpu.make_async_copy(
                head_low.at[rows], head_low_hbm.at[rows], load_sems.at[len(loads) + 3 + step]
            )
        )
    for load in loads:
        load.start()
    tile = tile_rows(row_count, 2)
    total_live = live_total(sides_ref)
    batch = [batch_vectors(bn_ref, chunk, chunks) for chunk in range(chunks)]
    zero = jnp.zeros((8, LANES), F32)
    wide = jnp.zeros((8, width), F32)
    mapping = head_map(BF16)
    for part in range(3):
        head_weights[:, part * PAD_WIDTH : (part + 1) * PAD_WIDTH] = dot(
            weight_ref[part], mapping
        ).astype(BF16)
    saves[0].start()
    out_weight[...] = dot_rows(mapping, weight_ref[3]).astype(BF16)
    spread[...] = jnp.zeros_like(spread)

    def first_norm(first, size, _):
        rows = pl.ds(first, size)
        unit, _ = centered(input_ref[rows, :].astype(F32))
        first_low[rows, :] = (unit * table_ref[0:1, :] + table_ref[1:2, :]).astype(BF16)
        return 0

    input_load.wait()
    for_rows(row_count, ROW_TILE, first_norm)

    for load in loads[0:4]:
        load.wait()

    def batch_back(first, size, _):
        rows = pl.ds(first, size)
        live = row_mask(first, size, LANES, total_live)
        unit, _ = centered(x1_ref[rows, :])
        value = unit * table_ref[3:4, :] + table_ref[4:5, :]
        for chunk in range(chunks):
            lanes = chunk_lanes(chunk)
            mean, scale = batch[chunk]
            count = bn_ref[2 * chunks : 2 * chunks + 1, :]
            standard = (e_ref[chunk, rows, :] - mean) * scale
            inner = (
                back_ref[chunk : chunk + 1, :]
                + standard * back_ref[chunks + chunk : chunks + chunk + 1, :]
            ) / count
            grad = scale * table_ref[5:6, lanes] * (dn_ref[chunk, rows, :] - inner)
            grad = grad * slope_ref[chunk, rows, :]
            conv_grad[chunk, pl.ds(LEAD + first, size), :] = jnp.where(live, grad, 0.0)
            conv_in[chunk, pl.ds(first, size), :] = value[:, lanes]
        return 0

    for_rows(row_count, ROW_TILE, batch_back)

    taps = [tap_vectors(table_ref, 11, chunk) for chunk in range(chunks)]

    def back_step(row, side, masks, carry):
        rows = pl.ds(row, 8)
        result = []
        for chunk in range(chunks):
            held = conv_in[chunk, rows, :]
            own = jnp.where(masks[0], held, 0.0)
            total, tap_sums = conv_backward(
                conv_grad, chunk, row, side, masks, taps[chunk], own, carry[chunk]
            )
            conv_in[chunk, rows, :] = jnp.where(masks[0], total, held)
            result.append(tap_sums)
        return tuple(result)

    tap_sums = for_groups(sides_ref, back_step, ((zero,) * 9,) * chunks)
    for chunk in range(chunks):
        for index, value in enumerate(tap_sums[chunk]):
            grads_ref[5 + index : 6 + index, chunk_lanes(chunk)] = jnp.sum(
                value, axis=0, keepdims=True
            )

    for load in loads[4:6]:
        load.wait()

    @pl.loop(0, row_count // tile)
    def _(step):
        rows = pl.ds(pl.multiple_of(step * tile, 16), tile)
        result = dot(mixed_ref[rows, :], out_weight[...])
        for chunk in range(chunks):
            attention_out[chunk, rows, :] = result[:, chunk_lanes(chunk)]

    def second_back(first, size, carry):
        rows = pl.ds(first, size)
        live = row_mask(first, size, width, total_live)
        grad = jnp.concatenate([conv_in[chunk, rows, :] for chunk in range(chunks)], axis=1)
        grad = jnp.where(live, grad, 0.0)
        unit, scale = centered(x1_ref[rows, :])
        total = dx2_ref[rows, :] + norm_back(grad * table_ref[3:4, :], unit, scale)
        dx2_ref[rows, :] = total
        low_rows[rows, :] = (total * table_ref[2:3, :]).astype(BF16)
        held = jnp.concatenate([attention_out[chunk, rows, :] for chunk in range(chunks)], axis=1)
        return (
            carry[0] + fold(total * held),
            carry[1] + fold(grad * unit),
            carry[2] + fold(grad),
        )

    sums = for_rows(row_count, ROW_TILE, second_back, (wide, wide, wide))
    saves[1].start()
    for index in range(3):
        grads_ref[2 + index : 3 + index, :] = jnp.sum(sums[index], axis=0, keepdims=True)

    out_sum[...] = jnp.zeros_like(out_sum)

    @pl.loop(0, row_count // tile)
    def _(step):
        rows = pl.ds(pl.multiple_of(step * tile, 16), tile)
        mixed_grad[rows, :] = dot_lanes(low_rows[rows, :], out_weight[...])
        out_sum[...] += dot_rows(mixed_ref[rows, :], low_rows[rows, :])

    pool[...] = jnp.zeros_like(pool)

    low = out_sum[...].astype(BF16)
    weight_grad_ref[3] = dot(mapping, low).astype(BF16)
    sharp_sums[...] = jnp.zeros_like(sharp_sums)

    for load in loads[6:]:
        load.wait()

    def crop_step(members):
        units_of = [(member, half) for member in range(len(members)) for half in range(2)]
        grads, blocks, sums, results = [], [], [], []
        for member, half in units_of:
            crop, rows, keep = members[member]
            lanes = half_lanes(half)
            value = split(jnp.where(keep, qkv_ref[rows, lanes[2]], 0.0))
            grad = split(jnp.where(keep, mixed_grad[rows, lanes[0]], 0.0))
            grads.append(grad)
            blocks.append(dot_split(dot_rows, value, grad))
        value_grads = []
        for index, (member, half) in enumerate(units_of):
            for pair in range(2):
                shares = attention_ref[members[member][0], 2 * half + pair]
                spread_pair(spread, member, half, pair, shares)
            shares = (spread[member, half, 0], spread[member, half, 1])
            value_grads.append(dot_split(dot_lanes, grads[index], shares))
        for (member, half), block in zip(units_of, blocks):
            crop = members[member][0]
            query_sums = []
            for pair in range(2):
                index = 2 * half + pair
                shares = attention_ref[crop, index]
                scores = scores_ref[crop, index]
                part = pair_part(block, pair)
                part = shares * (part - jnp.sum(part * shares, axis=0, keepdims=True))
                total = jnp.sum(part * scores, axis=0, keepdims=True)
                sharp_sums[index, pl.ds(crop, 1), :] = total
                sharpness = pair_sharpness(sharp_ref, index)
                query_sums.append(total * sharpness)
                spread_pair(spread, member, 2 + half, pair, part * sharpness)
            sums.append(jnp.concatenate(query_sums, axis=1))
        for index, (member, half) in enumerate(units_of):
            crop, rows, keep = members[member]
            lanes = half_lanes(half)
            query, query_scale = units(jnp.where(keep, qkv_ref[rows, lanes[0]], 0.0))
            key, key_scale = units(jnp.where(keep, qkv_ref[rows, lanes[1]], 0.0))
            slopes = (spread[member, 2 + half, 0], spread[member, 2 + half, 1])
            query_grad = dot_split(dot, split(key), slopes)
            query_grad = query_scale * (query_grad - query * sums[index])
            key_grad = dot_split(dot_lanes, split(query), slopes)
            key_grad = key_scale * (
                key_grad - key * jnp.sum(key_grad * key, axis=0, keepdims=True)
            )
            results.append((query_grad, key_grad, value_grads[index]))
        for (member, half), grads in zip(units_of, results):
            _, rows, keep = members[member]
            for part, result in enumerate(grads):
                for side in range(HALF_WIDTH // LANES):
                    chunk = (part * PAD_WIDTH + half * HALF_WIDTH) // LANES + side
                    pool[chunk, rows, :] = jnp.where(
                        keep[:, 0:LANES], result[:, chunk_lanes(side)], pool[chunk, rows, :]
                    )

    for_crops(sides_ref, row_count, order_ref, start_ref, crop_step)

    grads_ref[0:2, :] = jnp.zeros((2, width), F32)
    grads_ref[14:16, :] = jnp.zeros((2, width), F32)
    lane = lax.broadcasted_iota(jnp.int32, (1, LANES), 1)
    total = jnp.zeros((1, LANES), F32)
    for head in range(HEAD_NUMBER):
        row = jnp.sum(sharp_sums[head // 2], axis=0, keepdims=True)
        row = jnp.where((lane >> 6) == head % 2, row, 0.0)
        total = jnp.where(lane == head, jnp.sum(row, axis=1, keepdims=True), total)
    grads_ref[14:15, 0:LANES] = total

    head_sum[...] = jnp.zeros_like(head_sum)
    for step in range(row_count // tile):
        rows = pl.ds(step * tile, tile)
        for chunk in range(3 * PAD_WIDTH // LANES):
            head_low[rows, chunk_lanes(chunk)] = pool[chunk, rows, :].astype(BF16)
        saves[2 + step].start()
        head_sum[...] += dot_rows(first_low[rows, :], head_low[rows, :])
    for part in range(3):
        low = head_sum[:, part * PAD_WIDTH : (part + 1) * PAD_WIDTH].astype(BF16)
        weight_grad_ref[part] = dot_lanes(low, mapping).astype(BF16)
    for save in saves:
        save.wait()


def mixing_backward(sides, sharpness, inputs, weights, table, saved, batch_sums, dx2, dn, back_sums):
    row_count, width = inputs.shape
    chunks = width // LANES
    crops = sides.shape[0]
    shape = jax.ShapeDtypeStruct
    x1, qkv, mixed, scores, attention, slope, e = saved
    return pl.pallas_call(
        mixing_backward_kernel,
        out_shape=(
            shape((row_count, 3 * PAD_WIDTH), BF16),
            shape((row_count, width), F32),
            shape((width, 3 * PAD_WIDTH), BF16),
            shape((4, width, width), BF16),
            shape((16, width), F32),
        ),
        in_specs=[SMEM_SPEC, SMEM_SPEC]
        + [ANY_SPEC, VMEM_SPEC, VMEM_SPEC]
        + [ANY_SPEC] * 7
        + [VMEM_SPEC, ANY_SPEC, ANY_SPEC, VMEM_SPEC],
        out_specs=(ANY_SPEC,) * 3 + (VMEM_SPEC,) * 2,
        scratch_shapes=[
            pltpu.VMEM((row_count, width), F32),
            pltpu.VMEM((row_count, 3 * PAD_WIDTH), F32),
            pltpu.VMEM((row_count, PAD_WIDTH), BF16),
            pltpu.VMEM((crops, HEAD_PAIRS, HDIM, LANES), F32),
            pltpu.VMEM((crops, HEAD_PAIRS, HDIM, LANES), F32),
            pltpu.VMEM((row_count, width), F32),
            pltpu.VMEM((width, 3 * PAD_WIDTH), BF16),
            pltpu.VMEM((PAD_WIDTH, width), BF16),
            pltpu.VMEM((3 * PAD_WIDTH // LANES, row_count, LANES), F32),
            pltpu.VMEM((chunks, LEAD + row_count + TAIL, LANES), F32),
            pltpu.VMEM((row_count, PAD_WIDTH), F32),
            pltpu.VMEM((row_count, width), BF16),
            pltpu.VMEM((row_count, 3 * PAD_WIDTH), BF16),
            pltpu.VMEM((CROP_GROUP, 4, 2, HALF_WIDTH, HALF_WIDTH), BF16),
            pltpu.VMEM((PAD_WIDTH, width), F32),
            pltpu.VMEM((width, 3 * PAD_WIDTH), F32),
            pltpu.VMEM((HEAD_PAIRS, crops, LANES), F32),
            pltpu.SMEM((2 * crops,), jnp.int32),
            pltpu.SMEM((crops,), jnp.int32),
            pltpu.SemaphoreType.DMA((12 + row_count // tile_rows(row_count, 2),)),
        ],
        compiler_params=pltpu.CompilerParams(vmem_limit_bytes=VMEM_LIMIT),
        name="mixing_backward",
    )(
        sides,
        sharpness,
        inputs,
        weights,
        table,
        x1,
        qkv,
        mixed,
        scores,
        attention,
        slope,
        e,
        batch_sums,
        dx2,
        dn,
        back_sums,
    )


MESH = pl.DeviceIdType.MESH


def greet(peers):
    barrier = pltpu.get_barrier_semaphore()
    for peer in peers:
        pl.semaphore_signal(barrier, inc=1, device_id=peer, device_id_type=MESH)
    pl.semaphore_wait(barrier, len(peers))


def push(source, target, send, receive, peer):
    copy = pltpu.make_async_remote_copy(
        src_ref=source,
        dst_ref=target,
        send_sem=send,
        recv_sem=receive,
        device_id=peer,
        device_id_type=MESH,
    )
    copy.start()
    return copy


def turned(place, step, count):
    return lax.rem(place + step, count)


def ring_peers(axis, count):
    place = lax.axis_index(axis)
    return [{axis: turned(place, step, count)} for step in range(1, count)]


def comm_params(identity):
    return pltpu.CompilerParams(
        collective_id=identity, has_side_effects=True, vmem_limit_bytes=VMEM_LIMIT
    )


def flip(value, bits):
    for bit in (1, 2, 4):
        if bits & bit:
            value = value + bit - 2 * bit * lax.rem(lax.div(value, bit), 2)
    return value


def flip_peers(axis, count):
    place = lax.axis_index(axis)
    return [{axis: flip(place, bits)} for bits in range(1, count)]


def sum_all_kernel(counts, part_ref, total_ref, parts, send, receive):
    n_dp, n_fsdp = counts
    dp, fsdp = lax.axis_index("dp"), lax.axis_index("fsdp")
    place = dp * n_fsdp + fsdp
    peers = [
        {"dp": flip(dp, outer), "fsdp": flip(fsdp, inner)}
        for inner in reversed(range(n_fsdp))
        for outer in reversed(range(n_dp))
        if inner or outer
    ]
    greet(peers)
    parts[place] = part_ref[...]
    copies = [
        push(part_ref, parts.at[place], send.at[k], receive.at[k], peer)
        for k, peer in enumerate(peers)
    ]
    for copy in copies:
        copy.wait()
    total = parts[0]
    for k in range(1, n_dp * n_fsdp):
        total = total + parts[k]
    total_ref[...] = total


def sum_all(part, counts, identity):
    size = counts[0] * counts[1]
    return pl.pallas_call(
        functools.partial(sum_all_kernel, counts),
        out_shape=jax.ShapeDtypeStruct(part.shape, F32),
        in_specs=[VMEM_SPEC],
        out_specs=VMEM_SPEC,
        scratch_shapes=[
            pltpu.VMEM((size, *part.shape), F32),
            pltpu.SemaphoreType.DMA((size - 1,)),
            pltpu.SemaphoreType.DMA((size - 1,)),
        ],
        compiler_params=comm_params(identity),
        name="sum_all",
    )(part)


def sum_pair_kernel(
    counts, part_ref, blocks_hbm, total_ref, sums_ref, parts, own, other, send, receive, sems
):
    n_dp, n_fsdp = counts
    dp, fsdp = lax.axis_index("dp"), lax.axis_index("fsdp")
    core = lax.rem(dp, 2)
    place = dp * n_fsdp + fsdp
    peers = [
        {"dp": flip(dp, outer), "fsdp": flip(fsdp, inner)}
        for inner in reversed(range(n_fsdp))
        for outer in reversed(range(n_dp))
        if inner or outer
    ]
    load = pltpu.make_async_copy(blocks_hbm.at[pl.ds(core * n_fsdp, n_fsdp)], own, sems.at[0])
    load.start()
    greet(peers)
    parts[place] = part_ref[...]
    copies = [
        push(part_ref, parts.at[place], send.at[k], receive.at[k], peer)
        for k, peer in enumerate(peers)
    ]
    blocks = push(
        blocks_hbm.at[pl.ds((1 - core) * n_fsdp, n_fsdp)],
        other,
        sems.at[1],
        sems.at[2],
        {"dp": flip(dp, 1)},
    )
    load.wait()
    blocks.wait_recv()
    for owner in range(n_fsdp):
        sums_ref[owner] = (own[owner].astype(F32) + other[owner].astype(F32)).astype(BF16)
    for copy in copies:
        copy.wait()
    total = parts[0]
    for k in range(1, n_dp * n_fsdp):
        total = total + parts[k]
    total_ref[...] = total
    blocks.wait_send()


def sum_pair(part, blocks, counts, identity):
    size = counts[0] * counts[1]
    half = (counts[1], *blocks.shape[1:])
    shape = jax.ShapeDtypeStruct
    return pl.pallas_call(
        functools.partial(sum_pair_kernel, counts),
        out_shape=(shape(part.shape, F32), shape(half, BF16)),
        in_specs=[VMEM_SPEC, ANY_SPEC],
        out_specs=(VMEM_SPEC, VMEM_SPEC),
        scratch_shapes=[
            pltpu.VMEM((size, *part.shape), F32),
            pltpu.VMEM(half, BF16),
            pltpu.VMEM(half, BF16),
            pltpu.SemaphoreType.DMA((size - 1,)),
            pltpu.SemaphoreType.DMA((size - 1,)),
            pltpu.SemaphoreType.DMA((3,)),
        ],
        compiler_params=comm_params(identity),
        name="sum_pair",
    )(part, blocks)


def gather_kernel(
    counts,
    masters_ref,
    table_ref,
    blocks_ref,
    full_table_ref,
    blocks,
    tables,
    stage,
    ring_send,
    ring_recv,
    table_send,
    table_recv,
    cross_send,
    cross_recv,
    pair_send,
    pair_recv,
):
    n_dp, n_fsdp = counts
    dp, fsdp = lax.axis_index("dp"), lax.axis_index("fsdp")
    shard, width = masters_ref.shape[1:]
    columns = table_ref.shape[1]
    across = lax.rem(dp + 2, 4)
    pair = dp + 1 - 2 * lax.rem(dp, 2)
    peers = flip_peers("fsdp", n_fsdp)
    greet(peers + [{"dp": across}, {"dp": pair}])

    def piece(block, owner):
        return blocks.at[block, pl.ds(pl.multiple_of(owner * shard, 16), shard), :]

    def origin(step):
        return flip(fsdp, step)

    stage[...] = jnp.zeros_like(stage)
    stage[0 : table_ref.shape[0], 0:columns] = table_ref[...]
    tables[fsdp] = stage[...].astype(BF16)
    blocks[dp, pl.ds(pl.multiple_of(fsdp * shard, 16), shard), :] = masters_ref[dp].astype(BF16)
    own = piece(dp, fsdp)
    ring = [
        push(own, own, ring_send.at[k], ring_recv.at[k], peer) for k, peer in enumerate(peers)
    ]
    table_copies = [
        push(tables.at[fsdp], tables.at[fsdp], table_send.at[k], table_recv.at[k], peer)
        for k, peer in enumerate(peers)
    ]
    crossing, pairing = [], []
    for step in range(n_fsdp):
        if step:
            ring[step - 1].wait_recv()
        part = piece(dp, origin(step))
        crossing.append(push(part, part, cross_send.at[step], cross_recv.at[step], {"dp": across}))
        pairing.append(
            push(part, part, pair_send.at[0, step], pair_recv.at[0, step], {"dp": pair})
        )
    for step in range(n_fsdp):
        crossing[step].wait_recv()
        part = piece(across, origin(step))
        pairing.append(
            push(part, part, pair_send.at[1, step], pair_recv.at[1, step], {"dp": pair})
        )
    for copy in table_copies:
        copy.wait_recv()
    total = None
    for owner in range(n_fsdp):
        lane = lax.broadcasted_iota(jnp.int32, (LANES, width), 0)
        target = lax.broadcasted_iota(jnp.int32, (LANES, width), 1)
        hit = (lane < columns) & (lane + owner * columns == target)
        term = dot(tables[owner], hit.astype(F32).astype(BF16))
        total = term if total is None else total + term
    full_table_ref[...] = total
    for copy in pairing:
        copy.wait_recv()
    blocks_ref[...] = blocks[...]
    for copy in ring + table_copies + crossing + pairing:
        copy.wait_send()


def gather_start(masters, coefficients, counts, identity):
    n_dp, n_fsdp = counts
    width = masters.shape[2]
    shape = jax.ShapeDtypeStruct
    dma = pltpu.SemaphoreType.DMA
    return pl.pallas_call(
        functools.partial(gather_kernel, counts),
        out_shape=(shape((4, width, width), BF16), shape((32, width), F32)),
        in_specs=[VMEM_SPEC, VMEM_SPEC],
        out_specs=(VMEM_SPEC, VMEM_SPEC),
        scratch_shapes=[
            pltpu.VMEM((4, width, width), BF16),
            pltpu.VMEM((n_fsdp, 32, LANES), BF16),
            pltpu.VMEM((32, LANES), F32),
            dma((n_fsdp - 1,)),
            dma((n_fsdp - 1,)),
            dma((n_fsdp - 1,)),
            dma((n_fsdp - 1,)),
            dma((n_fsdp,)),
            dma((n_fsdp,)),
            dma((2, n_fsdp)),
            dma((2, n_fsdp)),
        ],
        compiler_params=comm_params(identity),
        name="gather_start",
    )(masters, coefficients)


def owner_rows(owner, shard):
    return pl.ds(pl.multiple_of(owner * shard, 16), shard)


TABLE_ROWS = (
    [(0, row) for row in range(5)]
    + [(1, 13), (1, 14)]
    + [(1, row) for row in range(4)]
    + [(0, row) for row in range(5, 14)]
    + [(1, row) for row in range(4, 13)]
)


def settle_kernel(
    counts,
    place_ref,
    mix_hbm,
    feed_hbm,
    mix_table_ref,
    feed_table_ref,
    left_hbm,
    right_hbm,
    head_low_hbm,
    dx1_hbm,
    input_hbm,
    head_weights_hbm,
    coefficient_ref,
    grad_hbm,
    slots_hbm,
    rows_hbm,
    table_ref,
    out_hbm,
    left,
    right,
    head_low,
    dx1,
    inputs,
    head_weights,
    out,
    first_sums,
    pair_buf,
    cross_out,
    cross_buf,
    ring_out,
    ring_buf,
    feed_in,
    feed_buf,
    dp_buf,
    slot_out,
    slots,
    steps,
    rows_buf,
    table_stage,
    table_rows,
    table_out,
    table_buf,
    table_part,
    table_dp,
    feed_sum,
    mix,
    feed_ref,
    left_parts,
    grad_ref,
    load_sems,
    pair_send,
    pair_recv,
    cross_send,
    cross_recv,
    ring_send,
    ring_recv,
    feed_in_send,
    feed_in_recv,
    feed_send,
    feed_recv,
    dp_send,
    dp_recv,
    slot_send,
    slot_recv,
    twin_send,
    twin_recv,
    back_send,
    back_recv,
    last_send,
    last_recv,
    table_rows_send,
    table_rows_recv,
    table_send,
    table_recv,
    table_dp_send,
    table_dp_recv,
):
    n_dp, n_fsdp = counts
    dp, fsdp = lax.axis_index("dp"), lax.axis_index("fsdp")
    width = mix_hbm.shape[2]
    shard = width // n_fsdp
    core = lax.rem(dp, 2)
    across, pair, pair_across = flip(dp, 2), flip(dp, 1), flip(dp, 3)
    peers, dp_peers = flip_peers("fsdp", n_fsdp), flip_peers("dp", n_dp)
    to_pair, to_across = {"dp": pair}, {"dp": across}
    loads = [
        pltpu.make_async_copy(left_hbm.at[core], left, load_sems.at[0]),
        pltpu.make_async_copy(right_hbm.at[core], right, load_sems.at[1]),
    ]
    mix_loads = [
        pltpu.make_async_copy(mix_hbm.at[across], mix.at[0], load_sems.at[3]),
        pltpu.make_async_copy(mix_hbm.at[dp], mix.at[1], load_sems.at[4]),
    ]
    feed_load = pltpu.make_async_copy(feed_hbm, feed_ref, load_sems.at[5])
    for load in mix_loads:
        load.start()
    feed_load.start()
    row_count = dx1.shape[0]
    tile = tile_rows(row_count, 4)
    tiles = row_count // tile
    weight_load = pltpu.make_async_copy(head_weights_hbm, head_weights, load_sems.at[2])
    weight_load.start()
    tile_loads, tile_saves = [], []
    for step in range(tiles):
        rows = pl.ds(step * tile, tile)
        sems = [load_sems.at[8 + 4 * step + index] for index in range(4)]
        tile_loads.append(
            [
                pltpu.make_async_copy(head_low_hbm.at[rows], head_low.at[rows], sems[0]),
                pltpu.make_async_copy(dx1_hbm.at[rows], dx1.at[rows], sems[1]),
                pltpu.make_async_copy(input_hbm.at[rows], inputs.at[rows], sems[2]),
            ]
        )
        tile_saves.append(pltpu.make_async_copy(out.at[rows], out_hbm.at[rows], sems[3]))
        for load in tile_loads[step]:
            load.start()
    for load in loads:
        load.start()
    first_sums[...] = jnp.zeros_like(first_sums)

    def first_back(step):
        rows = pl.ds(step * tile, tile)
        if step == 0:
            weight_load.wait()
        for load in tile_loads[step]:
            load.wait()
        grad = dot_lanes(head_low[rows, :], head_weights[...])
        unit, scale = centered(inputs[rows, :].astype(F32))
        total = dx1[rows, :] + norm_back(grad * coefficient_ref[0:1, :], unit, scale)
        out[rows, :] = total.astype(BF16)
        tile_saves[step].start()
        first_sums[0] += fold(grad * unit)
        first_sums[1] += fold(grad)

    greet(peers + dp_peers)

    parts = list(reversed(range(n_fsdp // 2)))
    deep = 2 * shard

    def part_rows(part):
        first = lax.div(flip(fsdp, 2 * part), 2)
        return pl.ds(pl.multiple_of(first * deep, 16), deep)

    def owner_rows(owner):
        return pl.ds(pl.multiple_of(owner * shard, 16), shard)

    pairing = {}
    for part in parts:
        rows = part_rows(part)
        for side, block in enumerate((pair_across, pair)):
            pairing[part, side] = push(
                mix_hbm.at[block, rows],
                pair_buf.at[side, rows],
                pair_send.at[side, part],
                pair_recv.at[side, part],
                to_pair,
            )
    for load in mix_loads:
        load.wait()
    crossing = {}
    for part in parts:
        rows = part_rows(part)
        pairing[part, 0].wait_recv()
        cross_out[rows, :] = (
            mix[0, rows, :].astype(F32) + pair_buf[0, rows, :].astype(F32)
        ).astype(BF16)
        crossing[part] = push(
            cross_out.at[rows],
            cross_buf.at[rows],
            cross_send.at[part],
            cross_recv.at[part],
            to_across,
        )
    ring = {}
    for part in parts:
        rows = part_rows(part)
        pairing[part, 1].wait_recv()
        crossing[part].wait_recv()
        ring_out[rows, :] = (
            mix[1, rows, :].astype(F32)
            + pair_buf[1, rows, :].astype(F32)
            + cross_buf[rows, :].astype(F32)
        ).astype(BF16)
        for bits in (2 * part + 1, 2 * part):
            if bits:
                ring[bits] = push(
                    ring_out.at[owner_rows(flip(fsdp, bits))],
                    ring_buf.at[bits],
                    ring_send.at[bits - 1],
                    ring_recv.at[bits - 1],
                    peers[bits - 1],
                )

    pieces = feed_sum.shape[0] // 2
    side = lax.div(dp, 2)
    feed_load.wait()
    for piece in range(2 * pieces):
        total = feed_ref[0, piece].astype(F32)
        for owner in range(1, n_fsdp):
            total = total + feed_ref[owner, piece].astype(F32)
        feed_sum[piece] = total.astype(BF16)
    feeding = push(
        feed_sum.at[pl.ds((1 - side) * pieces, pieces)],
        feed_in,
        feed_in_send.at[0],
        feed_in_recv.at[0],
        to_across,
    )
    for step in range(tiles - tiles // 2):
        first_back(step)
    feeding.wait_recv()
    total = feed_sum[pl.ds(side * pieces, pieces)].astype(F32) + feed_in[...].astype(F32)
    feed_buf[dp] = total.astype(BF16)
    feeds = [
        push(feed_buf.at[dp], feed_buf.at[dp], feed_send.at[k], feed_recv.at[k], peer)
        for k, peer in enumerate(dp_peers)
    ]

    total = ring_out[owner_rows(fsdp), :].astype(F32)
    for bits in range(1, n_fsdp):
        ring[bits].wait_recv()
        total = total + ring_buf[bits].astype(F32)
    dp_buf[dp] = total
    gathering = [
        push(dp_buf.at[dp], dp_buf.at[dp], dp_send.at[k], dp_recv.at[k], peer)
        for k, peer in enumerate(dp_peers)
    ]
    for step in range(tiles - tiles // 2, tiles):
        first_back(step)

    table_stage[...] = jnp.zeros_like(table_stage)
    for row, (source, first) in enumerate(TABLE_ROWS):
        ref = mix_table_ref if source == 0 else feed_table_ref
        table_stage[row : row + 1, :] = ref[first : first + 1, :]
    for row in range(2):
        table_stage[row : row + 1, :] = jnp.sum(first_sums[row], axis=0, keepdims=True)
    table_stage[31:32, :] = mix_table_ref[14:15, :]
    quarter = table_stage.shape[0] // n_dp

    def quarter_rows(place):
        return pl.ds(pl.multiple_of(place * quarter, 8), quarter)

    table_rows[dp] = table_stage[quarter_rows(dp), :]
    quartering = [
        push(
            table_stage.at[quarter_rows(flip(dp, step + 1))],
            table_rows.at[dp],
            table_rows_send.at[step],
            table_rows_recv.at[step],
            peer,
        )
        for step, peer in enumerate(dp_peers)
    ]
    for copy in feeds:
        copy.wait_recv()
    for place in range(n_dp):
        for piece in range(pieces):
            block = n_dp + (place % 2 * 2 + place // 2) * pieces + piece
            grad_ref[block] = feed_buf[place, piece].astype(F32)
    for copy in gathering:
        copy.wait_recv()
    for place in range(n_dp):
        grad_ref[place] = dp_buf[place]
    tile_saves.append(pltpu.make_async_copy(grad_ref, grad_hbm, load_sems.at[6 + 2 + 4 * tiles]))
    tile_saves[-1].start()

    slotting = {}
    for bits in reversed(range(n_fsdp)):
        slot = 2 * flip(fsdp, bits) + core
        block, filled = jnp.int32(0), jnp.int32(0)
        for index in range(grad_ref.shape[0]):
            here = place_ref[index] == slot
            block = jnp.where(here, index, block)
            filled = jnp.where(here, 1, filled)
        value = (grad_ref[block] * filled.astype(F32)).astype(BF16)
        if bits:
            slot_out[bits - 1] = value
            slotting[bits] = push(
                slot_out.at[bits - 1],
                slots.at[core, owner_rows(fsdp), :],
                slot_send.at[bits - 1],
                slot_recv.at[bits - 1],
                peers[bits - 1],
            )
        else:
            slots[core, owner_rows(fsdp), :] = value
    for copy in quartering:
        copy.wait_recv()
    rest = table_rows[0]
    for place in range(1, n_dp):
        rest = rest + table_rows[place]
    sharp_row = lax.broadcasted_iota(jnp.int32, (quarter, LANES), 0) + dp * quarter == 31
    sharp_values = jnp.broadcast_to(rest[quarter - 1 : quarter, 0:LANES], (quarter, LANES))
    terms = []
    for _ in range(3):
        term = rest.astype(BF16).astype(F32)
        terms.append(term)
        rest = rest - term
    terms = jnp.concatenate(terms, axis=0).astype(BF16)
    columns = width // n_fsdp
    for owner in range(n_fsdp):
        lane = lax.broadcasted_iota(jnp.int32, (width, LANES), 1)
        source = lax.broadcasted_iota(jnp.int32, (width, LANES), 0)
        hit = ((lane < columns) & (lane + owner * columns == source)).astype(F32).astype(BF16)
        value = dot(terms, hit)
        value = value[0:quarter] + value[quarter : 2 * quarter] + value[2 * quarter :]
        table_out[owner] = jnp.where(sharp_row, sharp_values, value)
    table_buf[fsdp] = table_out[fsdp]
    tabling = [
        push(
            table_out.at[flip(fsdp, step + 1)],
            table_buf.at[fsdp],
            table_send.at[step],
            table_recv.at[step],
            peer,
        )
        for step, peer in enumerate(peers)
    ]
    for load in loads:
        load.wait()
    right_parts = split(right[...])
    for index, value in enumerate(split(left[...])):
        left_parts[index] = value
    twins = []
    for bits in range(n_fsdp):
        if bits:
            slotting[bits].wait_recv()
        part = slots.at[core, owner_rows(flip(fsdp, bits)), :]
        twins.append(push(part, part, twin_send.at[bits], twin_recv.at[bits], to_pair))

    grad = slots[core]
    back = {}
    for part in parts:
        rows = part_rows(part)
        half = split(dot(left_parts[0, rows, :], grad) + dot(left_parts[1, rows, :], grad))
        steps[rows, :] = dot_split(dot, half, right_parts).astype(BF16)
        for bits in (2 * part + 1, 2 * part):
            if bits:
                back[bits] = push(
                    steps.at[owner_rows(flip(fsdp, bits))],
                    rows_buf.at[2 * fsdp + core],
                    back_send.at[bits - 1],
                    back_recv.at[bits - 1],
                    peers[bits - 1],
                )
    rows_buf[2 * fsdp + core] = steps[owner_rows(fsdp), :]
    for copy in tabling:
        copy.wait_recv()
    total = table_buf[0]
    for owner in range(1, n_fsdp):
        total = total + table_buf[owner]
    table_part[...] = total
    table_dp[dp] = total
    table_dps = [
        push(table_part, table_dp.at[dp], table_dp_send.at[k], table_dp_recv.at[k], peer)
        for k, peer in enumerate(dp_peers)
    ]
    lasts = []
    for bits in range(n_fsdp):
        if bits:
            back[bits].wait_recv()
        part = rows_buf.at[2 * flip(fsdp, bits) + core]
        lasts.append(push(part, part, last_send.at[bits], last_recv.at[bits], to_pair))
    for copy in table_dps:
        copy.wait_recv()
    for place in range(n_dp):
        table_ref[place * quarter : (place + 1) * quarter, :] = table_dp[place]
    for copy in twins:
        copy.wait_recv()
    tile_saves.append(pltpu.make_async_copy(slots, slots_hbm, load_sems.at[6]))
    tile_saves[-1].start()
    for copy in lasts:
        copy.wait_recv()
    tile_saves.append(pltpu.make_async_copy(rows_buf, rows_hbm, load_sems.at[7]))
    tile_saves[-1].start()
    copies = [*pairing.values(), *crossing.values(), *ring.values(), *slotting.values()]
    copies += [*back.values(), feeding, *feeds, *quartering, *tabling, *table_dps, *gathering]
    for copy in copies + twins + lasts:
        copy.wait_send()
    for save in tile_saves:
        save.wait()


def settle(
    places, mix, feed, mix_table, feed_table, left, right, back, coefficients, counts, identity
):
    head_low, dx1, inputs, head_weights = back
    row_count = dx1.shape[0]
    tiles = row_count // tile_rows(row_count, 4)
    n_dp, n_fsdp = counts
    width = mix.shape[2]
    shard = width // n_fsdp
    blocks = n_dp + 2 * feed.shape[1]
    pieces = feed.shape[1] // 2
    inner, outer = n_fsdp - 1, n_dp - 1
    shape = jax.ShapeDtypeStruct
    dma = pltpu.SemaphoreType.DMA
    sizes = [(2, n_fsdp // 2), (n_fsdp // 2,), (inner,), (1,), (outer,), (outer,)]
    sizes += [(inner,), (n_fsdp,), (inner,), (n_fsdp,), (outer,), (inner,), (outer,)]
    return pl.pallas_call(
        functools.partial(settle_kernel, counts),
        out_shape=(
            shape((blocks, shard, width), F32),
            shape((2, width, width), BF16),
            shape((2 * n_fsdp, shard, width), BF16),
            shape((32, LANES), F32),
            shape(inputs.shape, BF16),
        ),
        in_specs=[SMEM_SPEC] + [ANY_SPEC] * 2 + [VMEM_SPEC] * 2 + [ANY_SPEC] * 6 + [VMEM_SPEC],
        out_specs=(ANY_SPEC,) * 3 + (VMEM_SPEC, ANY_SPEC),
        scratch_shapes=[
            pltpu.VMEM((width, width), F32),
            pltpu.VMEM((width, width), F32),
            pltpu.VMEM(head_low.shape, BF16),
            pltpu.VMEM(dx1.shape, F32),
            pltpu.VMEM(inputs.shape, BF16),
            pltpu.VMEM(head_weights.shape, BF16),
            pltpu.VMEM(inputs.shape, BF16),
            pltpu.VMEM((2, 8, width), F32),
            pltpu.VMEM((2, width, width), BF16),
            pltpu.VMEM((width, width), BF16),
            pltpu.VMEM((width, width), BF16),
            pltpu.VMEM((width, width), BF16),
            pltpu.VMEM((n_fsdp, shard, width), BF16),
            pltpu.VMEM((pieces, shard, width), BF16),
            pltpu.VMEM((n_dp, pieces, shard, width), BF16),
            pltpu.VMEM((n_dp, shard, width), F32),
            pltpu.VMEM((inner, shard, width), BF16),
            pltpu.VMEM((2, width, width), BF16),
            pltpu.VMEM((width, width), BF16),
            pltpu.VMEM((2 * n_fsdp, shard, width), BF16),
            pltpu.VMEM((32, width), F32),
            pltpu.VMEM((n_dp, 32 // n_dp, width), F32),
            pltpu.VMEM((n_fsdp, 32 // n_dp, LANES), F32),
            pltpu.VMEM((n_fsdp, 32 // n_dp, LANES), F32),
            pltpu.VMEM((32 // n_dp, LANES), F32),
            pltpu.VMEM((n_dp, 32 // n_dp, LANES), F32),
            pltpu.VMEM(feed.shape[1:], BF16),
            pltpu.VMEM((2, width, width), BF16),
            pltpu.VMEM(feed.shape, BF16),
            pltpu.VMEM((2, width, width), BF16),
            pltpu.VMEM((blocks, shard, width), F32),
            dma((9 + 4 * tiles,)),
        ]
        + [dma(size) for size in sizes for _ in range(2)],
        compiler_params=comm_params(identity),
        name="settle",
    )(places, mix, feed, mix_table, feed_table, left, right, *back, coefficients)


def finish_kernel(
    place_ref,
    table_ref,
    energy_ref,
    coefficient_ref,
    sharp_ref,
    sharp_energy_ref,
    grads_hbm,
    slots_hbm,
    rows_hbm,
    left_hbm,
    right_hbm,
    masters_hbm,
    tokens_hbm,
    grad_hbm,
    left_out_hbm,
    right_out_hbm,
    masters_out_hbm,
    low_hbm,
    tokens_out_hbm,
    table_grad_ref,
    energy_out_ref,
    coefficient_out_ref,
    sharp_grad_ref,
    sharp_energy_out_ref,
    sharp_out_ref,
    left,
    right,
    masters,
    low,
    tokens,
    grad_ref,
    slots_ref,
    rows_ref,
    sems,
):
    slot_count = slots_ref.shape[0]
    load_slots = pltpu.make_async_copy(slots_hbm, slots_ref, sems.at[10])
    load_rows = pltpu.make_async_copy(rows_hbm, rows_ref, sems.at[11])
    load_grads = pltpu.make_async_copy(grads_hbm, grad_ref, sems.at[12])
    load_slots.start()
    load_left = pltpu.make_async_copy(left_hbm, left, sems.at[0])
    load_right = pltpu.make_async_copy(right_hbm, right, sems.at[1])
    load_masters = pltpu.make_async_copy(masters_hbm, masters, sems.at[2])
    saves = [
        pltpu.make_async_copy(source, target, sems.at[3 + index])
        for index, (source, target) in enumerate(
            (
                (grad_ref, grad_hbm),
                (left, left_out_hbm),
                (right, right_out_hbm),
                (masters, masters_out_hbm),
                (low, low_hbm),
                (tokens, tokens_out_hbm),
            )
        )
    ]
    load_left.start()
    load_right.start()
    load_tokens = pltpu.make_async_copy(tokens_hbm, tokens, sems.at[9])
    load_tokens.start()
    load_grads.start()
    load_masters.start()
    load_rows.start()
    load_slots.wait()
    load_left.wait()
    for slot in range(slot_count):
        grad = slots_ref[slot]
        left[slot] = (
            covariance_forgetting * left[slot]
            + (1.0 - covariance_forgetting) * dot_lanes(grad, grad)
        )
    saves[1].start()
    load_right.wait()
    for slot in range(slot_count):
        grad = slots_ref[slot]
        right[slot] = (
            covariance_forgetting * right[slot]
            + (1.0 - covariance_forgetting) * dot_rows(grad, grad)
        )
    saves[2].start()
    load_tokens.wait()
    saves[5].start()
    load_grads.wait()
    saves[0].start()
    load_masters.wait()
    load_rows.wait()
    for block in range(masters.shape[0]):
        value = masters[block] - weight_rate * rows_ref[place_ref[block]].astype(F32)
        masters[block] = value
        low[block] = value.astype(BF16)
    saves[3].start()
    saves[4].start()
    count, columns = energy_ref.shape
    grad = table_ref[0:count, 0:columns]
    table_grad_ref[...] = grad
    energy = covariance_forgetting * energy_ref[...] + (1.0 - covariance_forgetting) * grad * grad
    energy_out_ref[...] = energy
    coefficient_out_ref[...] = coefficient_ref[...] - vector_rate * grad / (
        jnp.sqrt(energy) + energy_epsilon
    )
    grad = table_ref[31:32, 0:HEAD_NUMBER]
    grad = grad.reshape(HEAD_NUMBER)
    energy = covariance_forgetting * sharp_energy_ref[...] + (1.0 - covariance_forgetting) * grad * grad
    sharp_grad_ref[...] = grad
    sharp_energy_out_ref[...] = energy
    sharp_out_ref[...] = sharp_ref[...] - sharpness_step_size * grad / (
        jnp.sqrt(energy) + energy_epsilon
    )
    for save in saves:
        save.wait()


def finish(
    places,
    table,
    energy,
    coefficients,
    sharpness,
    sharpness_energy,
    grads,
    slots,
    rows,
    left,
    right,
    masters,
    tokens,
):
    shape = jax.ShapeDtypeStruct
    return pl.pallas_call(
        finish_kernel,
        out_shape=(
            shape(grads.shape, F32),
            shape(left.shape, F32),
            shape(right.shape, F32),
            shape(masters.shape, F32),
            shape(masters.shape, BF16),
            shape(tokens.shape, BF16),
            shape(energy.shape, F32),
            shape(energy.shape, F32),
            shape(energy.shape, F32),
            shape(sharpness.shape, F32),
            shape(sharpness.shape, F32),
            shape(sharpness.shape, F32),
        ),
        in_specs=[SMEM_SPEC] + [VMEM_SPEC] * 5 + [ANY_SPEC] * 7,
        out_specs=(ANY_SPEC,) * 6 + (VMEM_SPEC,) * 6,
        scratch_shapes=[
            pltpu.VMEM(left.shape, F32),
            pltpu.VMEM(right.shape, F32),
            pltpu.VMEM(masters.shape, F32),
            pltpu.VMEM(masters.shape, BF16),
            pltpu.VMEM(tokens.shape, BF16),
            pltpu.VMEM(grads.shape, F32),
            pltpu.VMEM(slots.shape, BF16),
            pltpu.VMEM(rows.shape, BF16),
            pltpu.SemaphoreType.DMA((13,)),
        ],
        compiler_params=pltpu.CompilerParams(vmem_limit_bytes=VMEM_LIMIT),
        name="finish",
    )(
        places,
        table,
        energy,
        coefficients,
        sharpness,
        sharpness_energy,
        grads,
        slots,
        rows,
        left,
        right,
        masters,
        tokens,
    )


def shards(
    patch_embeddings,
    view_side_tokens,
    projection_masters,
    channel_coefficients,
    head_sharpness,
    output_adjoint,
    leading_covariance,
    trailing_covariance,
    leading_root_preconditioner,
    trailing_root_preconditioner,
    channel_energy_average,
    sharpness_energy_average,
    storage_position_map,
):
    row_count, feature_count = patch_embeddings.shape
    block_count = projection_masters.shape[0]
    shard_rows = projection_masters.shape[1]
    slot_count = leading_covariance.shape[0]
    counts = (lax.axis_size("dp"), lax.axis_size("fsdp"))
    direct = counts[0] == 4 and slot_count == 2 and shard_rows % 16 == 0
    if direct:
        mixing_blocks, table = gather_start(projection_masters, channel_coefficients, counts, 0)
        grad_shape = (2 * counts[1], (block_count - 4) // 2, shard_rows, feature_count)
    else:
        full_table = lax.all_gather(channel_coefficients.astype(BF16), "fsdp", axis=1, tiled=True)
        table = full_table.astype(F32)
        mixing_blocks = lax.all_gather(
            projection_masters[:4].astype(BF16), "fsdp", axis=1, tiled=True
        )
        grad_shape = (1, block_count - 4, feature_count, feature_count)
    feed_blocks = lax.all_gather(projection_masters[4:].astype(BF16), "fsdp", axis=1, tiled=True)

    x1, qkv, mixed, scores, attention, slope, e, sums = mixing_forward(
        view_side_tokens, head_sharpness, patch_embeddings, mixing_blocks, table
    )
    batch_sums = sum_all(sums, counts, 1) if direct else lax.psum(sums, ("dp", "fsdp"))
    layer_output, dx2, dn, feed_grad, feed_table, back_part = feed_forward(
        view_side_tokens, x1, e, batch_sums, feed_blocks, table, output_adjoint, grad_shape
    )
    if direct:
        back_sums, feed_grad = sum_pair(back_part, feed_grad, counts, 2)
        feed_grad = lax.all_to_all(feed_grad, "fsdp", 0, 0, tiled=True)
    else:
        back_sums = lax.psum(back_part, ("dp", "fsdp"))
    head_low, dx1, head_weights, mixing_grad, mixing_table = mixing_backward(
        view_side_tokens,
        head_sharpness,
        patch_embeddings,
        mixing_blocks,
        table,
        (x1, qkv, mixed, scores, attention, slope, e),
        batch_sums,
        dx2,
        dn,
        back_sums,
    )
    if direct:
        grads, owned_grad, my_rows, table_total, tokens_grad = settle(
            storage_position_map,
            mixing_grad,
            feed_grad,
            mixing_table,
            feed_table,
            leading_root_preconditioner,
            trailing_root_preconditioner,
            (head_low, dx1, patch_embeddings, head_weights),
            table,
            counts,
            3,
        )
        results = list(
            finish(
                storage_position_map,
                table_total,
                channel_energy_average,
                channel_coefficients,
                head_sharpness,
                sharpness_energy_average,
                grads,
                owned_grad,
                my_rows,
                leading_covariance,
                trailing_covariance,
                projection_masters,
                tokens_grad,
            )
        )
        tokens_grad = results.pop(5)
        return (layer_output, tokens_grad, *results)
    first_grad = dot_lanes(head_low, head_weights)
    unit, scale = centered(patch_embeddings.astype(F32))
    incoming_tokens_grad = (dx1 + norm_back(first_grad * table[0], unit, scale)).astype(BF16)
    mixing_table = mixing_table.at[0].set(jnp.sum(first_grad * unit, axis=0))
    mixing_table = mixing_table.at[1].set(jnp.sum(first_grad, axis=0))
    sharpness_share = mixing_table[14, 0:HEAD_NUMBER]
    table_grad = jnp.stack([(mixing_table, feed_table)[source][row] for source, row in TABLE_ROWS])
    block_grad = jnp.concatenate([mixing_grad, feed_grad[0]], axis=0).astype(F32)
    denominator_sum = lax.axis_size("fsdp")
    tiled_part = jnp.broadcast_to(
        sharpness_share[None, :], (denominator_sum, sharpness_share.shape[0])
    )
    portion_derivative, catalog_portion, sharpness_normalizer = (
        lax.psum_scatter(block_grad, "fsdp", scatter_dimension=1, tiled=True),
        lax.psum_scatter(table_grad, "fsdp", scatter_dimension=1, tiled=True),
        lax.psum_scatter(tiled_part, "fsdp", scatter_dimension=0, tiled=True),
    )
    portion_derivative, catalog_portion, sharpness_normalizer = lax.psum(
        (portion_derivative, catalog_portion, sharpness_normalizer), "dp"
    )
    sharpness_derivative = sharpness_normalizer[0]
    shard_place = lax.axis_index("fsdp")
    slot_index = jnp.arange(denominator_sum * slot_count, dtype=jnp.int32)
    slot_match = storage_position_map[None, :] == slot_index[:, None]
    slot_filled = jnp.any(slot_match, axis=1).astype(jnp.float32)[:, None, None]
    slot_block = jnp.sum(
        jnp.where(slot_match, jnp.arange(block_count, dtype=jnp.int32)[None, :], 0), axis=1
    )
    my_filled = lax.dynamic_slice_in_dim(slot_filled, shard_place * slot_count, slot_count, 0)
    my_block = lax.dynamic_slice_in_dim(slot_block, shard_place * slot_count, slot_count, 0)
    whole_grad = lax.all_gather(portion_derivative, "fsdp", axis=1, tiled=True)
    owned_grad = jnp.take(whole_grad, my_block, axis=0) * my_filled
    leading_covariance_renewed = covariance_forgetting * leading_covariance + (
        1.0 - covariance_forgetting
    ) * jnp.einsum("sij,skj->sik", owned_grad, owned_grad, precision=lax.Precision.HIGHEST)
    trailing_covariance_renewed = covariance_forgetting * trailing_covariance + (
        1.0 - covariance_forgetting
    ) * jnp.einsum("sji,sjk->sik", owned_grad, owned_grad, precision=lax.Precision.HIGHEST)
    halfway = jnp.einsum(
        "sij,sjk->sik", leading_root_preconditioner, owned_grad, precision=lax.Precision.HIGHEST
    )
    conditioned = jnp.einsum(
        "sij,sjk->sik", halfway, trailing_root_preconditioner, precision=lax.Precision.HIGHEST
    )
    every_update = lax.all_gather(conditioned, "fsdp", axis=0, tiled=True)
    my_rows = lax.dynamic_slice_in_dim(every_update, shard_place * shard_rows, shard_rows, 1)
    update = jnp.take(my_rows, storage_position_map, axis=0)
    projection_updated = projection_masters - weight_rate * update
    channel_energy_renewed = (
        covariance_forgetting * channel_energy_average
        + (1.0 - covariance_forgetting) * catalog_portion * catalog_portion
    )
    channel_params_updated = channel_coefficients - vector_rate * catalog_portion / (
        jnp.sqrt(channel_energy_renewed) + energy_epsilon
    )
    sharpness_energy_renewed = (
        covariance_forgetting * sharpness_energy_average
        + (1.0 - covariance_forgetting) * sharpness_derivative * sharpness_derivative
    )
    sharpness_updated = head_sharpness - sharpness_step_size * sharpness_derivative / (
        jnp.sqrt(sharpness_energy_renewed) + energy_epsilon
    )
    return (
        layer_output,
        incoming_tokens_grad,
        portion_derivative,
        leading_covariance_renewed,
        trailing_covariance_renewed,
        projection_updated,
        projection_updated.astype(jnp.bfloat16),
        catalog_portion,
        channel_energy_renewed,
        channel_params_updated,
        sharpness_derivative,
        sharpness_energy_renewed,
        sharpness_updated,
    )


def solution(mesh):
    in_specs = (
        P(("dp", "fsdp"), None),
        P(("dp", "fsdp")),
        P(None, "fsdp", None),
        P(None, "fsdp"),
        P(),
        P(("dp", "fsdp"), None),
        P("fsdp", None, None),
        P("fsdp", None, None),
        P("fsdp", None, None),
        P("fsdp", None, None),
        P(None, "fsdp"),
        P(),
        P(),
    )
    out_specs = (
        P(("dp", "fsdp"), None),
        P(("dp", "fsdp"), None),
        P(None, "fsdp", None),
        P("fsdp", None, None),
        P("fsdp", None, None),
        P(None, "fsdp", None),
        P(None, "fsdp", None),
        P(None, "fsdp"),
        P(None, "fsdp"),
        P(None, "fsdp"),
        P(),
        P(),
        P(),
    )
    return jax.shard_map(shards, mesh=mesh, in_specs=in_specs, out_specs=out_specs, check_vma=False)
```

```python
import functools

import jax
import jax.numpy as jnp
from jax import lax
from jax.experimental import pallas as pl
from jax.experimental.pallas import tpu as pltpu
from jax.sharding import PartitionSpec as P

HEAD_NUMBER = 8
HDIM = 48
HEAD_PAD = 64
LANES = 128
HEAD_PAIRS = HEAD_NUMBER // 2
PAD_WIDTH = HEAD_NUMBER * HEAD_PAD
HALF_WIDTH = PAD_WIDTH // 2
LEAD = 16
TAIL = 32
SMALL_SIDE = 6
SMALL_WINDOW = 48
LARGE_WINDOW = 208
CROP_GROUP = 2
SAVE_ROWS = 64
ROW_TILE = 464
HIDDEN_PARTS = 6
VMEM_LIMIT = 60 * 2**20

norm_epsilon = 1e-06
batch_epsilon = 1e-05
attention_epsilon = 1e-06
covariance_forgetting = 0.5
weight_rate = 0.5
vector_rate = 0.1
sharpness_step_size = 2.0
energy_epsilon = 1e-08

F32 = jnp.float32
BF16 = jnp.bfloat16
VMEM_SPEC = pl.BlockSpec(memory_space=pltpu.VMEM)
ANY_SPEC = pl.BlockSpec(memory_space=pl.ANY)
SMEM_SPEC = pl.BlockSpec(memory_space=pltpu.SMEM)


def dot(left, right):
    return lax.dot_general(left, right, (((1,), (0,)), ((), ())), preferred_element_type=F32)


def dot_rows(left, right):
    return lax.dot_general(left, right, (((0,), (0,)), ((), ())), preferred_element_type=F32)


def dot_lanes(left, right):
    return lax.dot_general(left, right, (((1,), (1,)), ((), ())), preferred_element_type=F32)


def split(values):
    high = values.astype(BF16)
    return high, (values - high.astype(F32)).astype(BF16)


def dot_split(product, left, right):
    if product is dot_rows:
        return product(
            jnp.concatenate([left[0], left[0], left[1]], axis=0),
            jnp.concatenate([right[0], right[1], right[0]], axis=0),
        )
    rows = left[0].shape[0]
    both = product(jnp.concatenate(left, axis=0), right[0])
    return both[:rows] + both[rows:] + product(left[0], right[1])


def fold(values):
    total = values[0:8]
    for first in range(8, values.shape[0], 8):
        total = total + values[first : first + 8]
    return total


def gelu_parts(values):
    magnitude = jnp.abs(values) * 0.7071067811865476
    base = 1.0 + 0.3275911 * magnitude
    guess = pl.reciprocal(base, approx=True)
    slot = guess * (2.0 - base * guess)
    series = slot * (
        0.127414796
        + slot
        * (-0.142248368 + slot * (0.7107068705 + slot * (-0.7265760135 + slot * 0.5307027145)))
    )
    bell = jnp.exp(-0.5 * values * values)
    lower = series * bell
    return jnp.where(values >= 0, 1.0 - lower, lower), bell


def gelu_slope(values, share, bell):
    return share + values * bell * 0.3989422804014327


def head_map(dtype):
    feature = lax.broadcasted_iota(jnp.int32, (HEAD_NUMBER * HDIM, PAD_WIDTH), 0)
    lane = lax.broadcasted_iota(jnp.int32, (HEAD_NUMBER * HDIM, PAD_WIDTH), 1)
    inner = lane & (HEAD_PAD - 1)
    hit = (inner < HDIM) & ((lane >> 6) * HDIM + inner == feature)
    return hit.astype(F32).astype(dtype)


def centered(values):
    center = jnp.sum(values, axis=-1, keepdims=True) * (1.0 / values.shape[-1])
    shifted = values - center
    spread = jnp.sum(shifted * shifted, axis=-1, keepdims=True) * (1.0 / values.shape[-1])
    scale = lax.rsqrt(spread + norm_epsilon)
    return shifted * scale, scale


def norm_back(grad, unit, scale):
    size = 1.0 / grad.shape[-1]
    middle = jnp.sum(grad, axis=-1, keepdims=True) * size
    slope = jnp.sum(grad * unit, axis=-1, keepdims=True) * size
    return scale * (grad - middle - unit * slope)


def tile_rows(count, least):
    for parts in range(least, count // 16 + 1):
        if count % (16 * parts) == 0:
            return count // parts
    return count


def for_rows(count, tile, step, carry=0):
    def body(index, carry):
        return step(pl.multiple_of(index * tile, tile), tile, carry)

    if count // tile == 1:
        carry = step(0, tile, carry)
    else:
        carry = lax.fori_loop(0, count // tile, body, carry)
    if count % tile:
        carry = step(count - count % tile, count % tile, carry)
    return carry


def row_copies(pairs, first, size, sem):
    rows = pl.ds(first, size)
    return [
        pltpu.make_async_copy(
            source.at[:, rows] if chunked else source.at[rows],
            target.at[:, rows] if chunked else target.at[rows],
            sem,
        )
        for source, target, chunked in pairs
    ]


def live_total(sides_ref):
    return lax.fori_loop(
        0, sides_ref.shape[0], lambda c, t: t + sides_ref[c] * sides_ref[c], jnp.int32(0)
    )


def row_mask(first, rows, width, limit):
    return lax.broadcasted_iota(jnp.int32, (rows, width), 0) + first < limit


def save_rows(source, target, sem, first, rows):
    rows = pl.ds(pl.multiple_of(first, 8), rows)
    pltpu.make_async_copy(source.at[:, rows], target.at[:, rows], sem).start()


def for_groups(sides_ref, step, carry, saves=()):
    def save(first, last):
        def body(part, _):
            for source, target, sem in saves:
                save_rows(source, target, sem, part * SAVE_ROWS, SAVE_ROWS)
            return 0

        if saves:
            lax.fori_loop(first, last, body, 0)
        return last

    def crop_body(crop, state):
        start, saved, carry = state
        side = sides_ref[crop]
        cells = side * side
        inverse = 1.0 / jnp.full((8, LANES), side, jnp.int32).astype(F32)
        lines = lax.broadcasted_iota(jnp.int32, (8, LANES), 0)

        def group_body(group, carry):
            for part in range(2):
                row = pl.multiple_of((group * 2 + part) * 8, 8)
                place = lines + (row - start)
                line = ((place.astype(F32) + 0.5) * inverse).astype(jnp.int32)
                column = place - line * side
                inside = (place >= 0) & (place < cells)
                masks = (
                    inside,
                    column >= 1,
                    column < side - 1,
                    place >= side,
                    place < cells - side,
                )
                carry = step(row, side, masks, carry)
            return carry

        carry = lax.fori_loop(start // 16, (start + cells + 15) // 16, group_body, carry)
        saved = save(saved, (start + cells) // 16 * 16 // SAVE_ROWS)
        return start + cells, saved, carry

    state = (jnp.int32(0), jnp.int32(0), carry)
    _, saved, carry = lax.fori_loop(0, sides_ref.shape[0], crop_body, state)
    for source, target, sem in saves:
        done = source.shape[1] // SAVE_ROWS * SAVE_ROWS
        if done < source.shape[1]:
            save_rows(source, target, sem, done, source.shape[1] - done)
    if saves:
        save(saved, saves[0][0].shape[1] // SAVE_ROWS)
    return carry


def conv_forward(source, chunk, row, side, masks, taps):
    inside, left_ok, right_ok, up_ok, down_ok = masks
    total = None
    for shift in (-1, 0, 1):
        base = LEAD + row + shift * side
        middle = source[chunk, pl.ds(base, 8), :]
        left = jnp.where(left_ok, source[chunk, pl.ds(base - 1, 8), :], 0.0)
        right = jnp.where(right_ok, source[chunk, pl.ds(base + 1, 8), :], 0.0)
        first = 3 * (shift + 1)
        value = taps[first] * left + taps[first + 1] * middle + taps[first + 2] * right
        if shift == -1:
            value = jnp.where(up_ok, value, 0.0)
        if shift == 1:
            value = jnp.where(down_ok, value, 0.0)
        total = value if total is None else total + value
    return total


def conv_backward(source, chunk, row, side, masks, taps, own, tap_sums):
    inside, left_ok, right_ok, up_ok, down_ok = masks
    total = None
    tap_sums = list(tap_sums)
    for shift in (-1, 0, 1):
        base = LEAD + row + shift * side
        row_ok = {-1: up_ok, 0: None, 1: down_ok}[shift]
        for sway in (-1, 0, 1):
            column_ok = {-1: left_ok, 0: None, 1: right_ok}[sway]
            value = source[chunk, pl.ds(base + sway, 8), :]
            keep = inside
            if row_ok is not None:
                keep = keep & row_ok
            if column_ok is not None:
                keep = keep & column_ok
            value = jnp.where(keep, value, 0.0)
            index = 3 * (1 - shift) + (1 - sway)
            term = taps[index] * value
            total = term if total is None else total + term
            tap_sums[index] = tap_sums[index] + own * value
    return total, tuple(tap_sums)


def chunk_lanes(chunk):
    return slice(chunk * LANES, (chunk + 1) * LANES)


def tap_vectors(table_ref, first, chunk):
    return [
        jnp.broadcast_to(table_ref[first + k : first + k + 1, chunk_lanes(chunk)], (8, LANES))
        for k in range(9)
    ]


def for_crops(sides_ref, row_count, order_ref, start_ref, step):
    crops = sides_ref.shape[0]

    def scan(crop, state):
        start, large, small = state
        side = sides_ref[crop]
        start_ref[crop] = start
        is_small = side <= SMALL_SIDE
        order_ref[jnp.where(is_small, crops + small, large)] = crop
        return (
            start + side * side,
            large + jnp.where(is_small, 0, 1),
            small + jnp.where(is_small, 1, 0),
        )

    zero = jnp.int32(0)
    _, large, small = lax.fori_loop(0, crops, scan, (zero, zero, zero))
    for window, first, count in ((LARGE_WINDOW, 0, large), (SMALL_WINDOW, crops, small)):

        def group_body(group, _, window=window, first=first, count=count):
            members = []
            for member in range(CROP_GROUP):
                crop = order_ref[first + jnp.minimum(group * CROP_GROUP + member, count - 1)]
                start = start_ref[crop]
                side = sides_ref[crop]
                row = pl.multiple_of(jnp.minimum(start // 8, (row_count - window) // 8) * 8, 8)
                place = lax.broadcasted_iota(jnp.int32, (window, HALF_WIDTH), 0) + (row - start)
                members.append((crop, pl.ds(row, window), (place >= 0) & (place < side * side)))
            step(members)
            return 0

        lax.fori_loop(0, (count + CROP_GROUP - 1) // CROP_GROUP, group_body, 0)


def half_lanes(half):
    starts = [part * PAD_WIDTH + half * HALF_WIDTH for part in range(3)]
    return [slice(start, start + HALF_WIDTH) for start in starts]


def pair_lanes():
    return lax.broadcasted_iota(jnp.int32, (HDIM, LANES), 1) < HEAD_PAD


def pair_part(block, pair):
    first = pair * LANES
    lanes = slice(first, first + LANES)
    return jnp.where(
        pair_lanes(),
        block[first : first + HDIM, lanes],
        block[first + HEAD_PAD : first + HEAD_PAD + HDIM, lanes],
    )


def spread_pair(target, member, half, pair, values):
    first = pair * LANES
    lanes = slice(first, first + LANES)
    parts = split(values)
    for index in range(2):
        value = parts[index].astype(F32)
        target[member, half, index, first : first + HDIM, lanes] = jnp.where(
            pair_lanes(), value, 0.0
        ).astype(BF16)
        target[member, half, index, first + HEAD_PAD : first + HEAD_PAD + HDIM, lanes] = jnp.where(
            pair_lanes(), 0.0, value
        ).astype(BF16)


def pair_sharpness(sharp_ref, pair):
    lane = lax.broadcasted_iota(jnp.int32, (1, LANES), 1)
    return jnp.where(lane < HEAD_PAD, sharp_ref[2 * pair], sharp_ref[2 * pair + 1])


def units(values):
    scale = lax.rsqrt(jnp.sum(values * values, axis=0, keepdims=True) + attention_epsilon)
    return values * scale, scale


def mixing_forward_kernel(
    sides_ref,
    sharp_ref,
    input_ref,
    weight_ref,
    table_ref,
    x1_hbm,
    qkv_hbm,
    mixed_hbm,
    scores_hbm,
    attention_hbm,
    slope_hbm,
    e_hbm,
    sums_ref,
    x1_ref,
    qkv_ref,
    mixed_ref,
    scores_ref,
    attention_ref,
    slope_ref,
    e_ref,
    head_weights,
    out_weight,
    first_low,
    mixed,
    attention_out,
    conv_in,
    spread,
    order_ref,
    start_ref,
    sems,
):
    row_count, width = input_ref.shape
    chunks = width // LANES
    tile = tile_rows(row_count, 2)
    saves = [
        pltpu.make_async_copy(source, target, sems.at[index])
        for index, (source, target) in enumerate(
            (
                (qkv_ref, qkv_hbm),
                (scores_ref, scores_hbm),
                (attention_ref, attention_hbm),
                (mixed_ref, mixed_hbm),
                (x1_ref, x1_hbm),
                (slope_ref, slope_hbm),
                (e_ref, e_hbm),
            )
        )
    ]
    total_live = live_total(sides_ref)
    mapping = head_map(BF16)
    for part in range(3):
        head_weights[:, part * PAD_WIDTH : (part + 1) * PAD_WIDTH] = dot(
            weight_ref[part], mapping
        ).astype(BF16)
    spread[...] = jnp.zeros_like(spread)

    def first_norm(first, size, _):
        rows = pl.ds(first, size)
        unit, _ = centered(input_ref[rows, :].astype(F32))
        first_low[rows, :] = (unit * table_ref[0:1, :] + table_ref[1:2, :]).astype(BF16)
        mixed[rows, :] = jnp.zeros((size, PAD_WIDTH), F32)
        return 0

    for_rows(row_count, ROW_TILE, first_norm)

    @pl.loop(0, row_count // tile)
    def _(step):
        rows = pl.ds(pl.multiple_of(step * tile, 16), tile)
        for part in range(3):
            lanes = slice(part * PAD_WIDTH, (part + 1) * PAD_WIDTH)
            qkv_ref[rows, lanes] = dot(first_low[rows, :], head_weights[:, lanes])

    saves[0].start()

    def crop_step(members):
        units_of = [(member, half) for member in range(len(members)) for half in range(2)]
        blocks, results = [], []
        for member, half in units_of:
            crop, rows, keep = members[member]
            lanes = half_lanes(half)
            query = units(jnp.where(keep, qkv_ref[rows, lanes[0]], 0.0))[0]
            key = units(jnp.where(keep, qkv_ref[rows, lanes[1]], 0.0))[0]
            blocks.append(dot_split(dot_rows, split(key), split(query)))
        for (member, half), block in zip(units_of, blocks):
            crop = members[member][0]
            for pair in range(2):
                scores = pair_part(block, pair)
                scores_ref[crop, 2 * half + pair] = scores
                scores = scores * pair_sharpness(sharp_ref, 2 * half + pair)
                scores = jnp.exp(scores - jnp.max(scores, axis=0, keepdims=True))
                shares = scores / jnp.sum(scores, axis=0, keepdims=True)
                attention_ref[crop, 2 * half + pair] = shares
                spread_pair(spread, member, half, pair, shares)
        for member, half in units_of:
            rows = members[member][1]
            shares = (spread[member, half, 0], spread[member, half, 1])
            results.append(dot_split(dot, split(qkv_ref[rows, half_lanes(half)[2]]), shares))
        for (member, half), result in zip(units_of, results):
            _, rows, keep = members[member]
            lanes = half_lanes(half)[0]
            mixed[rows, lanes] = jnp.where(keep, result, mixed[rows, lanes])

    for_crops(sides_ref, row_count, order_ref, start_ref, crop_step)

    saves[1].start()
    saves[2].start()
    out_weight[...] = dot_rows(mapping, weight_ref[3]).astype(BF16)

    @pl.loop(0, row_count // tile)
    def _(step):
        rows = pl.ds(pl.multiple_of(step * tile, 16), tile)
        low = mixed[rows, :].astype(BF16)
        mixed_ref[rows, :] = low
        attention_out[rows, :] = dot(low, out_weight[...])

    saves[3].start()

    def second_norm(first, size, _):
        rows = pl.ds(first, size)
        value = input_ref[rows, :].astype(F32) + table_ref[2:3, :] * attention_out[rows, :]
        x1_ref[rows, :] = value
        unit, _ = centered(value)
        value = unit * table_ref[3:4, :] + table_ref[4:5, :]
        for chunk in range(chunks):
            conv_in[chunk, pl.ds(LEAD + first, size), :] = value[:, chunk_lanes(chunk)]
            slope_ref[chunk, rows, :] = jnp.zeros((size, LANES), F32)
            e_ref[chunk, rows, :] = jnp.zeros((size, LANES), F32)
        return 0

    for_rows(row_count, ROW_TILE, second_norm)
    saves[4].start()

    zero = jnp.zeros((8, LANES), F32)
    sums_ref[...] = zero
    taps = [tap_vectors(table_ref, 11, chunk) for chunk in range(chunks)]

    def conv_step(row, side, masks, carry):
        rows = pl.ds(row, 8)
        carry = list(carry)
        for chunk in range(chunks):
            value = conv_forward(conv_in, chunk, row, side, masks, taps[chunk])
            share, bell = gelu_parts(value)
            active = value * share
            slope = gelu_slope(value, share, bell)
            slope_ref[chunk, rows, :] = jnp.where(masks[0], slope, slope_ref[chunk, rows, :])
            e_ref[chunk, rows, :] = jnp.where(masks[0], active, e_ref[chunk, rows, :])
            active = jnp.where(masks[0], active, 0.0)
            carry[chunk] = carry[chunk] + active
            carry[chunks + chunk] = carry[chunks + chunk] + active * active
        return tuple(carry)

    sums = for_groups(
        sides_ref,
        conv_step,
        (zero,) * (2 * chunks),
        ((slope_ref, slope_hbm, sems.at[5]), (e_ref, e_hbm, sems.at[6])),
    )
    for index, value in enumerate(sums):
        sums_ref[index : index + 1, :] = jnp.sum(value, axis=0, keepdims=True)
    sums_ref[2 * chunks : 2 * chunks + 1, :] = jnp.full((1, LANES), total_live, jnp.int32).astype(F32)
    for save in saves:
        save.wait()


def mixing_forward(sides, sharpness, inputs, weights, table):
    row_count, width = inputs.shape
    crops = sides.shape[0]
    chunks = width // LANES
    shape = jax.ShapeDtypeStruct
    return pl.pallas_call(
        mixing_forward_kernel,
        out_shape=(
            shape((row_count, width), F32),
            shape((row_count, 3 * PAD_WIDTH), F32),
            shape((row_count, PAD_WIDTH), BF16),
            shape((crops, HEAD_PAIRS, HDIM, LANES), F32),
            shape((crops, HEAD_PAIRS, HDIM, LANES), F32),
            shape((chunks, row_count, LANES), F32),
            shape((chunks, row_count, LANES), F32),
            shape((8, LANES), F32),
        ),
        in_specs=[SMEM_SPEC, SMEM_SPEC, VMEM_SPEC, VMEM_SPEC, VMEM_SPEC],
        out_specs=(ANY_SPEC,) * 7 + (VMEM_SPEC,),
        scratch_shapes=[
            pltpu.VMEM((row_count, width), F32),
            pltpu.VMEM((row_count, 3 * PAD_WIDTH), F32),
            pltpu.VMEM((row_count, PAD_WIDTH), BF16),
            pltpu.VMEM((crops, HEAD_PAIRS, HDIM, LANES), F32),
            pltpu.VMEM((crops, HEAD_PAIRS, HDIM, LANES), F32),
            pltpu.VMEM((chunks, row_count, LANES), F32),
            pltpu.VMEM((chunks, row_count, LANES), F32),
            pltpu.VMEM((width, 3 * PAD_WIDTH), BF16),
            pltpu.VMEM((PAD_WIDTH, width), BF16),
            pltpu.VMEM((row_count, width), BF16),
            pltpu.VMEM((row_count, PAD_WIDTH), F32),
            pltpu.VMEM((row_count, width), F32),
            pltpu.VMEM((chunks, LEAD + row_count + TAIL, LANES), F32),
            pltpu.VMEM((CROP_GROUP, 2, 2, HALF_WIDTH, HALF_WIDTH), BF16),
            pltpu.SMEM((2 * crops,), jnp.int32),
            pltpu.SMEM((crops,), jnp.int32),
            pltpu.SemaphoreType.DMA((7,)),
        ],
        compiler_params=pltpu.CompilerParams(vmem_limit_bytes=VMEM_LIMIT),
        name="mixing_forward",
    )(sides, sharpness, inputs, weights, table)


def batch_vectors(bn_ref, chunk, chunks):
    count = bn_ref[2 * chunks : 2 * chunks + 1, :]
    mean = bn_ref[chunk : chunk + 1, :] / count
    scale = lax.rsqrt(bn_ref[chunks + chunk : chunks + chunk + 1, :] / count - mean * mean + batch_epsilon)
    return mean, scale


def feed_kernel(
    sides_ref,
    x1_hbm,
    e_hbm,
    bn_ref,
    weight_hbm,
    table_ref,
    adjoint_hbm,
    out_hbm,
    dx2_hbm,
    dn_hbm,
    weight_grad_hbm,
    grads_ref,
    back_sums_ref,
    e_ref,
    x1_ref,
    weight_ref,
    adjoint_ref,
    out_ref,
    dx2_ref,
    dn_ref,
    weight_grad_ref,
    up_weight,
    n_ref,
    z_ref,
    dw_ref,
    x2,
    unit,
    spread,
    third_low,
    hidden_low,
    feed,
    third_grad,
    feed_grad,
    pre_grad,
    grads,
    up_sum,
    down_sum,
    weight_low,
    sems,
    tile_sems,
):
    loads = [
        pltpu.make_async_copy(source, target, sems.at[index])
        for index, (source, target) in enumerate(
            (
                (x1_hbm, x1_ref),
                (weight_hbm, weight_ref),
                (adjoint_hbm, adjoint_ref),
            )
        )
    ]
    saves = [
        pltpu.make_async_copy(source, target, sems.at[4 + index])
        for index, (source, target) in enumerate(
            (
                (out_ref, out_hbm),
                (dx2_ref, dx2_hbm),
                (weight_grad_ref, weight_grad_hbm),
                (dn_ref, dn_hbm),
            )
        )
    ]

    tiled = [(e_hbm, e_ref, True)]

    def start_tile(first, size, _):
        for load in row_copies(tiled, first, size, tile_sems.at[lax.div(first, ROW_TILE)]):
            load.start()
        return 0

    for_rows(x1_hbm.shape[0], ROW_TILE, start_tile)
    for load in loads:
        load.start()
    row_count, width = x1_ref.shape
    chunks = width // LANES
    expand = weight_ref.shape[0] // 2
    tile = tile_rows(row_count, 4)
    total_live = live_total(sides_ref)
    hidden = expand * width
    batch = [batch_vectors(bn_ref, chunk, chunks) for chunk in range(chunks)]
    zero = jnp.zeros((8, LANES), F32)

    def down_weight():
        return weight_ref[expand : 2 * expand].reshape(hidden, width)

    def normalize(first, size, _):
        for load in row_copies(tiled, first, size, tile_sems.at[lax.div(first, ROW_TILE)]):
            load.wait()
        rows = pl.ds(first, size)
        live = row_mask(first, size, LANES, total_live)
        for chunk in range(chunks):
            lanes = chunk_lanes(chunk)
            mean, scale = batch[chunk]
            value = (e_ref[chunk, rows, :] - mean) * scale
            value = value * table_ref[5:6, lanes] + table_ref[6:7, lanes]
            n_ref[chunk, pl.ds(LEAD + first, size), :] = jnp.where(live, value, 0.0)
            z_ref[chunk, rows, :] = jnp.zeros((size, LANES), F32)
            dn_ref[chunk, rows, :] = jnp.zeros((size, LANES), F32)
        return 0

    for_rows(row_count, ROW_TILE, normalize)

    taps = [tap_vectors(table_ref, 20, chunk) for chunk in range(chunks)]

    def conv_step(row, side, masks, carry):
        rows = pl.ds(row, 8)
        for chunk in range(chunks):
            value = conv_forward(n_ref, chunk, row, side, masks, taps[chunk])
            z_ref[chunk, rows, :] = jnp.where(masks[0], value, z_ref[chunk, rows, :])
        return carry

    for_groups(sides_ref, conv_step, 0)

    for load in loads:
        load.wait()
    for part in range(expand):
        up_weight[:, part * width : (part + 1) * width] = weight_ref[part]
    up_sum[...] = jnp.zeros_like(up_sum)
    down_sum[...] = jnp.zeros_like(down_sum)
    grads[...] = jnp.zeros_like(grads)

    def z_rows(rows):
        return jnp.concatenate([z_ref[chunk, rows, :] for chunk in range(chunks)], axis=1)

    def before(base):
        rows = pl.ds(base, tile)
        value = x1_ref[rows, :] + table_ref[7:8, :] * z_rows(rows)
        x2[...] = value
        value, scale = centered(value)
        unit[...] = value
        spread[...] = jnp.broadcast_to(scale, (tile, LANES))
        third_low[...] = (value * table_ref[8:9, :] + table_ref[9:10, :]).astype(BF16)
        feed_grad[...] = (entry_rows(base) * table_ref[10:11, :]).astype(BF16)

    def entry_rows(base):
        live = row_mask(base, tile, width, total_live)
        return jnp.where(live, adjoint_ref[pl.ds(base, tile), :].astype(F32), 0.0)

    @pl.loop(0, row_count // tile)
    def _(step):
        base = pl.multiple_of(step * tile, 16)
        rows = pl.ds(base, tile)
        before(base)

        def hidden_lanes(part):
            return slice(part * hidden // HIDDEN_PARTS, (part + 1) * hidden // HIDDEN_PARTS)

        def products(part):
            lanes = hidden_lanes(part)
            return (
                dot(third_low[...], up_weight[:, lanes]),
                dot_lanes(feed_grad[...], down_weight()[lanes]),
            )

        ahead = products(0)
        for part in range(HIDDEN_PARTS):
            lanes = hidden_lanes(part)
            value, hidden_grad = ahead
            if part + 1 < HIDDEN_PARTS:
                ahead = products(part + 1)
            share, bell = gelu_parts(value)
            hidden_low[:, lanes] = (value * share).astype(BF16)
            pre_grad[:, lanes] = (hidden_grad * gelu_slope(value, share, bell)).astype(BF16)
        feed[...] = dot(hidden_low[...], down_weight())
        third_grad[...] = dot_lanes(pre_grad[...], up_weight[...])
        down_sum[...] += dot_rows(feed_grad[...], hidden_low[...])
        up_sum[...] += dot_rows(third_low[...], pre_grad[...])

        value = x2[...] + table_ref[10:11, :] * feed[...]
        live = row_mask(base, tile, width, total_live)
        out_ref[rows, :] = jnp.where(live, value, 0.0).astype(BF16)
        entry = entry_rows(base)
        grads[0] += fold(entry * feed[...])
        grad = third_grad[...]
        value = unit[...]
        total = entry + norm_back(grad * table_ref[8:9, :], value, spread[:, 0:1])
        dx2_ref[rows, :] = total
        scaled = total * table_ref[7:8, :]
        for chunk in range(chunks):
            dw_ref[chunk, pl.ds(LEAD + base, tile), :] = scaled[:, chunk_lanes(chunk)]
        grads[1] += fold(total * z_rows(rows))
        grads[2] += fold(grad * value)
        grads[3] += fold(grad)

    saves[0].start()
    saves[1].start()

    for part in range(expand):
        lanes = slice(part * width, (part + 1) * width)
        weight_low[part] = up_sum[:, lanes].astype(BF16)
        weight_low[expand + part] = down_sum[:, lanes].T.astype(BF16)

    owners, pieces, shard, _ = weight_grad_ref.shape
    inner = width // shard
    for owner in range(owners):
        rows = slice(owner % inner * shard, (owner % inner + 1) * shard)
        for piece in range(pieces):
            weight_grad_ref[owner, piece] = weight_low[owner // inner * pieces + piece, rows, :]

    saves[2].start()

    back_sums_ref[...] = zero
    for index, source in enumerate((1, 2, 3, 0)):
        grads_ref[index : index + 1, :] = jnp.sum(grads[source], axis=0, keepdims=True)
    def back_step(row, side, masks, carry):
        rows = pl.ds(row, 8)
        result = []
        for chunk in range(chunks):
            mean, scale = batch[chunk]
            sums = carry[chunk]
            own = jnp.where(masks[0], n_ref[chunk, pl.ds(LEAD + row, 8), :], 0.0)
            total, tap_sums = conv_backward(
                dw_ref, chunk, row, side, masks, taps[chunk], own, sums[0:9]
            )
            dn_ref[chunk, rows, :] = jnp.where(masks[0], total, dn_ref[chunk, rows, :])
            total = jnp.where(masks[0], total, 0.0)
            standard = (e_ref[chunk, rows, :] - mean) * scale
            result.append((*tap_sums, sums[9] + total * standard, sums[10] + total))
        return tuple(result)

    sums = for_groups(
        sides_ref, back_step, ((zero,) * 11,) * chunks, ((dn_ref, dn_hbm, sems.at[7]),)
    )
    for chunk in range(chunks):
        lanes = chunk_lanes(chunk)
        for index, value in enumerate(sums[chunk]):
            value = jnp.sum(value, axis=0, keepdims=True)
            grads_ref[4 + index : 5 + index, lanes] = value
            if index == 9:
                back_sums_ref[chunks + chunk : chunks + chunk + 1, :] = value
            if index == 10:
                back_sums_ref[chunk : chunk + 1, :] = value
    for save in saves:
        save.wait()


def feed_forward(sides, x1, e, batch_sums, weights, table, adjoint, grad_shape):
    row_count, width = x1.shape
    chunks = width // LANES
    expand = weights.shape[0] // 2
    tile = tile_rows(row_count, 4)
    shape = jax.ShapeDtypeStruct
    return pl.pallas_call(
        feed_kernel,
        out_shape=(
            shape((row_count, width), BF16),
            shape((row_count, width), F32),
            shape((chunks, row_count, LANES), F32),
            shape(grad_shape, BF16),
            shape((16, width), F32),
            shape((8, LANES), F32),
        ),
        in_specs=[SMEM_SPEC, ANY_SPEC, ANY_SPEC, VMEM_SPEC, ANY_SPEC, VMEM_SPEC, ANY_SPEC],
        out_specs=(ANY_SPEC,) * 4 + (VMEM_SPEC,) * 2,
        scratch_shapes=[
            pltpu.VMEM((chunks, row_count, LANES), F32),
            pltpu.VMEM((row_count, width), F32),
            pltpu.VMEM(weights.shape, BF16),
            pltpu.VMEM((row_count, width), BF16),
            pltpu.VMEM((row_count, width), BF16),
            pltpu.VMEM((row_count, width), F32),
            pltpu.VMEM((chunks, row_count, LANES), F32),
            pltpu.VMEM(grad_shape, BF16),
            pltpu.VMEM((width, expand * width), BF16),
            pltpu.VMEM((chunks, LEAD + row_count + TAIL, LANES), F32),
            pltpu.VMEM((chunks, row_count, LANES), F32),
            pltpu.VMEM((chunks, LEAD + row_count + TAIL, LANES), F32),
            pltpu.VMEM((tile, width), F32),
            pltpu.VMEM((tile, width), F32),
            pltpu.VMEM((tile, LANES), F32),
            pltpu.VMEM((tile, width), BF16),
            pltpu.VMEM((tile, expand * width), BF16),
            pltpu.VMEM((tile, width), F32),
            pltpu.VMEM((tile, width), F32),
            pltpu.VMEM((tile, width), BF16),
            pltpu.VMEM((tile, expand * width), BF16),
            pltpu.VMEM((4, 8, width), F32),
            pltpu.VMEM((width, expand * width), F32),
            pltpu.VMEM((width, expand * width), F32),
            pltpu.VMEM(weights.shape, BF16),
            pltpu.SemaphoreType.DMA((8,)),
            pltpu.SemaphoreType.DMA(((row_count + ROW_TILE - 1) // ROW_TILE,)),
        ],
        compiler_params=pltpu.CompilerParams(vmem_limit_bytes=VMEM_LIMIT),
        name="feed_forward",
    )(sides, x1, e, batch_sums, weights, table, adjoint)


def mixing_backward_kernel(
    sides_ref,
    sharp_ref,
    input_hbm,
    weight_ref,
    table_ref,
    x1_hbm,
    qkv_hbm,
    mixed_hbm,
    scores_hbm,
    attention_hbm,
    slope_hbm,
    e_hbm,
    bn_ref,
    dx2_hbm,
    dn_hbm,
    back_ref,
    head_low_hbm,
    dx1_hbm,
    head_weights_hbm,
    weight_grad_ref,
    grads_ref,
    x1_ref,
    qkv_ref,
    mixed_ref,
    scores_ref,
    attention_ref,
    dx2_ref,
    head_weights,
    out_weight,
    pool,
    conv_grad,
    mixed_grad,
    first_low,
    head_low,
    spread,
    out_sum,
    head_sum,
    sharp_sums,
    order_ref,
    start_ref,
    load_sems,
    tile_sems,
):
    row_count, width = input_hbm.shape
    low_rows, input_ref = head_low.at[:, 0:width], head_low.at[:, PAD_WIDTH : PAD_WIDTH + width]
    tile = tile_rows(row_count, 2)
    input_load = pltpu.make_async_copy(input_hbm, input_ref, load_sems.at[11 + row_count // tile])
    input_load.start()
    chunks = width // LANES
    slope_ref, e_ref = pool.at[0:chunks], pool.at[chunks : 2 * chunks]
    dn_ref, conv_in = pool.at[2 * chunks : 3 * chunks], pool.at[3 * chunks : 4 * chunks]
    attention_out = slope_ref
    loads = [
        pltpu.make_async_copy(source, target, load_sems.at[index])
        for index, (source, target) in enumerate(
            (
                (mixed_hbm, mixed_ref),
                (dx2_hbm, dx2_ref),
                (qkv_hbm, qkv_ref),
                (scores_hbm, scores_ref),
                (attention_hbm, attention_ref),
            )
        )
    ]
    saves = [
        pltpu.make_async_copy(source, target, load_sems.at[len(loads) + index])
        for index, (source, target) in enumerate(
            (
                (head_weights, head_weights_hbm),
                (dx2_ref, dx1_hbm),
            )
        )
    ]
    for step in range(row_count // tile):
        rows = pl.ds(step * tile, tile)
        saves.append(
            pltpu.make_async_copy(
                head_low.at[rows], head_low_hbm.at[rows], load_sems.at[len(loads) + 3 + step]
            )
        )
    tiled = [
        (x1_hbm, x1_ref, False),
        (slope_hbm, slope_ref, True),
        (e_hbm, e_ref, True),
        (dn_hbm, dn_ref, True),
    ]

    def start_tile(first, size, _):
        for load in row_copies(tiled, first, size, tile_sems.at[lax.div(first, ROW_TILE)]):
            load.start()
        return 0

    for_rows(row_count, ROW_TILE, start_tile)
    for load in loads:
        load.start()
    tile = tile_rows(row_count, 2)
    total_live = live_total(sides_ref)
    batch = [batch_vectors(bn_ref, chunk, chunks) for chunk in range(chunks)]
    zero = jnp.zeros((8, LANES), F32)
    wide = jnp.zeros((8, width), F32)
    mapping = head_map(BF16)
    for part in range(3):
        head_weights[:, part * PAD_WIDTH : (part + 1) * PAD_WIDTH] = dot(
            weight_ref[part], mapping
        ).astype(BF16)
    saves[0].start()
    out_weight[...] = dot_rows(mapping, weight_ref[3]).astype(BF16)
    spread[...] = jnp.zeros_like(spread)

    def first_norm(first, size, _):
        rows = pl.ds(first, size)
        unit, _ = centered(input_ref[rows, :].astype(F32))
        first_low[rows, :] = (unit * table_ref[0:1, :] + table_ref[1:2, :]).astype(BF16)
        return 0

    input_load.wait()
    for_rows(row_count, ROW_TILE, first_norm)


    def batch_back(first, size, _):
        for load in row_copies(tiled, first, size, tile_sems.at[lax.div(first, ROW_TILE)]):
            load.wait()
        rows = pl.ds(first, size)
        live = row_mask(first, size, LANES, total_live)
        unit, _ = centered(x1_ref[rows, :])
        value = unit * table_ref[3:4, :] + table_ref[4:5, :]
        for chunk in range(chunks):
            lanes = chunk_lanes(chunk)
            mean, scale = batch[chunk]
            count = bn_ref[2 * chunks : 2 * chunks + 1, :]
            standard = (e_ref[chunk, rows, :] - mean) * scale
            inner = (
                back_ref[chunk : chunk + 1, :]
                + standard * back_ref[chunks + chunk : chunks + chunk + 1, :]
            ) / count
            grad = scale * table_ref[5:6, lanes] * (dn_ref[chunk, rows, :] - inner)
            grad = grad * slope_ref[chunk, rows, :]
            conv_grad[chunk, pl.ds(LEAD + first, size), :] = jnp.where(live, grad, 0.0)
            conv_in[chunk, pl.ds(first, size), :] = value[:, lanes]
        return 0

    for_rows(row_count, ROW_TILE, batch_back)

    taps = [tap_vectors(table_ref, 11, chunk) for chunk in range(chunks)]

    def back_step(row, side, masks, carry):
        rows = pl.ds(row, 8)
        result = []
        for chunk in range(chunks):
            held = conv_in[chunk, rows, :]
            own = jnp.where(masks[0], held, 0.0)
            total, tap_sums = conv_backward(
                conv_grad, chunk, row, side, masks, taps[chunk], own, carry[chunk]
            )
            conv_in[chunk, rows, :] = jnp.where(masks[0], total, held)
            result.append(tap_sums)
        return tuple(result)

    tap_sums = for_groups(sides_ref, back_step, ((zero,) * 9,) * chunks)
    for chunk in range(chunks):
        for index, value in enumerate(tap_sums[chunk]):
            grads_ref[5 + index : 6 + index, chunk_lanes(chunk)] = jnp.sum(
                value, axis=0, keepdims=True
            )

    for load in loads[0:2]:
        load.wait()

    @pl.loop(0, row_count // tile)
    def _(step):
        rows = pl.ds(pl.multiple_of(step * tile, 16), tile)
        result = dot(mixed_ref[rows, :], out_weight[...])
        for chunk in range(chunks):
            attention_out[chunk, rows, :] = result[:, chunk_lanes(chunk)]

    def second_back(first, size, carry):
        rows = pl.ds(first, size)
        live = row_mask(first, size, width, total_live)
        grad = jnp.concatenate([conv_in[chunk, rows, :] for chunk in range(chunks)], axis=1)
        grad = jnp.where(live, grad, 0.0)
        unit, scale = centered(x1_ref[rows, :])
        total = dx2_ref[rows, :] + norm_back(grad * table_ref[3:4, :], unit, scale)
        dx2_ref[rows, :] = total
        low_rows[rows, :] = (total * table_ref[2:3, :]).astype(BF16)
        held = jnp.concatenate([attention_out[chunk, rows, :] for chunk in range(chunks)], axis=1)
        return (
            carry[0] + fold(total * held),
            carry[1] + fold(grad * unit),
            carry[2] + fold(grad),
        )

    sums = for_rows(row_count, ROW_TILE, second_back, (wide, wide, wide))
    saves[1].start()
    for index in range(3):
        grads_ref[2 + index : 3 + index, :] = jnp.sum(sums[index], axis=0, keepdims=True)

    out_sum[...] = jnp.zeros_like(out_sum)

    @pl.loop(0, row_count // tile)
    def _(step):
        rows = pl.ds(pl.multiple_of(step * tile, 16), tile)
        mixed_grad[rows, :] = dot_lanes(low_rows[rows, :], out_weight[...])
        out_sum[...] += dot_rows(mixed_ref[rows, :], low_rows[rows, :])

    pool[...] = jnp.zeros_like(pool)

    low = out_sum[...].astype(BF16)
    weight_grad_ref[3] = dot(mapping, low).astype(BF16)
    sharp_sums[...] = jnp.zeros_like(sharp_sums)

    for load in loads[2:]:
        load.wait()

    def crop_step(members):
        units_of = [(member, half) for member in range(len(members)) for half in range(2)]
        grads, blocks, sums, results = [], [], [], []
        for member, half in units_of:
            crop, rows, keep = members[member]
            lanes = half_lanes(half)
            value = split(jnp.where(keep, qkv_ref[rows, lanes[2]], 0.0))
            grad = split(jnp.where(keep, mixed_grad[rows, lanes[0]], 0.0))
            grads.append(grad)
            blocks.append(dot_split(dot_rows, value, grad))
        value_grads = []
        for index, (member, half) in enumerate(units_of):
            for pair in range(2):
                shares = attention_ref[members[member][0], 2 * half + pair]
                spread_pair(spread, member, half, pair, shares)
            shares = (spread[member, half, 0], spread[member, half, 1])
            value_grads.append(dot_split(dot_lanes, grads[index], shares))
        for (member, half), block in zip(units_of, blocks):
            crop = members[member][0]
            query_sums = []
            for pair in range(2):
                index = 2 * half + pair
                shares = attention_ref[crop, index]
                scores = scores_ref[crop, index]
                part = pair_part(block, pair)
                part = shares * (part - jnp.sum(part * shares, axis=0, keepdims=True))
                total = jnp.sum(part * scores, axis=0, keepdims=True)
                sharp_sums[index, pl.ds(crop, 1), :] = total
                sharpness = pair_sharpness(sharp_ref, index)
                query_sums.append(total * sharpness)
                spread_pair(spread, member, 2 + half, pair, part * sharpness)
            sums.append(jnp.concatenate(query_sums, axis=1))
        for index, (member, half) in enumerate(units_of):
            crop, rows, keep = members[member]
            lanes = half_lanes(half)
            query, query_scale = units(jnp.where(keep, qkv_ref[rows, lanes[0]], 0.0))
            key, key_scale = units(jnp.where(keep, qkv_ref[rows, lanes[1]], 0.0))
            slopes = (spread[member, 2 + half, 0], spread[member, 2 + half, 1])
            query_grad = dot_split(dot, split(key), slopes)
            query_grad = query_scale * (query_grad - query * sums[index])
            key_grad = dot_split(dot_lanes, split(query), slopes)
            key_grad = key_scale * (
                key_grad - key * jnp.sum(key_grad * key, axis=0, keepdims=True)
            )
            results.append((query_grad, key_grad, value_grads[index]))
        for (member, half), grads in zip(units_of, results):
            _, rows, keep = members[member]
            for part, result in enumerate(grads):
                for side in range(HALF_WIDTH // LANES):
                    chunk = (part * PAD_WIDTH + half * HALF_WIDTH) // LANES + side
                    pool[chunk, rows, :] = jnp.where(
                        keep[:, 0:LANES], result[:, chunk_lanes(side)], pool[chunk, rows, :]
                    )

    for_crops(sides_ref, row_count, order_ref, start_ref, crop_step)

    grads_ref[0:2, :] = jnp.zeros((2, width), F32)
    grads_ref[14:16, :] = jnp.zeros((2, width), F32)
    lane = lax.broadcasted_iota(jnp.int32, (1, LANES), 1)
    total = jnp.zeros((1, LANES), F32)
    for head in range(HEAD_NUMBER):
        row = jnp.sum(sharp_sums[head // 2], axis=0, keepdims=True)
        row = jnp.where((lane >> 6) == head % 2, row, 0.0)
        total = jnp.where(lane == head, jnp.sum(row, axis=1, keepdims=True), total)
    grads_ref[14:15, 0:LANES] = total

    head_sum[...] = jnp.zeros_like(head_sum)
    for step in range(row_count // tile):
        rows = pl.ds(step * tile, tile)
        for chunk in range(3 * PAD_WIDTH // LANES):
            head_low[rows, chunk_lanes(chunk)] = pool[chunk, rows, :].astype(BF16)
        saves[2 + step].start()
        head_sum[...] += dot_rows(first_low[rows, :], head_low[rows, :])
    for part in range(3):
        low = head_sum[:, part * PAD_WIDTH : (part + 1) * PAD_WIDTH].astype(BF16)
        weight_grad_ref[part] = dot_lanes(low, mapping).astype(BF16)
    for save in saves:
        save.wait()


def mixing_backward(sides, sharpness, inputs, weights, table, saved, batch_sums, dx2, dn, back_sums):
    row_count, width = inputs.shape
    chunks = width // LANES
    crops = sides.shape[0]
    shape = jax.ShapeDtypeStruct
    x1, qkv, mixed, scores, attention, slope, e = saved
    return pl.pallas_call(
        mixing_backward_kernel,
        out_shape=(
            shape((row_count, 3 * PAD_WIDTH), BF16),
            shape((row_count, width), F32),
            shape((width, 3 * PAD_WIDTH), BF16),
            shape((4, width, width), BF16),
            shape((16, width), F32),
        ),
        in_specs=[SMEM_SPEC, SMEM_SPEC]
        + [ANY_SPEC, VMEM_SPEC, VMEM_SPEC]
        + [ANY_SPEC] * 7
        + [VMEM_SPEC, ANY_SPEC, ANY_SPEC, VMEM_SPEC],
        out_specs=(ANY_SPEC,) * 3 + (VMEM_SPEC,) * 2,
        scratch_shapes=[
            pltpu.VMEM((row_count, width), F32),
            pltpu.VMEM((row_count, 3 * PAD_WIDTH), F32),
            pltpu.VMEM((row_count, PAD_WIDTH), BF16),
            pltpu.VMEM((crops, HEAD_PAIRS, HDIM, LANES), F32),
            pltpu.VMEM((crops, HEAD_PAIRS, HDIM, LANES), F32),
            pltpu.VMEM((row_count, width), F32),
            pltpu.VMEM((width, 3 * PAD_WIDTH), BF16),
            pltpu.VMEM((PAD_WIDTH, width), BF16),
            pltpu.VMEM((3 * PAD_WIDTH // LANES, row_count, LANES), F32),
            pltpu.VMEM((chunks, LEAD + row_count + TAIL, LANES), F32),
            pltpu.VMEM((row_count, PAD_WIDTH), F32),
            pltpu.VMEM((row_count, width), BF16),
            pltpu.VMEM((row_count, 3 * PAD_WIDTH), BF16),
            pltpu.VMEM((CROP_GROUP, 4, 2, HALF_WIDTH, HALF_WIDTH), BF16),
            pltpu.VMEM((PAD_WIDTH, width), F32),
            pltpu.VMEM((width, 3 * PAD_WIDTH), F32),
            pltpu.VMEM((HEAD_PAIRS, crops, LANES), F32),
            pltpu.SMEM((2 * crops,), jnp.int32),
            pltpu.SMEM((crops,), jnp.int32),
            pltpu.SemaphoreType.DMA((12 + row_count // tile_rows(row_count, 2),)),
            pltpu.SemaphoreType.DMA(((row_count + ROW_TILE - 1) // ROW_TILE,)),
        ],
        compiler_params=pltpu.CompilerParams(vmem_limit_bytes=VMEM_LIMIT),
        name="mixing_backward",
    )(
        sides,
        sharpness,
        inputs,
        weights,
        table,
        x1,
        qkv,
        mixed,
        scores,
        attention,
        slope,
        e,
        batch_sums,
        dx2,
        dn,
        back_sums,
    )


MESH = pl.DeviceIdType.MESH


def greet(peers):
    barrier = pltpu.get_barrier_semaphore()
    for peer in peers:
        pl.semaphore_signal(barrier, inc=1, device_id=peer, device_id_type=MESH)
    pl.semaphore_wait(barrier, len(peers))


def push(source, target, send, receive, peer):
    copy = pltpu.make_async_remote_copy(
        src_ref=source,
        dst_ref=target,
        send_sem=send,
        recv_sem=receive,
        device_id=peer,
        device_id_type=MESH,
    )
    copy.start()
    return copy


def turned(place, step, count):
    return lax.rem(place + step, count)


def ring_peers(axis, count):
    place = lax.axis_index(axis)
    return [{axis: turned(place, step, count)} for step in range(1, count)]


def comm_params(identity):
    return pltpu.CompilerParams(
        collective_id=identity, has_side_effects=True, vmem_limit_bytes=VMEM_LIMIT
    )


def flip(value, bits):
    for bit in (1, 2, 4):
        if bits & bit:
            value = value + bit - 2 * bit * lax.rem(lax.div(value, bit), 2)
    return value


def flip_peers(axis, count):
    place = lax.axis_index(axis)
    return [{axis: flip(place, bits)} for bits in range(1, count)]


def sum_all_kernel(counts, part_ref, total_ref, parts, send, receive):
    n_dp, n_fsdp = counts
    dp, fsdp = lax.axis_index("dp"), lax.axis_index("fsdp")
    place = dp * n_fsdp + fsdp
    peers = [
        {"dp": flip(dp, outer), "fsdp": flip(fsdp, inner)}
        for inner in reversed(range(n_fsdp))
        for outer in reversed(range(n_dp))
        if inner or outer
    ]
    greet(peers)
    parts[place] = part_ref[...]
    copies = [
        push(part_ref, parts.at[place], send.at[k], receive.at[k], peer)
        for k, peer in enumerate(peers)
    ]
    for copy in copies:
        copy.wait()
    total = parts[0]
    for k in range(1, n_dp * n_fsdp):
        total = total + parts[k]
    total_ref[...] = total


def sum_all(part, counts, identity):
    size = counts[0] * counts[1]
    return pl.pallas_call(
        functools.partial(sum_all_kernel, counts),
        out_shape=jax.ShapeDtypeStruct(part.shape, F32),
        in_specs=[VMEM_SPEC],
        out_specs=VMEM_SPEC,
        scratch_shapes=[
            pltpu.VMEM((size, *part.shape), F32),
            pltpu.SemaphoreType.DMA((size - 1,)),
            pltpu.SemaphoreType.DMA((size - 1,)),
        ],
        compiler_params=comm_params(identity),
        name="sum_all",
    )(part)


def sum_pair_kernel(
    counts, part_ref, blocks_hbm, total_ref, sums_hbm, parts, own, other, sums_ref, send, receive, sems
):
    n_dp, n_fsdp = counts
    dp, fsdp = lax.axis_index("dp"), lax.axis_index("fsdp")
    core = lax.rem(dp, 2)
    place = dp * n_fsdp + fsdp
    peers = [
        {"dp": flip(dp, outer), "fsdp": flip(fsdp, inner)}
        for inner in reversed(range(n_fsdp))
        for outer in reversed(range(n_dp))
        if inner or outer
    ]
    load = pltpu.make_async_copy(blocks_hbm.at[pl.ds(core * n_fsdp, n_fsdp)], own, sems.at[0])
    load.start()
    greet(peers)
    parts[place] = part_ref[...]
    copies = [
        push(part_ref, parts.at[place], send.at[k], receive.at[k], peer)
        for k, peer in enumerate(peers)
    ]
    blocks = push(
        blocks_hbm.at[pl.ds((1 - core) * n_fsdp, n_fsdp)],
        other,
        sems.at[1],
        sems.at[2],
        {"dp": flip(dp, 1)},
    )
    load.wait()
    blocks.wait_recv()
    for owner in range(n_fsdp):
        sums_ref[owner] = (own[owner].astype(F32) + other[owner].astype(F32)).astype(BF16)
    save = pltpu.make_async_copy(sums_ref, sums_hbm, sems.at[3])
    save.start()
    for copy in copies:
        copy.wait()
    total = parts[0]
    for k in range(1, n_dp * n_fsdp):
        total = total + parts[k]
    total_ref[...] = total
    blocks.wait_send()
    save.wait()


def sum_pair(part, blocks, counts, identity):
    size = counts[0] * counts[1]
    half = (counts[1], *blocks.shape[1:])
    shape = jax.ShapeDtypeStruct
    return pl.pallas_call(
        functools.partial(sum_pair_kernel, counts),
        out_shape=(shape(part.shape, F32), shape(half, BF16)),
        in_specs=[VMEM_SPEC, ANY_SPEC],
        out_specs=(VMEM_SPEC, ANY_SPEC),
        scratch_shapes=[
            pltpu.VMEM((size, *part.shape), F32),
            pltpu.VMEM(half, BF16),
            pltpu.VMEM(half, BF16),
            pltpu.VMEM(half, BF16),
            pltpu.SemaphoreType.DMA((size - 1,)),
            pltpu.SemaphoreType.DMA((size - 1,)),
            pltpu.SemaphoreType.DMA((4,)),
        ],
        compiler_params=comm_params(identity),
        name="sum_pair",
    )(part, blocks)


def gather_kernel(
    counts,
    masters_hbm,
    table_ref,
    blocks_hbm,
    full_table_ref,
    blocks,
    masters,
    tables,
    stage,
    ring_send,
    ring_recv,
    table_send,
    table_recv,
    cross_send,
    cross_recv,
    pair_send,
    pair_recv,
    local_sems,
):
    n_dp, n_fsdp = counts
    dp, fsdp = lax.axis_index("dp"), lax.axis_index("fsdp")
    shard, width = masters_hbm.shape[1:]
    columns = table_ref.shape[1]
    load = pltpu.make_async_copy(masters_hbm.at[dp], masters, local_sems.at[0])
    load.start()
    across = lax.rem(dp + 2, 4)
    pair = dp + 1 - 2 * lax.rem(dp, 2)
    peers = flip_peers("fsdp", n_fsdp)
    greet(peers + [{"dp": across}, {"dp": pair}])

    def piece(block, owner):
        return blocks.at[block, pl.ds(pl.multiple_of(owner * shard, 16), shard), :]

    def origin(step):
        return flip(fsdp, step)

    stage[...] = jnp.zeros_like(stage)
    stage[0 : table_ref.shape[0], 0:columns] = table_ref[...]
    tables[fsdp] = stage[...].astype(BF16)
    load.wait()
    blocks[dp, pl.ds(pl.multiple_of(fsdp * shard, 16), shard), :] = masters[...].astype(BF16)
    own = piece(dp, fsdp)
    ring = [
        push(own, own, ring_send.at[k], ring_recv.at[k], peer) for k, peer in enumerate(peers)
    ]
    table_copies = [
        push(tables.at[fsdp], tables.at[fsdp], table_send.at[k], table_recv.at[k], peer)
        for k, peer in enumerate(peers)
    ]
    crossing, pairing = [], []
    for step in range(n_fsdp):
        if step:
            ring[step - 1].wait_recv()
        part = piece(dp, origin(step))
        crossing.append(push(part, part, cross_send.at[step], cross_recv.at[step], {"dp": across}))
        pairing.append(
            push(part, part, pair_send.at[0, step], pair_recv.at[0, step], {"dp": pair})
        )
    for step in range(n_fsdp):
        crossing[step].wait_recv()
        part = piece(across, origin(step))
        pairing.append(
            push(part, part, pair_send.at[1, step], pair_recv.at[1, step], {"dp": pair})
        )
    for copy in table_copies:
        copy.wait_recv()
    total = None
    for owner in range(n_fsdp):
        lane = lax.broadcasted_iota(jnp.int32, (LANES, width), 0)
        target = lax.broadcasted_iota(jnp.int32, (LANES, width), 1)
        hit = (lane < columns) & (lane + owner * columns == target)
        term = dot(tables[owner], hit.astype(F32).astype(BF16))
        total = term if total is None else total + term
    full_table_ref[...] = total
    for copy in pairing:
        copy.wait_recv()
    save = pltpu.make_async_copy(blocks, blocks_hbm, local_sems.at[1])
    save.start()
    for copy in ring + table_copies + crossing + pairing:
        copy.wait_send()
    save.wait()


def gather_start(masters, coefficients, counts, identity):
    n_dp, n_fsdp = counts
    width = masters.shape[2]
    shape = jax.ShapeDtypeStruct
    dma = pltpu.SemaphoreType.DMA
    return pl.pallas_call(
        functools.partial(gather_kernel, counts),
        out_shape=(shape((4, width, width), BF16), shape((32, width), F32)),
        in_specs=[ANY_SPEC, VMEM_SPEC],
        out_specs=(ANY_SPEC, VMEM_SPEC),
        scratch_shapes=[
            pltpu.VMEM((4, width, width), BF16),
            pltpu.VMEM(masters.shape[1:], F32),
            pltpu.VMEM((n_fsdp, 32, LANES), BF16),
            pltpu.VMEM((32, LANES), F32),
            dma((n_fsdp - 1,)),
            dma((n_fsdp - 1,)),
            dma((n_fsdp - 1,)),
            dma((n_fsdp - 1,)),
            dma((n_fsdp,)),
            dma((n_fsdp,)),
            dma((2, n_fsdp)),
            dma((2, n_fsdp)),
            dma((2,)),
        ],
        compiler_params=comm_params(identity),
        name="gather_start",
    )(masters, coefficients)


def owner_rows(owner, shard):
    return pl.ds(pl.multiple_of(owner * shard, 16), shard)


TABLE_ROWS = (
    [(0, row) for row in range(5)]
    + [(1, 13), (1, 14)]
    + [(1, row) for row in range(4)]
    + [(0, row) for row in range(5, 14)]
    + [(1, row) for row in range(4, 13)]
)


def settle_kernel(
    counts,
    place_ref,
    mix_hbm,
    feed_hbm,
    mix_table_ref,
    feed_table_ref,
    left_hbm,
    right_hbm,
    head_low_hbm,
    dx1_hbm,
    input_hbm,
    head_weights_hbm,
    coefficient_ref,
    grad_hbm,
    slots_hbm,
    rows_hbm,
    table_ref,
    out_hbm,
    left,
    right,
    head_low,
    dx1,
    inputs,
    head_weights,
    out,
    first_sums,
    pair_buf,
    cross_out,
    cross_buf,
    ring_out,
    ring_buf,
    feed_in,
    feed_buf,
    dp_buf,
    slot_out,
    slots,
    steps,
    rows_buf,
    table_stage,
    table_rows,
    table_out,
    table_buf,
    table_part,
    table_dp,
    feed_sum,
    mix,
    feed_ref,
    left_parts,
    grad_ref,
    load_sems,
    pair_send,
    pair_recv,
    cross_send,
    cross_recv,
    ring_send,
    ring_recv,
    feed_in_send,
    feed_in_recv,
    feed_send,
    feed_recv,
    dp_send,
    dp_recv,
    slot_send,
    slot_recv,
    twin_send,
    twin_recv,
    back_send,
    back_recv,
    last_send,
    last_recv,
    table_rows_send,
    table_rows_recv,
    table_send,
    table_recv,
    table_dp_send,
    table_dp_recv,
):
    n_dp, n_fsdp = counts
    dp, fsdp = lax.axis_index("dp"), lax.axis_index("fsdp")
    width = mix_hbm.shape[2]
    shard = width // n_fsdp
    core = lax.rem(dp, 2)
    across, pair, pair_across = flip(dp, 2), flip(dp, 1), flip(dp, 3)
    peers, dp_peers = flip_peers("fsdp", n_fsdp), flip_peers("dp", n_dp)
    to_pair, to_across = {"dp": pair}, {"dp": across}
    loads = [
        pltpu.make_async_copy(left_hbm.at[core], left, load_sems.at[0]),
        pltpu.make_async_copy(right_hbm.at[core], right, load_sems.at[1]),
    ]
    mix_loads = [
        pltpu.make_async_copy(mix_hbm.at[across], mix.at[0], load_sems.at[3]),
        pltpu.make_async_copy(mix_hbm.at[dp], mix.at[1], load_sems.at[4]),
    ]
    feed_load = pltpu.make_async_copy(feed_hbm, feed_ref, load_sems.at[5])
    for load in mix_loads:
        load.start()
    feed_load.start()
    row_count = dx1.shape[0]
    tile = tile_rows(row_count, 4)
    tiles = row_count // tile
    weight_load = pltpu.make_async_copy(head_weights_hbm, head_weights, load_sems.at[2])
    weight_load.start()
    tile_loads, tile_saves = [], []
    for step in range(tiles):
        rows = pl.ds(step * tile, tile)
        sems = [load_sems.at[8 + 4 * step + index] for index in range(4)]
        tile_loads.append(
            [
                pltpu.make_async_copy(head_low_hbm.at[rows], head_low.at[rows], sems[0]),
                pltpu.make_async_copy(dx1_hbm.at[rows], dx1.at[rows], sems[1]),
                pltpu.make_async_copy(input_hbm.at[rows], inputs.at[rows], sems[2]),
            ]
        )
        tile_saves.append(pltpu.make_async_copy(out.at[rows], out_hbm.at[rows], sems[3]))
        for load in tile_loads[step]:
            load.start()
    for load in loads:
        load.start()
    first_sums[...] = jnp.zeros_like(first_sums)

    def first_back(step):
        rows = pl.ds(step * tile, tile)
        if step == 0:
            weight_load.wait()
        for load in tile_loads[step]:
            load.wait()
        grad = dot_lanes(head_low[rows, :], head_weights[...])
        unit, scale = centered(inputs[rows, :].astype(F32))
        total = dx1[rows, :] + norm_back(grad * coefficient_ref[0:1, :], unit, scale)
        out[rows, :] = total.astype(BF16)
        tile_saves[step].start()
        first_sums[0] += fold(grad * unit)
        first_sums[1] += fold(grad)

    greet(peers + dp_peers)

    parts = list(reversed(range(n_fsdp // 2)))
    deep = 2 * shard

    def part_rows(part):
        first = lax.div(flip(fsdp, 2 * part), 2)
        return pl.ds(pl.multiple_of(first * deep, 16), deep)

    def owner_rows(owner):
        return pl.ds(pl.multiple_of(owner * shard, 16), shard)

    pairing = {}
    for part in parts:
        rows = part_rows(part)
        for side, block in enumerate((pair_across, pair)):
            pairing[part, side] = push(
                mix_hbm.at[block, rows],
                pair_buf.at[side, rows],
                pair_send.at[side, part],
                pair_recv.at[side, part],
                to_pair,
            )
    for load in mix_loads:
        load.wait()
    crossing = {}
    for part in parts:
        rows = part_rows(part)
        pairing[part, 0].wait_recv()
        cross_out[rows, :] = (
            mix[0, rows, :].astype(F32) + pair_buf[0, rows, :].astype(F32)
        ).astype(BF16)
        crossing[part] = push(
            cross_out.at[rows],
            cross_buf.at[rows],
            cross_send.at[part],
            cross_recv.at[part],
            to_across,
        )
    ring = {}
    for part in parts:
        rows = part_rows(part)
        pairing[part, 1].wait_recv()
        crossing[part].wait_recv()
        ring_out[rows, :] = (
            mix[1, rows, :].astype(F32)
            + pair_buf[1, rows, :].astype(F32)
            + cross_buf[rows, :].astype(F32)
        ).astype(BF16)
        for bits in (2 * part + 1, 2 * part):
            if bits:
                ring[bits] = push(
                    ring_out.at[owner_rows(flip(fsdp, bits))],
                    ring_buf.at[bits],
                    ring_send.at[bits - 1],
                    ring_recv.at[bits - 1],
                    peers[bits - 1],
                )

    pieces = feed_sum.shape[0] // 2
    side = lax.div(dp, 2)
    feed_load.wait()
    for piece in range(2 * pieces):
        total = feed_ref[0, piece].astype(F32)
        for owner in range(1, n_fsdp):
            total = total + feed_ref[owner, piece].astype(F32)
        feed_sum[piece] = total.astype(BF16)
    feeding = push(
        feed_sum.at[pl.ds((1 - side) * pieces, pieces)],
        feed_in,
        feed_in_send.at[0],
        feed_in_recv.at[0],
        to_across,
    )
    for step in range(tiles - tiles // 2):
        first_back(step)
    feeding.wait_recv()
    total = feed_sum[pl.ds(side * pieces, pieces)].astype(F32) + feed_in[...].astype(F32)
    feed_buf[dp] = total.astype(BF16)
    feeds = [
        push(feed_buf.at[dp], feed_buf.at[dp], feed_send.at[k], feed_recv.at[k], peer)
        for k, peer in enumerate(dp_peers)
    ]

    total = ring_out[owner_rows(fsdp), :].astype(F32)
    for bits in range(1, n_fsdp):
        ring[bits].wait_recv()
        total = total + ring_buf[bits].astype(F32)
    dp_buf[dp] = total
    gathering = [
        push(dp_buf.at[dp], dp_buf.at[dp], dp_send.at[k], dp_recv.at[k], peer)
        for k, peer in enumerate(dp_peers)
    ]
    for step in range(tiles - tiles // 2, tiles):
        first_back(step)

    table_stage[...] = jnp.zeros_like(table_stage)
    for row, (source, first) in enumerate(TABLE_ROWS):
        ref = mix_table_ref if source == 0 else feed_table_ref
        table_stage[row : row + 1, :] = ref[first : first + 1, :]
    for row in range(2):
        table_stage[row : row + 1, :] = jnp.sum(first_sums[row], axis=0, keepdims=True)
    table_stage[31:32, :] = mix_table_ref[14:15, :]
    quarter = table_stage.shape[0] // n_dp

    def quarter_rows(place):
        return pl.ds(pl.multiple_of(place * quarter, 8), quarter)

    table_rows[dp] = table_stage[quarter_rows(dp), :]
    quartering = [
        push(
            table_stage.at[quarter_rows(flip(dp, step + 1))],
            table_rows.at[dp],
            table_rows_send.at[step],
            table_rows_recv.at[step],
            peer,
        )
        for step, peer in enumerate(dp_peers)
    ]
    for copy in feeds:
        copy.wait_recv()
    for place in range(n_dp):
        for piece in range(pieces):
            block = n_dp + (place % 2 * 2 + place // 2) * pieces + piece
            grad_ref[block] = feed_buf[place, piece].astype(F32)
    for copy in gathering:
        copy.wait_recv()
    for place in range(n_dp):
        grad_ref[place] = dp_buf[place]
    tile_saves.append(pltpu.make_async_copy(grad_ref, grad_hbm, load_sems.at[6 + 2 + 4 * tiles]))
    tile_saves[-1].start()

    slotting = {}
    for bits in reversed(range(n_fsdp)):
        slot = 2 * flip(fsdp, bits) + core
        block, filled = jnp.int32(0), jnp.int32(0)
        for index in range(grad_ref.shape[0]):
            here = place_ref[index] == slot
            block = jnp.where(here, index, block)
            filled = jnp.where(here, 1, filled)
        value = (grad_ref[block] * filled.astype(F32)).astype(BF16)
        if bits:
            slot_out[bits - 1] = value
            slotting[bits] = push(
                slot_out.at[bits - 1],
                slots.at[core, owner_rows(fsdp), :],
                slot_send.at[bits - 1],
                slot_recv.at[bits - 1],
                peers[bits - 1],
            )
        else:
            slots[core, owner_rows(fsdp), :] = value
    for copy in quartering:
        copy.wait_recv()
    rest = table_rows[0]
    for place in range(1, n_dp):
        rest = rest + table_rows[place]
    sharp_row = lax.broadcasted_iota(jnp.int32, (quarter, LANES), 0) + dp * quarter == 31
    sharp_values = jnp.broadcast_to(rest[quarter - 1 : quarter, 0:LANES], (quarter, LANES))
    terms = []
    for _ in range(3):
        term = rest.astype(BF16).astype(F32)
        terms.append(term)
        rest = rest - term
    terms = jnp.concatenate(terms, axis=0).astype(BF16)
    columns = width // n_fsdp
    for owner in range(n_fsdp):
        lane = lax.broadcasted_iota(jnp.int32, (width, LANES), 1)
        source = lax.broadcasted_iota(jnp.int32, (width, LANES), 0)
        hit = ((lane < columns) & (lane + owner * columns == source)).astype(F32).astype(BF16)
        value = dot(terms, hit)
        value = value[0:quarter] + value[quarter : 2 * quarter] + value[2 * quarter :]
        table_out[owner] = jnp.where(sharp_row, sharp_values, value)
    table_buf[fsdp] = table_out[fsdp]
    tabling = [
        push(
            table_out.at[flip(fsdp, step + 1)],
            table_buf.at[fsdp],
            table_send.at[step],
            table_recv.at[step],
            peer,
        )
        for step, peer in enumerate(peers)
    ]
    for load in loads:
        load.wait()
    right_parts = split(right[...])
    for index, value in enumerate(split(left[...])):
        left_parts[index] = value
    twins = []
    for bits in range(n_fsdp):
        if bits:
            slotting[bits].wait_recv()
        part = slots.at[core, owner_rows(flip(fsdp, bits)), :]
        twins.append(push(part, part, twin_send.at[bits], twin_recv.at[bits], to_pair))

    grad = slots[core]
    back = {}
    for part in parts:
        rows = part_rows(part)
        half = split(dot(left_parts[0, rows, :], grad) + dot(left_parts[1, rows, :], grad))
        steps[rows, :] = dot_split(dot, half, right_parts).astype(BF16)
        for bits in (2 * part + 1, 2 * part):
            if bits:
                back[bits] = push(
                    steps.at[owner_rows(flip(fsdp, bits))],
                    rows_buf.at[2 * fsdp + core],
                    back_send.at[bits - 1],
                    back_recv.at[bits - 1],
                    peers[bits - 1],
                )
    rows_buf[2 * fsdp + core] = steps[owner_rows(fsdp), :]
    for copy in tabling:
        copy.wait_recv()
    total = table_buf[0]
    for owner in range(1, n_fsdp):
        total = total + table_buf[owner]
    table_part[...] = total
    table_dp[dp] = total
    table_dps = [
        push(table_part, table_dp.at[dp], table_dp_send.at[k], table_dp_recv.at[k], peer)
        for k, peer in enumerate(dp_peers)
    ]
    lasts = []
    for bits in range(n_fsdp):
        if bits:
            back[bits].wait_recv()
        part = rows_buf.at[2 * flip(fsdp, bits) + core]
        lasts.append(push(part, part, last_send.at[bits], last_recv.at[bits], to_pair))
    for copy in table_dps:
        copy.wait_recv()
    for place in range(n_dp):
        table_ref[place * quarter : (place + 1) * quarter, :] = table_dp[place]
    for copy in twins:
        copy.wait_recv()
    tile_saves.append(pltpu.make_async_copy(slots, slots_hbm, load_sems.at[6]))
    tile_saves[-1].start()
    for copy in lasts:
        copy.wait_recv()
    tile_saves.append(pltpu.make_async_copy(rows_buf, rows_hbm, load_sems.at[7]))
    tile_saves[-1].start()
    copies = [*pairing.values(), *crossing.values(), *ring.values(), *slotting.values()]
    copies += [*back.values(), feeding, *feeds, *quartering, *tabling, *table_dps, *gathering]
    for copy in copies + twins + lasts:
        copy.wait_send()
    for save in tile_saves:
        save.wait()


def settle(
    places, mix, feed, mix_table, feed_table, left, right, back, coefficients, counts, identity
):
    head_low, dx1, inputs, head_weights = back
    row_count = dx1.shape[0]
    tiles = row_count // tile_rows(row_count, 4)
    n_dp, n_fsdp = counts
    width = mix.shape[2]
    shard = width // n_fsdp
    blocks = n_dp + 2 * feed.shape[1]
    pieces = feed.shape[1] // 2
    inner, outer = n_fsdp - 1, n_dp - 1
    shape = jax.ShapeDtypeStruct
    dma = pltpu.SemaphoreType.DMA
    sizes = [(2, n_fsdp // 2), (n_fsdp // 2,), (inner,), (1,), (outer,), (outer,)]
    sizes += [(inner,), (n_fsdp,), (inner,), (n_fsdp,), (outer,), (inner,), (outer,)]
    return pl.pallas_call(
        functools.partial(settle_kernel, counts),
        out_shape=(
            shape((blocks, shard, width), F32),
            shape((2, width, width), BF16),
            shape((2 * n_fsdp, shard, width), BF16),
            shape((32, LANES), F32),
            shape(inputs.shape, BF16),
        ),
        in_specs=[SMEM_SPEC] + [ANY_SPEC] * 2 + [VMEM_SPEC] * 2 + [ANY_SPEC] * 6 + [VMEM_SPEC],
        out_specs=(ANY_SPEC,) * 3 + (VMEM_SPEC, ANY_SPEC),
        scratch_shapes=[
            pltpu.VMEM((width, width), F32),
            pltpu.VMEM((width, width), F32),
            pltpu.VMEM(head_low.shape, BF16),
            pltpu.VMEM(dx1.shape, F32),
            pltpu.VMEM(inputs.shape, BF16),
            pltpu.VMEM(head_weights.shape, BF16),
            pltpu.VMEM(inputs.shape, BF16),
            pltpu.VMEM((2, 8, width), F32),
            pltpu.VMEM((2, width, width), BF16),
            pltpu.VMEM((width, width), BF16),
            pltpu.VMEM((width, width), BF16),
            pltpu.VMEM((width, width), BF16),
            pltpu.VMEM((n_fsdp, shard, width), BF16),
            pltpu.VMEM((pieces, shard, width), BF16),
            pltpu.VMEM((n_dp, pieces, shard, width), BF16),
            pltpu.VMEM((n_dp, shard, width), F32),
            pltpu.VMEM((inner, shard, width), BF16),
            pltpu.VMEM((2, width, width), BF16),
            pltpu.VMEM((width, width), BF16),
            pltpu.VMEM((2 * n_fsdp, shard, width), BF16),
            pltpu.VMEM((32, width), F32),
            pltpu.VMEM((n_dp, 32 // n_dp, width), F32),
            pltpu.VMEM((n_fsdp, 32 // n_dp, LANES), F32),
            pltpu.VMEM((n_fsdp, 32 // n_dp, LANES), F32),
            pltpu.VMEM((32 // n_dp, LANES), F32),
            pltpu.VMEM((n_dp, 32 // n_dp, LANES), F32),
            pltpu.VMEM(feed.shape[1:], BF16),
            pltpu.VMEM((2, width, width), BF16),
            pltpu.VMEM(feed.shape, BF16),
            pltpu.VMEM((2, width, width), BF16),
            pltpu.VMEM((blocks, shard, width), F32),
            dma((9 + 4 * tiles,)),
        ]
        + [dma(size) for size in sizes for _ in range(2)],
        compiler_params=comm_params(identity),
        name="settle",
    )(places, mix, feed, mix_table, feed_table, left, right, *back, coefficients)


def finish_kernel(
    place_ref,
    table_ref,
    energy_ref,
    coefficient_ref,
    sharp_ref,
    sharp_energy_ref,
    grads_hbm,
    slots_hbm,
    rows_hbm,
    left_hbm,
    right_hbm,
    masters_hbm,
    tokens_hbm,
    grad_hbm,
    left_out_hbm,
    right_out_hbm,
    masters_out_hbm,
    low_hbm,
    tokens_out_hbm,
    table_grad_ref,
    energy_out_ref,
    coefficient_out_ref,
    sharp_grad_ref,
    sharp_energy_out_ref,
    sharp_out_ref,
    left,
    right,
    masters,
    low,
    tokens,
    grad_ref,
    slots_ref,
    rows_ref,
    sems,
):
    slot_count = slots_ref.shape[0]
    load_slots = pltpu.make_async_copy(slots_hbm, slots_ref, sems.at[10])
    load_rows = pltpu.make_async_copy(rows_hbm, rows_ref, sems.at[11])
    load_grads = pltpu.make_async_copy(grads_hbm, grad_ref, sems.at[12])
    load_slots.start()
    load_left = pltpu.make_async_copy(left_hbm, left, sems.at[0])
    load_right = pltpu.make_async_copy(right_hbm, right, sems.at[1])
    load_masters = pltpu.make_async_copy(masters_hbm, masters, sems.at[2])
    saves = [
        pltpu.make_async_copy(source, target, sems.at[3 + index])
        for index, (source, target) in enumerate(
            (
                (grad_ref, grad_hbm),
                (left, left_out_hbm),
                (right, right_out_hbm),
                (masters, masters_out_hbm),
                (low, low_hbm),
                (tokens, tokens_out_hbm),
            )
        )
    ]
    load_left.start()
    load_right.start()
    load_tokens = pltpu.make_async_copy(tokens_hbm, tokens, sems.at[9])
    load_tokens.start()
    load_grads.start()
    load_masters.start()
    load_rows.start()
    load_slots.wait()
    load_left.wait()
    for slot in range(slot_count):
        grad = slots_ref[slot]
        left[slot] = (
            covariance_forgetting * left[slot]
            + (1.0 - covariance_forgetting) * dot_lanes(grad, grad)
        )
    saves[1].start()
    load_right.wait()
    for slot in range(slot_count):
        grad = slots_ref[slot]
        right[slot] = (
            covariance_forgetting * right[slot]
            + (1.0 - covariance_forgetting) * dot_rows(grad, grad)
        )
    saves[2].start()
    load_tokens.wait()
    saves[5].start()
    load_grads.wait()
    saves[0].start()
    load_masters.wait()
    load_rows.wait()
    for block in range(masters.shape[0]):
        value = masters[block] - weight_rate * rows_ref[place_ref[block]].astype(F32)
        masters[block] = value
        low[block] = value.astype(BF16)
    saves[3].start()
    saves[4].start()
    count, columns = energy_ref.shape
    grad = table_ref[0:count, 0:columns]
    table_grad_ref[...] = grad
    energy = covariance_forgetting * energy_ref[...] + (1.0 - covariance_forgetting) * grad * grad
    energy_out_ref[...] = energy
    coefficient_out_ref[...] = coefficient_ref[...] - vector_rate * grad / (
        jnp.sqrt(energy) + energy_epsilon
    )
    grad = table_ref[31:32, 0:HEAD_NUMBER]
    grad = grad.reshape(HEAD_NUMBER)
    energy = covariance_forgetting * sharp_energy_ref[...] + (1.0 - covariance_forgetting) * grad * grad
    sharp_grad_ref[...] = grad
    sharp_energy_out_ref[...] = energy
    sharp_out_ref[...] = sharp_ref[...] - sharpness_step_size * grad / (
        jnp.sqrt(energy) + energy_epsilon
    )
    for save in saves:
        save.wait()


def finish(
    places,
    table,
    energy,
    coefficients,
    sharpness,
    sharpness_energy,
    grads,
    slots,
    rows,
    left,
    right,
    masters,
    tokens,
):
    shape = jax.ShapeDtypeStruct
    return pl.pallas_call(
        finish_kernel,
        out_shape=(
            shape(grads.shape, F32),
            shape(left.shape, F32),
            shape(right.shape, F32),
            shape(masters.shape, F32),
            shape(masters.shape, BF16),
            shape(tokens.shape, BF16),
            shape(energy.shape, F32),
            shape(energy.shape, F32),
            shape(energy.shape, F32),
            shape(sharpness.shape, F32),
            shape(sharpness.shape, F32),
            shape(sharpness.shape, F32),
        ),
        in_specs=[SMEM_SPEC] + [VMEM_SPEC] * 5 + [ANY_SPEC] * 7,
        out_specs=(ANY_SPEC,) * 6 + (VMEM_SPEC,) * 6,
        scratch_shapes=[
            pltpu.VMEM(left.shape, F32),
            pltpu.VMEM(right.shape, F32),
            pltpu.VMEM(masters.shape, F32),
            pltpu.VMEM(masters.shape, BF16),
            pltpu.VMEM(tokens.shape, BF16),
            pltpu.VMEM(grads.shape, F32),
            pltpu.VMEM(slots.shape, BF16),
            pltpu.VMEM(rows.shape, BF16),
            pltpu.SemaphoreType.DMA((13,)),
        ],
        compiler_params=pltpu.CompilerParams(vmem_limit_bytes=VMEM_LIMIT),
        name="finish",
    )(
        places,
        table,
        energy,
        coefficients,
        sharpness,
        sharpness_energy,
        grads,
        slots,
        rows,
        left,
        right,
        masters,
        tokens,
    )


def shards(
    patch_embeddings,
    view_side_tokens,
    projection_masters,
    channel_coefficients,
    head_sharpness,
    output_adjoint,
    leading_covariance,
    trailing_covariance,
    leading_root_preconditioner,
    trailing_root_preconditioner,
    channel_energy_average,
    sharpness_energy_average,
    storage_position_map,
):
    row_count, feature_count = patch_embeddings.shape
    block_count = projection_masters.shape[0]
    shard_rows = projection_masters.shape[1]
    slot_count = leading_covariance.shape[0]
    counts = (lax.axis_size("dp"), lax.axis_size("fsdp"))
    direct = counts[0] == 4 and slot_count == 2 and shard_rows % 16 == 0
    if direct:
        mixing_blocks, table = gather_start(projection_masters, channel_coefficients, counts, 0)
        grad_shape = (2 * counts[1], (block_count - 4) // 2, shard_rows, feature_count)
    else:
        full_table = lax.all_gather(channel_coefficients.astype(BF16), "fsdp", axis=1, tiled=True)
        table = full_table.astype(F32)
        mixing_blocks = lax.all_gather(
            projection_masters[:4].astype(BF16), "fsdp", axis=1, tiled=True
        )
        grad_shape = (1, block_count - 4, feature_count, feature_count)
    feed_blocks = lax.all_gather(projection_masters[4:].astype(BF16), "fsdp", axis=1, tiled=True)

    x1, qkv, mixed, scores, attention, slope, e, sums = mixing_forward(
        view_side_tokens, head_sharpness, patch_embeddings, mixing_blocks, table
    )
    batch_sums = sum_all(sums, counts, 1) if direct else lax.psum(sums, ("dp", "fsdp"))
    layer_output, dx2, dn, feed_grad, feed_table, back_part = feed_forward(
        view_side_tokens, x1, e, batch_sums, feed_blocks, table, output_adjoint, grad_shape
    )
    if direct:
        back_sums, feed_grad = sum_pair(back_part, feed_grad, counts, 2)
        feed_grad = lax.all_to_all(feed_grad, "fsdp", 0, 0, tiled=True)
    else:
        back_sums = lax.psum(back_part, ("dp", "fsdp"))
    head_low, dx1, head_weights, mixing_grad, mixing_table = mixing_backward(
        view_side_tokens,
        head_sharpness,
        patch_embeddings,
        mixing_blocks,
        table,
        (x1, qkv, mixed, scores, attention, slope, e),
        batch_sums,
        dx2,
        dn,
        back_sums,
    )
    if direct:
        grads, owned_grad, my_rows, table_total, tokens_grad = settle(
            storage_position_map,
            mixing_grad,
            feed_grad,
            mixing_table,
            feed_table,
            leading_root_preconditioner,
            trailing_root_preconditioner,
            (head_low, dx1, patch_embeddings, head_weights),
            table,
            counts,
            3,
        )
        results = list(
            finish(
                storage_position_map,
                table_total,
                channel_energy_average,
                channel_coefficients,
                head_sharpness,
                sharpness_energy_average,
                grads,
                owned_grad,
                my_rows,
                leading_covariance,
                trailing_covariance,
                projection_masters,
                tokens_grad,
            )
        )
        tokens_grad = results.pop(5)
        return (layer_output, tokens_grad, *results)
    first_grad = dot_lanes(head_low, head_weights)
    unit, scale = centered(patch_embeddings.astype(F32))
    incoming_tokens_grad = (dx1 + norm_back(first_grad * table[0], unit, scale)).astype(BF16)
    mixing_table = mixing_table.at[0].set(jnp.sum(first_grad * unit, axis=0))
    mixing_table = mixing_table.at[1].set(jnp.sum(first_grad, axis=0))
    sharpness_share = mixing_table[14, 0:HEAD_NUMBER]
    table_grad = jnp.stack([(mixing_table, feed_table)[source][row] for source, row in TABLE_ROWS])
    block_grad = jnp.concatenate([mixing_grad, feed_grad[0]], axis=0).astype(F32)
    denominator_sum = lax.axis_size("fsdp")
    tiled_part = jnp.broadcast_to(
        sharpness_share[None, :], (denominator_sum, sharpness_share.shape[0])
    )
    portion_derivative, catalog_portion, sharpness_normalizer = (
        lax.psum_scatter(block_grad, "fsdp", scatter_dimension=1, tiled=True),
        lax.psum_scatter(table_grad, "fsdp", scatter_dimension=1, tiled=True),
        lax.psum_scatter(tiled_part, "fsdp", scatter_dimension=0, tiled=True),
    )
    portion_derivative, catalog_portion, sharpness_normalizer = lax.psum(
        (portion_derivative, catalog_portion, sharpness_normalizer), "dp"
    )
    sharpness_derivative = sharpness_normalizer[0]
    shard_place = lax.axis_index("fsdp")
    slot_index = jnp.arange(denominator_sum * slot_count, dtype=jnp.int32)
    slot_match = storage_position_map[None, :] == slot_index[:, None]
    slot_filled = jnp.any(slot_match, axis=1).astype(jnp.float32)[:, None, None]
    slot_block = jnp.sum(
        jnp.where(slot_match, jnp.arange(block_count, dtype=jnp.int32)[None, :], 0), axis=1
    )
    my_filled = lax.dynamic_slice_in_dim(slot_filled, shard_place * slot_count, slot_count, 0)
    my_block = lax.dynamic_slice_in_dim(slot_block, shard_place * slot_count, slot_count, 0)
    whole_grad = lax.all_gather(portion_derivative, "fsdp", axis=1, tiled=True)
    owned_grad = jnp.take(whole_grad, my_block, axis=0) * my_filled
    leading_covariance_renewed = covariance_forgetting * leading_covariance + (
        1.0 - covariance_forgetting
    ) * jnp.einsum("sij,skj->sik", owned_grad, owned_grad, precision=lax.Precision.HIGHEST)
    trailing_covariance_renewed = covariance_forgetting * trailing_covariance + (
        1.0 - covariance_forgetting
    ) * jnp.einsum("sji,sjk->sik", owned_grad, owned_grad, precision=lax.Precision.HIGHEST)
    halfway = jnp.einsum(
        "sij,sjk->sik", leading_root_preconditioner, owned_grad, precision=lax.Precision.HIGHEST
    )
    conditioned = jnp.einsum(
        "sij,sjk->sik", halfway, trailing_root_preconditioner, precision=lax.Precision.HIGHEST
    )
    every_update = lax.all_gather(conditioned, "fsdp", axis=0, tiled=True)
    my_rows = lax.dynamic_slice_in_dim(every_update, shard_place * shard_rows, shard_rows, 1)
    update = jnp.take(my_rows, storage_position_map, axis=0)
    projection_updated = projection_masters - weight_rate * update
    channel_energy_renewed = (
        covariance_forgetting * channel_energy_average
        + (1.0 - covariance_forgetting) * catalog_portion * catalog_portion
    )
    channel_params_updated = channel_coefficients - vector_rate * catalog_portion / (
        jnp.sqrt(channel_energy_renewed) + energy_epsilon
    )
    sharpness_energy_renewed = (
        covariance_forgetting * sharpness_energy_average
        + (1.0 - covariance_forgetting) * sharpness_derivative * sharpness_derivative
    )
    sharpness_updated = head_sharpness - sharpness_step_size * sharpness_derivative / (
        jnp.sqrt(sharpness_energy_renewed) + energy_epsilon
    )
    return (
        layer_output,
        incoming_tokens_grad,
        portion_derivative,
        leading_covariance_renewed,
        trailing_covariance_renewed,
        projection_updated,
        projection_updated.astype(jnp.bfloat16),
        catalog_portion,
        channel_energy_renewed,
        channel_params_updated,
        sharpness_derivative,
        sharpness_energy_renewed,
        sharpness_updated,
    )


def solution(mesh):
    in_specs = (
        P(("dp", "fsdp"), None),
        P(("dp", "fsdp")),
        P(None, "fsdp", None),
        P(None, "fsdp"),
        P(),
        P(("dp", "fsdp"), None),
        P("fsdp", None, None),
        P("fsdp", None, None),
        P("fsdp", None, None),
        P("fsdp", None, None),
        P(None, "fsdp"),
        P(),
        P(),
    )
    out_specs = (
        P(("dp", "fsdp"), None),
        P(("dp", "fsdp"), None),
        P(None, "fsdp", None),
        P("fsdp", None, None),
        P("fsdp", None, None),
        P(None, "fsdp", None),
        P(None, "fsdp", None),
        P(None, "fsdp"),
        P(None, "fsdp"),
        P(None, "fsdp"),
        P(),
        P(),
        P(),
    )
    return jax.shard_map(shards, mesh=mesh, in_specs=in_specs, out_specs=out_specs, check_vma=False)
```

```python
import functools

import jax
import jax.numpy as jnp
from jax import lax
from jax.experimental import pallas as pl
from jax.experimental.pallas import tpu as pltpu
from jax.sharding import PartitionSpec as P

HEAD_NUMBER = 8
HDIM = 48
HEAD_PAD = 64
LANES = 128
HEAD_PAIRS = HEAD_NUMBER // 2
PAD_WIDTH = HEAD_NUMBER * HEAD_PAD
HALF_WIDTH = PAD_WIDTH // 2
LEAD = 16
TAIL = 32
SMALL_SIDE = 6
SMALL_WINDOW = 48
LARGE_WINDOW = 208
CROP_GROUP = 2
SAVE_ROWS = 64
ROW_TILE = 464
HIDDEN_PARTS = 6
VMEM_LIMIT = 60 * 2**20

norm_epsilon = 1e-06
batch_epsilon = 1e-05
attention_epsilon = 1e-06
covariance_forgetting = 0.5
weight_rate = 0.5
vector_rate = 0.1
sharpness_step_size = 2.0
energy_epsilon = 1e-08

F32 = jnp.float32
BF16 = jnp.bfloat16
VMEM_SPEC = pl.BlockSpec(memory_space=pltpu.VMEM)
ANY_SPEC = pl.BlockSpec(memory_space=pl.ANY)
SMEM_SPEC = pl.BlockSpec(memory_space=pltpu.SMEM)


def dot(left, right):
    return lax.dot_general(left, right, (((1,), (0,)), ((), ())), preferred_element_type=F32)


def dot_rows(left, right):
    return lax.dot_general(left, right, (((0,), (0,)), ((), ())), preferred_element_type=F32)


def dot_lanes(left, right):
    return lax.dot_general(left, right, (((1,), (1,)), ((), ())), preferred_element_type=F32)


def split(values):
    high = values.astype(BF16)
    return high, (values - high.astype(F32)).astype(BF16)


def dot_split(product, left, right):
    if product is dot_rows:
        return product(
            jnp.concatenate([left[0], left[0], left[1]], axis=0),
            jnp.concatenate([right[0], right[1], right[0]], axis=0),
        )
    rows = left[0].shape[0]
    both = product(jnp.concatenate(left, axis=0), right[0])
    return both[:rows] + both[rows:] + product(left[0], right[1])


def fold(values):
    total = values[0:8]
    for first in range(8, values.shape[0], 8):
        total = total + values[first : first + 8]
    return total


def gelu_parts(values):
    magnitude = jnp.abs(values) * 0.7071067811865476
    base = 1.0 + 0.3275911 * magnitude
    guess = pl.reciprocal(base, approx=True)
    slot = guess * (2.0 - base * guess)
    series = slot * (
        0.127414796
        + slot
        * (-0.142248368 + slot * (0.7107068705 + slot * (-0.7265760135 + slot * 0.5307027145)))
    )
    bell = jnp.exp(-0.5 * values * values)
    lower = series * bell
    return jnp.where(values >= 0, 1.0 - lower, lower), bell


def gelu_slope(values, share, bell):
    return share + values * bell * 0.3989422804014327


def head_map(dtype):
    feature = lax.broadcasted_iota(jnp.int32, (HEAD_NUMBER * HDIM, PAD_WIDTH), 0)
    lane = lax.broadcasted_iota(jnp.int32, (HEAD_NUMBER * HDIM, PAD_WIDTH), 1)
    inner = lane & (HEAD_PAD - 1)
    hit = (inner < HDIM) & ((lane >> 6) * HDIM + inner == feature)
    return hit.astype(F32).astype(dtype)


def centered(values):
    center = jnp.sum(values, axis=-1, keepdims=True) * (1.0 / values.shape[-1])
    shifted = values - center
    spread = jnp.sum(shifted * shifted, axis=-1, keepdims=True) * (1.0 / values.shape[-1])
    scale = lax.rsqrt(spread + norm_epsilon)
    return shifted * scale, scale


def norm_back(grad, unit, scale):
    size = 1.0 / grad.shape[-1]
    middle = jnp.sum(grad, axis=-1, keepdims=True) * size
    slope = jnp.sum(grad * unit, axis=-1, keepdims=True) * size
    return scale * (grad - middle - unit * slope)


def tile_rows(count, least):
    for parts in range(least, count // 16 + 1):
        if count % (16 * parts) == 0:
            return count // parts
    return count


def for_rows(count, tile, step, carry=0):
    def body(index, carry):
        return step(pl.multiple_of(index * tile, tile), tile, carry)

    if count // tile == 1:
        carry = step(0, tile, carry)
    else:
        carry = lax.fori_loop(0, count // tile, body, carry)
    if count % tile:
        carry = step(count - count % tile, count % tile, carry)
    return carry


def row_copies(pairs, first, size, sem):
    rows = pl.ds(first, size)
    return [
        pltpu.make_async_copy(
            source.at[:, rows] if chunked else source.at[rows],
            target.at[:, rows] if chunked else target.at[rows],
            sem,
        )
        for source, target, chunked in pairs
    ]


def live_total(sides_ref):
    return lax.fori_loop(
        0, sides_ref.shape[0], lambda c, t: t + sides_ref[c] * sides_ref[c], jnp.int32(0)
    )


def row_mask(first, rows, width, limit):
    return lax.broadcasted_iota(jnp.int32, (rows, width), 0) + first < limit


def save_rows(source, target, sem, first, rows):
    rows = pl.ds(pl.multiple_of(first, 8), rows)
    pltpu.make_async_copy(source.at[:, rows], target.at[:, rows], sem).start()


def for_groups(sides_ref, step, carry, saves=()):
    def save(first, last):
        def body(part, _):
            for source, target, sem in saves:
                save_rows(source, target, sem, part * SAVE_ROWS, SAVE_ROWS)
            return 0

        if saves:
            lax.fori_loop(first, last, body, 0)
        return last

    def crop_body(crop, state):
        start, saved, carry = state
        side = sides_ref[crop]
        cells = side * side
        inverse = 1.0 / jnp.full((8, LANES), side, jnp.int32).astype(F32)
        lines = lax.broadcasted_iota(jnp.int32, (8, LANES), 0)

        def group_body(group, carry):
            for part in range(2):
                row = pl.multiple_of((group * 2 + part) * 8, 8)
                place = lines + (row - start)
                line = ((place.astype(F32) + 0.5) * inverse).astype(jnp.int32)
                column = place - line * side
                inside = (place >= 0) & (place < cells)
                masks = (
                    inside,
                    column >= 1,
                    column < side - 1,
                    place >= side,
                    place < cells - side,
                )
                carry = step(row, side, masks, carry)
            return carry

        carry = lax.fori_loop(start // 16, (start + cells + 15) // 16, group_body, carry)
        saved = save(saved, (start + cells) // 16 * 16 // SAVE_ROWS)
        return start + cells, saved, carry

    state = (jnp.int32(0), jnp.int32(0), carry)
    _, saved, carry = lax.fori_loop(0, sides_ref.shape[0], crop_body, state)
    for source, target, sem in saves:
        done = source.shape[1] // SAVE_ROWS * SAVE_ROWS
        if done < source.shape[1]:
            save_rows(source, target, sem, done, source.shape[1] - done)
    if saves:
        save(saved, saves[0][0].shape[1] // SAVE_ROWS)
    return carry


def conv_forward(source, chunk, row, side, masks, taps):
    inside, left_ok, right_ok, up_ok, down_ok = masks
    total = None
    for shift in (-1, 0, 1):
        base = LEAD + row + shift * side
        middle = source[chunk, pl.ds(base, 8), :]
        left = jnp.where(left_ok, source[chunk, pl.ds(base - 1, 8), :], 0.0)
        right = jnp.where(right_ok, source[chunk, pl.ds(base + 1, 8), :], 0.0)
        first = 3 * (shift + 1)
        value = taps[first] * left + taps[first + 1] * middle + taps[first + 2] * right
        if shift == -1:
            value = jnp.where(up_ok, value, 0.0)
        if shift == 1:
            value = jnp.where(down_ok, value, 0.0)
        total = value if total is None else total + value
    return total


def conv_backward(source, chunk, row, side, masks, taps, own, tap_sums):
    inside, left_ok, right_ok, up_ok, down_ok = masks
    total = None
    tap_sums = list(tap_sums)
    for shift in (-1, 0, 1):
        base = LEAD + row + shift * side
        row_ok = {-1: up_ok, 0: None, 1: down_ok}[shift]
        for sway in (-1, 0, 1):
            column_ok = {-1: left_ok, 0: None, 1: right_ok}[sway]
            value = source[chunk, pl.ds(base + sway, 8), :]
            keep = inside
            if row_ok is not None:
                keep = keep & row_ok
            if column_ok is not None:
                keep = keep & column_ok
            value = jnp.where(keep, value, 0.0)
            index = 3 * (1 - shift) + (1 - sway)
            term = taps[index] * value
            total = term if total is None else total + term
            tap_sums[index] = tap_sums[index] + own * value
    return total, tuple(tap_sums)


def chunk_lanes(chunk):
    return slice(chunk * LANES, (chunk + 1) * LANES)


def tap_vectors(table_ref, first, chunk):
    return [
        jnp.broadcast_to(table_ref[first + k : first + k + 1, chunk_lanes(chunk)], (8, LANES))
        for k in range(9)
    ]


def for_crops(sides_ref, row_count, order_ref, start_ref, step):
    crops = sides_ref.shape[0]

    def scan(crop, state):
        start, large, small = state
        side = sides_ref[crop]
        start_ref[crop] = start
        is_small = side <= SMALL_SIDE
        order_ref[jnp.where(is_small, crops + small, large)] = crop
        return (
            start + side * side,
            large + jnp.where(is_small, 0, 1),
            small + jnp.where(is_small, 1, 0),
        )

    zero = jnp.int32(0)
    _, large, small = lax.fori_loop(0, crops, scan, (zero, zero, zero))
    for window, first, count in ((LARGE_WINDOW, 0, large), (SMALL_WINDOW, crops, small)):

        def group_body(group, _, window=window, first=first, count=count):
            members = []
            for member in range(CROP_GROUP):
                crop = order_ref[first + jnp.minimum(group * CROP_GROUP + member, count - 1)]
                start = start_ref[crop]
                side = sides_ref[crop]
                row = pl.multiple_of(jnp.minimum(start // 8, (row_count - window) // 8) * 8, 8)
                place = lax.broadcasted_iota(jnp.int32, (window, HALF_WIDTH), 0) + (row - start)
                members.append((crop, pl.ds(row, window), (place >= 0) & (place < side * side)))
            step(members)
            return 0

        lax.fori_loop(0, (count + CROP_GROUP - 1) // CROP_GROUP, group_body, 0)


def half_lanes(half):
    starts = [part * PAD_WIDTH + half * HALF_WIDTH for part in range(3)]
    return [slice(start, start + HALF_WIDTH) for start in starts]


def pair_lanes():
    return lax.broadcasted_iota(jnp.int32, (HDIM, LANES), 1) < HEAD_PAD


def pair_part(block, pair):
    first = pair * LANES
    lanes = slice(first, first + LANES)
    return jnp.where(
        pair_lanes(),
        block[first : first + HDIM, lanes],
        block[first + HEAD_PAD : first + HEAD_PAD + HDIM, lanes],
    )


def spread_pair(target, member, half, pair, values):
    first = pair * LANES
    lanes = slice(first, first + LANES)
    parts = split(values)
    for index in range(2):
        value = parts[index].astype(F32)
        target[member, half, index, first : first + HDIM, lanes] = jnp.where(
            pair_lanes(), value, 0.0
        ).astype(BF16)
        target[member, half, index, first + HEAD_PAD : first + HEAD_PAD + HDIM, lanes] = jnp.where(
            pair_lanes(), 0.0, value
        ).astype(BF16)


def pair_sharpness(sharp_ref, pair):
    lane = lax.broadcasted_iota(jnp.int32, (1, LANES), 1)
    return jnp.where(lane < HEAD_PAD, sharp_ref[2 * pair], sharp_ref[2 * pair + 1])


def units(values):
    scale = lax.rsqrt(jnp.sum(values * values, axis=0, keepdims=True) + attention_epsilon)
    return values * scale, scale


def mixing_forward_kernel(
    sides_ref,
    sharp_ref,
    input_ref,
    weight_ref,
    table_ref,
    x1_hbm,
    qkv_hbm,
    mixed_hbm,
    scores_hbm,
    attention_hbm,
    slope_hbm,
    e_hbm,
    sums_ref,
    x1_ref,
    qkv_ref,
    mixed_ref,
    scores_ref,
    attention_ref,
    slope_ref,
    e_ref,
    head_weights,
    out_weight,
    first_low,
    mixed,
    conv_in,
    spread,
    order_ref,
    start_ref,
    sems,
):
    row_count, width = input_ref.shape
    chunks = width // LANES
    saves = [
        pltpu.make_async_copy(source, target, sems.at[index])
        for index, (source, target) in enumerate(
            (
                (qkv_ref, qkv_hbm),
                (scores_ref, scores_hbm),
                (attention_ref, attention_hbm),
                (mixed_ref, mixed_hbm),
                (x1_ref, x1_hbm),
                (slope_ref, slope_hbm),
                (e_ref, e_hbm),
            )
        )
    ]
    total_live = live_total(sides_ref)
    mapping = head_map(BF16)
    for part in range(3):
        head_weights[:, part * PAD_WIDTH : (part + 1) * PAD_WIDTH] = dot(
            weight_ref[part], mapping
        ).astype(BF16)
    spread[...] = jnp.zeros_like(spread)

    def first_norm(first, size, _):
        rows = pl.ds(first, size)
        unit, _ = centered(input_ref[rows, :].astype(F32))
        first_low[rows, :] = (unit * table_ref[0:1, :] + table_ref[1:2, :]).astype(BF16)
        mixed[rows, :] = jnp.zeros((size, PAD_WIDTH), F32)
        return 0

    near = tile_rows(row_count, 4)
    first_norm(0, near, 0)
    for first in range(0, row_count, near):
        if first + near < row_count:
            first_norm(first + near, near, 0)
        rows = pl.ds(first, near)
        qkv_ref[rows, :] = dot(first_low[rows, :], head_weights[...])
    saves[0].start()

    def crop_step(members):
        units_of = [(member, half) for member in range(len(members)) for half in range(2)]
        blocks, results = [], []
        for member, half in units_of:
            crop, rows, keep = members[member]
            lanes = half_lanes(half)
            query = units(jnp.where(keep, qkv_ref[rows, lanes[0]], 0.0))[0]
            key = units(jnp.where(keep, qkv_ref[rows, lanes[1]], 0.0))[0]
            blocks.append(dot_split(dot_rows, split(key), split(query)))
        for (member, half), block in zip(units_of, blocks):
            crop = members[member][0]
            for pair in range(2):
                scores = pair_part(block, pair)
                scores_ref[crop, 2 * half + pair] = scores
                scores = scores * pair_sharpness(sharp_ref, 2 * half + pair)
                scores = jnp.exp(scores - jnp.max(scores, axis=0, keepdims=True))
                shares = scores / jnp.sum(scores, axis=0, keepdims=True)
                attention_ref[crop, 2 * half + pair] = shares
                spread_pair(spread, member, half, pair, shares)
        for member, half in units_of:
            rows = members[member][1]
            shares = (spread[member, half, 0], spread[member, half, 1])
            results.append(dot_split(dot, split(qkv_ref[rows, half_lanes(half)[2]]), shares))
        for (member, half), result in zip(units_of, results):
            _, rows, keep = members[member]
            lanes = half_lanes(half)[0]
            mixed[rows, lanes] = jnp.where(keep, result, mixed[rows, lanes])

    for_crops(sides_ref, row_count, order_ref, start_ref, crop_step)

    saves[1].start()
    saves[2].start()
    out_weight[...] = dot_rows(mapping, weight_ref[3]).astype(BF16)

    def attention_rows(first):
        rows = pl.ds(first, near)
        low = mixed[rows, :].astype(BF16)
        mixed_ref[rows, :] = low
        return dot(low, out_weight[...])

    ahead = attention_rows(0)
    for first in range(0, row_count, near):
        rows = pl.ds(first, near)
        held = ahead
        if first + near < row_count:
            ahead = attention_rows(first + near)
        value = input_ref[rows, :].astype(F32) + table_ref[2:3, :] * held
        x1_ref[rows, :] = value
        unit, _ = centered(value)
        value = unit * table_ref[3:4, :] + table_ref[4:5, :]
        for chunk in range(chunks):
            conv_in[chunk, pl.ds(LEAD + first, near), :] = value[:, chunk_lanes(chunk)]
            slope_ref[chunk, rows, :] = jnp.zeros((near, LANES), F32)
            e_ref[chunk, rows, :] = jnp.zeros((near, LANES), F32)
    saves[3].start()
    saves[4].start()

    zero = jnp.zeros((8, LANES), F32)
    sums_ref[...] = zero
    taps = [tap_vectors(table_ref, 11, chunk) for chunk in range(chunks)]

    def conv_step(row, side, masks, carry):
        rows = pl.ds(row, 8)
        carry = list(carry)
        for chunk in range(chunks):
            value = conv_forward(conv_in, chunk, row, side, masks, taps[chunk])
            share, bell = gelu_parts(value)
            active = value * share
            slope = gelu_slope(value, share, bell)
            slope_ref[chunk, rows, :] = jnp.where(masks[0], slope, slope_ref[chunk, rows, :])
            e_ref[chunk, rows, :] = jnp.where(masks[0], active, e_ref[chunk, rows, :])
            active = jnp.where(masks[0], active, 0.0)
            carry[chunk] = carry[chunk] + active
            carry[chunks + chunk] = carry[chunks + chunk] + active * active
        return tuple(carry)

    sums = for_groups(
        sides_ref,
        conv_step,
        (zero,) * (2 * chunks),
        ((slope_ref, slope_hbm, sems.at[5]), (e_ref, e_hbm, sems.at[6])),
    )
    for index, value in enumerate(sums):
        sums_ref[index : index + 1, :] = jnp.sum(value, axis=0, keepdims=True)
    sums_ref[2 * chunks : 2 * chunks + 1, :] = jnp.full((1, LANES), total_live, jnp.int32).astype(F32)
    for save in saves:
        save.wait()


def mixing_forward(sides, sharpness, inputs, weights, table):
    row_count, width = inputs.shape
    crops = sides.shape[0]
    chunks = width // LANES
    shape = jax.ShapeDtypeStruct
    return pl.pallas_call(
        mixing_forward_kernel,
        out_shape=(
            shape((row_count, width), F32),
            shape((row_count, 3 * PAD_WIDTH), F32),
            shape((row_count, PAD_WIDTH), BF16),
            shape((crops, HEAD_PAIRS, HDIM, LANES), F32),
            shape((crops, HEAD_PAIRS, HDIM, LANES), F32),
            shape((chunks, row_count, LANES), F32),
            shape((chunks, row_count, LANES), F32),
            shape((8, LANES), F32),
        ),
        in_specs=[SMEM_SPEC, SMEM_SPEC, VMEM_SPEC, VMEM_SPEC, VMEM_SPEC],
        out_specs=(ANY_SPEC,) * 7 + (VMEM_SPEC,),
        scratch_shapes=[
            pltpu.VMEM((row_count, width), F32),
            pltpu.VMEM((row_count, 3 * PAD_WIDTH), F32),
            pltpu.VMEM((row_count, PAD_WIDTH), BF16),
            pltpu.VMEM((crops, HEAD_PAIRS, HDIM, LANES), F32),
            pltpu.VMEM((crops, HEAD_PAIRS, HDIM, LANES), F32),
            pltpu.VMEM((chunks, row_count, LANES), F32),
            pltpu.VMEM((chunks, row_count, LANES), F32),
            pltpu.VMEM((width, 3 * PAD_WIDTH), BF16),
            pltpu.VMEM((PAD_WIDTH, width), BF16),
            pltpu.VMEM((row_count, width), BF16),
            pltpu.VMEM((row_count, PAD_WIDTH), F32),
            pltpu.VMEM((chunks, LEAD + row_count + TAIL, LANES), F32),
            pltpu.VMEM((CROP_GROUP, 2, 2, HALF_WIDTH, HALF_WIDTH), BF16),
            pltpu.SMEM((2 * crops,), jnp.int32),
            pltpu.SMEM((crops,), jnp.int32),
            pltpu.SemaphoreType.DMA((7,)),
        ],
        compiler_params=pltpu.CompilerParams(vmem_limit_bytes=VMEM_LIMIT),
        name="mixing_forward",
    )(sides, sharpness, inputs, weights, table)


def batch_vectors(bn_ref, chunk, chunks):
    count = bn_ref[2 * chunks : 2 * chunks + 1, :]
    mean = bn_ref[chunk : chunk + 1, :] / count
    scale = lax.rsqrt(bn_ref[chunks + chunk : chunks + chunk + 1, :] / count - mean * mean + batch_epsilon)
    return mean, scale


def feed_kernel(
    sides_ref,
    x1_hbm,
    e_hbm,
    bn_ref,
    weight_hbm,
    table_ref,
    adjoint_hbm,
    out_hbm,
    dx2_hbm,
    dn_hbm,
    weight_grad_hbm,
    grads_ref,
    back_sums_ref,
    e_ref,
    x1_ref,
    weight_ref,
    adjoint_ref,
    out_ref,
    dx2_ref,
    dn_ref,
    weight_grad_ref,
    up_weight,
    n_ref,
    z_ref,
    dw_ref,
    x2,
    unit,
    spread,
    third_low,
    hidden_low,
    feed,
    third_grad,
    feed_grad,
    pre_grad,
    grads,
    up_sum,
    down_sum,
    weight_low,
    sems,
    tile_sems,
):
    loads = [
        pltpu.make_async_copy(source, target, sems.at[index])
        for index, (source, target) in enumerate(
            (
                (x1_hbm, x1_ref),
                (weight_hbm, weight_ref),
                (adjoint_hbm, adjoint_ref),
            )
        )
    ]
    saves = [
        pltpu.make_async_copy(source, target, sems.at[4 + index])
        for index, (source, target) in enumerate(
            (
                (out_ref, out_hbm),
                (dx2_ref, dx2_hbm),
                (weight_grad_ref, weight_grad_hbm),
                (dn_ref, dn_hbm),
            )
        )
    ]

    tiled = [(e_hbm, e_ref, True)]

    def start_tile(first, size, _):
        for load in row_copies(tiled, first, size, tile_sems.at[lax.div(first, ROW_TILE)]):
            load.start()
        return 0

    for_rows(x1_hbm.shape[0], ROW_TILE, start_tile)
    for load in loads:
        load.start()
    row_count, width = x1_ref.shape
    chunks = width // LANES
    expand = weight_ref.shape[0] // 2
    tile = tile_rows(row_count, 4)
    total_live = live_total(sides_ref)
    hidden = expand * width
    batch = [batch_vectors(bn_ref, chunk, chunks) for chunk in range(chunks)]
    zero = jnp.zeros((8, LANES), F32)

    def down_weight():
        return weight_ref[expand : 2 * expand].reshape(hidden, width)

    def normalize(first, size, _):
        for load in row_copies(tiled, first, size, tile_sems.at[lax.div(first, ROW_TILE)]):
            load.wait()
        rows = pl.ds(first, size)
        live = row_mask(first, size, LANES, total_live)
        for chunk in range(chunks):
            lanes = chunk_lanes(chunk)
            mean, scale = batch[chunk]
            value = (e_ref[chunk, rows, :] - mean) * scale
            value = value * table_ref[5:6, lanes] + table_ref[6:7, lanes]
            n_ref[chunk, pl.ds(LEAD + first, size), :] = jnp.where(live, value, 0.0)
            z_ref[chunk, rows, :] = jnp.zeros((size, LANES), F32)
            dn_ref[chunk, rows, :] = jnp.zeros((size, LANES), F32)
        return 0

    for_rows(row_count, ROW_TILE, normalize)

    taps = [tap_vectors(table_ref, 20, chunk) for chunk in range(chunks)]

    def conv_step(row, side, masks, carry):
        rows = pl.ds(row, 8)
        for chunk in range(chunks):
            value = conv_forward(n_ref, chunk, row, side, masks, taps[chunk])
            z_ref[chunk, rows, :] = jnp.where(masks[0], value, z_ref[chunk, rows, :])
        return carry

    for_groups(sides_ref, conv_step, 0)

    for load in loads:
        load.wait()
    for part in range(expand):
        up_weight[:, part * width : (part + 1) * width] = weight_ref[part]
    up_sum[...] = jnp.zeros_like(up_sum)
    down_sum[...] = jnp.zeros_like(down_sum)
    grads[...] = jnp.zeros_like(grads)

    def z_rows(rows):
        return jnp.concatenate([z_ref[chunk, rows, :] for chunk in range(chunks)], axis=1)

    def before(base):
        rows = pl.ds(base, tile)
        value = x1_ref[rows, :] + table_ref[7:8, :] * z_rows(rows)
        x2[...] = value
        value, scale = centered(value)
        unit[...] = value
        spread[...] = jnp.broadcast_to(scale, (tile, LANES))
        third_low[...] = (value * table_ref[8:9, :] + table_ref[9:10, :]).astype(BF16)
        feed_grad[...] = (entry_rows(base) * table_ref[10:11, :]).astype(BF16)

    def entry_rows(base):
        live = row_mask(base, tile, width, total_live)
        return jnp.where(live, adjoint_ref[pl.ds(base, tile), :].astype(F32), 0.0)

    @pl.loop(0, row_count // tile)
    def _(step):
        base = pl.multiple_of(step * tile, 16)
        rows = pl.ds(base, tile)
        before(base)

        def hidden_lanes(part):
            return slice(part * hidden // HIDDEN_PARTS, (part + 1) * hidden // HIDDEN_PARTS)

        def products(part):
            lanes = hidden_lanes(part)
            return (
                dot(third_low[...], up_weight[:, lanes]),
                dot_lanes(feed_grad[...], down_weight()[lanes]),
            )

        ahead = products(0)
        for part in range(HIDDEN_PARTS):
            lanes = hidden_lanes(part)
            value, hidden_grad = ahead
            if part + 1 < HIDDEN_PARTS:
                ahead = products(part + 1)
            share, bell = gelu_parts(value)
            hidden_low[:, lanes] = (value * share).astype(BF16)
            pre_grad[:, lanes] = (hidden_grad * gelu_slope(value, share, bell)).astype(BF16)
        feed[...] = dot(hidden_low[...], down_weight())
        third_grad[...] = dot_lanes(pre_grad[...], up_weight[...])
        down_sum[...] += dot_rows(feed_grad[...], hidden_low[...])
        up_sum[...] += dot_rows(third_low[...], pre_grad[...])

        value = x2[...] + table_ref[10:11, :] * feed[...]
        live = row_mask(base, tile, width, total_live)
        out_ref[rows, :] = jnp.where(live, value, 0.0).astype(BF16)
        entry = entry_rows(base)
        grads[0] += fold(entry * feed[...])
        grad = third_grad[...]
        value = unit[...]
        total = entry + norm_back(grad * table_ref[8:9, :], value, spread[:, 0:1])
        dx2_ref[rows, :] = total
        scaled = total * table_ref[7:8, :]
        for chunk in range(chunks):
            dw_ref[chunk, pl.ds(LEAD + base, tile), :] = scaled[:, chunk_lanes(chunk)]
        grads[1] += fold(total * z_rows(rows))
        grads[2] += fold(grad * value)
        grads[3] += fold(grad)

    saves[0].start()
    saves[1].start()

    for part in range(expand):
        lanes = slice(part * width, (part + 1) * width)
        weight_low[part] = up_sum[:, lanes].astype(BF16)
        weight_low[expand + part] = down_sum[:, lanes].T.astype(BF16)

    owners, pieces, shard, _ = weight_grad_ref.shape
    inner = width // shard
    for owner in range(owners):
        rows = slice(owner % inner * shard, (owner % inner + 1) * shard)
        for piece in range(pieces):
            weight_grad_ref[owner, piece] = weight_low[owner // inner * pieces + piece, rows, :]

    saves[2].start()

    back_sums_ref[...] = zero
    for index, source in enumerate((1, 2, 3, 0)):
        grads_ref[index : index + 1, :] = jnp.sum(grads[source], axis=0, keepdims=True)
    def back_step(row, side, masks, carry):
        rows = pl.ds(row, 8)
        result = []
        for chunk in range(chunks):
            mean, scale = batch[chunk]
            sums = carry[chunk]
            own = jnp.where(masks[0], n_ref[chunk, pl.ds(LEAD + row, 8), :], 0.0)
            total, tap_sums = conv_backward(
                dw_ref, chunk, row, side, masks, taps[chunk], own, sums[0:9]
            )
            dn_ref[chunk, rows, :] = jnp.where(masks[0], total, dn_ref[chunk, rows, :])
            total = jnp.where(masks[0], total, 0.0)
            standard = (e_ref[chunk, rows, :] - mean) * scale
            result.append((*tap_sums, sums[9] + total * standard, sums[10] + total))
        return tuple(result)

    sums = for_groups(
        sides_ref, back_step, ((zero,) * 11,) * chunks, ((dn_ref, dn_hbm, sems.at[7]),)
    )
    for chunk in range(chunks):
        lanes = chunk_lanes(chunk)
        for index, value in enumerate(sums[chunk]):
            value = jnp.sum(value, axis=0, keepdims=True)
            grads_ref[4 + index : 5 + index, lanes] = value
            if index == 9:
                back_sums_ref[chunks + chunk : chunks + chunk + 1, :] = value
            if index == 10:
                back_sums_ref[chunk : chunk + 1, :] = value
    for save in saves:
        save.wait()


def feed_forward(sides, x1, e, batch_sums, weights, table, adjoint, grad_shape):
    row_count, width = x1.shape
    chunks = width // LANES
    expand = weights.shape[0] // 2
    tile = tile_rows(row_count, 4)
    shape = jax.ShapeDtypeStruct
    return pl.pallas_call(
        feed_kernel,
        out_shape=(
            shape((row_count, width), BF16),
            shape((row_count, width), F32),
            shape((chunks, row_count, LANES), F32),
            shape(grad_shape, BF16),
            shape((16, width), F32),
            shape((8, LANES), F32),
        ),
        in_specs=[SMEM_SPEC, ANY_SPEC, ANY_SPEC, VMEM_SPEC, ANY_SPEC, VMEM_SPEC, ANY_SPEC],
        out_specs=(ANY_SPEC,) * 4 + (VMEM_SPEC,) * 2,
        scratch_shapes=[
            pltpu.VMEM((chunks, row_count, LANES), F32),
            pltpu.VMEM((row_count, width), F32),
            pltpu.VMEM(weights.shape, BF16),
            pltpu.VMEM((row_count, width), BF16),
            pltpu.VMEM((row_count, width), BF16),
            pltpu.VMEM((row_count, width), F32),
            pltpu.VMEM((chunks, row_count, LANES), F32),
            pltpu.VMEM(grad_shape, BF16),
            pltpu.VMEM((width, expand * width), BF16),
            pltpu.VMEM((chunks, LEAD + row_count + TAIL, LANES), F32),
            pltpu.VMEM((chunks, row_count, LANES), F32),
            pltpu.VMEM((chunks, LEAD + row_count + TAIL, LANES), F32),
            pltpu.VMEM((tile, width), F32),
            pltpu.VMEM((tile, width), F32),
            pltpu.VMEM((tile, LANES), F32),
            pltpu.VMEM((tile, width), BF16),
            pltpu.VMEM((tile, expand * width), BF16),
            pltpu.VMEM((tile, width), F32),
            pltpu.VMEM((tile, width), F32),
            pltpu.VMEM((tile, width), BF16),
            pltpu.VMEM((tile, expand * width), BF16),
            pltpu.VMEM((4, 8, width), F32),
            pltpu.VMEM((width, expand * width), F32),
            pltpu.VMEM((width, expand * width), F32),
            pltpu.VMEM(weights.shape, BF16),
            pltpu.SemaphoreType.DMA((8,)),
            pltpu.SemaphoreType.DMA(((row_count + ROW_TILE - 1) // ROW_TILE,)),
        ],
        compiler_params=pltpu.CompilerParams(vmem_limit_bytes=VMEM_LIMIT),
        name="feed_forward",
    )(sides, x1, e, batch_sums, weights, table, adjoint)


def mixing_backward_kernel(
    sides_ref,
    sharp_ref,
    input_hbm,
    weight_ref,
    table_ref,
    x1_hbm,
    qkv_hbm,
    mixed_hbm,
    scores_hbm,
    attention_hbm,
    slope_hbm,
    e_hbm,
    bn_ref,
    dx2_hbm,
    dn_hbm,
    back_ref,
    head_low_hbm,
    dx1_hbm,
    head_weights_hbm,
    weight_grad_ref,
    grads_ref,
    x1_ref,
    qkv_ref,
    mixed_ref,
    scores_ref,
    attention_ref,
    dx2_ref,
    head_weights,
    out_weight,
    pool,
    conv_grad,
    mixed_grad,
    first_low,
    head_low,
    spread,
    out_sum,
    head_sum,
    sharp_sums,
    order_ref,
    start_ref,
    load_sems,
    tile_sems,
):
    row_count, width = input_hbm.shape
    low_rows, input_ref = head_low.at[:, 0:width], head_low.at[:, PAD_WIDTH : PAD_WIDTH + width]
    tile = tile_rows(row_count, 2)
    input_load = pltpu.make_async_copy(input_hbm, input_ref, load_sems.at[11 + row_count // tile])
    input_load.start()
    chunks = width // LANES
    slope_ref, e_ref = pool.at[0:chunks], pool.at[chunks : 2 * chunks]
    dn_ref, conv_in = pool.at[2 * chunks : 3 * chunks], pool.at[3 * chunks : 4 * chunks]
    attention_out = slope_ref
    loads = [
        pltpu.make_async_copy(source, target, load_sems.at[index])
        for index, (source, target) in enumerate(
            (
                (mixed_hbm, mixed_ref),
                (dx2_hbm, dx2_ref),
                (qkv_hbm, qkv_ref),
                (scores_hbm, scores_ref),
                (attention_hbm, attention_ref),
            )
        )
    ]
    saves = [
        pltpu.make_async_copy(source, target, load_sems.at[len(loads) + index])
        for index, (source, target) in enumerate(
            (
                (head_weights, head_weights_hbm),
                (dx2_ref, dx1_hbm),
            )
        )
    ]
    for step in range(row_count // tile):
        rows = pl.ds(step * tile, tile)
        saves.append(
            pltpu.make_async_copy(
                head_low.at[rows], head_low_hbm.at[rows], load_sems.at[len(loads) + 3 + step]
            )
        )
    tiled = [
        (x1_hbm, x1_ref, False),
        (slope_hbm, slope_ref, True),
        (e_hbm, e_ref, True),
        (dn_hbm, dn_ref, True),
    ]

    def start_tile(first, size, _):
        for load in row_copies(tiled, first, size, tile_sems.at[lax.div(first, ROW_TILE)]):
            load.start()
        return 0

    for_rows(row_count, ROW_TILE, start_tile)
    for load in loads:
        load.start()
    tile = tile_rows(row_count, 2)
    total_live = live_total(sides_ref)
    batch = [batch_vectors(bn_ref, chunk, chunks) for chunk in range(chunks)]
    zero = jnp.zeros((8, LANES), F32)
    wide = jnp.zeros((8, width), F32)
    mapping = head_map(BF16)
    for part in range(3):
        head_weights[:, part * PAD_WIDTH : (part + 1) * PAD_WIDTH] = dot(
            weight_ref[part], mapping
        ).astype(BF16)
    saves[0].start()
    out_weight[...] = dot_rows(mapping, weight_ref[3]).astype(BF16)
    spread[...] = jnp.zeros_like(spread)

    def first_norm(first, size, _):
        rows = pl.ds(first, size)
        unit, _ = centered(input_ref[rows, :].astype(F32))
        first_low[rows, :] = (unit * table_ref[0:1, :] + table_ref[1:2, :]).astype(BF16)
        return 0

    input_load.wait()
    for_rows(row_count, ROW_TILE, first_norm)


    def batch_back(first, size, _):
        for load in row_copies(tiled, first, size, tile_sems.at[lax.div(first, ROW_TILE)]):
            load.wait()
        rows = pl.ds(first, size)
        live = row_mask(first, size, LANES, total_live)
        unit, _ = centered(x1_ref[rows, :])
        value = unit * table_ref[3:4, :] + table_ref[4:5, :]
        for chunk in range(chunks):
            lanes = chunk_lanes(chunk)
            mean, scale = batch[chunk]
            count = bn_ref[2 * chunks : 2 * chunks + 1, :]
            standard = (e_ref[chunk, rows, :] - mean) * scale
            inner = (
                back_ref[chunk : chunk + 1, :]
                + standard * back_ref[chunks + chunk : chunks + chunk + 1, :]
            ) / count
            grad = scale * table_ref[5:6, lanes] * (dn_ref[chunk, rows, :] - inner)
            grad = grad * slope_ref[chunk, rows, :]
            conv_grad[chunk, pl.ds(LEAD + first, size), :] = jnp.where(live, grad, 0.0)
            conv_in[chunk, pl.ds(first, size), :] = value[:, lanes]
        return 0

    for_rows(row_count, ROW_TILE, batch_back)

    taps = [tap_vectors(table_ref, 11, chunk) for chunk in range(chunks)]

    def back_step(row, side, masks, carry):
        rows = pl.ds(row, 8)
        result = []
        for chunk in range(chunks):
            held = conv_in[chunk, rows, :]
            own = jnp.where(masks[0], held, 0.0)
            total, tap_sums = conv_backward(
                conv_grad, chunk, row, side, masks, taps[chunk], own, carry[chunk]
            )
            conv_in[chunk, rows, :] = jnp.where(masks[0], total, held)
            result.append(tap_sums)
        return tuple(result)

    tap_sums = for_groups(sides_ref, back_step, ((zero,) * 9,) * chunks)
    for chunk in range(chunks):
        for index, value in enumerate(tap_sums[chunk]):
            grads_ref[5 + index : 6 + index, chunk_lanes(chunk)] = jnp.sum(
                value, axis=0, keepdims=True
            )

    for load in loads[0:2]:
        load.wait()

    def attention_rows(first):
        return dot(mixed_ref[pl.ds(first, near), :], out_weight[...])

    near = tile_rows(row_count, 4)
    out_sum[...] = jnp.zeros_like(out_sum)
    ahead = attention_rows(0)
    sums = [jnp.zeros((8, width), F32)] * 3
    for first in range(0, row_count, near):
        rows = pl.ds(first, near)
        held = ahead
        if first + near < row_count:
            ahead = attention_rows(first + near)
        live = row_mask(first, near, width, total_live)
        grad = jnp.concatenate([conv_in[chunk, rows, :] for chunk in range(chunks)], axis=1)
        grad = jnp.where(live, grad, 0.0)
        unit, scale = centered(x1_ref[rows, :])
        total = dx2_ref[rows, :] + norm_back(grad * table_ref[3:4, :], unit, scale)
        dx2_ref[rows, :] = total
        low = (total * table_ref[2:3, :]).astype(BF16)
        sums[0] = sums[0] + fold(total * held)
        sums[1] = sums[1] + fold(grad * unit)
        sums[2] = sums[2] + fold(grad)
        mixed_grad[rows, :] = dot_lanes(low, out_weight[...])
        out_sum[...] += dot_rows(mixed_ref[rows, :], low)
    saves[1].start()
    for index in range(3):
        grads_ref[2 + index : 3 + index, :] = jnp.sum(sums[index], axis=0, keepdims=True)

    pool[...] = jnp.zeros_like(pool)

    low = out_sum[...].astype(BF16)
    weight_grad_ref[3] = dot(mapping, low).astype(BF16)
    sharp_sums[...] = jnp.zeros_like(sharp_sums)

    for load in loads[2:]:
        load.wait()

    def crop_step(members):
        units_of = [(member, half) for member in range(len(members)) for half in range(2)]
        grads, blocks, sums, results = [], [], [], []
        for member, half in units_of:
            crop, rows, keep = members[member]
            lanes = half_lanes(half)
            value = split(jnp.where(keep, qkv_ref[rows, lanes[2]], 0.0))
            grad = split(jnp.where(keep, mixed_grad[rows, lanes[0]], 0.0))
            grads.append(grad)
            blocks.append(dot_split(dot_rows, value, grad))
        value_grads = []
        for index, (member, half) in enumerate(units_of):
            for pair in range(2):
                shares = attention_ref[members[member][0], 2 * half + pair]
                spread_pair(spread, member, half, pair, shares)
            shares = (spread[member, half, 0], spread[member, half, 1])
            value_grads.append(dot_split(dot_lanes, grads[index], shares))
        for (member, half), block in zip(units_of, blocks):
            crop = members[member][0]
            query_sums = []
            for pair in range(2):
                index = 2 * half + pair
                shares = attention_ref[crop, index]
                scores = scores_ref[crop, index]
                part = pair_part(block, pair)
                part = shares * (part - jnp.sum(part * shares, axis=0, keepdims=True))
                total = jnp.sum(part * scores, axis=0, keepdims=True)
                sharp_sums[index, pl.ds(crop, 1), :] = total
                sharpness = pair_sharpness(sharp_ref, index)
                query_sums.append(total * sharpness)
                spread_pair(spread, member, 2 + half, pair, part * sharpness)
            sums.append(jnp.concatenate(query_sums, axis=1))
        for index, (member, half) in enumerate(units_of):
            crop, rows, keep = members[member]
            lanes = half_lanes(half)
            query, query_scale = units(jnp.where(keep, qkv_ref[rows, lanes[0]], 0.0))
            key, key_scale = units(jnp.where(keep, qkv_ref[rows, lanes[1]], 0.0))
            slopes = (spread[member, 2 + half, 0], spread[member, 2 + half, 1])
            query_grad = dot_split(dot, split(key), slopes)
            query_grad = query_scale * (query_grad - query * sums[index])
            key_grad = dot_split(dot_lanes, split(query), slopes)
            key_grad = key_scale * (
                key_grad - key * jnp.sum(key_grad * key, axis=0, keepdims=True)
            )
            results.append((query_grad, key_grad, value_grads[index]))
        for (member, half), grads in zip(units_of, results):
            _, rows, keep = members[member]
            for part, result in enumerate(grads):
                for side in range(HALF_WIDTH // LANES):
                    chunk = (part * PAD_WIDTH + half * HALF_WIDTH) // LANES + side
                    pool[chunk, rows, :] = jnp.where(
                        keep[:, 0:LANES], result[:, chunk_lanes(side)], pool[chunk, rows, :]
                    )

    for_crops(sides_ref, row_count, order_ref, start_ref, crop_step)

    grads_ref[0:2, :] = jnp.zeros((2, width), F32)
    grads_ref[14:16, :] = jnp.zeros((2, width), F32)
    lane = lax.broadcasted_iota(jnp.int32, (1, LANES), 1)
    total = jnp.zeros((1, LANES), F32)
    for head in range(HEAD_NUMBER):
        row = jnp.sum(sharp_sums[head // 2], axis=0, keepdims=True)
        row = jnp.where((lane >> 6) == head % 2, row, 0.0)
        total = jnp.where(lane == head, jnp.sum(row, axis=1, keepdims=True), total)
    grads_ref[14:15, 0:LANES] = total

    head_sum[...] = jnp.zeros_like(head_sum)
    for step in range(row_count // tile):
        rows = pl.ds(step * tile, tile)
        for chunk in range(3 * PAD_WIDTH // LANES):
            head_low[rows, chunk_lanes(chunk)] = pool[chunk, rows, :].astype(BF16)
        saves[2 + step].start()
        head_sum[...] += dot_rows(first_low[rows, :], head_low[rows, :])
    for part in range(3):
        low = head_sum[:, part * PAD_WIDTH : (part + 1) * PAD_WIDTH].astype(BF16)
        weight_grad_ref[part] = dot_lanes(low, mapping).astype(BF16)
    for save in saves:
        save.wait()


def mixing_backward(sides, sharpness, inputs, weights, table, saved, batch_sums, dx2, dn, back_sums):
    row_count, width = inputs.shape
    chunks = width // LANES
    crops = sides.shape[0]
    shape = jax.ShapeDtypeStruct
    x1, qkv, mixed, scores, attention, slope, e = saved
    return pl.pallas_call(
        mixing_backward_kernel,
        out_shape=(
            shape((row_count, 3 * PAD_WIDTH), BF16),
            shape((row_count, width), F32),
            shape((width, 3 * PAD_WIDTH), BF16),
            shape((4, width, width), BF16),
            shape((16, width), F32),
        ),
        in_specs=[SMEM_SPEC, SMEM_SPEC]
        + [ANY_SPEC, VMEM_SPEC, VMEM_SPEC]
        + [ANY_SPEC] * 7
        + [VMEM_SPEC, ANY_SPEC, ANY_SPEC, VMEM_SPEC],
        out_specs=(ANY_SPEC,) * 3 + (VMEM_SPEC,) * 2,
        scratch_shapes=[
            pltpu.VMEM((row_count, width), F32),
            pltpu.VMEM((row_count, 3 * PAD_WIDTH), F32),
            pltpu.VMEM((row_count, PAD_WIDTH), BF16),
            pltpu.VMEM((crops, HEAD_PAIRS, HDIM, LANES), F32),
            pltpu.VMEM((crops, HEAD_PAIRS, HDIM, LANES), F32),
            pltpu.VMEM((row_count, width), F32),
            pltpu.VMEM((width, 3 * PAD_WIDTH), BF16),
            pltpu.VMEM((PAD_WIDTH, width), BF16),
            pltpu.VMEM((3 * PAD_WIDTH // LANES, row_count, LANES), F32),
            pltpu.VMEM((chunks, LEAD + row_count + TAIL, LANES), F32),
            pltpu.VMEM((row_count, PAD_WIDTH), F32),
            pltpu.VMEM((row_count, width), BF16),
            pltpu.VMEM((row_count, 3 * PAD_WIDTH), BF16),
            pltpu.VMEM((CROP_GROUP, 4, 2, HALF_WIDTH, HALF_WIDTH), BF16),
            pltpu.VMEM((PAD_WIDTH, width), F32),
            pltpu.VMEM((width, 3 * PAD_WIDTH), F32),
            pltpu.VMEM((HEAD_PAIRS, crops, LANES), F32),
            pltpu.SMEM((2 * crops,), jnp.int32),
            pltpu.SMEM((crops,), jnp.int32),
            pltpu.SemaphoreType.DMA((12 + row_count // tile_rows(row_count, 2),)),
            pltpu.SemaphoreType.DMA(((row_count + ROW_TILE - 1) // ROW_TILE,)),
        ],
        compiler_params=pltpu.CompilerParams(vmem_limit_bytes=VMEM_LIMIT),
        name="mixing_backward",
    )(
        sides,
        sharpness,
        inputs,
        weights,
        table,
        x1,
        qkv,
        mixed,
        scores,
        attention,
        slope,
        e,
        batch_sums,
        dx2,
        dn,
        back_sums,
    )


MESH = pl.DeviceIdType.MESH


def greet(peers):
    barrier = pltpu.get_barrier_semaphore()
    for peer in peers:
        pl.semaphore_signal(barrier, inc=1, device_id=peer, device_id_type=MESH)
    pl.semaphore_wait(barrier, len(peers))


def push(source, target, send, receive, peer):
    copy = pltpu.make_async_remote_copy(
        src_ref=source,
        dst_ref=target,
        send_sem=send,
        recv_sem=receive,
        device_id=peer,
        device_id_type=MESH,
    )
    copy.start()
    return copy


def turned(place, step, count):
    return lax.rem(place + step, count)


def ring_peers(axis, count):
    place = lax.axis_index(axis)
    return [{axis: turned(place, step, count)} for step in range(1, count)]


def comm_params(identity):
    return pltpu.CompilerParams(
        collective_id=identity, has_side_effects=True, vmem_limit_bytes=VMEM_LIMIT
    )


def flip(value, bits):
    for bit in (1, 2, 4):
        if bits & bit:
            value = value + bit - 2 * bit * lax.rem(lax.div(value, bit), 2)
    return value


def flip_peers(axis, count):
    place = lax.axis_index(axis)
    return [{axis: flip(place, bits)} for bits in range(1, count)]


def sum_all_kernel(counts, part_ref, total_ref, parts, send, receive):
    n_dp, n_fsdp = counts
    dp, fsdp = lax.axis_index("dp"), lax.axis_index("fsdp")
    place = dp * n_fsdp + fsdp
    peers = [
        {"dp": flip(dp, outer), "fsdp": flip(fsdp, inner)}
        for inner in reversed(range(n_fsdp))
        for outer in reversed(range(n_dp))
        if inner or outer
    ]
    greet(peers)
    parts[place] = part_ref[...]
    copies = [
        push(part_ref, parts.at[place], send.at[k], receive.at[k], peer)
        for k, peer in enumerate(peers)
    ]
    for copy in copies:
        copy.wait()
    total = parts[0]
    for k in range(1, n_dp * n_fsdp):
        total = total + parts[k]
    total_ref[...] = total


def sum_all(part, counts, identity):
    size = counts[0] * counts[1]
    return pl.pallas_call(
        functools.partial(sum_all_kernel, counts),
        out_shape=jax.ShapeDtypeStruct(part.shape, F32),
        in_specs=[VMEM_SPEC],
        out_specs=VMEM_SPEC,
        scratch_shapes=[
            pltpu.VMEM((size, *part.shape), F32),
            pltpu.SemaphoreType.DMA((size - 1,)),
            pltpu.SemaphoreType.DMA((size - 1,)),
        ],
        compiler_params=comm_params(identity),
        name="sum_all",
    )(part)


def sum_pair_kernel(
    counts, part_ref, blocks_hbm, total_ref, sums_hbm, parts, own, other, sums_ref, send, receive, sems
):
    n_dp, n_fsdp = counts
    dp, fsdp = lax.axis_index("dp"), lax.axis_index("fsdp")
    core = lax.rem(dp, 2)
    place = dp * n_fsdp + fsdp
    peers = [
        {"dp": flip(dp, outer), "fsdp": flip(fsdp, inner)}
        for inner in reversed(range(n_fsdp))
        for outer in reversed(range(n_dp))
        if inner or outer
    ]
    load = pltpu.make_async_copy(blocks_hbm.at[pl.ds(core * n_fsdp, n_fsdp)], own, sems.at[0])
    load.start()
    greet(peers)
    parts[place] = part_ref[...]
    copies = [
        push(part_ref, parts.at[place], send.at[k], receive.at[k], peer)
        for k, peer in enumerate(peers)
    ]
    blocks = push(
        blocks_hbm.at[pl.ds((1 - core) * n_fsdp, n_fsdp)],
        other,
        sems.at[1],
        sems.at[2],
        {"dp": flip(dp, 1)},
    )
    load.wait()
    blocks.wait_recv()
    for owner in range(n_fsdp):
        sums_ref[owner] = (own[owner].astype(F32) + other[owner].astype(F32)).astype(BF16)
    save = pltpu.make_async_copy(sums_ref, sums_hbm, sems.at[3])
    save.start()
    for copy in copies:
        copy.wait()
    total = parts[0]
    for k in range(1, n_dp * n_fsdp):
        total = total + parts[k]
    total_ref[...] = total
    blocks.wait_send()
    save.wait()


def sum_pair(part, blocks, counts, identity):
    size = counts[0] * counts[1]
    half = (counts[1], *blocks.shape[1:])
    shape = jax.ShapeDtypeStruct
    return pl.pallas_call(
        functools.partial(sum_pair_kernel, counts),
        out_shape=(shape(part.shape, F32), shape(half, BF16)),
        in_specs=[VMEM_SPEC, ANY_SPEC],
        out_specs=(VMEM_SPEC, ANY_SPEC),
        scratch_shapes=[
            pltpu.VMEM((size, *part.shape), F32),
            pltpu.VMEM(half, BF16),
            pltpu.VMEM(half, BF16),
            pltpu.VMEM(half, BF16),
            pltpu.SemaphoreType.DMA((size - 1,)),
            pltpu.SemaphoreType.DMA((size - 1,)),
            pltpu.SemaphoreType.DMA((4,)),
        ],
        compiler_params=comm_params(identity),
        name="sum_pair",
    )(part, blocks)


def gather_kernel(
    counts,
    masters_hbm,
    table_ref,
    blocks_hbm,
    full_table_ref,
    blocks,
    masters,
    tables,
    stage,
    ring_send,
    ring_recv,
    table_send,
    table_recv,
    cross_send,
    cross_recv,
    pair_send,
    pair_recv,
    local_sems,
):
    n_dp, n_fsdp = counts
    dp, fsdp = lax.axis_index("dp"), lax.axis_index("fsdp")
    shard, width = masters_hbm.shape[1:]
    columns = table_ref.shape[1]
    load = pltpu.make_async_copy(masters_hbm.at[dp], masters, local_sems.at[0])
    load.start()
    across = lax.rem(dp + 2, 4)
    pair = dp + 1 - 2 * lax.rem(dp, 2)
    peers = flip_peers("fsdp", n_fsdp)
    greet(peers + [{"dp": across}, {"dp": pair}])

    def piece(block, owner):
        return blocks.at[block, pl.ds(pl.multiple_of(owner * shard, 16), shard), :]

    def origin(step):
        return flip(fsdp, step)

    stage[...] = jnp.zeros_like(stage)
    stage[0 : table_ref.shape[0], 0:columns] = table_ref[...]
    tables[fsdp] = stage[...].astype(BF16)
    load.wait()
    blocks[dp, pl.ds(pl.multiple_of(fsdp * shard, 16), shard), :] = masters[...].astype(BF16)
    own = piece(dp, fsdp)
    ring = [
        push(own, own, ring_send.at[k], ring_recv.at[k], peer) for k, peer in enumerate(peers)
    ]
    table_copies = [
        push(tables.at[fsdp], tables.at[fsdp], table_send.at[k], table_recv.at[k], peer)
        for k, peer in enumerate(peers)
    ]
    crossing, pairing = [], []
    for step in range(n_fsdp):
        if step:
            ring[step - 1].wait_recv()
        part = piece(dp, origin(step))
        crossing.append(push(part, part, cross_send.at[step], cross_recv.at[step], {"dp": across}))
        pairing.append(
            push(part, part, pair_send.at[0, step], pair_recv.at[0, step], {"dp": pair})
        )
    for step in range(n_fsdp):
        crossing[step].wait_recv()
        part = piece(across, origin(step))
        pairing.append(
            push(part, part, pair_send.at[1, step], pair_recv.at[1, step], {"dp": pair})
        )
    for copy in table_copies:
        copy.wait_recv()
    total = None
    for owner in range(n_fsdp):
        lane = lax.broadcasted_iota(jnp.int32, (LANES, width), 0)
        target = lax.broadcasted_iota(jnp.int32, (LANES, width), 1)
        hit = (lane < columns) & (lane + owner * columns == target)
        term = dot(tables[owner], hit.astype(F32).astype(BF16))
        total = term if total is None else total + term
    full_table_ref[...] = total
    for copy in pairing:
        copy.wait_recv()
    save = pltpu.make_async_copy(blocks, blocks_hbm, local_sems.at[1])
    save.start()
    for copy in ring + table_copies + crossing + pairing:
        copy.wait_send()
    save.wait()


def gather_start(masters, coefficients, counts, identity):
    n_dp, n_fsdp = counts
    width = masters.shape[2]
    shape = jax.ShapeDtypeStruct
    dma = pltpu.SemaphoreType.DMA
    return pl.pallas_call(
        functools.partial(gather_kernel, counts),
        out_shape=(shape((4, width, width), BF16), shape((32, width), F32)),
        in_specs=[ANY_SPEC, VMEM_SPEC],
        out_specs=(ANY_SPEC, VMEM_SPEC),
        scratch_shapes=[
            pltpu.VMEM((4, width, width), BF16),
            pltpu.VMEM(masters.shape[1:], F32),
            pltpu.VMEM((n_fsdp, 32, LANES), BF16),
            pltpu.VMEM((32, LANES), F32),
            dma((n_fsdp - 1,)),
            dma((n_fsdp - 1,)),
            dma((n_fsdp - 1,)),
            dma((n_fsdp - 1,)),
            dma((n_fsdp,)),
            dma((n_fsdp,)),
            dma((2, n_fsdp)),
            dma((2, n_fsdp)),
            dma((2,)),
        ],
        compiler_params=comm_params(identity),
        name="gather_start",
    )(masters, coefficients)


def owner_rows(owner, shard):
    return pl.ds(pl.multiple_of(owner * shard, 16), shard)


TABLE_ROWS = (
    [(0, row) for row in range(5)]
    + [(1, 13), (1, 14)]
    + [(1, row) for row in range(4)]
    + [(0, row) for row in range(5, 14)]
    + [(1, row) for row in range(4, 13)]
)


def settle_kernel(
    counts,
    place_ref,
    mix_hbm,
    feed_hbm,
    mix_table_ref,
    feed_table_ref,
    left_hbm,
    right_hbm,
    head_low_hbm,
    dx1_hbm,
    input_hbm,
    head_weights_hbm,
    coefficient_ref,
    grad_hbm,
    slots_hbm,
    rows_hbm,
    table_ref,
    out_hbm,
    left,
    right,
    head_low,
    dx1,
    inputs,
    head_weights,
    out,
    first_sums,
    pair_buf,
    cross_out,
    cross_buf,
    ring_out,
    ring_buf,
    feed_in,
    feed_buf,
    dp_buf,
    slot_out,
    slots,
    steps,
    rows_buf,
    table_stage,
    table_rows,
    table_out,
    table_buf,
    table_part,
    table_dp,
    feed_sum,
    mix,
    feed_ref,
    left_parts,
    grad_ref,
    load_sems,
    pair_send,
    pair_recv,
    cross_send,
    cross_recv,
    ring_send,
    ring_recv,
    feed_in_send,
    feed_in_recv,
    feed_send,
    feed_recv,
    dp_send,
    dp_recv,
    slot_send,
    slot_recv,
    twin_send,
    twin_recv,
    back_send,
    back_recv,
    last_send,
    last_recv,
    table_rows_send,
    table_rows_recv,
    table_send,
    table_recv,
    table_dp_send,
    table_dp_recv,
):
    n_dp, n_fsdp = counts
    dp, fsdp = lax.axis_index("dp"), lax.axis_index("fsdp")
    width = mix_hbm.shape[2]
    shard = width // n_fsdp
    core = lax.rem(dp, 2)
    across, pair, pair_across = flip(dp, 2), flip(dp, 1), flip(dp, 3)
    peers, dp_peers = flip_peers("fsdp", n_fsdp), flip_peers("dp", n_dp)
    to_pair, to_across = {"dp": pair}, {"dp": across}
    loads = [
        pltpu.make_async_copy(left_hbm.at[core], left, load_sems.at[0]),
        pltpu.make_async_copy(right_hbm.at[core], right, load_sems.at[1]),
    ]
    mix_loads = [
        pltpu.make_async_copy(mix_hbm.at[across], mix.at[0], load_sems.at[3]),
        pltpu.make_async_copy(mix_hbm.at[dp], mix.at[1], load_sems.at[4]),
    ]
    feed_load = pltpu.make_async_copy(feed_hbm, feed_ref, load_sems.at[5])
    for load in mix_loads:
        load.start()
    feed_load.start()
    row_count = dx1.shape[0]
    tile = tile_rows(row_count, 4)
    tiles = row_count // tile
    weight_load = pltpu.make_async_copy(head_weights_hbm, head_weights, load_sems.at[2])
    weight_load.start()
    tile_loads, tile_saves = [], []
    for step in range(tiles):
        rows = pl.ds(step * tile, tile)
        sems = [load_sems.at[8 + 4 * step + index] for index in range(4)]
        tile_loads.append(
            [
                pltpu.make_async_copy(head_low_hbm.at[rows], head_low.at[rows], sems[0]),
                pltpu.make_async_copy(dx1_hbm.at[rows], dx1.at[rows], sems[1]),
                pltpu.make_async_copy(input_hbm.at[rows], inputs.at[rows], sems[2]),
            ]
        )
        tile_saves.append(pltpu.make_async_copy(out.at[rows], out_hbm.at[rows], sems[3]))
        for load in tile_loads[step]:
            load.start()
    for load in loads:
        load.start()
    first_sums[...] = jnp.zeros_like(first_sums)

    def first_back(step):
        rows = pl.ds(step * tile, tile)
        if step == 0:
            weight_load.wait()
        for load in tile_loads[step]:
            load.wait()
        grad = dot_lanes(head_low[rows, :], head_weights[...])
        unit, scale = centered(inputs[rows, :].astype(F32))
        total = dx1[rows, :] + norm_back(grad * coefficient_ref[0:1, :], unit, scale)
        out[rows, :] = total.astype(BF16)
        tile_saves[step].start()
        first_sums[0] += fold(grad * unit)
        first_sums[1] += fold(grad)

    greet(peers + dp_peers)

    parts = list(reversed(range(n_fsdp // 2)))
    deep = 2 * shard

    def part_rows(part):
        first = lax.div(flip(fsdp, 2 * part), 2)
        return pl.ds(pl.multiple_of(first * deep, 16), deep)

    def owner_rows(owner):
        return pl.ds(pl.multiple_of(owner * shard, 16), shard)

    pairing = {}
    for part in parts:
        rows = part_rows(part)
        for side, block in enumerate((pair_across, pair)):
            pairing[part, side] = push(
                mix_hbm.at[block, rows],
                pair_buf.at[side, rows],
                pair_send.at[side, part],
                pair_recv.at[side, part],
                to_pair,
            )
    for load in mix_loads:
        load.wait()
    crossing = {}
    for part in parts:
        rows = part_rows(part)
        pairing[part, 0].wait_recv()
        cross_out[rows, :] = (
            mix[0, rows, :].astype(F32) + pair_buf[0, rows, :].astype(F32)
        ).astype(BF16)
        crossing[part] = push(
            cross_out.at[rows],
            cross_buf.at[rows],
            cross_send.at[part],
            cross_recv.at[part],
            to_across,
        )
    ring = {}
    for part in parts:
        rows = part_rows(part)
        pairing[part, 1].wait_recv()
        crossing[part].wait_recv()
        ring_out[rows, :] = (
            mix[1, rows, :].astype(F32)
            + pair_buf[1, rows, :].astype(F32)
            + cross_buf[rows, :].astype(F32)
        ).astype(BF16)
        for bits in (2 * part + 1, 2 * part):
            if bits:
                ring[bits] = push(
                    ring_out.at[owner_rows(flip(fsdp, bits))],
                    ring_buf.at[bits],
                    ring_send.at[bits - 1],
                    ring_recv.at[bits - 1],
                    peers[bits - 1],
                )

    slot_blocks = []
    for bits in range(n_fsdp):
        slot = 2 * flip(fsdp, bits) + core
        block, filled = jnp.int32(0), jnp.float32(0.0)
        for index in range(grad_ref.shape[0]):
            here = place_ref[index] == slot
            block = jnp.where(here, index, block)
            filled = jnp.where(here, 1.0, filled)
        slot_blocks.append((block, filled))

    pieces = feed_sum.shape[0] // 2
    side = lax.div(dp, 2)
    feed_load.wait()
    for piece in range(2 * pieces):
        total = feed_ref[0, piece].astype(F32)
        for owner in range(1, n_fsdp):
            total = total + feed_ref[owner, piece].astype(F32)
        feed_sum[piece] = total.astype(BF16)
    feeding = push(
        feed_sum.at[pl.ds((1 - side) * pieces, pieces)],
        feed_in,
        feed_in_send.at[0],
        feed_in_recv.at[0],
        to_across,
    )
    for step in range(tiles - tiles // 2):
        first_back(step)
    feeding.wait_recv()
    total = feed_sum[pl.ds(side * pieces, pieces)].astype(F32) + feed_in[...].astype(F32)
    feed_buf[dp] = total.astype(BF16)
    feeds = [
        push(feed_buf.at[dp], feed_buf.at[dp], feed_send.at[k], feed_recv.at[k], peer)
        for k, peer in enumerate(dp_peers)
    ]

    total = ring_out[owner_rows(fsdp), :].astype(F32)
    for bits in range(1, n_fsdp):
        ring[bits].wait_recv()
        total = total + ring_buf[bits].astype(F32)
    dp_buf[dp] = total
    gathering = [
        push(dp_buf.at[dp], dp_buf.at[dp], dp_send.at[k], dp_recv.at[k], peer)
        for k, peer in enumerate(dp_peers)
    ]
    for step in range(tiles - tiles // 2, tiles):
        first_back(step)

    table_stage[...] = jnp.zeros_like(table_stage)
    for row, (source, first) in enumerate(TABLE_ROWS):
        ref = mix_table_ref if source == 0 else feed_table_ref
        table_stage[row : row + 1, :] = ref[first : first + 1, :]
    for row in range(2):
        table_stage[row : row + 1, :] = jnp.sum(first_sums[row], axis=0, keepdims=True)
    table_stage[31:32, :] = mix_table_ref[14:15, :]
    quarter = table_stage.shape[0] // n_dp

    def quarter_rows(place):
        return pl.ds(pl.multiple_of(place * quarter, 8), quarter)

    table_rows[dp] = table_stage[quarter_rows(dp), :]
    quartering = [
        push(
            table_stage.at[quarter_rows(flip(dp, step + 1))],
            table_rows.at[dp],
            table_rows_send.at[step],
            table_rows_recv.at[step],
            peer,
        )
        for step, peer in enumerate(dp_peers)
    ]
    for copy in feeds:
        copy.wait_recv()
    for place in range(n_dp):
        for piece in range(pieces):
            block = n_dp + (place % 2 * 2 + place // 2) * pieces + piece
            grad_ref[block] = feed_buf[place, piece].astype(F32)
    for copy in gathering:
        copy.wait_recv()
    for place in range(n_dp):
        grad_ref[place] = dp_buf[place]
    tile_saves.append(pltpu.make_async_copy(grad_ref, grad_hbm, load_sems.at[6 + 2 + 4 * tiles]))
    tile_saves[-1].start()

    slotting = {}
    for bits in reversed(range(n_fsdp)):
        block, filled = slot_blocks[bits]
        value = (grad_ref[block] * filled).astype(BF16)
        if bits:
            slot_out[bits - 1] = value
            slotting[bits] = push(
                slot_out.at[bits - 1],
                slots.at[core, owner_rows(fsdp), :],
                slot_send.at[bits - 1],
                slot_recv.at[bits - 1],
                peers[bits - 1],
            )
        else:
            slots[core, owner_rows(fsdp), :] = value
    for copy in quartering:
        copy.wait_recv()
    rest = table_rows[0]
    for place in range(1, n_dp):
        rest = rest + table_rows[place]
    sharp_row = lax.broadcasted_iota(jnp.int32, (quarter, LANES), 0) + dp * quarter == 31
    sharp_values = jnp.broadcast_to(rest[quarter - 1 : quarter, 0:LANES], (quarter, LANES))
    terms = []
    for _ in range(3):
        term = rest.astype(BF16).astype(F32)
        terms.append(term)
        rest = rest - term
    terms = jnp.concatenate(terms, axis=0).astype(BF16)
    columns = width // n_fsdp
    for owner in range(n_fsdp):
        lane = lax.broadcasted_iota(jnp.int32, (width, LANES), 1)
        source = lax.broadcasted_iota(jnp.int32, (width, LANES), 0)
        hit = ((lane < columns) & (lane + owner * columns == source)).astype(F32).astype(BF16)
        value = dot(terms, hit)
        value = value[0:quarter] + value[quarter : 2 * quarter] + value[2 * quarter :]
        table_out[owner] = jnp.where(sharp_row, sharp_values, value)
    table_buf[fsdp] = table_out[fsdp]
    tabling = [
        push(
            table_out.at[flip(fsdp, step + 1)],
            table_buf.at[fsdp],
            table_send.at[step],
            table_recv.at[step],
            peer,
        )
        for step, peer in enumerate(peers)
    ]
    for load in loads:
        load.wait()
    right_parts = split(right[...])
    for index, value in enumerate(split(left[...])):
        left_parts[index] = value
    twins = []
    for bits in range(n_fsdp):
        if bits:
            slotting[bits].wait_recv()
        part = slots.at[core, owner_rows(flip(fsdp, bits)), :]
        twins.append(push(part, part, twin_send.at[bits], twin_recv.at[bits], to_pair))

    grad = slots[core]
    back = {}
    for part in parts:
        rows = part_rows(part)
        half = split(dot(left_parts[0, rows, :], grad) + dot(left_parts[1, rows, :], grad))
        steps[rows, :] = dot_split(dot, half, right_parts).astype(BF16)
        for bits in (2 * part + 1, 2 * part):
            if bits:
                back[bits] = push(
                    steps.at[owner_rows(flip(fsdp, bits))],
                    rows_buf.at[2 * fsdp + core],
                    back_send.at[bits - 1],
                    back_recv.at[bits - 1],
                    peers[bits - 1],
                )
    rows_buf[2 * fsdp + core] = steps[owner_rows(fsdp), :]
    for copy in tabling:
        copy.wait_recv()
    total = table_buf[0]
    for owner in range(1, n_fsdp):
        total = total + table_buf[owner]
    table_part[...] = total
    table_dp[dp] = total
    table_dps = [
        push(table_part, table_dp.at[dp], table_dp_send.at[k], table_dp_recv.at[k], peer)
        for k, peer in enumerate(dp_peers)
    ]
    lasts = []
    for bits in range(n_fsdp):
        if bits:
            back[bits].wait_recv()
        part = rows_buf.at[2 * flip(fsdp, bits) + core]
        lasts.append(push(part, part, last_send.at[bits], last_recv.at[bits], to_pair))
    for copy in table_dps:
        copy.wait_recv()
    for place in range(n_dp):
        table_ref[place * quarter : (place + 1) * quarter, :] = table_dp[place]
    for copy in twins:
        copy.wait_recv()
    tile_saves.append(pltpu.make_async_copy(slots, slots_hbm, load_sems.at[6]))
    tile_saves[-1].start()
    for copy in lasts:
        copy.wait_recv()
    tile_saves.append(pltpu.make_async_copy(rows_buf, rows_hbm, load_sems.at[7]))
    tile_saves[-1].start()
    copies = [*pairing.values(), *crossing.values(), *ring.values(), *slotting.values()]
    copies += [*back.values(), feeding, *feeds, *quartering, *tabling, *table_dps, *gathering]
    for copy in copies + twins + lasts:
        copy.wait_send()
    for save in tile_saves:
        save.wait()


def settle(
    places, mix, feed, mix_table, feed_table, left, right, back, coefficients, counts, identity
):
    head_low, dx1, inputs, head_weights = back
    row_count = dx1.shape[0]
    tiles = row_count // tile_rows(row_count, 4)
    n_dp, n_fsdp = counts
    width = mix.shape[2]
    shard = width // n_fsdp
    blocks = n_dp + 2 * feed.shape[1]
    pieces = feed.shape[1] // 2
    inner, outer = n_fsdp - 1, n_dp - 1
    shape = jax.ShapeDtypeStruct
    dma = pltpu.SemaphoreType.DMA
    sizes = [(2, n_fsdp // 2), (n_fsdp // 2,), (inner,), (1,), (outer,), (outer,)]
    sizes += [(inner,), (n_fsdp,), (inner,), (n_fsdp,), (outer,), (inner,), (outer,)]
    return pl.pallas_call(
        functools.partial(settle_kernel, counts),
        out_shape=(
            shape((blocks, shard, width), F32),
            shape((2, width, width), BF16),
            shape((2 * n_fsdp, shard, width), BF16),
            shape((32, LANES), F32),
            shape(inputs.shape, BF16),
        ),
        in_specs=[SMEM_SPEC] + [ANY_SPEC] * 2 + [VMEM_SPEC] * 2 + [ANY_SPEC] * 6 + [VMEM_SPEC],
        out_specs=(ANY_SPEC,) * 3 + (VMEM_SPEC, ANY_SPEC),
        scratch_shapes=[
            pltpu.VMEM((width, width), F32),
            pltpu.VMEM((width, width), F32),
            pltpu.VMEM(head_low.shape, BF16),
            pltpu.VMEM(dx1.shape, F32),
            pltpu.VMEM(inputs.shape, BF16),
            pltpu.VMEM(head_weights.shape, BF16),
            pltpu.VMEM(inputs.shape, BF16),
            pltpu.VMEM((2, 8, width), F32),
            pltpu.VMEM((2, width, width), BF16),
            pltpu.VMEM((width, width), BF16),
            pltpu.VMEM((width, width), BF16),
            pltpu.VMEM((width, width), BF16),
            pltpu.VMEM((n_fsdp, shard, width), BF16),
            pltpu.VMEM((pieces, shard, width), BF16),
            pltpu.VMEM((n_dp, pieces, shard, width), BF16),
            pltpu.VMEM((n_dp, shard, width), F32),
            pltpu.VMEM((inner, shard, width), BF16),
            pltpu.VMEM((2, width, width), BF16),
            pltpu.VMEM((width, width), BF16),
            pltpu.VMEM((2 * n_fsdp, shard, width), BF16),
            pltpu.VMEM((32, width), F32),
            pltpu.VMEM((n_dp, 32 // n_dp, width), F32),
            pltpu.VMEM((n_fsdp, 32 // n_dp, LANES), F32),
            pltpu.VMEM((n_fsdp, 32 // n_dp, LANES), F32),
            pltpu.VMEM((32 // n_dp, LANES), F32),
            pltpu.VMEM((n_dp, 32 // n_dp, LANES), F32),
            pltpu.VMEM(feed.shape[1:], BF16),
            pltpu.VMEM((2, width, width), BF16),
            pltpu.VMEM(feed.shape, BF16),
            pltpu.VMEM((2, width, width), BF16),
            pltpu.VMEM((blocks, shard, width), F32),
            dma((9 + 4 * tiles,)),
        ]
        + [dma(size) for size in sizes for _ in range(2)],
        compiler_params=comm_params(identity),
        name="settle",
    )(places, mix, feed, mix_table, feed_table, left, right, *back, coefficients)


def finish_kernel(
    place_ref,
    table_ref,
    energy_ref,
    coefficient_ref,
    sharp_ref,
    sharp_energy_ref,
    grads_hbm,
    slots_hbm,
    rows_hbm,
    left_hbm,
    right_hbm,
    masters_hbm,
    tokens_hbm,
    grad_hbm,
    left_out_hbm,
    right_out_hbm,
    masters_out_hbm,
    low_hbm,
    tokens_out_hbm,
    table_grad_ref,
    energy_out_ref,
    coefficient_out_ref,
    sharp_grad_ref,
    sharp_energy_out_ref,
    sharp_out_ref,
    left,
    right,
    masters,
    low,
    tokens,
    grad_ref,
    slots_ref,
    rows_ref,
    sems,
):
    slot_count = slots_ref.shape[0]
    load_slots = pltpu.make_async_copy(slots_hbm, slots_ref, sems.at[10])
    load_rows = pltpu.make_async_copy(rows_hbm, rows_ref, sems.at[11])
    load_grads = pltpu.make_async_copy(grads_hbm, grad_ref, sems.at[12])
    load_slots.start()
    load_left = pltpu.make_async_copy(left_hbm, left, sems.at[0])
    load_right = pltpu.make_async_copy(right_hbm, right, sems.at[1])
    load_masters = pltpu.make_async_copy(masters_hbm, masters, sems.at[2])
    saves = [
        pltpu.make_async_copy(source, target, sems.at[3 + index])
        for index, (source, target) in enumerate(
            (
                (grad_ref, grad_hbm),
                (left, left_out_hbm),
                (right, right_out_hbm),
                (masters, masters_out_hbm),
                (low, low_hbm),
                (tokens, tokens_out_hbm),
            )
        )
    ]
    load_left.start()
    load_right.start()
    load_tokens = pltpu.make_async_copy(tokens_hbm, tokens, sems.at[9])
    load_tokens.start()
    load_grads.start()
    load_masters.start()
    load_rows.start()
    load_slots.wait()
    load_left.wait()
    for slot in range(slot_count):
        grad = slots_ref[slot]
        left[slot] = (
            covariance_forgetting * left[slot]
            + (1.0 - covariance_forgetting) * dot_lanes(grad, grad)
        )
    saves[1].start()
    load_right.wait()
    for slot in range(slot_count):
        grad = slots_ref[slot]
        right[slot] = (
            covariance_forgetting * right[slot]
            + (1.0 - covariance_forgetting) * dot_rows(grad, grad)
        )
    saves[2].start()
    load_tokens.wait()
    saves[5].start()
    load_grads.wait()
    saves[0].start()
    load_masters.wait()
    load_rows.wait()
    for block in range(masters.shape[0]):
        value = masters[block] - weight_rate * rows_ref[place_ref[block]].astype(F32)
        masters[block] = value
        low[block] = value.astype(BF16)
    saves[3].start()
    saves[4].start()
    count, columns = energy_ref.shape
    grad = table_ref[0:count, 0:columns]
    table_grad_ref[...] = grad
    energy = covariance_forgetting * energy_ref[...] + (1.0 - covariance_forgetting) * grad * grad
    energy_out_ref[...] = energy
    coefficient_out_ref[...] = coefficient_ref[...] - vector_rate * grad / (
        jnp.sqrt(energy) + energy_epsilon
    )
    grad = table_ref[31:32, 0:HEAD_NUMBER]
    grad = grad.reshape(HEAD_NUMBER)
    energy = covariance_forgetting * sharp_energy_ref[...] + (1.0 - covariance_forgetting) * grad * grad
    sharp_grad_ref[...] = grad
    sharp_energy_out_ref[...] = energy
    sharp_out_ref[...] = sharp_ref[...] - sharpness_step_size * grad / (
        jnp.sqrt(energy) + energy_epsilon
    )
    for save in saves:
        save.wait()


def finish(
    places,
    table,
    energy,
    coefficients,
    sharpness,
    sharpness_energy,
    grads,
    slots,
    rows,
    left,
    right,
    masters,
    tokens,
):
    shape = jax.ShapeDtypeStruct
    return pl.pallas_call(
        finish_kernel,
        out_shape=(
            shape(grads.shape, F32),
            shape(left.shape, F32),
            shape(right.shape, F32),
            shape(masters.shape, F32),
            shape(masters.shape, BF16),
            shape(tokens.shape, BF16),
            shape(energy.shape, F32),
            shape(energy.shape, F32),
            shape(energy.shape, F32),
            shape(sharpness.shape, F32),
            shape(sharpness.shape, F32),
            shape(sharpness.shape, F32),
        ),
        in_specs=[SMEM_SPEC] + [VMEM_SPEC] * 5 + [ANY_SPEC] * 7,
        out_specs=(ANY_SPEC,) * 6 + (VMEM_SPEC,) * 6,
        scratch_shapes=[
            pltpu.VMEM(left.shape, F32),
            pltpu.VMEM(right.shape, F32),
            pltpu.VMEM(masters.shape, F32),
            pltpu.VMEM(masters.shape, BF16),
            pltpu.VMEM(tokens.shape, BF16),
            pltpu.VMEM(grads.shape, F32),
            pltpu.VMEM(slots.shape, BF16),
            pltpu.VMEM(rows.shape, BF16),
            pltpu.SemaphoreType.DMA((13,)),
        ],
        compiler_params=pltpu.CompilerParams(vmem_limit_bytes=VMEM_LIMIT),
        name="finish",
    )(
        places,
        table,
        energy,
        coefficients,
        sharpness,
        sharpness_energy,
        grads,
        slots,
        rows,
        left,
        right,
        masters,
        tokens,
    )


def shards(
    patch_embeddings,
    view_side_tokens,
    projection_masters,
    channel_coefficients,
    head_sharpness,
    output_adjoint,
    leading_covariance,
    trailing_covariance,
    leading_root_preconditioner,
    trailing_root_preconditioner,
    channel_energy_average,
    sharpness_energy_average,
    storage_position_map,
):
    row_count, feature_count = patch_embeddings.shape
    block_count = projection_masters.shape[0]
    shard_rows = projection_masters.shape[1]
    slot_count = leading_covariance.shape[0]
    counts = (lax.axis_size("dp"), lax.axis_size("fsdp"))
    direct = counts[0] == 4 and slot_count == 2 and shard_rows % 16 == 0
    if direct:
        mixing_blocks, table = gather_start(projection_masters, channel_coefficients, counts, 0)
        grad_shape = (2 * counts[1], (block_count - 4) // 2, shard_rows, feature_count)
    else:
        full_table = lax.all_gather(channel_coefficients.astype(BF16), "fsdp", axis=1, tiled=True)
        table = full_table.astype(F32)
        mixing_blocks = lax.all_gather(
            projection_masters[:4].astype(BF16), "fsdp", axis=1, tiled=True
        )
        grad_shape = (1, block_count - 4, feature_count, feature_count)
    feed_blocks = lax.all_gather(projection_masters[4:].astype(BF16), "fsdp", axis=1, tiled=True)

    x1, qkv, mixed, scores, attention, slope, e, sums = mixing_forward(
        view_side_tokens, head_sharpness, patch_embeddings, mixing_blocks, table
    )
    batch_sums = sum_all(sums, counts, 1) if direct else lax.psum(sums, ("dp", "fsdp"))
    layer_output, dx2, dn, feed_grad, feed_table, back_part = feed_forward(
        view_side_tokens, x1, e, batch_sums, feed_blocks, table, output_adjoint, grad_shape
    )
    if direct:
        back_sums, feed_grad = sum_pair(back_part, feed_grad, counts, 2)
        feed_grad = lax.all_to_all(feed_grad, "fsdp", 0, 0, tiled=True)
    else:
        back_sums = lax.psum(back_part, ("dp", "fsdp"))
    head_low, dx1, head_weights, mixing_grad, mixing_table = mixing_backward(
        view_side_tokens,
        head_sharpness,
        patch_embeddings,
        mixing_blocks,
        table,
        (x1, qkv, mixed, scores, attention, slope, e),
        batch_sums,
        dx2,
        dn,
        back_sums,
    )
    if direct:
        grads, owned_grad, my_rows, table_total, tokens_grad = settle(
            storage_position_map,
            mixing_grad,
            feed_grad,
            mixing_table,
            feed_table,
            leading_root_preconditioner,
            trailing_root_preconditioner,
            (head_low, dx1, patch_embeddings, head_weights),
            table,
            counts,
            3,
        )
        results = list(
            finish(
                storage_position_map,
                table_total,
                channel_energy_average,
                channel_coefficients,
                head_sharpness,
                sharpness_energy_average,
                grads,
                owned_grad,
                my_rows,
                leading_covariance,
                trailing_covariance,
                projection_masters,
                tokens_grad,
            )
        )
        tokens_grad = results.pop(5)
        return (layer_output, tokens_grad, *results)
    first_grad = dot_lanes(head_low, head_weights)
    unit, scale = centered(patch_embeddings.astype(F32))
    incoming_tokens_grad = (dx1 + norm_back(first_grad * table[0], unit, scale)).astype(BF16)
    mixing_table = mixing_table.at[0].set(jnp.sum(first_grad * unit, axis=0))
    mixing_table = mixing_table.at[1].set(jnp.sum(first_grad, axis=0))
    sharpness_share = mixing_table[14, 0:HEAD_NUMBER]
    table_grad = jnp.stack([(mixing_table, feed_table)[source][row] for source, row in TABLE_ROWS])
    block_grad = jnp.concatenate([mixing_grad, feed_grad[0]], axis=0).astype(F32)
    denominator_sum = lax.axis_size("fsdp")
    tiled_part = jnp.broadcast_to(
        sharpness_share[None, :], (denominator_sum, sharpness_share.shape[0])
    )
    portion_derivative, catalog_portion, sharpness_normalizer = (
        lax.psum_scatter(block_grad, "fsdp", scatter_dimension=1, tiled=True),
        lax.psum_scatter(table_grad, "fsdp", scatter_dimension=1, tiled=True),
        lax.psum_scatter(tiled_part, "fsdp", scatter_dimension=0, tiled=True),
    )
    portion_derivative, catalog_portion, sharpness_normalizer = lax.psum(
        (portion_derivative, catalog_portion, sharpness_normalizer), "dp"
    )
    sharpness_derivative = sharpness_normalizer[0]
    shard_place = lax.axis_index("fsdp")
    slot_index = jnp.arange(denominator_sum * slot_count, dtype=jnp.int32)
    slot_match = storage_position_map[None, :] == slot_index[:, None]
    slot_filled = jnp.any(slot_match, axis=1).astype(jnp.float32)[:, None, None]
    slot_block = jnp.sum(
        jnp.where(slot_match, jnp.arange(block_count, dtype=jnp.int32)[None, :], 0), axis=1
    )
    my_filled = lax.dynamic_slice_in_dim(slot_filled, shard_place * slot_count, slot_count, 0)
    my_block = lax.dynamic_slice_in_dim(slot_block, shard_place * slot_count, slot_count, 0)
    whole_grad = lax.all_gather(portion_derivative, "fsdp", axis=1, tiled=True)
    owned_grad = jnp.take(whole_grad, my_block, axis=0) * my_filled
    leading_covariance_renewed = covariance_forgetting * leading_covariance + (
        1.0 - covariance_forgetting
    ) * jnp.einsum("sij,skj->sik", owned_grad, owned_grad, precision=lax.Precision.HIGHEST)
    trailing_covariance_renewed = covariance_forgetting * trailing_covariance + (
        1.0 - covariance_forgetting
    ) * jnp.einsum("sji,sjk->sik", owned_grad, owned_grad, precision=lax.Precision.HIGHEST)
    halfway = jnp.einsum(
        "sij,sjk->sik", leading_root_preconditioner, owned_grad, precision=lax.Precision.HIGHEST
    )
    conditioned = jnp.einsum(
        "sij,sjk->sik", halfway, trailing_root_preconditioner, precision=lax.Precision.HIGHEST
    )
    every_update = lax.all_gather(conditioned, "fsdp", axis=0, tiled=True)
    my_rows = lax.dynamic_slice_in_dim(every_update, shard_place * shard_rows, shard_rows, 1)
    update = jnp.take(my_rows, storage_position_map, axis=0)
    projection_updated = projection_masters - weight_rate * update
    channel_energy_renewed = (
        covariance_forgetting * channel_energy_average
        + (1.0 - covariance_forgetting) * catalog_portion * catalog_portion
    )
    channel_params_updated = channel_coefficients - vector_rate * catalog_portion / (
        jnp.sqrt(channel_energy_renewed) + energy_epsilon
    )
    sharpness_energy_renewed = (
        covariance_forgetting * sharpness_energy_average
        + (1.0 - covariance_forgetting) * sharpness_derivative * sharpness_derivative
    )
    sharpness_updated = head_sharpness - sharpness_step_size * sharpness_derivative / (
        jnp.sqrt(sharpness_energy_renewed) + energy_epsilon
    )
    return (
        layer_output,
        incoming_tokens_grad,
        portion_derivative,
        leading_covariance_renewed,
        trailing_covariance_renewed,
        projection_updated,
        projection_updated.astype(jnp.bfloat16),
        catalog_portion,
        channel_energy_renewed,
        channel_params_updated,
        sharpness_derivative,
        sharpness_energy_renewed,
        sharpness_updated,
    )


def solution(mesh):
    in_specs = (
        P(("dp", "fsdp"), None),
        P(("dp", "fsdp")),
        P(None, "fsdp", None),
        P(None, "fsdp"),
        P(),
        P(("dp", "fsdp"), None),
        P("fsdp", None, None),
        P("fsdp", None, None),
        P("fsdp", None, None),
        P("fsdp", None, None),
        P(None, "fsdp"),
        P(),
        P(),
    )
    out_specs = (
        P(("dp", "fsdp"), None),
        P(("dp", "fsdp"), None),
        P(None, "fsdp", None),
        P("fsdp", None, None),
        P("fsdp", None, None),
        P(None, "fsdp", None),
        P(None, "fsdp", None),
        P(None, "fsdp"),
        P(None, "fsdp"),
        P(None, "fsdp"),
        P(),
        P(),
        P(),
    )
    return jax.shard_map(shards, mesh=mesh, in_specs=in_specs, out_specs=out_specs, check_vma=False)
```

```python
import functools

import jax
import jax.numpy as jnp
from jax import lax
from jax.experimental import pallas as pl
from jax.experimental.pallas import tpu as pltpu
from jax.sharding import PartitionSpec as P

HEAD_NUMBER = 8
HDIM = 48
HEAD_PAD = 64
LANES = 128
HEAD_PAIRS = HEAD_NUMBER // 2
PAD_WIDTH = HEAD_NUMBER * HEAD_PAD
HALF_WIDTH = PAD_WIDTH // 2
LEAD = 16
TAIL = 32
SMALL_SIDE = 6
SMALL_WINDOW = 48
LARGE_WINDOW = 208
CROP_GROUP = 2
SAVE_ROWS = 64
ROW_TILE = 464
HIDDEN_PARTS = 6
VMEM_LIMIT = 60 * 2**20

norm_epsilon = 1e-06
batch_epsilon = 1e-05
attention_epsilon = 1e-06
covariance_forgetting = 0.5
weight_rate = 0.5
vector_rate = 0.1
sharpness_step_size = 2.0
energy_epsilon = 1e-08

F32 = jnp.float32
BF16 = jnp.bfloat16
VMEM_SPEC = pl.BlockSpec(memory_space=pltpu.VMEM)
ANY_SPEC = pl.BlockSpec(memory_space=pl.ANY)
SMEM_SPEC = pl.BlockSpec(memory_space=pltpu.SMEM)


def dot(left, right):
    return lax.dot_general(left, right, (((1,), (0,)), ((), ())), preferred_element_type=F32)


def dot_rows(left, right):
    return lax.dot_general(left, right, (((0,), (0,)), ((), ())), preferred_element_type=F32)


def dot_lanes(left, right):
    return lax.dot_general(left, right, (((1,), (1,)), ((), ())), preferred_element_type=F32)


def split(values):
    high = values.astype(BF16)
    return high, (values - high.astype(F32)).astype(BF16)


def dot_split(product, left, right):
    if product is dot_rows:
        return product(
            jnp.concatenate([left[0], left[0], left[1]], axis=0),
            jnp.concatenate([right[0], right[1], right[0]], axis=0),
        )
    rows = left[0].shape[0]
    both = product(jnp.concatenate(left, axis=0), right[0])
    return both[:rows] + both[rows:] + product(left[0], right[1])


def fold(values):
    total = values[0:8]
    for first in range(8, values.shape[0], 8):
        total = total + values[first : first + 8]
    return total


def gelu_parts(values):
    magnitude = jnp.abs(values) * 0.7071067811865476
    base = 1.0 + 0.3275911 * magnitude
    guess = pl.reciprocal(base, approx=True)
    slot = guess * (2.0 - base * guess)
    series = slot * (
        0.127414796
        + slot
        * (-0.142248368 + slot * (0.7107068705 + slot * (-0.7265760135 + slot * 0.5307027145)))
    )
    bell = jnp.exp(-0.5 * values * values)
    lower = series * bell
    return jnp.where(values >= 0, 1.0 - lower, lower), bell


def gelu_slope(values, share, bell):
    return share + values * bell * 0.3989422804014327


def head_map(dtype):
    feature = lax.broadcasted_iota(jnp.int32, (HEAD_NUMBER * HDIM, PAD_WIDTH), 0)
    lane = lax.broadcasted_iota(jnp.int32, (HEAD_NUMBER * HDIM, PAD_WIDTH), 1)
    inner = lane & (HEAD_PAD - 1)
    hit = (inner < HDIM) & ((lane >> 6) * HDIM + inner == feature)
    return hit.astype(F32).astype(dtype)


def centered(values):
    center = jnp.sum(values, axis=-1, keepdims=True) * (1.0 / values.shape[-1])
    shifted = values - center
    spread = jnp.sum(shifted * shifted, axis=-1, keepdims=True) * (1.0 / values.shape[-1])
    scale = lax.rsqrt(spread + norm_epsilon)
    return shifted * scale, scale


def norm_back(grad, unit, scale):
    size = 1.0 / grad.shape[-1]
    middle = jnp.sum(grad, axis=-1, keepdims=True) * size
    slope = jnp.sum(grad * unit, axis=-1, keepdims=True) * size
    return scale * (grad - middle - unit * slope)


def tile_rows(count, least):
    for parts in range(least, count // 16 + 1):
        if count % (16 * parts) == 0:
            return count // parts
    return count


def for_rows(count, tile, step, carry=0):
    def body(index, carry):
        return step(pl.multiple_of(index * tile, tile), tile, carry)

    if count // tile == 1:
        carry = step(0, tile, carry)
    else:
        carry = lax.fori_loop(0, count // tile, body, carry)
    if count % tile:
        carry = step(count - count % tile, count % tile, carry)
    return carry


def row_copies(pairs, first, size, sem):
    rows = pl.ds(first, size)
    return [
        pltpu.make_async_copy(
            source.at[:, rows] if chunked else source.at[rows],
            target.at[:, rows] if chunked else target.at[rows],
            sem,
        )
        for source, target, chunked in pairs
    ]


def live_total(sides_ref):
    return lax.fori_loop(
        0, sides_ref.shape[0], lambda c, t: t + sides_ref[c] * sides_ref[c], jnp.int32(0)
    )


def row_mask(first, rows, width, limit):
    return lax.broadcasted_iota(jnp.int32, (rows, width), 0) + first < limit


def save_rows(source, target, sem, first, rows):
    rows = pl.ds(pl.multiple_of(first, 8), rows)
    pltpu.make_async_copy(source.at[:, rows], target.at[:, rows], sem).start()


def for_groups(sides_ref, step, carry, saves=()):
    def save(first, last):
        def body(part, _):
            for source, target, sem in saves:
                save_rows(source, target, sem, part * SAVE_ROWS, SAVE_ROWS)
            return 0

        if saves:
            lax.fori_loop(first, last, body, 0)
        return last

    def crop_body(crop, state):
        start, saved, carry = state
        side = sides_ref[crop]
        cells = side * side
        inverse = 1.0 / jnp.full((8, LANES), side, jnp.int32).astype(F32)
        lines = lax.broadcasted_iota(jnp.int32, (8, LANES), 0)

        def group_body(group, carry):
            for part in range(2):
                row = pl.multiple_of((group * 2 + part) * 8, 8)
                place = lines + (row - start)
                line = ((place.astype(F32) + 0.5) * inverse).astype(jnp.int32)
                column = place - line * side
                inside = (place >= 0) & (place < cells)
                masks = (
                    inside,
                    column >= 1,
                    column < side - 1,
                    place >= side,
                    place < cells - side,
                )
                carry = step(row, side, masks, carry)
            return carry

        carry = lax.fori_loop(start // 16, (start + cells + 15) // 16, group_body, carry)
        saved = save(saved, (start + cells) // 16 * 16 // SAVE_ROWS)
        return start + cells, saved, carry

    state = (jnp.int32(0), jnp.int32(0), carry)
    _, saved, carry = lax.fori_loop(0, sides_ref.shape[0], crop_body, state)
    for source, target, sem in saves:
        done = source.shape[1] // SAVE_ROWS * SAVE_ROWS
        if done < source.shape[1]:
            save_rows(source, target, sem, done, source.shape[1] - done)
    if saves:
        save(saved, saves[0][0].shape[1] // SAVE_ROWS)
    return carry


def conv_forward(source, chunk, row, side, masks, taps):
    inside, left_ok, right_ok, up_ok, down_ok = masks
    total = None
    for shift in (-1, 0, 1):
        base = LEAD + row + shift * side
        middle = source[chunk, pl.ds(base, 8), :]
        left = jnp.where(left_ok, source[chunk, pl.ds(base - 1, 8), :], 0.0)
        right = jnp.where(right_ok, source[chunk, pl.ds(base + 1, 8), :], 0.0)
        first = 3 * (shift + 1)
        value = taps[first] * left + taps[first + 1] * middle + taps[first + 2] * right
        if shift == -1:
            value = jnp.where(up_ok, value, 0.0)
        if shift == 1:
            value = jnp.where(down_ok, value, 0.0)
        total = value if total is None else total + value
    return total


def conv_backward(source, chunk, row, side, masks, taps, own, tap_sums):
    inside, left_ok, right_ok, up_ok, down_ok = masks
    total = None
    tap_sums = list(tap_sums)
    for shift in (-1, 0, 1):
        base = LEAD + row + shift * side
        row_ok = {-1: up_ok, 0: None, 1: down_ok}[shift]
        for sway in (-1, 0, 1):
            column_ok = {-1: left_ok, 0: None, 1: right_ok}[sway]
            value = source[chunk, pl.ds(base + sway, 8), :]
            keep = inside
            if row_ok is not None:
                keep = keep & row_ok
            if column_ok is not None:
                keep = keep & column_ok
            value = jnp.where(keep, value, 0.0)
            index = 3 * (1 - shift) + (1 - sway)
            term = taps[index] * value
            total = term if total is None else total + term
            tap_sums[index] = tap_sums[index] + own * value
    return total, tuple(tap_sums)


def chunk_lanes(chunk):
    return slice(chunk * LANES, (chunk + 1) * LANES)


def tap_vectors(table_ref, first, chunk):
    return [
        jnp.broadcast_to(table_ref[first + k : first + k + 1, chunk_lanes(chunk)], (8, LANES))
        for k in range(9)
    ]


def for_crops(sides_ref, row_count, order_ref, start_ref, step):
    crops = sides_ref.shape[0]

    def scan(crop, state):
        start, large, small = state
        side = sides_ref[crop]
        start_ref[crop] = start
        is_small = side <= SMALL_SIDE
        order_ref[jnp.where(is_small, crops + small, large)] = crop
        return (
            start + side * side,
            large + jnp.where(is_small, 0, 1),
            small + jnp.where(is_small, 1, 0),
        )

    zero = jnp.int32(0)
    _, large, small = lax.fori_loop(0, crops, scan, (zero, zero, zero))
    for window, first, count in ((LARGE_WINDOW, 0, large), (SMALL_WINDOW, crops, small)):

        def group_body(group, _, window=window, first=first, count=count):
            members = []
            for member in range(CROP_GROUP):
                crop = order_ref[first + jnp.minimum(group * CROP_GROUP + member, count - 1)]
                start = start_ref[crop]
                side = sides_ref[crop]
                row = pl.multiple_of(jnp.minimum(start // 8, (row_count - window) // 8) * 8, 8)
                place = lax.broadcasted_iota(jnp.int32, (window, HALF_WIDTH), 0) + (row - start)
                members.append((crop, pl.ds(row, window), (place >= 0) & (place < side * side)))
            step(members)
            return 0

        lax.fori_loop(0, (count + CROP_GROUP - 1) // CROP_GROUP, group_body, 0)


def half_lanes(half):
    starts = [part * PAD_WIDTH + half * HALF_WIDTH for part in range(3)]
    return [slice(start, start + HALF_WIDTH) for start in starts]


def pair_lanes():
    return lax.broadcasted_iota(jnp.int32, (HDIM, LANES), 1) < HEAD_PAD


def pair_part(block, pair):
    first = pair * LANES
    lanes = slice(first, first + LANES)
    return jnp.where(
        pair_lanes(),
        block[first : first + HDIM, lanes],
        block[first + HEAD_PAD : first + HEAD_PAD + HDIM, lanes],
    )


def spread_pair(target, member, half, pair, values):
    first = pair * LANES
    lanes = slice(first, first + LANES)
    parts = split(values)
    for index in range(2):
        value = parts[index].astype(F32)
        target[member, half, index, first : first + HDIM, lanes] = jnp.where(
            pair_lanes(), value, 0.0
        ).astype(BF16)
        target[member, half, index, first + HEAD_PAD : first + HEAD_PAD + HDIM, lanes] = jnp.where(
            pair_lanes(), 0.0, value
        ).astype(BF16)


def pair_sharpness(sharp_ref, pair):
    lane = lax.broadcasted_iota(jnp.int32, (1, LANES), 1)
    return jnp.where(lane < HEAD_PAD, sharp_ref[2 * pair], sharp_ref[2 * pair + 1])


def units(values):
    scale = lax.rsqrt(jnp.sum(values * values, axis=0, keepdims=True) + attention_epsilon)
    return values * scale, scale


def mixing_forward_kernel(
    sides_ref,
    sharp_ref,
    input_hbm,
    weight_ref,
    table_ref,
    x1_hbm,
    qkv_hbm,
    mixed_hbm,
    scores_hbm,
    attention_hbm,
    slope_hbm,
    e_hbm,
    sums_ref,
    input_ref,
    x1_ref,
    qkv_ref,
    mixed_ref,
    scores_ref,
    attention_ref,
    slope_ref,
    e_ref,
    head_weights,
    out_weight,
    first_low,
    mixed,
    conv_in,
    spread,
    order_ref,
    start_ref,
    sems,
):
    row_count, width = input_ref.shape
    load = pltpu.make_async_copy(input_hbm, input_ref, sems.at[7])
    load.start()
    chunks = width // LANES
    saves = [
        pltpu.make_async_copy(source, target, sems.at[index])
        for index, (source, target) in enumerate(
            (
                (qkv_ref, qkv_hbm),
                (scores_ref, scores_hbm),
                (attention_ref, attention_hbm),
                (mixed_ref, mixed_hbm),
                (x1_ref, x1_hbm),
                (slope_ref, slope_hbm),
                (e_ref, e_hbm),
            )
        )
    ]
    total_live = live_total(sides_ref)
    mapping = head_map(BF16)
    for part in range(3):
        head_weights[:, part * PAD_WIDTH : (part + 1) * PAD_WIDTH] = dot(
            weight_ref[part], mapping
        ).astype(BF16)
    spread[...] = jnp.zeros_like(spread)

    def first_norm(first, size, _):
        rows = pl.ds(first, size)
        unit, _ = centered(input_ref[rows, :].astype(F32))
        first_low[rows, :] = (unit * table_ref[0:1, :] + table_ref[1:2, :]).astype(BF16)
        mixed[rows, :] = jnp.zeros((size, PAD_WIDTH), F32)
        return 0

    near = tile_rows(row_count, 4)
    load.wait()
    first_norm(0, near, 0)
    for first in range(0, row_count, near):
        if first + near < row_count:
            first_norm(first + near, near, 0)
        rows = pl.ds(first, near)
        qkv_ref[rows, :] = dot(first_low[rows, :], head_weights[...])
    saves[0].start()

    def crop_step(members):
        units_of = [(member, half) for member in range(len(members)) for half in range(2)]
        blocks, results = [], []
        for member, half in units_of:
            crop, rows, keep = members[member]
            lanes = half_lanes(half)
            query = units(jnp.where(keep, qkv_ref[rows, lanes[0]], 0.0))[0]
            key = units(jnp.where(keep, qkv_ref[rows, lanes[1]], 0.0))[0]
            blocks.append(dot_split(dot_rows, split(key), split(query)))
        for (member, half), block in zip(units_of, blocks):
            crop = members[member][0]
            for pair in range(2):
                scores = pair_part(block, pair)
                scores_ref[crop, 2 * half + pair] = scores
                scores = scores * pair_sharpness(sharp_ref, 2 * half + pair)
                scores = jnp.exp(scores - jnp.max(scores, axis=0, keepdims=True))
                shares = scores / jnp.sum(scores, axis=0, keepdims=True)
                attention_ref[crop, 2 * half + pair] = shares
                spread_pair(spread, member, half, pair, shares)
        for member, half in units_of:
            rows = members[member][1]
            shares = (spread[member, half, 0], spread[member, half, 1])
            results.append(dot_split(dot, split(qkv_ref[rows, half_lanes(half)[2]]), shares))
        for (member, half), result in zip(units_of, results):
            _, rows, keep = members[member]
            lanes = half_lanes(half)[0]
            mixed[rows, lanes] = jnp.where(keep, result, mixed[rows, lanes])

    for_crops(sides_ref, row_count, order_ref, start_ref, crop_step)

    saves[1].start()
    saves[2].start()
    out_weight[...] = dot_rows(mapping, weight_ref[3]).astype(BF16)

    def attention_rows(first):
        rows = pl.ds(first, near)
        low = mixed[rows, :].astype(BF16)
        mixed_ref[rows, :] = low
        return dot(low, out_weight[...])

    ahead = attention_rows(0)
    for first in range(0, row_count, near):
        rows = pl.ds(first, near)
        held = ahead
        if first + near < row_count:
            ahead = attention_rows(first + near)
        value = input_ref[rows, :].astype(F32) + table_ref[2:3, :] * held
        x1_ref[rows, :] = value
        unit, _ = centered(value)
        value = unit * table_ref[3:4, :] + table_ref[4:5, :]
        for chunk in range(chunks):
            conv_in[chunk, pl.ds(LEAD + first, near), :] = value[:, chunk_lanes(chunk)]
            slope_ref[chunk, rows, :] = jnp.zeros((near, LANES), F32)
            e_ref[chunk, rows, :] = jnp.zeros((near, LANES), F32)
    saves[3].start()
    saves[4].start()

    zero = jnp.zeros((8, LANES), F32)
    sums_ref[...] = zero
    taps = [tap_vectors(table_ref, 11, chunk) for chunk in range(chunks)]

    def conv_step(row, side, masks, carry):
        rows = pl.ds(row, 8)
        carry = list(carry)
        for chunk in range(chunks):
            value = conv_forward(conv_in, chunk, row, side, masks, taps[chunk])
            share, bell = gelu_parts(value)
            active = value * share
            slope = gelu_slope(value, share, bell)
            slope_ref[chunk, rows, :] = jnp.where(masks[0], slope, slope_ref[chunk, rows, :])
            e_ref[chunk, rows, :] = jnp.where(masks[0], active, e_ref[chunk, rows, :])
            active = jnp.where(masks[0], active, 0.0)
            carry[chunk] = carry[chunk] + active
            carry[chunks + chunk] = carry[chunks + chunk] + active * active
        return tuple(carry)

    sums = for_groups(
        sides_ref,
        conv_step,
        (zero,) * (2 * chunks),
        ((slope_ref, slope_hbm, sems.at[5]), (e_ref, e_hbm, sems.at[6])),
    )
    for index, value in enumerate(sums):
        sums_ref[index : index + 1, :] = jnp.sum(value, axis=0, keepdims=True)
    sums_ref[2 * chunks : 2 * chunks + 1, :] = jnp.full((1, LANES), total_live, jnp.int32).astype(F32)
    for save in saves:
        save.wait()


def mixing_forward(sides, sharpness, inputs, weights, table):
    row_count, width = inputs.shape
    crops = sides.shape[0]
    chunks = width // LANES
    shape = jax.ShapeDtypeStruct
    return pl.pallas_call(
        mixing_forward_kernel,
        out_shape=(
            shape((row_count, width), F32),
            shape((row_count, 3 * PAD_WIDTH), F32),
            shape((row_count, PAD_WIDTH), BF16),
            shape((crops, HEAD_PAIRS, HDIM, LANES), F32),
            shape((crops, HEAD_PAIRS, HDIM, LANES), F32),
            shape((chunks, row_count, LANES), F32),
            shape((chunks, row_count, LANES), F32),
            shape((8, LANES), F32),
        ),
        in_specs=[SMEM_SPEC, SMEM_SPEC, ANY_SPEC, VMEM_SPEC, VMEM_SPEC],
        out_specs=(ANY_SPEC,) * 7 + (VMEM_SPEC,),
        scratch_shapes=[
            pltpu.VMEM((row_count, width), BF16),
            pltpu.VMEM((row_count, width), F32),
            pltpu.VMEM((row_count, 3 * PAD_WIDTH), F32),
            pltpu.VMEM((row_count, PAD_WIDTH), BF16),
            pltpu.VMEM((crops, HEAD_PAIRS, HDIM, LANES), F32),
            pltpu.VMEM((crops, HEAD_PAIRS, HDIM, LANES), F32),
            pltpu.VMEM((chunks, row_count, LANES), F32),
            pltpu.VMEM((chunks, row_count, LANES), F32),
            pltpu.VMEM((width, 3 * PAD_WIDTH), BF16),
            pltpu.VMEM((PAD_WIDTH, width), BF16),
            pltpu.VMEM((row_count, width), BF16),
            pltpu.VMEM((row_count, PAD_WIDTH), F32),
            pltpu.VMEM((chunks, LEAD + row_count + TAIL, LANES), F32),
            pltpu.VMEM((CROP_GROUP, 2, 2, HALF_WIDTH, HALF_WIDTH), BF16),
            pltpu.SMEM((2 * crops,), jnp.int32),
            pltpu.SMEM((crops,), jnp.int32),
            pltpu.SemaphoreType.DMA((8,)),
        ],
        compiler_params=pltpu.CompilerParams(vmem_limit_bytes=VMEM_LIMIT),
        name="mixing_forward",
    )(sides, sharpness, inputs, weights, table)


def batch_vectors(bn_ref, chunk, chunks):
    count = bn_ref[2 * chunks : 2 * chunks + 1, :]
    mean = bn_ref[chunk : chunk + 1, :] / count
    scale = lax.rsqrt(bn_ref[chunks + chunk : chunks + chunk + 1, :] / count - mean * mean + batch_epsilon)
    return mean, scale


def feed_kernel(
    sides_ref,
    x1_hbm,
    e_hbm,
    bn_ref,
    weight_hbm,
    table_ref,
    adjoint_hbm,
    out_hbm,
    dx2_hbm,
    dn_hbm,
    weight_grad_hbm,
    grads_ref,
    back_sums_ref,
    e_ref,
    x1_ref,
    weight_ref,
    adjoint_ref,
    out_ref,
    dx2_ref,
    dn_ref,
    weight_grad_ref,
    up_weight,
    n_ref,
    z_ref,
    dw_ref,
    x2,
    unit,
    spread,
    third_low,
    hidden_low,
    feed,
    third_grad,
    feed_grad,
    pre_grad,
    grads,
    up_sum,
    down_sum,
    weight_low,
    sems,
    tile_sems,
):
    loads = [
        pltpu.make_async_copy(source, target, sems.at[index])
        for index, (source, target) in enumerate(
            (
                (x1_hbm, x1_ref),
                (weight_hbm, weight_ref),
                (adjoint_hbm, adjoint_ref),
            )
        )
    ]
    saves = [
        pltpu.make_async_copy(source, target, sems.at[4 + index])
        for index, (source, target) in enumerate(
            (
                (out_ref, out_hbm),
                (dx2_ref, dx2_hbm),
                (weight_grad_ref, weight_grad_hbm),
                (dn_ref, dn_hbm),
            )
        )
    ]

    tiled = [(e_hbm, e_ref, True)]

    def start_tile(first, size, _):
        for load in row_copies(tiled, first, size, tile_sems.at[lax.div(first, ROW_TILE)]):
            load.start()
        return 0

    for_rows(x1_hbm.shape[0], ROW_TILE, start_tile)
    for load in loads:
        load.start()
    row_count, width = x1_ref.shape
    chunks = width // LANES
    expand = weight_ref.shape[0] // 2
    tile = tile_rows(row_count, 4)
    total_live = live_total(sides_ref)
    hidden = expand * width
    batch = [batch_vectors(bn_ref, chunk, chunks) for chunk in range(chunks)]
    zero = jnp.zeros((8, LANES), F32)

    def down_weight():
        return weight_ref[expand : 2 * expand].reshape(hidden, width)

    def normalize(first, size, _):
        for load in row_copies(tiled, first, size, tile_sems.at[lax.div(first, ROW_TILE)]):
            load.wait()
        rows = pl.ds(first, size)
        live = row_mask(first, size, LANES, total_live)
        for chunk in range(chunks):
            lanes = chunk_lanes(chunk)
            mean, scale = batch[chunk]
            value = (e_ref[chunk, rows, :] - mean) * scale
            value = value * table_ref[5:6, lanes] + table_ref[6:7, lanes]
            n_ref[chunk, pl.ds(LEAD + first, size), :] = jnp.where(live, value, 0.0)
            z_ref[chunk, rows, :] = jnp.zeros((size, LANES), F32)
            dn_ref[chunk, rows, :] = jnp.zeros((size, LANES), F32)
        return 0

    for_rows(row_count, ROW_TILE, normalize)

    taps = [tap_vectors(table_ref, 20, chunk) for chunk in range(chunks)]

    def conv_step(row, side, masks, carry):
        rows = pl.ds(row, 8)
        for chunk in range(chunks):
            value = conv_forward(n_ref, chunk, row, side, masks, taps[chunk])
            z_ref[chunk, rows, :] = jnp.where(masks[0], value, z_ref[chunk, rows, :])
        return carry

    for_groups(sides_ref, conv_step, 0)

    for load in loads:
        load.wait()
    for part in range(expand):
        up_weight[:, part * width : (part + 1) * width] = weight_ref[part]
    up_sum[...] = jnp.zeros_like(up_sum)
    down_sum[...] = jnp.zeros_like(down_sum)
    grads[...] = jnp.zeros_like(grads)

    def z_rows(rows):
        return jnp.concatenate([z_ref[chunk, rows, :] for chunk in range(chunks)], axis=1)

    def before(base):
        rows = pl.ds(base, tile)
        value = x1_ref[rows, :] + table_ref[7:8, :] * z_rows(rows)
        x2[...] = value
        value, scale = centered(value)
        unit[...] = value
        spread[...] = jnp.broadcast_to(scale, (tile, LANES))
        third_low[...] = (value * table_ref[8:9, :] + table_ref[9:10, :]).astype(BF16)
        feed_grad[...] = (entry_rows(base) * table_ref[10:11, :]).astype(BF16)

    def entry_rows(base):
        live = row_mask(base, tile, width, total_live)
        return jnp.where(live, adjoint_ref[pl.ds(base, tile), :].astype(F32), 0.0)

    @pl.loop(0, row_count // tile)
    def _(step):
        base = pl.multiple_of(step * tile, 16)
        rows = pl.ds(base, tile)
        before(base)

        def hidden_lanes(part):
            return slice(part * hidden // HIDDEN_PARTS, (part + 1) * hidden // HIDDEN_PARTS)

        def products(part):
            lanes = hidden_lanes(part)
            return (
                dot(third_low[...], up_weight[:, lanes]),
                dot_lanes(feed_grad[...], down_weight()[lanes]),
            )

        ahead = products(0)
        for part in range(HIDDEN_PARTS):
            lanes = hidden_lanes(part)
            value, hidden_grad = ahead
            if part + 1 < HIDDEN_PARTS:
                ahead = products(part + 1)
            share, bell = gelu_parts(value)
            hidden_low[:, lanes] = (value * share).astype(BF16)
            pre_grad[:, lanes] = (hidden_grad * gelu_slope(value, share, bell)).astype(BF16)
        feed[...] = dot(hidden_low[...], down_weight())
        third_grad[...] = dot_lanes(pre_grad[...], up_weight[...])
        down_sum[...] += dot_rows(feed_grad[...], hidden_low[...])
        up_sum[...] += dot_rows(third_low[...], pre_grad[...])

        value = x2[...] + table_ref[10:11, :] * feed[...]
        live = row_mask(base, tile, width, total_live)
        out_ref[rows, :] = jnp.where(live, value, 0.0).astype(BF16)
        entry = entry_rows(base)
        grads[0] += fold(entry * feed[...])
        grad = third_grad[...]
        value = unit[...]
        total = entry + norm_back(grad * table_ref[8:9, :], value, spread[:, 0:1])
        dx2_ref[rows, :] = total
        scaled = total * table_ref[7:8, :]
        for chunk in range(chunks):
            dw_ref[chunk, pl.ds(LEAD + base, tile), :] = scaled[:, chunk_lanes(chunk)]
        grads[1] += fold(total * z_rows(rows))
        grads[2] += fold(grad * value)
        grads[3] += fold(grad)

    saves[0].start()
    saves[1].start()

    for part in range(expand):
        lanes = slice(part * width, (part + 1) * width)
        weight_low[part] = up_sum[:, lanes].astype(BF16)
        weight_low[expand + part] = down_sum[:, lanes].T.astype(BF16)

    owners, pieces, shard, _ = weight_grad_ref.shape
    inner = width // shard
    for owner in range(owners):
        rows = slice(owner % inner * shard, (owner % inner + 1) * shard)
        for piece in range(pieces):
            weight_grad_ref[owner, piece] = weight_low[owner // inner * pieces + piece, rows, :]

    saves[2].start()

    back_sums_ref[...] = zero
    for index, source in enumerate((1, 2, 3, 0)):
        grads_ref[index : index + 1, :] = jnp.sum(grads[source], axis=0, keepdims=True)
    def back_step(row, side, masks, carry):
        rows = pl.ds(row, 8)
        result = []
        for chunk in range(chunks):
            mean, scale = batch[chunk]
            sums = carry[chunk]
            own = jnp.where(masks[0], n_ref[chunk, pl.ds(LEAD + row, 8), :], 0.0)
            total, tap_sums = conv_backward(
                dw_ref, chunk, row, side, masks, taps[chunk], own, sums[0:9]
            )
            dn_ref[chunk, rows, :] = jnp.where(masks[0], total, dn_ref[chunk, rows, :])
            total = jnp.where(masks[0], total, 0.0)
            standard = (e_ref[chunk, rows, :] - mean) * scale
            result.append((*tap_sums, sums[9] + total * standard, sums[10] + total))
        return tuple(result)

    sums = for_groups(
        sides_ref, back_step, ((zero,) * 11,) * chunks, ((dn_ref, dn_hbm, sems.at[7]),)
    )
    for chunk in range(chunks):
        lanes = chunk_lanes(chunk)
        for index, value in enumerate(sums[chunk]):
            value = jnp.sum(value, axis=0, keepdims=True)
            grads_ref[4 + index : 5 + index, lanes] = value
            if index == 9:
                back_sums_ref[chunks + chunk : chunks + chunk + 1, :] = value
            if index == 10:
                back_sums_ref[chunk : chunk + 1, :] = value
    for save in saves:
        save.wait()


def feed_forward(sides, x1, e, batch_sums, weights, table, adjoint, grad_shape):
    row_count, width = x1.shape
    chunks = width // LANES
    expand = weights.shape[0] // 2
    tile = tile_rows(row_count, 4)
    shape = jax.ShapeDtypeStruct
    return pl.pallas_call(
        feed_kernel,
        out_shape=(
            shape((row_count, width), BF16),
            shape((row_count, width), F32),
            shape((chunks, row_count, LANES), F32),
            shape(grad_shape, BF16),
            shape((16, width), F32),
            shape((8, LANES), F32),
        ),
        in_specs=[SMEM_SPEC, ANY_SPEC, ANY_SPEC, VMEM_SPEC, ANY_SPEC, VMEM_SPEC, ANY_SPEC],
        out_specs=(ANY_SPEC,) * 4 + (VMEM_SPEC,) * 2,
        scratch_shapes=[
            pltpu.VMEM((chunks, row_count, LANES), F32),
            pltpu.VMEM((row_count, width), F32),
            pltpu.VMEM(weights.shape, BF16),
            pltpu.VMEM((row_count, width), BF16),
            pltpu.VMEM((row_count, width), BF16),
            pltpu.VMEM((row_count, width), F32),
            pltpu.VMEM((chunks, row_count, LANES), F32),
            pltpu.VMEM(grad_shape, BF16),
            pltpu.VMEM((width, expand * width), BF16),
            pltpu.VMEM((chunks, LEAD + row_count + TAIL, LANES), F32),
            pltpu.VMEM((chunks, row_count, LANES), F32),
            pltpu.VMEM((chunks, LEAD + row_count + TAIL, LANES), F32),
            pltpu.VMEM((tile, width), F32),
            pltpu.VMEM((tile, width), F32),
            pltpu.VMEM((tile, LANES), F32),
            pltpu.VMEM((tile, width), BF16),
            pltpu.VMEM((tile, expand * width), BF16),
            pltpu.VMEM((tile, width), F32),
            pltpu.VMEM((tile, width), F32),
            pltpu.VMEM((tile, width), BF16),
            pltpu.VMEM((tile, expand * width), BF16),
            pltpu.VMEM((4, 8, width), F32),
            pltpu.VMEM((width, expand * width), F32),
            pltpu.VMEM((width, expand * width), F32),
            pltpu.VMEM(weights.shape, BF16),
            pltpu.SemaphoreType.DMA((8,)),
            pltpu.SemaphoreType.DMA(((row_count + ROW_TILE - 1) // ROW_TILE,)),
        ],
        compiler_params=pltpu.CompilerParams(vmem_limit_bytes=VMEM_LIMIT),
        name="feed_forward",
    )(sides, x1, e, batch_sums, weights, table, adjoint)


def mixing_backward_kernel(
    sides_ref,
    sharp_ref,
    input_hbm,
    weight_ref,
    table_ref,
    x1_hbm,
    qkv_hbm,
    mixed_hbm,
    scores_hbm,
    attention_hbm,
    slope_hbm,
    e_hbm,
    bn_ref,
    dx2_hbm,
    dn_hbm,
    back_ref,
    head_low_hbm,
    dx1_hbm,
    head_weights_hbm,
    weight_grad_ref,
    grads_ref,
    x1_ref,
    qkv_ref,
    mixed_ref,
    scores_ref,
    attention_ref,
    dx2_ref,
    head_weights,
    out_weight,
    pool,
    conv_grad,
    mixed_grad,
    first_low,
    head_low,
    spread,
    out_sum,
    head_sum,
    sharp_sums,
    order_ref,
    start_ref,
    load_sems,
    tile_sems,
):
    row_count, width = input_hbm.shape
    low_rows, input_ref = head_low.at[:, 0:width], head_low.at[:, PAD_WIDTH : PAD_WIDTH + width]
    near = tile_rows(row_count, 4)
    input_load = pltpu.make_async_copy(input_hbm, input_ref, load_sems.at[11 + row_count // near])
    input_load.start()
    chunks = width // LANES
    slope_ref, e_ref = pool.at[0:chunks], pool.at[chunks : 2 * chunks]
    dn_ref, conv_in = pool.at[2 * chunks : 3 * chunks], pool.at[3 * chunks : 4 * chunks]
    attention_out = slope_ref
    loads = [
        pltpu.make_async_copy(source, target, load_sems.at[index])
        for index, (source, target) in enumerate(
            (
                (mixed_hbm, mixed_ref),
                (dx2_hbm, dx2_ref),
                (qkv_hbm, qkv_ref),
                (scores_hbm, scores_ref),
                (attention_hbm, attention_ref),
            )
        )
    ]
    saves = [
        pltpu.make_async_copy(source, target, load_sems.at[len(loads) + index])
        for index, (source, target) in enumerate(
            (
                (head_weights, head_weights_hbm),
                (dx2_ref, dx1_hbm),
            )
        )
    ]
    for step in range(row_count // near):
        rows = pl.ds(step * near, near)
        saves.append(
            pltpu.make_async_copy(
                head_low.at[rows], head_low_hbm.at[rows], load_sems.at[len(loads) + 3 + step]
            )
        )
    tiled = [
        (x1_hbm, x1_ref, False),
        (slope_hbm, slope_ref, True),
        (e_hbm, e_ref, True),
        (dn_hbm, dn_ref, True),
    ]

    def start_tile(first, size, _):
        for load in row_copies(tiled, first, size, tile_sems.at[lax.div(first, ROW_TILE)]):
            load.start()
        return 0

    for_rows(row_count, ROW_TILE, start_tile)
    for load in loads:
        load.start()
    total_live = live_total(sides_ref)
    batch = [batch_vectors(bn_ref, chunk, chunks) for chunk in range(chunks)]
    zero = jnp.zeros((8, LANES), F32)
    wide = jnp.zeros((8, width), F32)
    mapping = head_map(BF16)
    for part in range(3):
        head_weights[:, part * PAD_WIDTH : (part + 1) * PAD_WIDTH] = dot(
            weight_ref[part], mapping
        ).astype(BF16)
    saves[0].start()
    out_weight[...] = dot_rows(mapping, weight_ref[3]).astype(BF16)
    spread[...] = jnp.zeros_like(spread)

    def first_norm(first, size, _):
        rows = pl.ds(first, size)
        unit, _ = centered(input_ref[rows, :].astype(F32))
        first_low[rows, :] = (unit * table_ref[0:1, :] + table_ref[1:2, :]).astype(BF16)
        return 0

    input_load.wait()
    for_rows(row_count, ROW_TILE, first_norm)


    def batch_back(first, size, _):
        for load in row_copies(tiled, first, size, tile_sems.at[lax.div(first, ROW_TILE)]):
            load.wait()
        rows = pl.ds(first, size)
        live = row_mask(first, size, LANES, total_live)
        unit, _ = centered(x1_ref[rows, :])
        value = unit * table_ref[3:4, :] + table_ref[4:5, :]
        for chunk in range(chunks):
            lanes = chunk_lanes(chunk)
            mean, scale = batch[chunk]
            count = bn_ref[2 * chunks : 2 * chunks + 1, :]
            standard = (e_ref[chunk, rows, :] - mean) * scale
            inner = (
                back_ref[chunk : chunk + 1, :]
                + standard * back_ref[chunks + chunk : chunks + chunk + 1, :]
            ) / count
            grad = scale * table_ref[5:6, lanes] * (dn_ref[chunk, rows, :] - inner)
            grad = grad * slope_ref[chunk, rows, :]
            conv_grad[chunk, pl.ds(LEAD + first, size), :] = jnp.where(live, grad, 0.0)
            conv_in[chunk, pl.ds(first, size), :] = value[:, lanes]
        return 0

    for_rows(row_count, ROW_TILE, batch_back)

    taps = [tap_vectors(table_ref, 11, chunk) for chunk in range(chunks)]

    def back_step(row, side, masks, carry):
        rows = pl.ds(row, 8)
        result = []
        for chunk in range(chunks):
            held = conv_in[chunk, rows, :]
            own = jnp.where(masks[0], held, 0.0)
            total, tap_sums = conv_backward(
                conv_grad, chunk, row, side, masks, taps[chunk], own, carry[chunk]
            )
            conv_in[chunk, rows, :] = jnp.where(masks[0], total, held)
            result.append(tap_sums)
        return tuple(result)

    tap_sums = for_groups(sides_ref, back_step, ((zero,) * 9,) * chunks)
    for chunk in range(chunks):
        for index, value in enumerate(tap_sums[chunk]):
            grads_ref[5 + index : 6 + index, chunk_lanes(chunk)] = jnp.sum(
                value, axis=0, keepdims=True
            )

    for load in loads[0:2]:
        load.wait()

    def attention_rows(first):
        return dot(mixed_ref[pl.ds(first, near), :], out_weight[...])

    out_sum[...] = jnp.zeros_like(out_sum)
    ahead = attention_rows(0)
    sums = [jnp.zeros((8, width), F32)] * 3
    for first in range(0, row_count, near):
        rows = pl.ds(first, near)
        held = ahead
        if first + near < row_count:
            ahead = attention_rows(first + near)
        live = row_mask(first, near, width, total_live)
        grad = jnp.concatenate([conv_in[chunk, rows, :] for chunk in range(chunks)], axis=1)
        grad = jnp.where(live, grad, 0.0)
        unit, scale = centered(x1_ref[rows, :])
        total = dx2_ref[rows, :] + norm_back(grad * table_ref[3:4, :], unit, scale)
        dx2_ref[rows, :] = total
        low = (total * table_ref[2:3, :]).astype(BF16)
        sums[0] = sums[0] + fold(total * held)
        sums[1] = sums[1] + fold(grad * unit)
        sums[2] = sums[2] + fold(grad)
        mixed_grad[rows, :] = dot_lanes(low, out_weight[...])
        out_sum[...] += dot_rows(mixed_ref[rows, :], low)
    saves[1].start()
    for index in range(3):
        grads_ref[2 + index : 3 + index, :] = jnp.sum(sums[index], axis=0, keepdims=True)

    pool[...] = jnp.zeros_like(pool)

    low = out_sum[...].astype(BF16)
    weight_grad_ref[3] = dot(mapping, low).astype(BF16)
    sharp_sums[...] = jnp.zeros_like(sharp_sums)

    for load in loads[2:]:
        load.wait()

    def crop_step(members):
        units_of = [(member, half) for member in range(len(members)) for half in range(2)]
        grads, blocks, sums, results = [], [], [], []
        for member, half in units_of:
            crop, rows, keep = members[member]
            lanes = half_lanes(half)
            value = split(jnp.where(keep, qkv_ref[rows, lanes[2]], 0.0))
            grad = split(jnp.where(keep, mixed_grad[rows, lanes[0]], 0.0))
            grads.append(grad)
            blocks.append(dot_split(dot_rows, value, grad))
        value_grads = []
        for index, (member, half) in enumerate(units_of):
            for pair in range(2):
                shares = attention_ref[members[member][0], 2 * half + pair]
                spread_pair(spread, member, half, pair, shares)
            shares = (spread[member, half, 0], spread[member, half, 1])
            value_grads.append(dot_split(dot_lanes, grads[index], shares))
        for (member, half), block in zip(units_of, blocks):
            crop = members[member][0]
            query_sums = []
            for pair in range(2):
                index = 2 * half + pair
                shares = attention_ref[crop, index]
                scores = scores_ref[crop, index]
                part = pair_part(block, pair)
                part = shares * (part - jnp.sum(part * shares, axis=0, keepdims=True))
                total = jnp.sum(part * scores, axis=0, keepdims=True)
                sharp_sums[index, pl.ds(crop, 1), :] = total
                sharpness = pair_sharpness(sharp_ref, index)
                query_sums.append(total * sharpness)
                spread_pair(spread, member, 2 + half, pair, part * sharpness)
            sums.append(jnp.concatenate(query_sums, axis=1))
        for index, (member, half) in enumerate(units_of):
            crop, rows, keep = members[member]
            lanes = half_lanes(half)
            query, query_scale = units(jnp.where(keep, qkv_ref[rows, lanes[0]], 0.0))
            key, key_scale = units(jnp.where(keep, qkv_ref[rows, lanes[1]], 0.0))
            slopes = (spread[member, 2 + half, 0], spread[member, 2 + half, 1])
            query_grad = dot_split(dot, split(key), slopes)
            query_grad = query_scale * (query_grad - query * sums[index])
            key_grad = dot_split(dot_lanes, split(query), slopes)
            key_grad = key_scale * (
                key_grad - key * jnp.sum(key_grad * key, axis=0, keepdims=True)
            )
            results.append((query_grad, key_grad, value_grads[index]))
        for (member, half), grads in zip(units_of, results):
            _, rows, keep = members[member]
            for part, result in enumerate(grads):
                for side in range(HALF_WIDTH // LANES):
                    chunk = (part * PAD_WIDTH + half * HALF_WIDTH) // LANES + side
                    pool[chunk, rows, :] = jnp.where(
                        keep[:, 0:LANES], result[:, chunk_lanes(side)], pool[chunk, rows, :]
                    )

    for_crops(sides_ref, row_count, order_ref, start_ref, crop_step)

    grads_ref[0:2, :] = jnp.zeros((2, width), F32)
    grads_ref[14:16, :] = jnp.zeros((2, width), F32)
    lane = lax.broadcasted_iota(jnp.int32, (1, LANES), 1)
    total = jnp.zeros((1, LANES), F32)
    for head in range(HEAD_NUMBER):
        row = jnp.sum(sharp_sums[head // 2], axis=0, keepdims=True)
        row = jnp.where((lane >> 6) == head % 2, row, 0.0)
        total = jnp.where(lane == head, jnp.sum(row, axis=1, keepdims=True), total)
    grads_ref[14:15, 0:LANES] = total

    head_sum[...] = jnp.zeros_like(head_sum)

    def round_rows(step):
        rows = pl.ds(step * near, near)
        for chunk in range(3 * PAD_WIDTH // LANES):
            head_low[rows, chunk_lanes(chunk)] = pool[chunk, rows, :].astype(BF16)
        saves[2 + step].start()

    round_rows(0)
    for step in range(row_count // near):
        if step + 1 < row_count // near:
            round_rows(step + 1)
        rows = pl.ds(step * near, near)
        head_sum[...] += dot_rows(first_low[rows, :], head_low[rows, :])
    for part in range(3):
        low = head_sum[:, part * PAD_WIDTH : (part + 1) * PAD_WIDTH].astype(BF16)
        weight_grad_ref[part] = dot_lanes(low, mapping).astype(BF16)
    for save in saves:
        save.wait()


def mixing_backward(sides, sharpness, inputs, weights, table, saved, batch_sums, dx2, dn, back_sums):
    row_count, width = inputs.shape
    chunks = width // LANES
    crops = sides.shape[0]
    shape = jax.ShapeDtypeStruct
    x1, qkv, mixed, scores, attention, slope, e = saved
    return pl.pallas_call(
        mixing_backward_kernel,
        out_shape=(
            shape((row_count, 3 * PAD_WIDTH), BF16),
            shape((row_count, width), F32),
            shape((width, 3 * PAD_WIDTH), BF16),
            shape((4, width, width), BF16),
            shape((16, width), F32),
        ),
        in_specs=[SMEM_SPEC, SMEM_SPEC]
        + [ANY_SPEC, VMEM_SPEC, VMEM_SPEC]
        + [ANY_SPEC] * 7
        + [VMEM_SPEC, ANY_SPEC, ANY_SPEC, VMEM_SPEC],
        out_specs=(ANY_SPEC,) * 3 + (VMEM_SPEC,) * 2,
        scratch_shapes=[
            pltpu.VMEM((row_count, width), F32),
            pltpu.VMEM((row_count, 3 * PAD_WIDTH), F32),
            pltpu.VMEM((row_count, PAD_WIDTH), BF16),
            pltpu.VMEM((crops, HEAD_PAIRS, HDIM, LANES), F32),
            pltpu.VMEM((crops, HEAD_PAIRS, HDIM, LANES), F32),
            pltpu.VMEM((row_count, width), F32),
            pltpu.VMEM((width, 3 * PAD_WIDTH), BF16),
            pltpu.VMEM((PAD_WIDTH, width), BF16),
            pltpu.VMEM((3 * PAD_WIDTH // LANES, row_count, LANES), F32),
            pltpu.VMEM((chunks, LEAD + row_count + TAIL, LANES), F32),
            pltpu.VMEM((row_count, PAD_WIDTH), F32),
            pltpu.VMEM((row_count, width), BF16),
            pltpu.VMEM((row_count, 3 * PAD_WIDTH), BF16),
            pltpu.VMEM((CROP_GROUP, 4, 2, HALF_WIDTH, HALF_WIDTH), BF16),
            pltpu.VMEM((PAD_WIDTH, width), F32),
            pltpu.VMEM((width, 3 * PAD_WIDTH), F32),
            pltpu.VMEM((HEAD_PAIRS, crops, LANES), F32),
            pltpu.SMEM((2 * crops,), jnp.int32),
            pltpu.SMEM((crops,), jnp.int32),
            pltpu.SemaphoreType.DMA((12 + row_count // tile_rows(row_count, 4),)),
            pltpu.SemaphoreType.DMA(((row_count + ROW_TILE - 1) // ROW_TILE,)),
        ],
        compiler_params=pltpu.CompilerParams(vmem_limit_bytes=VMEM_LIMIT),
        name="mixing_backward",
    )(
        sides,
        sharpness,
        inputs,
        weights,
        table,
        x1,
        qkv,
        mixed,
        scores,
        attention,
        slope,
        e,
        batch_sums,
        dx2,
        dn,
        back_sums,
    )


MESH = pl.DeviceIdType.MESH


def greet(peers):
    barrier = pltpu.get_barrier_semaphore()
    for peer in peers:
        pl.semaphore_signal(barrier, inc=1, device_id=peer, device_id_type=MESH)
    pl.semaphore_wait(barrier, len(peers))


def push(source, target, send, receive, peer):
    copy = pltpu.make_async_remote_copy(
        src_ref=source,
        dst_ref=target,
        send_sem=send,
        recv_sem=receive,
        device_id=peer,
        device_id_type=MESH,
    )
    copy.start()
    return copy


def turned(place, step, count):
    return lax.rem(place + step, count)


def ring_peers(axis, count):
    place = lax.axis_index(axis)
    return [{axis: turned(place, step, count)} for step in range(1, count)]


def comm_params(identity):
    return pltpu.CompilerParams(
        collective_id=identity, has_side_effects=True, vmem_limit_bytes=VMEM_LIMIT
    )


def flip(value, bits):
    for bit in (1, 2, 4):
        if bits & bit:
            value = value + bit - 2 * bit * lax.rem(lax.div(value, bit), 2)
    return value


def flip_peers(axis, count):
    place = lax.axis_index(axis)
    return [{axis: flip(place, bits)} for bits in range(1, count)]


def sum_all_kernel(counts, part_ref, total_ref, parts, send, receive):
    n_dp, n_fsdp = counts
    dp, fsdp = lax.axis_index("dp"), lax.axis_index("fsdp")
    place = dp * n_fsdp + fsdp
    peers = [
        {"dp": flip(dp, outer), "fsdp": flip(fsdp, inner)}
        for inner in reversed(range(n_fsdp))
        for outer in reversed(range(n_dp))
        if inner or outer
    ]
    greet(peers)
    parts[place] = part_ref[...]
    copies = [
        push(part_ref, parts.at[place], send.at[k], receive.at[k], peer)
        for k, peer in enumerate(peers)
    ]
    for copy in copies:
        copy.wait()
    total = parts[0]
    for k in range(1, n_dp * n_fsdp):
        total = total + parts[k]
    total_ref[...] = total


def sum_all(part, counts, identity):
    size = counts[0] * counts[1]
    return pl.pallas_call(
        functools.partial(sum_all_kernel, counts),
        out_shape=jax.ShapeDtypeStruct(part.shape, F32),
        in_specs=[VMEM_SPEC],
        out_specs=VMEM_SPEC,
        scratch_shapes=[
            pltpu.VMEM((size, *part.shape), F32),
            pltpu.SemaphoreType.DMA((size - 1,)),
            pltpu.SemaphoreType.DMA((size - 1,)),
        ],
        compiler_params=comm_params(identity),
        name="sum_all",
    )(part)


def sum_pair_kernel(
    counts, part_ref, blocks_hbm, total_ref, sums_hbm, parts, own, other, sums_ref, send, receive, sems
):
    n_dp, n_fsdp = counts
    dp, fsdp = lax.axis_index("dp"), lax.axis_index("fsdp")
    core = lax.rem(dp, 2)
    place = dp * n_fsdp + fsdp
    peers = [
        {"dp": flip(dp, outer), "fsdp": flip(fsdp, inner)}
        for inner in reversed(range(n_fsdp))
        for outer in reversed(range(n_dp))
        if inner or outer
    ]
    load = pltpu.make_async_copy(blocks_hbm.at[pl.ds(core * n_fsdp, n_fsdp)], own, sems.at[0])
    load.start()
    greet(peers)
    parts[place] = part_ref[...]
    copies = [
        push(part_ref, parts.at[place], send.at[k], receive.at[k], peer)
        for k, peer in enumerate(peers)
    ]
    blocks = push(
        blocks_hbm.at[pl.ds((1 - core) * n_fsdp, n_fsdp)],
        other,
        sems.at[1],
        sems.at[2],
        {"dp": flip(dp, 1)},
    )
    load.wait()
    blocks.wait_recv()
    for owner in range(n_fsdp):
        sums_ref[owner] = (own[owner].astype(F32) + other[owner].astype(F32)).astype(BF16)
    save = pltpu.make_async_copy(sums_ref, sums_hbm, sems.at[3])
    save.start()
    for copy in copies:
        copy.wait()
    total = parts[0]
    for k in range(1, n_dp * n_fsdp):
        total = total + parts[k]
    total_ref[...] = total
    blocks.wait_send()
    save.wait()


def sum_pair(part, blocks, counts, identity):
    size = counts[0] * counts[1]
    half = (counts[1], *blocks.shape[1:])
    shape = jax.ShapeDtypeStruct
    return pl.pallas_call(
        functools.partial(sum_pair_kernel, counts),
        out_shape=(shape(part.shape, F32), shape(half, BF16)),
        in_specs=[VMEM_SPEC, ANY_SPEC],
        out_specs=(VMEM_SPEC, ANY_SPEC),
        scratch_shapes=[
            pltpu.VMEM((size, *part.shape), F32),
            pltpu.VMEM(half, BF16),
            pltpu.VMEM(half, BF16),
            pltpu.VMEM(half, BF16),
            pltpu.SemaphoreType.DMA((size - 1,)),
            pltpu.SemaphoreType.DMA((size - 1,)),
            pltpu.SemaphoreType.DMA((4,)),
        ],
        compiler_params=comm_params(identity),
        name="sum_pair",
    )(part, blocks)


def gather_kernel(
    counts,
    masters_hbm,
    table_ref,
    blocks_hbm,
    full_table_ref,
    blocks,
    masters,
    tables,
    stage,
    ring_send,
    ring_recv,
    table_send,
    table_recv,
    cross_send,
    cross_recv,
    pair_send,
    pair_recv,
    local_sems,
):
    n_dp, n_fsdp = counts
    dp, fsdp = lax.axis_index("dp"), lax.axis_index("fsdp")
    shard, width = masters_hbm.shape[1:]
    columns = table_ref.shape[1]
    load = pltpu.make_async_copy(masters_hbm.at[dp], masters, local_sems.at[0])
    load.start()
    across = lax.rem(dp + 2, 4)
    pair = dp + 1 - 2 * lax.rem(dp, 2)
    peers = flip_peers("fsdp", n_fsdp)
    greet(peers + [{"dp": across}, {"dp": pair}])

    def piece(block, owner):
        return blocks.at[block, pl.ds(pl.multiple_of(owner * shard, 16), shard), :]

    def origin(step):
        return flip(fsdp, step)

    stage[...] = jnp.zeros_like(stage)
    stage[0 : table_ref.shape[0], 0:columns] = table_ref[...]
    tables[fsdp] = stage[...].astype(BF16)
    load.wait()
    blocks[dp, pl.ds(pl.multiple_of(fsdp * shard, 16), shard), :] = masters[...].astype(BF16)
    own = piece(dp, fsdp)
    ring = [
        push(own, own, ring_send.at[k], ring_recv.at[k], peer) for k, peer in enumerate(peers)
    ]
    table_copies = [
        push(tables.at[fsdp], tables.at[fsdp], table_send.at[k], table_recv.at[k], peer)
        for k, peer in enumerate(peers)
    ]
    crossing, pairing = [], []
    for step in range(n_fsdp):
        if step:
            ring[step - 1].wait_recv()
        part = piece(dp, origin(step))
        crossing.append(push(part, part, cross_send.at[step], cross_recv.at[step], {"dp": across}))
        pairing.append(
            push(part, part, pair_send.at[0, step], pair_recv.at[0, step], {"dp": pair})
        )
    for step in range(n_fsdp):
        crossing[step].wait_recv()
        part = piece(across, origin(step))
        pairing.append(
            push(part, part, pair_send.at[1, step], pair_recv.at[1, step], {"dp": pair})
        )
    for copy in table_copies:
        copy.wait_recv()
    total = None
    for owner in range(n_fsdp):
        lane = lax.broadcasted_iota(jnp.int32, (LANES, width), 0)
        target = lax.broadcasted_iota(jnp.int32, (LANES, width), 1)
        hit = (lane < columns) & (lane + owner * columns == target)
        term = dot(tables[owner], hit.astype(F32).astype(BF16))
        total = term if total is None else total + term
    full_table_ref[...] = total
    for copy in pairing:
        copy.wait_recv()
    save = pltpu.make_async_copy(blocks, blocks_hbm, local_sems.at[1])
    save.start()
    for copy in ring + table_copies + crossing + pairing:
        copy.wait_send()
    save.wait()


def gather_start(masters, coefficients, counts, identity):
    n_dp, n_fsdp = counts
    width = masters.shape[2]
    shape = jax.ShapeDtypeStruct
    dma = pltpu.SemaphoreType.DMA
    return pl.pallas_call(
        functools.partial(gather_kernel, counts),
        out_shape=(shape((4, width, width), BF16), shape((32, width), F32)),
        in_specs=[ANY_SPEC, VMEM_SPEC],
        out_specs=(ANY_SPEC, VMEM_SPEC),
        scratch_shapes=[
            pltpu.VMEM((4, width, width), BF16),
            pltpu.VMEM(masters.shape[1:], F32),
            pltpu.VMEM((n_fsdp, 32, LANES), BF16),
            pltpu.VMEM((32, LANES), F32),
            dma((n_fsdp - 1,)),
            dma((n_fsdp - 1,)),
            dma((n_fsdp - 1,)),
            dma((n_fsdp - 1,)),
            dma((n_fsdp,)),
            dma((n_fsdp,)),
            dma((2, n_fsdp)),
            dma((2, n_fsdp)),
            dma((2,)),
        ],
        compiler_params=comm_params(identity),
        name="gather_start",
    )(masters, coefficients)


def owner_rows(owner, shard):
    return pl.ds(pl.multiple_of(owner * shard, 16), shard)


TABLE_ROWS = (
    [(0, row) for row in range(5)]
    + [(1, 13), (1, 14)]
    + [(1, row) for row in range(4)]
    + [(0, row) for row in range(5, 14)]
    + [(1, row) for row in range(4, 13)]
)


def settle_kernel(
    counts,
    place_ref,
    mix_hbm,
    feed_hbm,
    mix_table_ref,
    feed_table_ref,
    left_hbm,
    right_hbm,
    head_low_hbm,
    dx1_hbm,
    input_hbm,
    head_weights_hbm,
    coefficient_ref,
    grad_hbm,
    slots_hbm,
    rows_hbm,
    table_ref,
    out_hbm,
    left,
    right,
    head_low,
    dx1,
    inputs,
    head_weights,
    out,
    first_sums,
    pair_buf,
    cross_out,
    cross_buf,
    ring_out,
    ring_buf,
    feed_in,
    feed_buf,
    dp_buf,
    slot_out,
    slots,
    steps,
    rows_buf,
    table_stage,
    table_rows,
    table_out,
    table_buf,
    table_part,
    table_dp,
    feed_sum,
    mix,
    feed_ref,
    left_parts,
    grad_ref,
    load_sems,
    pair_send,
    pair_recv,
    cross_send,
    cross_recv,
    ring_send,
    ring_recv,
    feed_in_send,
    feed_in_recv,
    feed_send,
    feed_recv,
    dp_send,
    dp_recv,
    slot_send,
    slot_recv,
    twin_send,
    twin_recv,
    back_send,
    back_recv,
    last_send,
    last_recv,
    table_rows_send,
    table_rows_recv,
    table_send,
    table_recv,
    table_dp_send,
    table_dp_recv,
):
    n_dp, n_fsdp = counts
    dp, fsdp = lax.axis_index("dp"), lax.axis_index("fsdp")
    width = mix_hbm.shape[2]
    shard = width // n_fsdp
    core = lax.rem(dp, 2)
    across, pair, pair_across = flip(dp, 2), flip(dp, 1), flip(dp, 3)
    peers, dp_peers = flip_peers("fsdp", n_fsdp), flip_peers("dp", n_dp)
    to_pair, to_across = {"dp": pair}, {"dp": across}
    loads = [
        pltpu.make_async_copy(left_hbm.at[core], left, load_sems.at[0]),
        pltpu.make_async_copy(right_hbm.at[core], right, load_sems.at[1]),
    ]
    mix_loads = [
        pltpu.make_async_copy(mix_hbm.at[across], mix.at[0], load_sems.at[3]),
        pltpu.make_async_copy(mix_hbm.at[dp], mix.at[1], load_sems.at[4]),
    ]
    feed_load = pltpu.make_async_copy(feed_hbm, feed_ref, load_sems.at[5])
    for load in mix_loads:
        load.start()
    feed_load.start()
    row_count = dx1.shape[0]
    tile = tile_rows(row_count, 4)
    tiles = row_count // tile
    weight_load = pltpu.make_async_copy(head_weights_hbm, head_weights, load_sems.at[2])
    weight_load.start()
    tile_loads, tile_saves = [], []
    for step in range(tiles):
        rows = pl.ds(step * tile, tile)
        sems = [load_sems.at[8 + 4 * step + index] for index in range(4)]
        tile_loads.append(
            [
                pltpu.make_async_copy(head_low_hbm.at[rows], head_low.at[rows], sems[0]),
                pltpu.make_async_copy(dx1_hbm.at[rows], dx1.at[rows], sems[1]),
                pltpu.make_async_copy(input_hbm.at[rows], inputs.at[rows], sems[2]),
            ]
        )
        tile_saves.append(pltpu.make_async_copy(out.at[rows], out_hbm.at[rows], sems[3]))
        for load in tile_loads[step]:
            load.start()
    for load in loads:
        load.start()
    first_sums[...] = jnp.zeros_like(first_sums)

    def first_back(step):
        rows = pl.ds(step * tile, tile)
        if step == 0:
            weight_load.wait()
        for load in tile_loads[step]:
            load.wait()
        grad = dot_lanes(head_low[rows, :], head_weights[...])
        unit, scale = centered(inputs[rows, :].astype(F32))
        total = dx1[rows, :] + norm_back(grad * coefficient_ref[0:1, :], unit, scale)
        out[rows, :] = total.astype(BF16)
        tile_saves[step].start()
        first_sums[0] += fold(grad * unit)
        first_sums[1] += fold(grad)

    greet(peers + dp_peers)

    parts = list(reversed(range(n_fsdp // 2)))
    deep = 2 * shard

    def part_rows(part):
        first = lax.div(flip(fsdp, 2 * part), 2)
        return pl.ds(pl.multiple_of(first * deep, 16), deep)

    def owner_rows(owner):
        return pl.ds(pl.multiple_of(owner * shard, 16), shard)

    pairing = {}
    for part in parts:
        rows = part_rows(part)
        for side, block in enumerate((pair_across, pair)):
            pairing[part, side] = push(
                mix_hbm.at[block, rows],
                pair_buf.at[side, rows],
                pair_send.at[side, part],
                pair_recv.at[side, part],
                to_pair,
            )
    for load in mix_loads:
        load.wait()
    crossing = {}
    for part in parts:
        rows = part_rows(part)
        pairing[part, 0].wait_recv()
        cross_out[rows, :] = (
            mix[0, rows, :].astype(F32) + pair_buf[0, rows, :].astype(F32)
        ).astype(BF16)
        crossing[part] = push(
            cross_out.at[rows],
            cross_buf.at[rows],
            cross_send.at[part],
            cross_recv.at[part],
            to_across,
        )
    ring = {}
    for part in parts:
        rows = part_rows(part)
        pairing[part, 1].wait_recv()
        crossing[part].wait_recv()
        ring_out[rows, :] = (
            mix[1, rows, :].astype(F32)
            + pair_buf[1, rows, :].astype(F32)
            + cross_buf[rows, :].astype(F32)
        ).astype(BF16)
        for bits in (2 * part + 1, 2 * part):
            if bits:
                ring[bits] = push(
                    ring_out.at[owner_rows(flip(fsdp, bits))],
                    ring_buf.at[bits],
                    ring_send.at[bits - 1],
                    ring_recv.at[bits - 1],
                    peers[bits - 1],
                )

    slot_blocks = []
    for bits in range(n_fsdp):
        slot = 2 * flip(fsdp, bits) + core
        block, filled = jnp.int32(0), jnp.float32(0.0)
        for index in range(grad_ref.shape[0]):
            here = place_ref[index] == slot
            block = jnp.where(here, index, block)
            filled = jnp.where(here, 1.0, filled)
        slot_blocks.append((block, filled))

    pieces = feed_sum.shape[0] // 2
    side = lax.div(dp, 2)
    feed_load.wait()
    for piece in range(2 * pieces):
        total = feed_ref[0, piece].astype(F32)
        for owner in range(1, n_fsdp):
            total = total + feed_ref[owner, piece].astype(F32)
        feed_sum[piece] = total.astype(BF16)
    feeding = push(
        feed_sum.at[pl.ds((1 - side) * pieces, pieces)],
        feed_in,
        feed_in_send.at[0],
        feed_in_recv.at[0],
        to_across,
    )
    for step in range(tiles - tiles // 2):
        first_back(step)
    feeding.wait_recv()
    total = feed_sum[pl.ds(side * pieces, pieces)].astype(F32) + feed_in[...].astype(F32)
    feed_buf[dp] = total.astype(BF16)
    feeds = [
        push(feed_buf.at[dp], feed_buf.at[dp], feed_send.at[k], feed_recv.at[k], peer)
        for k, peer in enumerate(dp_peers)
    ]

    total = ring_out[owner_rows(fsdp), :].astype(F32)
    for bits in range(1, n_fsdp):
        ring[bits].wait_recv()
        total = total + ring_buf[bits].astype(F32)
    dp_buf[dp] = total
    gathering = [
        push(dp_buf.at[dp], dp_buf.at[dp], dp_send.at[k], dp_recv.at[k], peer)
        for k, peer in enumerate(dp_peers)
    ]
    for step in range(tiles - tiles // 2, tiles):
        first_back(step)

    table_stage[...] = jnp.zeros_like(table_stage)
    for row, (source, first) in enumerate(TABLE_ROWS):
        ref = mix_table_ref if source == 0 else feed_table_ref
        table_stage[row : row + 1, :] = ref[first : first + 1, :]
    for row in range(2):
        table_stage[row : row + 1, :] = jnp.sum(first_sums[row], axis=0, keepdims=True)
    table_stage[31:32, :] = mix_table_ref[14:15, :]
    quarter = table_stage.shape[0] // n_dp

    def quarter_rows(place):
        return pl.ds(pl.multiple_of(place * quarter, 8), quarter)

    table_rows[dp] = table_stage[quarter_rows(dp), :]
    quartering = [
        push(
            table_stage.at[quarter_rows(flip(dp, step + 1))],
            table_rows.at[dp],
            table_rows_send.at[step],
            table_rows_recv.at[step],
            peer,
        )
        for step, peer in enumerate(dp_peers)
    ]
    for copy in feeds:
        copy.wait_recv()
    for place in range(n_dp):
        for piece in range(pieces):
            block = n_dp + (place % 2 * 2 + place // 2) * pieces + piece
            grad_ref[block] = feed_buf[place, piece].astype(F32)
    for copy in gathering:
        copy.wait_recv()
    for place in range(n_dp):
        grad_ref[place] = dp_buf[place]
    tile_saves.append(pltpu.make_async_copy(grad_ref, grad_hbm, load_sems.at[6 + 2 + 4 * tiles]))
    tile_saves[-1].start()

    slotting = {}
    for bits in reversed(range(n_fsdp)):
        block, filled = slot_blocks[bits]
        value = (grad_ref[block] * filled).astype(BF16)
        if bits:
            slot_out[bits - 1] = value
            slotting[bits] = push(
                slot_out.at[bits - 1],
                slots.at[core, owner_rows(fsdp), :],
                slot_send.at[bits - 1],
                slot_recv.at[bits - 1],
                peers[bits - 1],
            )
        else:
            slots[core, owner_rows(fsdp), :] = value
    for copy in quartering:
        copy.wait_recv()
    rest = table_rows[0]
    for place in range(1, n_dp):
        rest = rest + table_rows[place]
    sharp_row = lax.broadcasted_iota(jnp.int32, (quarter, LANES), 0) + dp * quarter == 31
    sharp_values = jnp.broadcast_to(rest[quarter - 1 : quarter, 0:LANES], (quarter, LANES))
    terms = []
    for _ in range(3):
        term = rest.astype(BF16).astype(F32)
        terms.append(term)
        rest = rest - term
    terms = jnp.concatenate(terms, axis=0).astype(BF16)
    columns = width // n_fsdp
    for owner in range(n_fsdp):
        lane = lax.broadcasted_iota(jnp.int32, (width, LANES), 1)
        source = lax.broadcasted_iota(jnp.int32, (width, LANES), 0)
        hit = ((lane < columns) & (lane + owner * columns == source)).astype(F32).astype(BF16)
        value = dot(terms, hit)
        value = value[0:quarter] + value[quarter : 2 * quarter] + value[2 * quarter :]
        table_out[owner] = jnp.where(sharp_row, sharp_values, value)
    table_buf[fsdp] = table_out[fsdp]
    tabling = [
        push(
            table_out.at[flip(fsdp, step + 1)],
            table_buf.at[fsdp],
            table_send.at[step],
            table_recv.at[step],
            peer,
        )
        for step, peer in enumerate(peers)
    ]
    for load in loads:
        load.wait()
    right_parts = split(right[...])
    for index, value in enumerate(split(left[...])):
        left_parts[index] = value
    twins = []
    for bits in range(n_fsdp):
        if bits:
            slotting[bits].wait_recv()
        part = slots.at[core, owner_rows(flip(fsdp, bits)), :]
        twins.append(push(part, part, twin_send.at[bits], twin_recv.at[bits], to_pair))

    grad = slots[core]
    back = {}
    for part in parts:
        rows = part_rows(part)
        half = split(dot(left_parts[0, rows, :], grad) + dot(left_parts[1, rows, :], grad))
        steps[rows, :] = dot_split(dot, half, right_parts).astype(BF16)
        for bits in (2 * part + 1, 2 * part):
            if bits:
                back[bits] = push(
                    steps.at[owner_rows(flip(fsdp, bits))],
                    rows_buf.at[2 * fsdp + core],
                    back_send.at[bits - 1],
                    back_recv.at[bits - 1],
                    peers[bits - 1],
                )
    rows_buf[2 * fsdp + core] = steps[owner_rows(fsdp), :]
    for copy in tabling:
        copy.wait_recv()
    total = table_buf[0]
    for owner in range(1, n_fsdp):
        total = total + table_buf[owner]
    table_part[...] = total
    table_dp[dp] = total
    table_dps = [
        push(table_part, table_dp.at[dp], table_dp_send.at[k], table_dp_recv.at[k], peer)
        for k, peer in enumerate(dp_peers)
    ]
    lasts = []
    for bits in range(n_fsdp):
        if bits:
            back[bits].wait_recv()
        part = rows_buf.at[2 * flip(fsdp, bits) + core]
        lasts.append(push(part, part, last_send.at[bits], last_recv.at[bits], to_pair))
    for copy in table_dps:
        copy.wait_recv()
    for place in range(n_dp):
        table_ref[place * quarter : (place + 1) * quarter, :] = table_dp[place]
    for copy in twins:
        copy.wait_recv()
    tile_saves.append(pltpu.make_async_copy(slots, slots_hbm, load_sems.at[6]))
    tile_saves[-1].start()
    for copy in lasts:
        copy.wait_recv()
    tile_saves.append(pltpu.make_async_copy(rows_buf, rows_hbm, load_sems.at[7]))
    tile_saves[-1].start()
    copies = [*pairing.values(), *crossing.values(), *ring.values(), *slotting.values()]
    copies += [*back.values(), feeding, *feeds, *quartering, *tabling, *table_dps, *gathering]
    for copy in copies + twins + lasts:
        copy.wait_send()
    for save in tile_saves:
        save.wait()


def settle(
    places, mix, feed, mix_table, feed_table, left, right, back, coefficients, counts, identity
):
    head_low, dx1, inputs, head_weights = back
    row_count = dx1.shape[0]
    tiles = row_count // tile_rows(row_count, 4)
    n_dp, n_fsdp = counts
    width = mix.shape[2]
    shard = width // n_fsdp
    blocks = n_dp + 2 * feed.shape[1]
    pieces = feed.shape[1] // 2
    inner, outer = n_fsdp - 1, n_dp - 1
    shape = jax.ShapeDtypeStruct
    dma = pltpu.SemaphoreType.DMA
    sizes = [(2, n_fsdp // 2), (n_fsdp // 2,), (inner,), (1,), (outer,), (outer,)]
    sizes += [(inner,), (n_fsdp,), (inner,), (n_fsdp,), (outer,), (inner,), (outer,)]
    return pl.pallas_call(
        functools.partial(settle_kernel, counts),
        out_shape=(
            shape((blocks, shard, width), F32),
            shape((2, width, width), BF16),
            shape((2 * n_fsdp, shard, width), BF16),
            shape((32, LANES), F32),
            shape(inputs.shape, BF16),
        ),
        in_specs=[SMEM_SPEC] + [ANY_SPEC] * 2 + [VMEM_SPEC] * 2 + [ANY_SPEC] * 6 + [VMEM_SPEC],
        out_specs=(ANY_SPEC,) * 3 + (VMEM_SPEC, ANY_SPEC),
        scratch_shapes=[
            pltpu.VMEM((width, width), F32),
            pltpu.VMEM((width, width), F32),
            pltpu.VMEM(head_low.shape, BF16),
            pltpu.VMEM(dx1.shape, F32),
            pltpu.VMEM(inputs.shape, BF16),
            pltpu.VMEM(head_weights.shape, BF16),
            pltpu.VMEM(inputs.shape, BF16),
            pltpu.VMEM((2, 8, width), F32),
            pltpu.VMEM((2, width, width), BF16),
            pltpu.VMEM((width, width), BF16),
            pltpu.VMEM((width, width), BF16),
            pltpu.VMEM((width, width), BF16),
            pltpu.VMEM((n_fsdp, shard, width), BF16),
            pltpu.VMEM((pieces, shard, width), BF16),
            pltpu.VMEM((n_dp, pieces, shard, width), BF16),
            pltpu.VMEM((n_dp, shard, width), F32),
            pltpu.VMEM((inner, shard, width), BF16),
            pltpu.VMEM((2, width, width), BF16),
            pltpu.VMEM((width, width), BF16),
            pltpu.VMEM((2 * n_fsdp, shard, width), BF16),
            pltpu.VMEM((32, width), F32),
            pltpu.VMEM((n_dp, 32 // n_dp, width), F32),
            pltpu.VMEM((n_fsdp, 32 // n_dp, LANES), F32),
            pltpu.VMEM((n_fsdp, 32 // n_dp, LANES), F32),
            pltpu.VMEM((32 // n_dp, LANES), F32),
            pltpu.VMEM((n_dp, 32 // n_dp, LANES), F32),
            pltpu.VMEM(feed.shape[1:], BF16),
            pltpu.VMEM((2, width, width), BF16),
            pltpu.VMEM(feed.shape, BF16),
            pltpu.VMEM((2, width, width), BF16),
            pltpu.VMEM((blocks, shard, width), F32),
            dma((9 + 4 * tiles,)),
        ]
        + [dma(size) for size in sizes for _ in range(2)],
        compiler_params=comm_params(identity),
        name="settle",
    )(places, mix, feed, mix_table, feed_table, left, right, *back, coefficients)


def finish_kernel(
    place_ref,
    table_ref,
    energy_ref,
    coefficient_ref,
    sharp_ref,
    sharp_energy_ref,
    grads_hbm,
    slots_hbm,
    rows_hbm,
    left_hbm,
    right_hbm,
    masters_hbm,
    tokens_hbm,
    grad_hbm,
    left_out_hbm,
    right_out_hbm,
    masters_out_hbm,
    low_hbm,
    tokens_out_hbm,
    table_grad_ref,
    energy_out_ref,
    coefficient_out_ref,
    sharp_grad_ref,
    sharp_energy_out_ref,
    sharp_out_ref,
    left,
    right,
    masters,
    low,
    tokens,
    grad_ref,
    slots_ref,
    rows_ref,
    sems,
):
    slot_count = slots_ref.shape[0]
    load_slots = pltpu.make_async_copy(slots_hbm, slots_ref, sems.at[10])
    load_rows = pltpu.make_async_copy(rows_hbm, rows_ref, sems.at[11])
    load_grads = pltpu.make_async_copy(grads_hbm, grad_ref, sems.at[12])
    load_slots.start()
    load_left = pltpu.make_async_copy(left_hbm, left, sems.at[0])
    load_right = pltpu.make_async_copy(right_hbm, right, sems.at[1])
    load_masters = pltpu.make_async_copy(masters_hbm, masters, sems.at[2])
    saves = [
        pltpu.make_async_copy(source, target, sems.at[3 + index])
        for index, (source, target) in enumerate(
            (
                (grad_ref, grad_hbm),
                (left, left_out_hbm),
                (right, right_out_hbm),
                (masters, masters_out_hbm),
                (low, low_hbm),
                (tokens, tokens_out_hbm),
            )
        )
    ]
    load_left.start()
    load_right.start()
    load_tokens = pltpu.make_async_copy(tokens_hbm, tokens, sems.at[9])
    load_tokens.start()
    load_grads.start()
    load_masters.start()
    load_rows.start()
    load_slots.wait()
    load_left.wait()
    for slot in range(slot_count):
        grad = slots_ref[slot]
        left[slot] = (
            covariance_forgetting * left[slot]
            + (1.0 - covariance_forgetting) * dot_lanes(grad, grad)
        )
    saves[1].start()
    load_right.wait()
    for slot in range(slot_count):
        grad = slots_ref[slot]
        right[slot] = (
            covariance_forgetting * right[slot]
            + (1.0 - covariance_forgetting) * dot_rows(grad, grad)
        )
    saves[2].start()
    load_tokens.wait()
    saves[5].start()
    load_grads.wait()
    saves[0].start()
    load_masters.wait()
    load_rows.wait()
    for block in range(masters.shape[0]):
        value = masters[block] - weight_rate * rows_ref[place_ref[block]].astype(F32)
        masters[block] = value
        low[block] = value.astype(BF16)
    saves[3].start()
    saves[4].start()
    count, columns = energy_ref.shape
    grad = table_ref[0:count, 0:columns]
    table_grad_ref[...] = grad
    energy = covariance_forgetting * energy_ref[...] + (1.0 - covariance_forgetting) * grad * grad
    energy_out_ref[...] = energy
    coefficient_out_ref[...] = coefficient_ref[...] - vector_rate * grad / (
        jnp.sqrt(energy) + energy_epsilon
    )
    grad = table_ref[31:32, 0:HEAD_NUMBER]
    grad = grad.reshape(HEAD_NUMBER)
    energy = covariance_forgetting * sharp_energy_ref[...] + (1.0 - covariance_forgetting) * grad * grad
    sharp_grad_ref[...] = grad
    sharp_energy_out_ref[...] = energy
    sharp_out_ref[...] = sharp_ref[...] - sharpness_step_size * grad / (
        jnp.sqrt(energy) + energy_epsilon
    )
    for save in saves:
        save.wait()


def finish(
    places,
    table,
    energy,
    coefficients,
    sharpness,
    sharpness_energy,
    grads,
    slots,
    rows,
    left,
    right,
    masters,
    tokens,
):
    shape = jax.ShapeDtypeStruct
    return pl.pallas_call(
        finish_kernel,
        out_shape=(
            shape(grads.shape, F32),
            shape(left.shape, F32),
            shape(right.shape, F32),
            shape(masters.shape, F32),
            shape(masters.shape, BF16),
            shape(tokens.shape, BF16),
            shape(energy.shape, F32),
            shape(energy.shape, F32),
            shape(energy.shape, F32),
            shape(sharpness.shape, F32),
            shape(sharpness.shape, F32),
            shape(sharpness.shape, F32),
        ),
        in_specs=[SMEM_SPEC] + [VMEM_SPEC] * 5 + [ANY_SPEC] * 7,
        out_specs=(ANY_SPEC,) * 6 + (VMEM_SPEC,) * 6,
        scratch_shapes=[
            pltpu.VMEM(left.shape, F32),
            pltpu.VMEM(right.shape, F32),
            pltpu.VMEM(masters.shape, F32),
            pltpu.VMEM(masters.shape, BF16),
            pltpu.VMEM(tokens.shape, BF16),
            pltpu.VMEM(grads.shape, F32),
            pltpu.VMEM(slots.shape, BF16),
            pltpu.VMEM(rows.shape, BF16),
            pltpu.SemaphoreType.DMA((13,)),
        ],
        compiler_params=pltpu.CompilerParams(vmem_limit_bytes=VMEM_LIMIT),
        name="finish",
    )(
        places,
        table,
        energy,
        coefficients,
        sharpness,
        sharpness_energy,
        grads,
        slots,
        rows,
        left,
        right,
        masters,
        tokens,
    )


def shards(
    patch_embeddings,
    view_side_tokens,
    projection_masters,
    channel_coefficients,
    head_sharpness,
    output_adjoint,
    leading_covariance,
    trailing_covariance,
    leading_root_preconditioner,
    trailing_root_preconditioner,
    channel_energy_average,
    sharpness_energy_average,
    storage_position_map,
):
    row_count, feature_count = patch_embeddings.shape
    block_count = projection_masters.shape[0]
    shard_rows = projection_masters.shape[1]
    slot_count = leading_covariance.shape[0]
    counts = (lax.axis_size("dp"), lax.axis_size("fsdp"))
    direct = counts[0] == 4 and slot_count == 2 and shard_rows % 16 == 0
    if direct:
        mixing_blocks, table = gather_start(projection_masters, channel_coefficients, counts, 0)
        grad_shape = (2 * counts[1], (block_count - 4) // 2, shard_rows, feature_count)
    else:
        full_table = lax.all_gather(channel_coefficients.astype(BF16), "fsdp", axis=1, tiled=True)
        table = full_table.astype(F32)
        mixing_blocks = lax.all_gather(
            projection_masters[:4].astype(BF16), "fsdp", axis=1, tiled=True
        )
        grad_shape = (1, block_count - 4, feature_count, feature_count)
    feed_blocks = lax.all_gather(projection_masters[4:].astype(BF16), "fsdp", axis=1, tiled=True)

    x1, qkv, mixed, scores, attention, slope, e, sums = mixing_forward(
        view_side_tokens, head_sharpness, patch_embeddings, mixing_blocks, table
    )
    batch_sums = sum_all(sums, counts, 1) if direct else lax.psum(sums, ("dp", "fsdp"))
    layer_output, dx2, dn, feed_grad, feed_table, back_part = feed_forward(
        view_side_tokens, x1, e, batch_sums, feed_blocks, table, output_adjoint, grad_shape
    )
    if direct:
        back_sums, feed_grad = sum_pair(back_part, feed_grad, counts, 2)
        feed_grad = lax.all_to_all(feed_grad, "fsdp", 0, 0, tiled=True)
    else:
        back_sums = lax.psum(back_part, ("dp", "fsdp"))
    head_low, dx1, head_weights, mixing_grad, mixing_table = mixing_backward(
        view_side_tokens,
        head_sharpness,
        patch_embeddings,
        mixing_blocks,
        table,
        (x1, qkv, mixed, scores, attention, slope, e),
        batch_sums,
        dx2,
        dn,
        back_sums,
    )
    if direct:
        grads, owned_grad, my_rows, table_total, tokens_grad = settle(
            storage_position_map,
            mixing_grad,
            feed_grad,
            mixing_table,
            feed_table,
            leading_root_preconditioner,
            trailing_root_preconditioner,
            (head_low, dx1, patch_embeddings, head_weights),
            table,
            counts,
            3,
        )
        results = list(
            finish(
                storage_position_map,
                table_total,
                channel_energy_average,
                channel_coefficients,
                head_sharpness,
                sharpness_energy_average,
                grads,
                owned_grad,
                my_rows,
                leading_covariance,
                trailing_covariance,
                projection_masters,
                tokens_grad,
            )
        )
        tokens_grad = results.pop(5)
        return (layer_output, tokens_grad, *results)
    first_grad = dot_lanes(head_low, head_weights)
    unit, scale = centered(patch_embeddings.astype(F32))
    incoming_tokens_grad = (dx1 + norm_back(first_grad * table[0], unit, scale)).astype(BF16)
    mixing_table = mixing_table.at[0].set(jnp.sum(first_grad * unit, axis=0))
    mixing_table = mixing_table.at[1].set(jnp.sum(first_grad, axis=0))
    sharpness_share = mixing_table[14, 0:HEAD_NUMBER]
    table_grad = jnp.stack([(mixing_table, feed_table)[source][row] for source, row in TABLE_ROWS])
    block_grad = jnp.concatenate([mixing_grad, feed_grad[0]], axis=0).astype(F32)
    denominator_sum = lax.axis_size("fsdp")
    tiled_part = jnp.broadcast_to(
        sharpness_share[None, :], (denominator_sum, sharpness_share.shape[0])
    )
    portion_derivative, catalog_portion, sharpness_normalizer = (
        lax.psum_scatter(block_grad, "fsdp", scatter_dimension=1, tiled=True),
        lax.psum_scatter(table_grad, "fsdp", scatter_dimension=1, tiled=True),
        lax.psum_scatter(tiled_part, "fsdp", scatter_dimension=0, tiled=True),
    )
    portion_derivative, catalog_portion, sharpness_normalizer = lax.psum(
        (portion_derivative, catalog_portion, sharpness_normalizer), "dp"
    )
    sharpness_derivative = sharpness_normalizer[0]
    shard_place = lax.axis_index("fsdp")
    slot_index = jnp.arange(denominator_sum * slot_count, dtype=jnp.int32)
    slot_match = storage_position_map[None, :] == slot_index[:, None]
    slot_filled = jnp.any(slot_match, axis=1).astype(jnp.float32)[:, None, None]
    slot_block = jnp.sum(
        jnp.where(slot_match, jnp.arange(block_count, dtype=jnp.int32)[None, :], 0), axis=1
    )
    my_filled = lax.dynamic_slice_in_dim(slot_filled, shard_place * slot_count, slot_count, 0)
    my_block = lax.dynamic_slice_in_dim(slot_block, shard_place * slot_count, slot_count, 0)
    whole_grad = lax.all_gather(portion_derivative, "fsdp", axis=1, tiled=True)
    owned_grad = jnp.take(whole_grad, my_block, axis=0) * my_filled
    leading_covariance_renewed = covariance_forgetting * leading_covariance + (
        1.0 - covariance_forgetting
    ) * jnp.einsum("sij,skj->sik", owned_grad, owned_grad, precision=lax.Precision.HIGHEST)
    trailing_covariance_renewed = covariance_forgetting * trailing_covariance + (
        1.0 - covariance_forgetting
    ) * jnp.einsum("sji,sjk->sik", owned_grad, owned_grad, precision=lax.Precision.HIGHEST)
    halfway = jnp.einsum(
        "sij,sjk->sik", leading_root_preconditioner, owned_grad, precision=lax.Precision.HIGHEST
    )
    conditioned = jnp.einsum(
        "sij,sjk->sik", halfway, trailing_root_preconditioner, precision=lax.Precision.HIGHEST
    )
    every_update = lax.all_gather(conditioned, "fsdp", axis=0, tiled=True)
    my_rows = lax.dynamic_slice_in_dim(every_update, shard_place * shard_rows, shard_rows, 1)
    update = jnp.take(my_rows, storage_position_map, axis=0)
    projection_updated = projection_masters - weight_rate * update
    channel_energy_renewed = (
        covariance_forgetting * channel_energy_average
        + (1.0 - covariance_forgetting) * catalog_portion * catalog_portion
    )
    channel_params_updated = channel_coefficients - vector_rate * catalog_portion / (
        jnp.sqrt(channel_energy_renewed) + energy_epsilon
    )
    sharpness_energy_renewed = (
        covariance_forgetting * sharpness_energy_average
        + (1.0 - covariance_forgetting) * sharpness_derivative * sharpness_derivative
    )
    sharpness_updated = head_sharpness - sharpness_step_size * sharpness_derivative / (
        jnp.sqrt(sharpness_energy_renewed) + energy_epsilon
    )
    return (
        layer_output,
        incoming_tokens_grad,
        portion_derivative,
        leading_covariance_renewed,
        trailing_covariance_renewed,
        projection_updated,
        projection_updated.astype(jnp.bfloat16),
        catalog_portion,
        channel_energy_renewed,
        channel_params_updated,
        sharpness_derivative,
        sharpness_energy_renewed,
        sharpness_updated,
    )


def solution(mesh):
    in_specs = (
        P(("dp", "fsdp"), None),
        P(("dp", "fsdp")),
        P(None, "fsdp", None),
        P(None, "fsdp"),
        P(),
        P(("dp", "fsdp"), None),
        P("fsdp", None, None),
        P("fsdp", None, None),
        P("fsdp", None, None),
        P("fsdp", None, None),
        P(None, "fsdp"),
        P(),
        P(),
    )
    out_specs = (
        P(("dp", "fsdp"), None),
        P(("dp", "fsdp"), None),
        P(None, "fsdp", None),
        P("fsdp", None, None),
        P("fsdp", None, None),
        P(None, "fsdp", None),
        P(None, "fsdp", None),
        P(None, "fsdp"),
        P(None, "fsdp"),
        P(None, "fsdp"),
        P(),
        P(),
        P(),
    )
    return jax.shard_map(shards, mesh=mesh, in_specs=in_specs, out_specs=out_specs, check_vma=False)
```
